128 devices in a mesh: row: 4 (over x_hi, core), col: 32 (over x_lo, z, y).
Axes of the slice: x: 4 (x_hi: 2, x_lo: 2; x = x_hi * 2 + x_lo), y: 4, z: 4, core: 2. Of those that a mesh axis runs over, the one named last changes fastest.
Arguments:
- block_in: bfloat16 [32, 512, 2048], P('col', 'row'), may hold values from -6 to 6
- gain_attn: float32 [2048], replicated, may hold values from 0.25 to 1.75
- w_query: bfloat16 [2048, 2048], P('col', 'row'), may hold values from -0.125 to 0.125
- w_keyval: bfloat16 [2048, 4, 256], P('col', 'row'), may hold values from -0.125 to 0.125
- w_out: bfloat16 [2048, 2048], P('col', 'row'), may hold values from -0.5 to 0.5
- gain_ffn: float32 [2048], replicated, may hold values from 0.25 to 1.75
- w_shared_in: bfloat16 [2048, 2, 512], P('col', None, 'row'), may hold values from -0.125 to 0.125
- w_shared_out: bfloat16 [2048, 512], P('col', 'row'), may hold values from -0.5 to 0.5
- w_router: bfloat16 [2048, 256], replicated, may hold values from -0.0625 to 0.0625
- w_expert_in: bfloat16 [256, 2048, 1024], P(('row', 'col')), may hold values from -0.125 to 0.125
- w_expert_out: bfloat16 [256, 2048, 512], P(('row', 'col')), may hold values from -1 to 1
- doc_lengths: int32 [32, 4], P('col'), may hold values from 1 to 385, 512 in all within a row
- routes: int32 [32, 512, 8], P('col', 'row'), may hold values from 0 to 255, all different within a row; in each aligned block of 128 rows (0 to 127, 128 to 255, ..., all dimensions but the last counted through in order) at most 6 rows name the same one
- cotangent: bfloat16 [32, 512, 2048], P('col', 'row'), may hold values from -6 to 6
Outputs:
- block_out: bfloat16 [32, 512, 2048], P('col', 'row')
- grad_input: float32 [32, 512, 2048], P('col', 'row')
- grad_gain_attn: float32 [2048], replicated
- grad_query: float32 [2048, 2048], P('col', 'row')
- grad_keyval: float32 [2048, 4, 256], P('col', 'row')
- grad_out: float32 [2048, 2048], P('col', 'row')
- grad_gain_ffn: float32 [2048], replicated
- grad_shared_in: float32 [2048, 2, 512], P('col', None, 'row')
- grad_shared_out: float32 [2048, 512], P('col', 'row')
- grad_router: float32 [2048, 256], replicated
- grad_expert_in: float32 [256, 2048, 1024], P(('row', 'col'))
- grad_expert_out: float32 [256, 2048, 512], P(('row', 'col'))
The draws below stay inside these ranges and needn't reach their ends.
Inputs may be any that keep to these rules, and one draw needn't show every extreme that they name: Among the routes of the 128 tokens of one device (groups and rows in order) no expert is named more than 6 times. `doc_lengths`: each group's documents fill its 512 tokens in order; the longest has 385 tokens.
All inputs are finite; a program needn't handle non-finite values.
Results may differ from the reference program's by a relative error of at most 0.028.
Values may be sent and summed in bfloat16 or wider, within the bound.
A program may use at most 256 MiB of HBM per device.

```python
import math
import jax
import jax.numpy as jnp
import numpy as np
from jax import lax

D = 2048
HEADS = 16
KVH = 4
HD = 128
SFF = 512
EFF = 512
TOP = 8
TOK_DEV = 128
NDOC = 4
GROUP_TOK = 512
GROUPS = 32
EXPERTS = 256
CAP = 6


def level_of(key, shape, cuts, smallest, top_value):
    loudness, own = 1.0, jax.random.fold_in(key, 6)
    for axis_at, blocks in cuts:
        steps = jnp.exp(jax.random.uniform(jax.random.fold_in(own, axis_at), (blocks,), jnp.float32, smallest / len(cuts), top_value / len(cuts)))
        loudness = loudness * jnp.repeat(steps, shape[axis_at] // blocks).reshape([-1 if axis == axis_at else 1 for axis in range(len(shape))])
    return loudness


def length_profile(number_of, total, reach, skew):
    loads = [(1 << 20) // math.isqrt(rank ** skew) + 1 for rank in range(2, number_of + 1)]
    spare, holding = total - reach - (number_of - 1), [1] * (number_of - 1)
    while spare > 0:
        candidates = [i for i in range(number_of - 1) if holding[i] < reach]
        pool, budget = sum([loads[i] for i in candidates]), spare
        for i in candidates:
            more = min(reach - holding[i], max(1, budget * loads[i] // pool), spare)
            holding[i] = holding[i] + more
            spare = spare - more
    return np.array([reach] + holding)


def uneven(stream_key, number_of, total, reach, skew):
    if number_of == 2:
        one = jax.random.randint(stream_key, (), max(1, total - reach), min(reach, total - 1) + 1)
        return jnp.stack([one, total - one])
    sizes = jnp.asarray(length_profile(number_of, total, reach, skew), jnp.int32)
    twos = (number_of - 1) // 2
    giver, sink = sizes[1:1 + 2 * twos:2], sizes[2:2 + 2 * twos:2]
    room = jnp.minimum(giver - 1, reach - sink)
    moved = jax.random.randint(jax.random.fold_in(stream_key, 1), (twos,), 0, 1 << 20) % (room + 1)
    sizes = sizes.at[1:1 + 2 * twos:2].set(giver - moved).at[2:2 + 2 * twos:2].set(sink + moved)
    return sizes[jax.random.permutation(jax.random.fold_in(stream_key, 2), number_of)]


def deal_out(own_key, own, number, rows, amount, top, most, skew):
    sequence = jax.random.permutation(own_key, amount)
    packed, ordinary = portions_of(amount, rows * top, most, skew, True), portions_of(amount, rows * top, most, skew, False)
    places = jnp.arange(amount)

    def named(sizes, offset_by):
        used = int((sizes > 0).sum())
        fixed = max(1, used // 4)
        shifted = fixed + (places - fixed + offset_by * (used - fixed)) % max(1, amount - fixed)
        return jnp.zeros((amount,), jnp.int32).at[sequence[jnp.where(places < fixed, places, shifted)]].set(jnp.asarray(sizes, jnp.int32))

    sizes = jnp.where(number % 4 == 0, named(packed, number // 4), named(ordinary, number - number // 4 - 1))
    mixed = jax.random.permutation(jax.random.fold_in(own, 3), amount)
    donor, receiver = mixed[0:amount // 2 * 2:2], mixed[1:amount // 2 * 2:2]
    room = jnp.minimum(sizes[donor] - 1, most - sizes[receiver]) // 2
    room = jnp.where((donor == sequence[0]) | (receiver == sequence[0]) | (sizes[receiver] == 0), 0, jnp.maximum(room, 0))
    shifted = jax.random.randint(jax.random.fold_in(own, 4), (amount // 2,), 0, 1 << 20) % (room + 1)
    sizes = sizes.at[donor].add(-shifted).at[receiver].add(shifted)
    members = jnp.searchsorted(jnp.cumsum(sizes), jnp.arange(rows * top), side="right").astype(jnp.int32)
    grid = members.reshape(top, rows).T
    grid = grid[jax.random.permutation(jax.random.fold_in(own, 1), rows)]
    offset_by = jax.random.randint(jax.random.fold_in(own, 2), (rows, 1), 0, top)
    return jnp.take_along_axis(grid, (jnp.arange(top)[None, :] + offset_by) % top, axis=1)


def portions_of(count, total, bound, skew, full):
    weights = [(1 << 20) // math.isqrt(standing ** skew) + 1 for standing in range(1, count + 1)]
    largest = bound if full else min(bound, max(-(-total // count), total * weights[0] // sum(weights)))
    least = 1 if total - largest >= count - 1 else 0
    given, surplus = [largest] + [least] * (count - 1), total - largest - least * (count - 1)
    while surplus > 0:
        free = [i for i in range(1, count) if given[i] < largest] or [i for i in range(1, count) if given[i] < bound]
        mass, left = sum([weights[i] for i in free]), surplus
        for i in free:
            more = min(bound - given[i], max(1, left * weights[i] // mass), surplus)
            given[i] = given[i] + more
            surplus = surplus - more
    return np.array(given)


def noise(stream_key, extent, scale, reach, cuts=(), held_as=jnp.bfloat16):
    result = scale * jax.random.normal(stream_key, extent, jnp.float32)
    if cuts:
        result = result * level_of(stream_key, extent, cuts, -0.22, 0.18)
    return jnp.clip(result, -reach, reach).astype(held_as)


def setup_inputs(seed: int = 0) -> dict:
    streams_of = jax.random.split(jax.random.key(seed), 15)
    block_in = noise(streams_of[0], (GROUPS, GROUP_TOK, D), 1.0, 6.0, ((0, 32), (1, 4)))
    gain_attn = jnp.clip(1.0 + 0.15 * jax.random.normal(streams_of[1], (D,), jnp.float32), 0.25, 1.75)
    w_query = noise(streams_of[2], (D, HEADS * HD), D ** -0.5, 0.125, ((0, 32), (1, 4)))
    w_keyval = noise(streams_of[3], (D, KVH, 2 * HD), D ** -0.5, 0.125, ((0, 32), (1, 4)))
    w_out = noise(streams_of[4], (D, HEADS * HD), (HEADS * HD // 16) ** -0.5, 0.5, ((0, 32), (1, 4)))
    gain_ffn = jnp.clip(1.0 + 0.15 * jax.random.normal(streams_of[5], (D,), jnp.float32), 0.25, 1.75)
    w_shared_in = noise(streams_of[6], (D, 2, SFF), D ** -0.5, 0.125, ((0, 32), (2, 4)))
    w_shared_out = noise(streams_of[7], (D, SFF), (SFF // 4) ** -0.5, 0.5, ((0, 32), (1, 4)))
    w_router = noise(streams_of[8], (D, EXPERTS), (4 * D) ** -0.5, 0.0625)
    w_expert_in = noise(streams_of[9], (EXPERTS, D, 2 * EFF), D ** -0.5, 0.125, ((0, 128),))
    w_expert_out = noise(streams_of[10], (EXPERTS, D, EFF), (EFF // 16) ** -0.5, 1.0, ((0, 128),))
    doc_lengths = jax.vmap(lambda own: uneven(own, NDOC, GROUP_TOK, 3 * TOK_DEV + 1, 2))(jax.random.split(streams_of[11], GROUPS)).reshape((GROUPS, NDOC)).astype(jnp.int32)
    routes_keys = jax.random.split(jax.random.fold_in(streams_of[12], 1), GROUPS * GROUP_TOK // TOK_DEV)
    routes_turns = jax.random.permutation(jax.random.fold_in(streams_of[12], 3), GROUPS * GROUP_TOK // TOK_DEV)
    routes = jax.vmap(lambda own, number: deal_out(jax.random.fold_in(streams_of[12], 2), own, number, TOK_DEV, EXPERTS, TOP, CAP, 1))(routes_keys, routes_turns).reshape((GROUPS, GROUP_TOK, TOP))
    cotangent = noise(streams_of[13], (GROUPS, GROUP_TOK, D), 1.0, 6.0, ((0, 32), (1, 4)))
    return {"block_in": block_in, "gain_attn": gain_attn, "w_query": w_query, "w_keyval": w_keyval, "w_out": w_out, "gain_ffn": gain_ffn, "w_shared_in": w_shared_in, "w_shared_out": w_shared_out, "w_router": w_router, "w_expert_in": w_expert_in, "w_expert_out": w_expert_out, "doc_lengths": doc_lengths, "routes": routes, "cotangent": cotangent}


@jax.custom_vjp
def low(v):
    return lax.optimization_barrier(v.astype(jnp.bfloat16)).astype(jnp.float32)

@jax.custom_vjp
def low_back(v):
    return v

def low_keep(v):
    return (low(v), None)

def low_pass(kept, grad):
    return (grad,)

def back_keep(v):
    return (v, None)

def back_low(kept, grad):
    return (low(grad),)
low.defvjp(low_keep, low_pass)
low_back.defvjp(back_keep, back_low)
epsilon = 1e-06
rope_base = 10000.0
masked_score = -1e+30

def product(matrix, partner):
    return jnp.matmul(matrix, partner, precision=lax.Precision.HIGHEST)

def layout(lengths, token_count):
    bounds = jnp.cumsum(lengths).astype(jnp.int32)
    places = jnp.arange(token_count, dtype=jnp.int32)
    segment = lax.optimization_barrier(jnp.sum((places[:, None] >= bounds[None, :]).astype(jnp.int32), axis=1)).astype(jnp.int32)
    starts = bounds - lengths
    owners = segment[:, None] == jnp.arange(lengths.shape[0], dtype=jnp.int32)[None, :]
    begins = lax.optimization_barrier(jnp.sum(jnp.where(owners, starts[None, :], 0), axis=1)).astype(jnp.int32)
    return (segment, places - begins)

def rotary(positions, head_size):
    half_size = head_size // 2
    spread = jnp.arange(half_size, dtype=jnp.float32) * (2.0 / head_size)
    frequency = rope_base ** (-spread)
    angles = positions.astype(jnp.float32)[:, None] * frequency[None, :]
    return (jnp.cos(angles), jnp.sin(angles))

def rotate(values, cosine, sine_table):
    half_size = values.shape[-1] // 2
    leading = values[..., :half_size]
    trailing = values[..., half_size:]
    cosine = cosine[:, None, :]
    sine_table = sine_table[:, None, :]
    return jnp.concatenate([leading * cosine - trailing * sine_table, trailing * cosine + leading * sine_table], axis=-1)

def slot_tables(routes):
    blocks = routes.reshape(-1, TOK_DEV * TOP)
    block_count = blocks.shape[0]
    onehot = (blocks[:, :, None] == jnp.arange(EXPERTS, dtype=jnp.int32)[None, None, :]).astype(jnp.int32)
    earlier = jnp.cumsum(onehot, axis=1).astype(jnp.int32) - onehot
    route_rank = lax.optimization_barrier(jnp.sum(earlier * onehot, axis=2)).astype(jnp.int32)
    owner = jnp.arange(block_count, dtype=jnp.int32)[:, None]
    slot_index = blocks * (block_count * CAP) + owner * CAP + route_rank
    token_index = owner * TOK_DEV + jnp.arange(TOK_DEV * TOP, dtype=jnp.int32)[None, :] // TOP
    slot_table = jnp.zeros((EXPERTS * block_count * CAP,), jnp.int32).at[slot_index.reshape(-1)].set(token_index.reshape(-1) + 1)
    slot_table = slot_table.reshape(EXPERTS, block_count * CAP)
    row_valid = (slot_table > 0).astype(jnp.float32)
    row_index = jnp.maximum(slot_table - 1, 0).astype(jnp.int32)
    return (slot_index.reshape(-1, TOP), row_index, row_valid)

def reference(block_in, gain_attn, w_query, w_keyval, w_out, gain_ffn, w_shared_in, w_shared_out, w_router, w_expert_in, w_expert_out, doc_lengths, routes, cotangent):
    slot_index, row_index, row_valid = slot_tables(routes)
    route_ids = routes.reshape(-1, TOP)

    def forward(inputs, gain_a, query_w, keyval_w, out_w, gain_f, shared_in_w, shared_out_w, router_w, expert_in_w, expert_out_w):
        rows_all = inputs.reshape(-1, D)
        scale_one = lax.rsqrt(lax.optimization_barrier(jnp.mean(rows_all * rows_all, axis=1, keepdims=True)) + epsilon)
        normed_one = low(rows_all * scale_one * gain_a)

        def group_attention(pieces):
            normed, lengths = pieces
            segment, position = layout(lengths, GROUP_TOK)
            cosine, sine_table = rotary(position, HD)
            query_pre = low_back(product(normed, query_w)).reshape(GROUP_TOK, HEADS, HD)
            keyval_pre = low_back(product(normed, keyval_w.reshape(D, KVH * 2 * HD))).reshape(GROUP_TOK, KVH, 2 * HD)
            query_rot = low(rotate(query_pre, cosine, sine_table))
            key_rows = low(rotate(keyval_pre[..., :HD], cosine, sine_table))
            value_rows = low(keyval_pre[..., HD:])
            block_rows = min(512, GROUP_TOK)
            places = jnp.arange(GROUP_TOK, dtype=jnp.int32)

            def block_attention(block_index):
                first_row = block_index * block_rows
                query_block = lax.dynamic_slice_in_dim(query_rot, first_row, block_rows, 0).reshape(block_rows, KVH, HEADS // KVH, HD)
                rows_here = first_row + jnp.arange(block_rows, dtype=jnp.int32)
                seg_rows = lax.dynamic_slice_in_dim(segment, first_row, block_rows, 0)
                allowed = (seg_rows[:, None] == segment[None, :]) & (rows_here[:, None] >= places[None, :])
                scores = low_back(jnp.einsum('qagd,kad->agqk', query_block, key_rows, precision=lax.Precision.HIGHEST) * HD ** (-0.5))
                scores = jnp.where(allowed[None, None], scores, masked_score)
                weights = jax.nn.softmax(scores, axis=3)
                blended = jnp.einsum('agqk,kad->qagd', low(weights), value_rows, precision=lax.Precision.HIGHEST)
                return low(low_back(blended.reshape(block_rows, HEADS * HD)))
            attended = lax.map(jax.checkpoint(block_attention), jnp.arange(GROUP_TOK // block_rows, dtype=jnp.int32))
            attended = attended.reshape(GROUP_TOK, HEADS * HD)
            return low_back(product(attended, out_w.T))
        attn_branch = lax.map(jax.checkpoint(group_attention), (normed_one.reshape(GROUPS, GROUP_TOK, D), doc_lengths))
        hidden_state = rows_all + attn_branch.reshape(-1, D)
        scale_two = lax.rsqrt(lax.optimization_barrier(jnp.mean(hidden_state * hidden_state, axis=1, keepdims=True)) + epsilon)
        normed_two = low(hidden_state * scale_two * gain_f)
        shared_pre = low_back(product(normed_two, shared_in_w.reshape(D, 2 * SFF))).reshape(-1, 2, SFF)
        shared_hidden = low(jax.nn.silu(shared_pre[:, 0]) * shared_pre[:, 1])
        shared_branch = product(shared_hidden, shared_out_w.T)
        logits = low_back(product(normed_two, router_w))
        picked = jnp.take_along_axis(logits, route_ids, axis=1)
        scores_sig = jax.nn.sigmoid(picked)
        gate_weights = scores_sig / lax.optimization_barrier(jnp.sum(scores_sig, axis=1, keepdims=True))

        def expert_apply(pieces):
            weights_in, weights_out, index_rows, valid_rows = pieces
            expert_input = low_back(normed_two[index_rows] * valid_rows[:, None])
            expert_pre = low_back(product(expert_input, weights_in))
            expert_hidden = low(jax.nn.silu(expert_pre[:, :EFF]) * expert_pre[:, EFF:])
            return low(low_back(product(expert_hidden, weights_out.T)))
        expert_out = lax.map(jax.checkpoint(expert_apply), (expert_in_w, expert_out_w, row_index, row_valid)).reshape(-1, D)
        routed_branch = jnp.zeros_like(rows_all)
        for route_pos in range(TOP):
            routed_branch = routed_branch + gate_weights[:, route_pos:route_pos + 1] * expert_out[slot_index[:, route_pos]]
        return (hidden_state + shared_branch + routed_branch).reshape(GROUPS, GROUP_TOK, D)
    block_sum, pull_back = jax.vjp(forward, block_in.astype(jnp.float32), gain_attn.astype(jnp.float32), w_query.astype(jnp.float32), w_keyval.astype(jnp.float32), w_out.astype(jnp.float32), gain_ffn.astype(jnp.float32), w_shared_in.astype(jnp.float32), w_shared_out.astype(jnp.float32), w_router.astype(jnp.float32), w_expert_in.astype(jnp.float32), w_expert_out.astype(jnp.float32))
    grads = pull_back(cotangent.astype(jnp.float32))
    return (block_sum.astype(jnp.bfloat16), grads[0], grads[1], grads[2], grads[3], grads[4], grads[5], grads[6], grads[7], grads[8], grads[9], grads[10])
```

```python
import functools

import jax
import jax.numpy as jnp
from jax import lax
from jax.experimental import pallas as pl
from jax.experimental.pallas import tpu as pltpu
from jax.sharding import PartitionSpec as P

epsilon = 1e-06
rope_base = 10000.0
masked_score = -1e30


def layout(lengths, token_count):
    bounds = jnp.cumsum(lengths)
    places = jnp.arange(token_count, dtype=jnp.int32)
    segment = jnp.sum((places[:, None] >= bounds[None, :]).astype(jnp.int32), axis=1)
    starts = bounds - lengths
    owners = segment[:, None] == jnp.arange(lengths.shape[0], dtype=jnp.int32)[None, :]
    begins = jnp.sum(jnp.where(owners, starts[None, :], 0), axis=1)
    return (segment, places - begins)


def rotary(positions, head_size):
    half_size = head_size // 2
    spread = jnp.arange(half_size, dtype=jnp.float32) * (2.0 / head_size)
    frequency = rope_base ** (-spread)
    angles = positions.astype(jnp.float32)[:, None] * frequency[None, :]
    return (jnp.cos(angles), jnp.sin(angles))


def rotate(values, cosine, sine_table):
    half_size = values.shape[-1] // 2
    leading = values[..., :half_size]
    trailing = values[..., half_size:]
    cosine = cosine[:, None, :]
    sine_table = sine_table[:, None, :]
    return jnp.concatenate(
        [leading * cosine - trailing * sine_table, trailing * cosine + leading * sine_table],
        axis=-1,
    )


def normalize(values, gain):
    factor = lax.rsqrt(jnp.mean(values * values, axis=1, keepdims=True) + epsilon)
    return (factor, (values * factor * gain).astype(jnp.bfloat16))


def norm_back(values, factor, gain, incoming):
    weighted = gain * incoming
    gain_grad = jnp.sum(incoming * values * factor, axis=0)
    input_grad = factor * weighted - values * factor**3 * jnp.mean(
        weighted * values, axis=1, keepdims=True
    )
    return (gain_grad, input_grad)


def swish_parts(pre_act):
    logistic = jax.nn.sigmoid(pre_act)
    return (pre_act * logistic, logistic * (1.0 + pre_act * (1.0 - logistic)))


def matmul(matrix, partner):
    return jnp.dot(matrix, partner, preferred_element_type=jnp.float32)


def matmul_t(matrix, partner):
    return lax.dot_general(
        matrix, partner, (((1,), (1,)), ((), ())), preferred_element_type=jnp.float32
    )


def outer_sum(matrix, partner):
    return lax.dot_general(
        matrix, partner, (((0,), (0,)), ((), ())), preferred_element_type=jnp.float32
    )


def push_kernel(count, *refs):
    sources, targets = refs[:count], refs[count : 2 * count]
    send_sem, recv_sem, own_sem = refs[2 * count :]
    members = targets[0].shape[0]
    row, me = lax.axis_index("row"), lax.axis_index("col")
    barrier = pltpu.get_barrier_semaphore()

    def greet(step, carry):
        peer = lax.rem(me + step, members)
        pl.semaphore_signal(
            barrier, inc=1, device_id=(row, peer), device_id_type=pl.DeviceIdType.MESH
        )
        return carry

    lax.fori_loop(1, members, greet, 0)
    own = [
        pltpu.make_async_copy(sources[i], targets[i].at[me], own_sem.at[i]) for i in range(count)
    ]
    for copy in own:
        copy.start()
    pl.semaphore_wait(barrier, members - 1)
    for i in range(count):

        def push(step, carry, i=i):
            peer = lax.rem(me + step, members)
            pltpu.make_async_remote_copy(
                src_ref=sources[i],
                dst_ref=targets[i].at[me],
                send_sem=send_sem.at[i],
                recv_sem=recv_sem.at[i],
                device_id=(row, peer),
                device_id_type=pl.DeviceIdType.MESH,
            ).start()
            return carry

        lax.fori_loop(1, members, push, 0)
    for copy in own:
        copy.wait()
    for i in range(count):
        others = targets[i].at[pl.ds(0, members - 1)]
        pltpu.make_async_copy(others, others, recv_sem.at[i]).wait()
        pltpu.make_async_copy(others, others, send_sem.at[i]).wait()


def gather_weights(shards):
    members = lax.axis_size("col")
    count = len(shards)
    space = pl.BlockSpec(memory_space=pl.ANY)
    return pl.pallas_call(
        functools.partial(push_kernel, count),
        out_shape=[
            jax.ShapeDtypeStruct((members, *shard.shape), shard.dtype) for shard in shards
        ],
        in_specs=[space] * count,
        out_specs=[space] * count,
        scratch_shapes=[pltpu.SemaphoreType.DMA((count,))] * 3,
        compiler_params=pltpu.CompilerParams(collective_id=0, has_side_effects=True),
        name="gather_weights",
    )(*shards)


def scatter_sum(values):
    members = lax.axis_size("col")
    parts = values.reshape(members, values.shape[0] // members, values.shape[1])
    parts = lax.all_to_all(parts, "col", split_axis=0, concat_axis=0, tiled=True)
    return jnp.sum(parts, axis=0, dtype=jnp.float32)


def group_rows(values):
    return lax.all_gather(values, "row", axis=0, tiled=True)


def group_sums(producer, rows_dev):
    return lax.psum_scatter(
        producer(jnp.int32(0), lax.axis_size("row") * rows_dev),
        "row",
        scatter_dimension=0,
        tiled=True,
    )


def to_experts(values):
    return lax.all_to_all(values, ("row", "col"), split_axis=0, concat_axis=1, tiled=True)


def from_experts(values):
    return lax.all_to_all(values, ("row", "col"), split_axis=1, concat_axis=0, tiled=True)


def per_device(
    block_in,
    gain_attn,
    w_query,
    w_keyval,
    w_out,
    gain_ffn,
    w_shared_in,
    w_shared_out,
    w_router,
    w_expert_in,
    w_expert_out,
    doc_lengths,
    routes,
    cotangent,
):
    row_count = lax.axis_size("row")
    rows_dev = block_in.shape[1]
    model_width = block_in.shape[2]
    group_tok = rows_dev * row_count
    head_size = w_keyval.shape[2] // 2
    local_heads = w_query.shape[1] // head_size
    local_kv = w_keyval.shape[1]
    group_size = local_heads // local_kv
    expert_count = w_router.shape[1]
    expert_ff = w_expert_out.shape[2]
    top_k = routes.shape[2]
    capacity = max(2, 3 * rows_dev * top_k // (2 * expert_count))
    block_rows = min(512, group_tok)
    block_total = group_tok // block_rows
    inv_root = head_size ** (-0.5)
    inputs = block_in.reshape(rows_dev, model_width).astype(jnp.float32)
    gathered = gather_weights(
        [
            w_query,
            w_keyval.reshape(w_keyval.shape[0], -1),
            w_out,
            w_shared_in.reshape(w_shared_in.shape[0], -1),
            w_shared_out,
        ]
    )
    full_query, full_out, full_shared_out = (
        gathered[i].reshape(-1, gathered[i].shape[2]) for i in (0, 2, 4)
    )
    full_keyval = gathered[1].reshape(-1, *w_keyval.shape[1:])
    full_shared_in = gathered[3].reshape(-1, *w_shared_in.shape[1:])
    scale_one, normed_one = normalize(inputs, gain_attn)
    group_one = group_rows(normed_one)
    segment, position = layout(doc_lengths.reshape(-1), group_tok)
    cosine, sine_table = rotary(position, head_size)
    query_pre = matmul(group_one, full_query).reshape(group_tok, local_heads, head_size)
    query_rot = rotate(query_pre, cosine, sine_table).astype(jnp.bfloat16)
    keyval_pre = jnp.einsum(
        "td,dah->tah", group_one, full_keyval, preferred_element_type=jnp.float32
    )
    key_rows = rotate(keyval_pre[..., :head_size], cosine, sine_table).astype(jnp.bfloat16)
    value_rows = keyval_pre[..., head_size:].astype(jnp.bfloat16)
    places = jnp.arange(group_tok, dtype=jnp.int32)

    def block_scores(block_index):
        first_row = block_index * block_rows
        query_block = query_rot.reshape(block_rows, local_kv, group_size, head_size)
        rows_here = first_row + jnp.arange(block_rows, dtype=jnp.int32)
        allowed = (segment[:, None] == segment[None, :]) & (rows_here[:, None] >= places[None, :])
        scores = (
            jnp.einsum("qagd,kad->agqk", query_block, key_rows, preferred_element_type=jnp.float32)
            * inv_root
        )
        return (query_block, jnp.where(allowed[None, None], scores, masked_score))

    def attend_block(block_index):
        query_block, scores = block_scores(block_index)
        highest = jnp.max(scores, axis=3, keepdims=True)
        weights = jnp.exp(scores - highest)
        totals = jnp.sum(weights, axis=3, keepdims=True)
        weights_low = (weights / totals).astype(jnp.bfloat16)
        blended = jnp.einsum(
            "agqk,kad->qagd", weights_low, value_rows, preferred_element_type=jnp.float32
        )
        return (
            blended.reshape(block_rows, local_heads * head_size).astype(jnp.bfloat16),
            highest + jnp.log(totals),
        )

    attended, log_totals = lax.map(attend_block, jnp.arange(block_total, dtype=jnp.int32))
    attended = attended.reshape(group_tok, local_heads * head_size)

    def attn_term(offset, amount):
        return matmul_t(attended, full_out)

    hidden_state = inputs + group_sums(attn_term, rows_dev)
    scale_two, normed_two = normalize(hidden_state, gain_ffn)
    group_two = group_rows(normed_two)
    shared_pre = jnp.einsum(
        "td,dcf->tcf", group_two, full_shared_in, preferred_element_type=jnp.float32
    )
    shared_act, shared_slope = swish_parts(shared_pre[:, 0])
    shared_hidden = (shared_act * shared_pre[:, 1]).astype(jnp.bfloat16)

    def shared_term(offset, amount):
        return matmul_t(shared_hidden, full_shared_out)

    shared_branch = group_sums(shared_term, rows_dev)
    route_ids = routes.reshape(rows_dev, top_k)
    logits = matmul(normed_two, w_router)
    chosen = route_ids[:, :, None] == jnp.arange(expert_count, dtype=jnp.int32)[None, None, :]
    picked = jnp.sum(jnp.where(chosen, logits[:, None, :], 0.0), axis=2)
    scores_sig = jax.nn.sigmoid(picked)
    score_sum = jnp.sum(scores_sig, axis=1, keepdims=True)
    gate_weights = scores_sig / score_sum
    flat_routes = route_ids.reshape(-1)
    onehot = (flat_routes[:, None] == jnp.arange(expert_count, dtype=jnp.int32)[None, :]).astype(
        jnp.int32
    )
    earlier = jnp.cumsum(onehot, axis=0) - onehot
    route_rank = jnp.sum(earlier * onehot, axis=1)
    slot_index = flat_routes * capacity + route_rank
    slot_table = (
        jnp.zeros((expert_count * capacity,), jnp.int32)
        .at[slot_index]
        .set(jnp.arange(rows_dev * top_k, dtype=jnp.int32) + 1)
    )
    filled = slot_table > 0
    route_of = jnp.maximum(slot_table - 1, 0)
    zero_low = jnp.zeros((), jnp.bfloat16)
    send_rows = jnp.where(filled[:, None], normed_two[route_of // top_k], zero_low).reshape(
        expert_count, capacity, model_width
    )
    received = to_experts(send_rows)
    expert_pre = jnp.einsum(
        "esd,edf->esf", received, w_expert_in, preferred_element_type=jnp.float32
    )
    expert_act, expert_slope = swish_parts(expert_pre[..., :expert_ff])
    expert_hidden = (expert_act * expert_pre[..., expert_ff:]).astype(jnp.bfloat16)
    expert_out = jnp.einsum(
        "esf,edf->esd", expert_hidden, w_expert_out, preferred_element_type=jnp.float32
    ).astype(jnp.bfloat16)
    returned = from_experts(expert_out).reshape(expert_count * capacity, model_width)
    per_route = returned[slot_index].reshape(rows_dev, top_k, model_width)
    routed_branch = jnp.sum(gate_weights[:, :, None] * per_route, axis=1)
    block_out = (hidden_state + shared_branch + routed_branch).astype(jnp.bfloat16)
    grad_low = cotangent.reshape(rows_dev, model_width)
    grad_rows = grad_low.astype(jnp.float32)
    gate_grad = jnp.sum(grad_rows[:, None, :] * per_route, axis=2)
    score_grad = (gate_grad - jnp.sum(gate_grad * gate_weights, axis=1, keepdims=True)) / score_sum
    picked_grad = score_grad * scores_sig * (1.0 - scores_sig)
    logit_grad = jnp.sum(jnp.where(chosen, picked_grad[:, :, None], 0.0), axis=1).astype(
        jnp.bfloat16
    )
    router_grad = outer_sum(normed_two, logit_grad)
    router_input = matmul_t(logit_grad, w_router)
    route_grad = (
        (gate_weights[:, :, None] * grad_rows[:, None, :])
        .reshape(rows_dev * top_k, model_width)
        .astype(jnp.bfloat16)
    )
    send_grad = jnp.where(filled[:, None], route_grad[route_of], zero_low).reshape(
        expert_count, capacity, model_width
    )
    received_grad = to_experts(send_grad)
    hidden_grad = jnp.einsum(
        "esd,edf->esf", received_grad, w_expert_out, preferred_element_type=jnp.float32
    )
    grad_expert_out = jnp.einsum(
        "esd,esf->edf", received_grad, expert_hidden, preferred_element_type=jnp.float32
    )
    expert_pre_grad = jnp.concatenate(
        [hidden_grad * expert_pre[..., expert_ff:] * expert_slope, hidden_grad * expert_act], axis=2
    ).astype(jnp.bfloat16)
    grad_expert_in = jnp.einsum(
        "esd,esf->edf", received, expert_pre_grad, preferred_element_type=jnp.float32
    )
    slot_grad = jnp.einsum(
        "esf,edf->esd", expert_pre_grad, w_expert_in, preferred_element_type=jnp.float32
    ).astype(jnp.bfloat16)
    returned_grad = from_experts(slot_grad).reshape(expert_count * capacity, model_width)
    routed_input = jnp.sum(
        returned_grad[slot_index].reshape(rows_dev, top_k, model_width), axis=1, dtype=jnp.float32
    )
    group_grad = group_rows(grad_low)
    shared_hidden_grad = matmul(group_grad, full_shared_out)
    grad_shared_out = outer_sum(group_grad, shared_hidden)
    shared_pre_grad = jnp.stack(
        [shared_hidden_grad * shared_pre[:, 1] * shared_slope, shared_hidden_grad * shared_act],
        axis=1,
    ).astype(jnp.bfloat16)
    grad_shared_in = jnp.einsum(
        "td,tcf->dcf", group_two, shared_pre_grad, preferred_element_type=jnp.float32
    )

    def shared_back(offset, amount):
        return jnp.einsum(
            "tcf,dcf->td", shared_pre_grad, full_shared_in, preferred_element_type=jnp.float32
        )

    normed_two_grad = group_sums(shared_back, rows_dev) + router_input + routed_input
    gain_ffn_grad, hidden_back = norm_back(hidden_state, scale_two, gain_ffn, normed_two_grad)
    hidden_total = grad_rows + hidden_back
    branch_low = hidden_total.astype(jnp.bfloat16)
    group_branch = group_rows(branch_low)
    attended_grad = matmul(group_branch, full_out).astype(jnp.bfloat16)
    grad_out_w = outer_sum(group_branch, attended)

    def back_block(accums, block_index):
        key_acc, value_acc = accums
        query_block, scores = block_scores(block_index)
        out_block = attended_grad.reshape(block_rows, local_kv, group_size, head_size)
        probs_full = jnp.exp(scores - log_totals[block_index])
        prob_grad = jnp.einsum(
            "qagd,kad->agqk", out_block, value_rows, preferred_element_type=jnp.float32
        )
        row_delta = jnp.sum(probs_full * prob_grad, axis=3, keepdims=True)
        score_low = (probs_full * (prob_grad - row_delta)).astype(jnp.bfloat16)
        query_grad = (
            jnp.einsum("agqk,kad->qagd", score_low, key_rows, preferred_element_type=jnp.float32)
            * inv_root
        )
        key_acc = (
            key_acc
            + jnp.einsum(
                "agqk,qagd->kad", score_low, query_block, preferred_element_type=jnp.float32
            )
            * inv_root
        )
        value_acc = value_acc + jnp.einsum(
            "agqk,qagd->kad",
            probs_full.astype(jnp.bfloat16),
            out_block,
            preferred_element_type=jnp.float32,
        )
        return ((key_acc, value_acc), query_grad.reshape(block_rows, local_heads, head_size))

    zeros_kv = jnp.zeros((group_tok, local_kv, head_size), jnp.float32)
    (key_grad, value_grad), query_grad = lax.scan(
        back_block, (zeros_kv, zeros_kv), jnp.arange(block_total, dtype=jnp.int32)
    )
    query_grad = query_grad.reshape(group_tok, local_heads, head_size)
    query_pre_grad = (
        rotate(query_grad, cosine, -sine_table)
        .astype(jnp.bfloat16)
        .reshape(group_tok, local_heads * head_size)
    )
    keyval_pre_grad = jnp.concatenate(
        [rotate(key_grad, cosine, -sine_table), value_grad], axis=2
    ).astype(jnp.bfloat16)
    grad_query_w = outer_sum(group_one, query_pre_grad)
    grad_keyval_w = jnp.einsum(
        "td,tah->dah", group_one, keyval_pre_grad, preferred_element_type=jnp.float32
    )

    def attn_back(offset, amount):
        part_query = matmul_t(query_pre_grad, full_query)
        part_keyval = jnp.einsum(
            "tah,dah->td", keyval_pre_grad, full_keyval, preferred_element_type=jnp.float32
        )
        return part_query + part_keyval

    normed_one_grad = group_sums(attn_back, rows_dev)
    gain_attn_grad, input_back = norm_back(inputs, scale_one, gain_attn, normed_one_grad)
    input_total = hidden_total + input_back
    sum_first = scatter_sum(
        jnp.concatenate(
            [
                grad_out_w.astype(jnp.bfloat16),
                grad_shared_in.reshape(model_width, -1).astype(jnp.bfloat16),
                grad_shared_out.astype(jnp.bfloat16),
            ],
            axis=1,
        )
    )
    sum_last = scatter_sum(
        jnp.concatenate(
            [
                grad_query_w.astype(jnp.bfloat16),
                grad_keyval_w.reshape(model_width, -1).astype(jnp.bfloat16),
            ],
            axis=1,
        )
    )
    out_end = w_out.shape[1]
    in_end = out_end + w_shared_in.shape[1] * w_shared_in.shape[2]
    sum_out = sum_first[:, :out_end]
    sum_shared_in = sum_first[:, out_end:in_end].reshape(w_shared_in.shape)
    sum_shared_out = sum_first[:, in_end:]
    sum_query = sum_last[:, : w_query.shape[1]]
    sum_keyval = sum_last[:, w_query.shape[1] :].reshape(w_keyval.shape)
    router_sum = lax.psum(router_grad, ("row", "col"))
    gain_attn_sum, gain_ffn_sum = lax.psum((gain_attn_grad, gain_ffn_grad), ("row", "col"))
    return (
        block_out.reshape(1, rows_dev, model_width),
        input_total.reshape(1, rows_dev, model_width),
        gain_attn_sum,
        sum_query,
        sum_keyval,
        sum_out,
        gain_ffn_sum,
        sum_shared_in,
        sum_shared_out,
        router_sum,
        grad_expert_in,
        grad_expert_out,
    )


def solution(mesh):
    in_specs = (
        P("col", "row", None),
        P(),
        P("col", "row"),
        P("col", "row", None),
        P("col", "row"),
        P(),
        P("col", None, "row"),
        P("col", "row"),
        P(),
        P(("row", "col"), None, None),
        P(("row", "col"), None, None),
        P("col", None),
        P("col", "row", None),
        P("col", "row", None),
    )
    out_specs = (
        P("col", "row", None),
        P("col", "row", None),
        P(),
        P("col", "row"),
        P("col", "row", None),
        P("col", "row"),
        P(),
        P("col", None, "row"),
        P("col", "row"),
        P(),
        P(("row", "col"), None, None),
        P(("row", "col"), None, None),
    )
    return jax.shard_map(
        per_device, mesh=mesh, in_specs=in_specs, out_specs=out_specs, check_vma=False
    )
```

```python
import functools

import jax
import jax.numpy as jnp
from jax import lax
from jax.experimental import pallas as pl
from jax.experimental.pallas import tpu as pltpu
from jax.sharding import PartitionSpec as P

epsilon = 1e-06
rope_base = 10000.0
masked_score = -1e30

EXPERT_ROWS = 6
PAIR_ROWS = 12
PACKED_ROWS = 16
BLOCK_PAIRS = 16
BLOCK = BLOCK_PAIRS * PACKED_ROWS
BLOCK_EXPERTS = 2 * BLOCK_PAIRS
BLOCK_SLOTS = BLOCK_PAIRS * EXPERT_ROWS
QUARTER = 512
SIDE = 128
MESH = pl.DeviceIdType.MESH


def layout(lengths, token_count):
    bounds = jnp.cumsum(lengths)
    places = jnp.arange(token_count, dtype=jnp.int32)
    segment = jnp.sum((places[:, None] >= bounds[None, :]).astype(jnp.int32), axis=1)
    starts = bounds - lengths
    owners = segment[:, None] == jnp.arange(lengths.shape[0], dtype=jnp.int32)[None, :]
    begins = jnp.sum(jnp.where(owners, starts[None, :], 0), axis=1)
    return (segment, places - begins)


def rotary(positions, head_size):
    half_size = head_size // 2
    spread = jnp.arange(half_size, dtype=jnp.float32) * (2.0 / head_size)
    frequency = rope_base ** (-spread)
    angles = positions.astype(jnp.float32)[:, None] * frequency[None, :]
    return (jnp.cos(angles), jnp.sin(angles))


def rotate(values, cosine, sine_table):
    half_size = values.shape[-1] // 2
    leading = values[..., :half_size]
    trailing = values[..., half_size:]
    cosine = cosine[:, None, :]
    sine_table = sine_table[:, None, :]
    return jnp.concatenate(
        [leading * cosine - trailing * sine_table, trailing * cosine + leading * sine_table],
        axis=-1,
    )


def normalize(values, gain):
    factor = lax.rsqrt(jnp.mean(values * values, axis=1, keepdims=True) + epsilon)
    return (factor, (values * factor * gain).astype(jnp.bfloat16))


def norm_back(values, factor, gain, incoming):
    weighted = gain * incoming
    gain_grad = jnp.sum(incoming * values * factor, axis=0)
    input_grad = factor * weighted - values * factor**3 * jnp.mean(
        weighted * values, axis=1, keepdims=True
    )
    return (gain_grad, input_grad)


def swish_parts(pre_act):
    logistic = jax.nn.sigmoid(pre_act)
    return (pre_act * logistic, logistic * (1.0 + pre_act * (1.0 - logistic)))


def matmul(matrix, partner):
    return jnp.dot(matrix, partner, preferred_element_type=jnp.float32)


def matmul_t(matrix, partner):
    return lax.dot_general(
        matrix, partner, (((1,), (1,)), ((), ())), preferred_element_type=jnp.float32
    )


def outer_sum(matrix, partner):
    return lax.dot_general(
        matrix, partner, (((0,), (0,)), ((), ())), preferred_element_type=jnp.float32
    )


def split_low(values):
    high = values.astype(jnp.bfloat16)
    return high, (values - high.astype(jnp.float32)).astype(jnp.bfloat16)


def row_places():
    row, col = lax.axis_index("row"), lax.axis_index("col")
    chip, core = row // 2, lax.rem(row, 2)
    sibling = chip * 2 + (1 - core)
    partner = (1 - chip) * 2 + core
    across = (1 - chip) * 2 + (1 - core)
    return row, col, sibling, partner, across


def row_copies(sources, targets, send_sem, recv_sem):
    row, col, sibling, partner, _ = row_places()

    def send(origin, target, peer, i):
        return pltpu.make_async_remote_copy(
            src_ref=origin,
            dst_ref=target,
            send_sem=send_sem.at[i],
            recv_sem=recv_sem.at[i],
            device_id=(peer, col),
            device_id_type=MESH,
        )

    far, near, onward = [], [], []
    for i, (source, target) in enumerate(zip(sources, targets)):
        far.append(send(source, target.at[row], partner, 3 * i))
        near.append(send(source, target.at[row], sibling, 3 * i + 1))
        onward.append(send(target.at[partner], target.at[partner], sibling, 3 * i + 2))
    return far, near, onward


def greet(peers):
    barrier = pltpu.get_barrier_semaphore()
    for peer in peers:
        pl.semaphore_signal(barrier, inc=1, device_id=peer, device_id_type=MESH)


def await_greetings(count):
    pl.semaphore_wait(pltpu.get_barrier_semaphore(), count)


def row_gather_kernel(count, *refs):
    sources, targets = refs[:count], refs[count : 2 * count]
    send_sem, recv_sem, own_sem = refs[2 * count :]
    row, col, sibling, partner, _ = row_places()
    greet([(sibling, col), (partner, col)])
    own = [
        pltpu.make_async_copy(sources[i], targets[i].at[row], own_sem.at[i]) for i in range(count)
    ]
    for copy in own:
        copy.start()
    await_greetings(2)
    far, near, onward = row_copies(sources, targets, send_sem, recv_sem)
    for copy in far + near:
        copy.start()
    for first, second in zip(far, onward):
        first.wait_recv()
        second.start()
    for copy in own:
        copy.wait()
    for copy in far:
        copy.wait_send()
    for copy in near + onward:
        copy.wait()


def group_rows(values, call):
    count = len(values)
    space = pl.BlockSpec(memory_space=pl.ANY)
    gathered = pl.pallas_call(
        functools.partial(row_gather_kernel, count),
        out_shape=[jax.ShapeDtypeStruct((4, *part.shape), part.dtype) for part in values],
        in_specs=[space] * count,
        out_specs=[space] * count,
        scratch_shapes=[
            pltpu.SemaphoreType.DMA((3 * count,)),
            pltpu.SemaphoreType.DMA((3 * count,)),
            pltpu.SemaphoreType.DMA((count,)),
        ],
        compiler_params=pltpu.CompilerParams(collective_id=1 + call, has_side_effects=True),
        cost_estimate=pl.CostEstimate(flops=0, bytes_accessed=64 << 20, transcendentals=0),
        name="group_rows",
    )(*values)
    return [part.reshape(-1, part.shape[2]) for part in gathered]


def gather_kernel(shard, normed, grads, full, group_one, group_grad, *sems):
    send_sem, recv_sem, own_sem, row_send, row_recv = sems
    row, col, sibling, partner, _ = row_places()
    along_x, along_z, along_y = col // 16, lax.rem(col // 4, 4), lax.rem(col, 4)
    other_x = 1 - along_x
    half_rows = shard.shape[0] // 2

    def place(x, z, y):
        return x * 16 + z * 4 + y

    z_near = [lax.rem(along_z + i, 4) for i in (1, 3, 2)]
    y_near = [lax.rem(along_y + i, 4) for i in (1, 3, 2)]
    z_peers = [place(along_x, z, along_y) for z in z_near]
    y_peers = [place(along_x, along_z, y) for y in y_near]
    x_peer = place(other_x, along_z, along_y)
    greet([(row, peer) for peer in z_peers + y_peers + [x_peer]])
    greet([(sibling, col), (partner, col)])
    own = [
        pltpu.make_async_copy(shard, full.at[col], own_sem.at[0]),
        pltpu.make_async_copy(normed, group_one.at[row], own_sem.at[1]),
        pltpu.make_async_copy(grads, group_grad.at[row], own_sem.at[2]),
    ]
    for copy in own:
        copy.start()
    await_greetings(9)

    def pass_on(owner, half, peers, origin=None):
        rows = pl.ds(half * half_rows, half_rows)
        target = full.at[owner, rows]
        for peer in peers:
            pltpu.make_async_remote_copy(
                src_ref=target if origin is None else origin.at[rows],
                dst_ref=target,
                send_sem=send_sem,
                recv_sem=recv_sem.at[half * 32 + owner],
                device_id=(row, peer),
                device_id_type=MESH,
            ).start()

    def await_half(owner, half):
        target = full.at[owner, pl.ds(half * half_rows, half_rows)]
        pltpu.make_async_copy(target, target, recv_sem.at[half * 32 + owner]).wait()

    pass_on(col, 0, [x_peer], shard)
    pass_on(col, 1, [x_peer], shard)
    pass_on(col, 0, z_peers, shard)
    pass_on(col, 1, y_peers, shard)
    far, near, onward = row_copies([normed, grads], [group_one, group_grad], row_send, row_recv)
    far[0].start()
    near[0].start()
    await_half(x_peer, 0)
    pass_on(x_peer, 0, z_peers)
    await_half(x_peer, 1)
    pass_on(x_peer, 1, y_peers)
    pass_on(col, 0, y_peers, shard)
    pass_on(col, 1, z_peers, shard)
    pass_on(x_peer, 0, y_peers)
    pass_on(x_peer, 1, z_peers)
    far[1].start()
    near[1].start()
    for i in range(3):
        for x in (along_x, other_x):
            owner = place(x, z_near[i], along_y)
            await_half(owner, 0)
            pass_on(owner, 0, y_peers)
            owner = place(x, along_z, y_near[i])
            await_half(owner, 1)
            pass_on(owner, 1, z_peers)
    for first, second in zip(far, onward):
        first.wait_recv()
        second.start()
    for x in (along_x, other_x):
        for i in range(4):
            for j in range(3):
                await_half(place(x, lax.rem(along_z + i, 4), y_near[j]), 0)
                await_half(place(x, z_near[j], lax.rem(along_y + i, 4)), 1)
    for copy in own:
        copy.wait()
    for copy in far:
        copy.wait_send()
    for copy in near + onward:
        copy.wait()
    sent = full.at[pl.ds(0, 31)]
    pltpu.make_async_copy(sent, sent, send_sem).wait()


def gather_start(shard, normed, grads):
    space = pl.BlockSpec(memory_space=pl.ANY)
    full, group_one, group_grad = pl.pallas_call(
        gather_kernel,
        out_shape=[
            jax.ShapeDtypeStruct((32, *shard.shape), shard.dtype),
            jax.ShapeDtypeStruct((4, *normed.shape), normed.dtype),
            jax.ShapeDtypeStruct((4, *grads.shape), grads.dtype),
        ],
        in_specs=[space] * 3,
        out_specs=[space] * 3,
        scratch_shapes=[
            pltpu.SemaphoreType.DMA,
            pltpu.SemaphoreType.DMA((64,)),
            pltpu.SemaphoreType.DMA((3,)),
            pltpu.SemaphoreType.DMA((6,)),
            pltpu.SemaphoreType.DMA((6,)),
        ],
        compiler_params=pltpu.CompilerParams(collective_id=0, has_side_effects=True),
        cost_estimate=pl.CostEstimate(flops=0, bytes_accessed=200 << 20, transcendentals=0),
        name="gather_start",
    )(shard, normed, grads)
    return [part.reshape(-1, part.shape[2]) for part in (full, group_one, group_grad)]


def row_sum_kernel(parts, total, near, far, outgoing, send_sem, recv_sem):
    row, col, sibling, partner, across = row_places()
    barrier = pltpu.get_barrier_semaphore()
    for peer in (sibling, partner):
        pl.semaphore_signal(barrier, inc=1, device_id=(peer, col), device_id_type=MESH)
    pl.semaphore_wait(barrier, 2)

    def send(origin, target, peer, i):
        return pltpu.make_async_remote_copy(
            src_ref=origin,
            dst_ref=target,
            send_sem=send_sem.at[i],
            recv_sem=recv_sem.at[i],
            device_id=(peer, col),
            device_id_type=MESH,
        )

    first = send(parts.at[across], near.at[0], sibling, 0)
    second = send(parts.at[sibling], near.at[1], sibling, 1)
    first.start()
    second.start()
    first.wait_recv()
    outgoing[...] = (
        parts[partner].astype(jnp.float32) + near[0].astype(jnp.float32)
    ).astype(jnp.bfloat16)
    third = send(outgoing, far, partner, 2)
    third.start()
    second.wait_recv()
    total[...] = parts[row].astype(jnp.float32) + near[1].astype(jnp.float32)
    third.wait_recv()
    total[...] += far[...].astype(jnp.float32)
    first.wait_send()
    second.wait_send()
    third.wait_send()


def group_sums(partial_sums, call):
    width = partial_sums.shape[1]
    parts = partial_sums.astype(jnp.bfloat16).reshape(4, -1, width)
    rows = parts.shape[1]
    space = pl.BlockSpec(memory_space=pltpu.VMEM)
    return pl.pallas_call(
        row_sum_kernel,
        out_shape=jax.ShapeDtypeStruct((rows, width), jnp.float32),
        in_specs=[space],
        out_specs=space,
        scratch_shapes=[
            pltpu.VMEM((2, rows, width), jnp.bfloat16),
            pltpu.VMEM((rows, width), jnp.bfloat16),
            pltpu.VMEM((rows, width), jnp.bfloat16),
            pltpu.SemaphoreType.DMA((3,)),
            pltpu.SemaphoreType.DMA((3,)),
        ],
        compiler_params=pltpu.CompilerParams(
            collective_id=8 + call, has_side_effects=True, vmem_limit_bytes=32 << 20
        ),
        cost_estimate=pl.CostEstimate(flops=0, bytes_accessed=64 << 20, transcendentals=0),
        name="group_sums",
    )(parts)


def scatter_sum(values):
    parts = [part.astype(jnp.bfloat16).reshape(32, 64, -1) for part in values]
    widths = [part.shape[2] for part in parts]
    swapped = lax.all_to_all(
        jnp.concatenate(parts, axis=2), "col", split_axis=0, concat_axis=0, tiled=True
    )
    total = jnp.sum(swapped, axis=0, dtype=jnp.float32)
    ends = [sum(widths[: i + 1]) for i in range(len(widths))]
    return [total[:, end - width : end] for end, width in zip(ends, widths)]


def finish_kernel(gains, share, total, router, values, buffers, *sems):
    send_sem, recv_sem, own_sem, col_send, col_recv, row_send, row_recv = sems
    row, col, sibling, partner, _ = row_places()
    along_x, along_z, along_y = col // 16, lax.rem(col // 4, 4), lax.rem(col, 4)
    stages = (
        [(lax.rem(row + i, 4), col) for i in (1, 2, 3)],
        [(row, along_x * 16 + along_z * 4 + lax.rem(along_y + i, 4)) for i in (1, 2, 3)],
        [(row, along_x * 16 + lax.rem(along_z + i, 4) * 4 + along_y) for i in (1, 2, 3)],
        [(row, lax.rem(col + 16, 32))],
    )
    greet(stages[0])
    barrier = pltpu.get_barrier_semaphore()

    def greet_col(step, carry):
        peer = (row, lax.rem(col + step, 32))
        pl.semaphore_signal(barrier, inc=1, device_id=peer, device_id_type=MESH)
        return carry

    lax.fori_loop(1, 32, greet_col, 0)
    own = pltpu.make_async_copy(share, router.at[row, col], own_sem)
    own.start()
    values[0] = gains[...]
    await_greetings(34)

    def push(step, carry):
        pltpu.make_async_remote_copy(
            src_ref=share,
            dst_ref=router.at[row, col],
            send_sem=col_send,
            recv_sem=col_recv,
            device_id=(row, lax.rem(col + step, 32)),
            device_id_type=MESH,
        ).start()
        return carry

    lax.fori_loop(1, 32, push, 0)
    at = 0
    for stage, peers in enumerate(stages):
        copies = []
        for i, peer in enumerate(peers):
            copies.append(
                pltpu.make_async_remote_copy(
                    src_ref=values.at[stage],
                    dst_ref=buffers.at[at + i],
                    send_sem=send_sem.at[at + i],
                    recv_sem=recv_sem.at[at + i],
                    device_id=peer,
                    device_id_type=MESH,
                )
            )
        for copy in copies:
            copy.start()
        if stage == 0:
            own.wait()
            arrived = router.at[row, pl.ds(0, 31)]
            pltpu.make_async_copy(arrived, arrived, col_recv).wait()
            far, near, onward = row_copies([router.at[row]], [router], row_send, row_recv)
            far[0].start()
            near[0].start()
        for copy in copies:
            copy.wait()
        result = values[stage]
        for i in range(len(peers)):
            result = result + buffers[at + i]
        values[stage + 1] = result
        at += len(peers)
    total[...] = values[len(stages)]
    far[0].wait_recv()
    onward[0].start()
    sent = router.at[row, pl.ds(0, 31)]
    pltpu.make_async_copy(sent, sent, col_send).wait()
    far[0].wait_send()
    near[0].wait()
    onward[0].wait()


def finish(gains, share):
    space = pl.BlockSpec(memory_space=pltpu.VMEM)
    away = pl.BlockSpec(memory_space=pl.ANY)
    return pl.pallas_call(
        finish_kernel,
        out_shape=[
            jax.ShapeDtypeStruct(gains.shape, gains.dtype),
            jax.ShapeDtypeStruct((4, 32, *share.shape), share.dtype),
        ],
        in_specs=[space, away],
        out_specs=[space, away],
        scratch_shapes=[
            pltpu.VMEM((5, *gains.shape), gains.dtype),
            pltpu.VMEM((10, *gains.shape), gains.dtype),
            pltpu.SemaphoreType.DMA((10,)),
            pltpu.SemaphoreType.DMA((10,)),
            pltpu.SemaphoreType.DMA,
            pltpu.SemaphoreType.DMA,
            pltpu.SemaphoreType.DMA,
            pltpu.SemaphoreType.DMA((3,)),
            pltpu.SemaphoreType.DMA((3,)),
        ],
        compiler_params=pltpu.CompilerParams(collective_id=16, has_side_effects=True),
        cost_estimate=pl.CostEstimate(flops=0, bytes_accessed=64 << 20, transcendentals=0),
        name="finish",
    )(gains, share)


def packed_places(shape, axis):
    index = lax.broadcasted_iota(jnp.int32, shape, axis)
    pair, place = index // PACKED_ROWS, lax.rem(index, PACKED_ROWS)
    found = []
    for part in range(-1, 3):
        if part < 0:
            valid, slot = place < PAIR_ROWS, place
        else:
            valid, slot = place >= PAIR_ROWS, 3 * (place - PAIR_ROWS) + part
        second = (slot >= EXPERT_ROWS).astype(jnp.int32)
        found.append((valid, pair, second, slot - EXPERT_ROWS * second))
    return found


def token_marks(code_block):
    marks = []
    wide = (BLOCK, BLOCK_EXPERTS)
    lanes = lax.broadcasted_iota(jnp.int32, wide, 1)
    for (valid, pair, second, _), (tall, _, _, order) in zip(
        packed_places(wide, 0), packed_places((BLOCK, SIDE), 0)
    ):
        owner = ((lanes == 2 * pair + second) & valid).astype(jnp.float32).astype(jnp.bfloat16)
        found = matmul(owner, code_block)
        hit = (found == order.astype(jnp.float32)) & tall
        marks.append((owner, hit.astype(jnp.float32)))
    return marks


def pack_tokens_kernel(with_gates, code, values, *refs):
    packed = refs[-1]
    marks = token_marks(code[0])
    main = marks[0][1].astype(jnp.bfloat16)
    last = values[:, 3 * QUARTER :]
    for part in range(3):
        columns = slice(part * QUARTER, (part + 1) * QUARTER)
        both = jnp.concatenate([main, marks[part + 1][1].astype(jnp.bfloat16)], axis=1)
        rows = jnp.concatenate([values[:, columns], last], axis=0)
        packed[:, columns] = matmul(both, rows).astype(jnp.bfloat16)
    if with_gates:
        high, low = refs[0], refs[1]
        owner, hit = marks[0]
        lanes = lax.broadcasted_iota(jnp.int32, (BLOCK, SIDE), 1)
        of_high = jnp.sum(hit * matmul(owner, high[0]), axis=1, keepdims=True)
        of_low = jnp.sum(hit * matmul(owner, low[0]), axis=1, keepdims=True)
        side = jnp.where(lanes == 0, of_high, jnp.where(lanes == 1, of_low, 0.0))
        packed[:, 3 * QUARTER :] = side.astype(jnp.bfloat16)


def pack_tokens(code, values, gates=None):
    blocks = code.shape[0]
    width = 3 * QUARTER + (SIDE if gates is not None else 0)
    small = pl.BlockSpec((1, BLOCK_EXPERTS, SIDE), lambda i: (i, 0, 0))
    extra = [] if gates is None else list(gates)
    return pl.pallas_call(
        functools.partial(pack_tokens_kernel, gates is not None),
        grid=(blocks,),
        out_shape=jax.ShapeDtypeStruct((blocks * BLOCK, width), jnp.bfloat16),
        in_specs=[small, pl.BlockSpec(values.shape, lambda i: (0, 0))] + [small] * len(extra),
        out_specs=pl.BlockSpec((BLOCK, width), lambda i: (i, 0)),
        compiler_params=pltpu.CompilerParams(vmem_limit_bytes=32 << 20),
        cost_estimate=pl.CostEstimate(
            flops=blocks * BLOCK * 256 * width * 2, bytes_accessed=8 << 20, transcendentals=0
        ),
        name="pack_tokens",
    )(code, values, *extra)


def slot_marks():
    shape = (2 * BLOCK_SLOTS, BLOCK)
    rows = lax.broadcasted_iota(jnp.int32, shape, 0)
    marks = []
    for valid, pair, second, order in packed_places(shape, 1):
        hit = (rows == second * BLOCK_SLOTS + pair * EXPERT_ROWS + order) & valid
        marks.append(hit.astype(jnp.float32).astype(jnp.bfloat16))
    return marks


def unpack_slots_kernel(with_gates, packed, values, *refs):
    marks = slot_marks()
    last = jnp.zeros((2 * BLOCK_SLOTS, QUARTER), jnp.float32)
    for part in range(3):
        columns = slice(part * QUARTER, (part + 1) * QUARTER)
        found = matmul(marks[0], packed[:, columns]).astype(jnp.bfloat16)
        values[0, :, columns] = found[:BLOCK_SLOTS]
        values[1, :, columns] = found[BLOCK_SLOTS:]
        last = last + matmul(marks[part + 1], packed[:, columns])
    last = last.astype(jnp.bfloat16)
    values[0, :, 3 * QUARTER :] = last[:BLOCK_SLOTS]
    values[1, :, 3 * QUARTER :] = last[BLOCK_SLOTS:]
    if with_gates:
        side = matmul(marks[0], packed[:, 3 * QUARTER :])
        gate = side[:, 0:1] + side[:, 1:2]
        wide = jnp.broadcast_to(gate, (2 * BLOCK_SLOTS, SIDE))
        refs[0][0] = wide[:BLOCK_SLOTS]
        refs[0][1] = wide[BLOCK_SLOTS:]


def unpack_slots(packed, with_gates):
    blocks = packed.shape[0] // BLOCK
    width = packed.shape[1]
    slots = blocks * BLOCK_SLOTS
    shapes = [jax.ShapeDtypeStruct((2, slots, 4 * QUARTER), jnp.bfloat16)]
    specs = [pl.BlockSpec((2, BLOCK_SLOTS, 4 * QUARTER), lambda i: (0, i, 0))]
    if with_gates:
        shapes.append(jax.ShapeDtypeStruct((2, slots, SIDE), jnp.float32))
        specs.append(pl.BlockSpec((2, BLOCK_SLOTS, SIDE), lambda i: (0, i, 0)))
    return pl.pallas_call(
        functools.partial(unpack_slots_kernel, with_gates),
        grid=(blocks,),
        out_shape=shapes,
        in_specs=[pl.BlockSpec((BLOCK, width), lambda i: (i, 0))],
        out_specs=specs,
        compiler_params=pltpu.CompilerParams(vmem_limit_bytes=32 << 20),
        cost_estimate=pl.CostEstimate(
            flops=blocks * 2 * BLOCK_SLOTS * BLOCK * 6 * QUARTER * 2,
            bytes_accessed=14 << 20,
            transcendentals=0,
        ),
        name="unpack_slots",
    )(packed)


def pack_slots_kernel(with_side, values, *refs):
    packed = refs[-1]
    marks = slot_marks()
    last = jnp.concatenate([values[0, :, 3 * QUARTER :], values[1, :, 3 * QUARTER :]], axis=0)
    for part in range(3):
        columns = slice(part * QUARTER, (part + 1) * QUARTER)
        rows = jnp.concatenate([values[0, :, columns], values[1, :, columns]], axis=0)
        found = outer_sum(marks[0], rows) + outer_sum(marks[part + 1], last)
        packed[:, columns] = found.astype(jnp.bfloat16)
    if with_side:
        side = jnp.concatenate([refs[0][0], refs[0][1]], axis=0)
        packed[:, 3 * QUARTER :] = outer_sum(marks[0], side).astype(jnp.bfloat16)


def pack_slots(values, side=None):
    slots = values.shape[1]
    blocks = slots // BLOCK_SLOTS
    width = 3 * QUARTER + (SIDE if side is not None else 0)
    extra = [] if side is None else [side]
    return pl.pallas_call(
        functools.partial(pack_slots_kernel, side is not None),
        grid=(blocks,),
        out_shape=jax.ShapeDtypeStruct((blocks * BLOCK, width), jnp.bfloat16),
        in_specs=[pl.BlockSpec((2, BLOCK_SLOTS, 4 * QUARTER), lambda i: (0, i, 0))]
        + [pl.BlockSpec((2, BLOCK_SLOTS, SIDE), lambda i: (0, i, 0))] * len(extra),
        out_specs=pl.BlockSpec((BLOCK, width), lambda i: (i, 0)),
        compiler_params=pltpu.CompilerParams(vmem_limit_bytes=32 << 20),
        cost_estimate=pl.CostEstimate(
            flops=blocks * 2 * BLOCK_SLOTS * BLOCK * 6 * QUARTER * 2,
            bytes_accessed=14 << 20,
            transcendentals=0,
        ),
        name="pack_slots",
    )(values, *extra)


def sum_tokens_kernel(with_side, code, packed, total, *refs):
    @pl.when(pl.program_id(0) == 0)
    def _():
        total[...] = jnp.zeros_like(total)

    marks = token_marks(code[0])
    main = marks[0][1].astype(jnp.bfloat16)
    last = jnp.zeros((total.shape[0], QUARTER), jnp.float32)
    for part in range(3):
        columns = slice(part * QUARTER, (part + 1) * QUARTER)
        total[:, columns] += outer_sum(main, packed[:, columns])
        last = last + outer_sum(marks[part + 1][1].astype(jnp.bfloat16), packed[:, columns])
    total[:, 3 * QUARTER :] += last
    if with_side:
        owner = marks[0][0].astype(jnp.float32)
        side = packed[:, 3 * QUARTER :].astype(jnp.float32)
        spread = [(side[:, i : i + 1] * owner).astype(jnp.bfloat16) for i in range(2)]
        refs[0][0] = outer_sum(main, spread[0]) + outer_sum(main, spread[1])


def sum_tokens(code, packed, with_side):
    blocks = code.shape[0]
    tokens, width = code.shape[2], packed.shape[1]
    shapes = [jax.ShapeDtypeStruct((tokens, 4 * QUARTER), jnp.float32)]
    specs = [pl.BlockSpec((tokens, 4 * QUARTER), lambda i: (0, 0))]
    if with_side:
        shapes.append(jax.ShapeDtypeStruct((blocks, tokens, BLOCK_EXPERTS), jnp.float32))
        specs.append(pl.BlockSpec((1, tokens, BLOCK_EXPERTS), lambda i: (i, 0, 0)))
    return pl.pallas_call(
        functools.partial(sum_tokens_kernel, with_side),
        grid=(blocks,),
        out_shape=shapes,
        in_specs=[
            pl.BlockSpec((1, BLOCK_EXPERTS, tokens), lambda i: (i, 0, 0)),
            pl.BlockSpec((BLOCK, width), lambda i: (i, 0)),
        ],
        out_specs=specs,
        compiler_params=pltpu.CompilerParams(vmem_limit_bytes=32 << 20),
        cost_estimate=pl.CostEstimate(
            flops=blocks * BLOCK * 128 * 6 * QUARTER * 2,
            bytes_accessed=8 << 20,
            transcendentals=0,
        ),
        name="sum_tokens",
    )(code, packed)


def exchange(packed):
    pairs = packed.reshape(-1, PACKED_ROWS, packed.shape[1])
    swapped = lax.all_to_all(pairs, ("row", "col"), split_axis=0, concat_axis=0, tiled=True)
    return swapped.reshape(packed.shape)


def per_device(
    block_in,
    gain_attn,
    w_query,
    w_keyval,
    w_out,
    gain_ffn,
    w_shared_in,
    w_shared_out,
    w_router,
    w_expert_in,
    w_expert_out,
    doc_lengths,
    routes,
    cotangent,
):
    row_count = lax.axis_size("row")
    rows_dev = block_in.shape[1]
    model_width = block_in.shape[2]
    group_tok = rows_dev * row_count
    head_size = w_keyval.shape[2] // 2
    local_heads = w_query.shape[1] // head_size
    local_kv = w_keyval.shape[1]
    group_size = local_heads // local_kv
    expert_count = w_router.shape[1]
    expert_ff = w_expert_out.shape[2]
    top_k = routes.shape[2]
    inv_root = head_size ** (-0.5)

    route_ids = routes.reshape(rows_dev, top_k)
    experts = jnp.arange(expert_count, dtype=jnp.int32)
    chosen = jnp.any(route_ids[:, :, None] == experts[None, None, :], axis=1)
    chosen_low = chosen.astype(jnp.bfloat16)
    tokens = jnp.arange(rows_dev, dtype=jnp.int32)
    before = (tokens[None, :] < tokens[:, None]).astype(jnp.bfloat16)
    order = matmul(before, chosen_low)
    code = jnp.where(chosen, order, -1.0).astype(jnp.bfloat16).T
    code = code.reshape(-1, BLOCK_EXPERTS, rows_dev)

    inputs = block_in.reshape(rows_dev, model_width).astype(jnp.float32)
    grad_low = cotangent.reshape(rows_dev, model_width)
    grad_rows = grad_low.astype(jnp.float32)
    scale_one, normed_one = normalize(inputs, gain_attn)
    shards = [w_query, w_keyval, w_out, w_shared_in, w_shared_out]
    shards = [part.reshape(part.shape[0], -1) for part in shards]
    full, group_one, group_grad = gather_start(
        jnp.concatenate(shards, axis=1), normed_one, grad_low
    )
    full_parts, end = [], 0
    for part in shards:
        full_parts.append(full[:, end : end + part.shape[1]])
        end += part.shape[1]
    full_query, full_keyval, full_out, full_shared_in, full_shared_out = full_parts

    segment, position = layout(doc_lengths.reshape(-1), group_tok)
    cosine, sine_table = rotary(position, head_size)
    query_pre = matmul(group_one, full_query).reshape(group_tok, local_heads, head_size)
    query_rot = rotate(query_pre, cosine, sine_table).astype(jnp.bfloat16)
    keyval_pre = matmul(group_one, full_keyval).reshape(group_tok, local_kv, 2 * head_size)
    key_rows = rotate(keyval_pre[..., :head_size], cosine, sine_table).astype(jnp.bfloat16)
    value_rows = keyval_pre[..., head_size:].astype(jnp.bfloat16)
    places = jnp.arange(group_tok, dtype=jnp.int32)
    allowed = (segment[:, None] == segment[None, :]) & (places[:, None] >= places[None, :])
    query_block = query_rot.reshape(group_tok, local_kv, group_size, head_size)

    def block_scores():
        scores = (
            jnp.einsum("qagd,kad->agqk", query_block, key_rows, preferred_element_type=jnp.float32)
            * inv_root
        )
        return jnp.where(allowed[None, None], scores, masked_score)

    scores = block_scores()
    highest = jnp.max(scores, axis=3, keepdims=True)
    weights = jnp.exp(scores - highest)
    totals = jnp.sum(weights, axis=3, keepdims=True)
    weights_low = (weights / totals).astype(jnp.bfloat16)
    attended = (
        jnp.einsum("agqk,kad->qagd", weights_low, value_rows, preferred_element_type=jnp.float32)
        .reshape(group_tok, local_heads * head_size)
        .astype(jnp.bfloat16)
    )
    log_totals = highest + jnp.log(totals)
    hidden_state = inputs + group_sums(matmul_t(attended, full_out), 0)
    scale_two, normed_two = normalize(hidden_state, gain_ffn)

    logits = matmul(normed_two, w_router)
    scores_sig = jnp.where(chosen, jax.nn.sigmoid(logits), 0.0)
    score_sum = jnp.sum(scores_sig, axis=1, keepdims=True)
    gate_weights = scores_sig / score_sum
    gates = [
        part.T.reshape(-1, BLOCK_EXPERTS, rows_dev) for part in split_low(gate_weights)
    ]
    received = exchange(pack_tokens(code, normed_two, gates))
    send_grads, received = lax.optimization_barrier((pack_tokens(code, grad_low), received))
    received_grads = exchange(send_grads)

    group_two = lax.all_gather(normed_two, "row", axis=0, tiled=True)
    shared_width = full_shared_in.shape[1] // 2
    shared_pre = matmul(group_two, full_shared_in)
    shared_gate, shared_up = shared_pre[:, :shared_width], shared_pre[:, shared_width:]
    shared_act, shared_slope = swish_parts(shared_gate)
    shared_hidden = (shared_act * shared_up).astype(jnp.bfloat16)
    shared_hidden_grad = matmul(group_grad, full_shared_out)
    grad_shared_out = outer_sum(group_grad, shared_hidden)
    shared_pre_grad = jnp.concatenate(
        [shared_hidden_grad * shared_up * shared_slope, shared_hidden_grad * shared_act], axis=1
    ).astype(jnp.bfloat16)
    grad_shared_in = outer_sum(group_two, shared_pre_grad)
    shared_sums = lax.psum_scatter(
        jnp.concatenate(
            [
                matmul_t(shared_hidden, full_shared_out).astype(jnp.bfloat16),
                matmul_t(shared_pre_grad, full_shared_in).astype(jnp.bfloat16),
            ],
            axis=1,
        ),
        "row",
        scatter_dimension=0,
        tiled=True,
    ).astype(jnp.float32)
    shared_branch, shared_input = shared_sums[:, :model_width], shared_sums[:, model_width:]

    expert_in, gate_wide = unpack_slots(received, True)
    gate = gate_wide[:, :, :1]
    expert_pre = jnp.einsum(
        "esd,edf->esf", expert_in, w_expert_in, preferred_element_type=jnp.float32
    )
    expert_act, expert_slope = swish_parts(expert_pre[..., :expert_ff])
    expert_hidden = (expert_act * expert_pre[..., expert_ff:]).astype(jnp.bfloat16)
    expert_out = (
        gate
        * jnp.einsum(
            "esf,edf->esd", expert_hidden, w_expert_out, preferred_element_type=jnp.float32
        )
    ).astype(jnp.bfloat16)
    send_out, received_grads = lax.optimization_barrier((pack_slots(expert_out), received_grads))
    returned = exchange(send_out)

    (expert_grads,) = unpack_slots(received_grads, False)
    plain_grad = jnp.einsum(
        "esd,edf->esf", expert_grads, w_expert_out, preferred_element_type=jnp.float32
    )
    gate_grad = jnp.sum(plain_grad * expert_hidden.astype(jnp.float32), axis=2, keepdims=True)
    gate_high, gate_low = split_low(gate_grad)
    lanes = jnp.arange(SIDE, dtype=jnp.int32)[None, None, :]
    side = jnp.where(lanes == 0, gate_high, jnp.where(lanes == 1, gate_low, 0)).astype(jnp.bfloat16)
    hidden_grad = gate * plain_grad
    expert_pre_grad = jnp.concatenate(
        [hidden_grad * expert_pre[..., expert_ff:] * expert_slope, hidden_grad * expert_act], axis=2
    ).astype(jnp.bfloat16)
    slot_grad = jnp.einsum(
        "esf,edf->esd", expert_pre_grad, w_expert_in, preferred_element_type=jnp.float32
    ).astype(jnp.bfloat16)
    send_back, returned = lax.optimization_barrier((pack_slots(slot_grad, side), returned))
    returned_grad = exchange(send_back)
    out_grad = (gate * expert_grads.astype(jnp.float32)).astype(jnp.bfloat16)
    grad_expert_out = jnp.einsum(
        "esd,esf->edf", out_grad, expert_hidden, preferred_element_type=jnp.float32
    )
    grad_expert_in = jnp.einsum(
        "esd,esf->edf", expert_in, expert_pre_grad, preferred_element_type=jnp.float32
    )
    (routed_branch,) = sum_tokens(code, returned, False)
    block_out = (hidden_state + shared_branch + routed_branch).astype(jnp.bfloat16)

    routed_input, gate_grads = sum_tokens(code, returned_grad, True)
    gate_grads = gate_grads.transpose(1, 0, 2).reshape(rows_dev, expert_count)
    score_grad = (
        gate_grads - jnp.sum(gate_grads * gate_weights, axis=1, keepdims=True)
    ) / score_sum
    logit_grad = (score_grad * scores_sig * (1.0 - scores_sig)).astype(jnp.bfloat16)
    router_input = matmul_t(logit_grad, w_router)
    normed_two_grad = shared_input + router_input + routed_input
    gain_ffn_grad, hidden_back = norm_back(hidden_state, scale_two, gain_ffn, normed_two_grad)
    hidden_total = grad_rows + hidden_back
    group_branch, group_logit = group_rows([hidden_total.astype(jnp.bfloat16), logit_grad], 0)
    attended_grad = matmul(group_branch, full_out).astype(jnp.bfloat16)
    grad_out_w = outer_sum(group_branch, attended)
    share_width = model_width // row_count
    router_part = outer_sum(
        lax.dynamic_slice_in_dim(group_two, lax.axis_index("row") * share_width, share_width, 1),
        group_logit,
    )
    sum_shared_in, sum_shared_out, sum_out, router_share = scatter_sum(
        [grad_shared_in, grad_shared_out, grad_out_w, router_part]
    )

    out_block = attended_grad.reshape(group_tok, local_kv, group_size, head_size)
    probs_full = jnp.exp(block_scores() - log_totals)
    prob_grad = jnp.einsum(
        "qagd,kad->agqk", out_block, value_rows, preferred_element_type=jnp.float32
    )
    row_delta = jnp.sum(probs_full * prob_grad, axis=3, keepdims=True)
    score_low = (probs_full * (prob_grad - row_delta)).astype(jnp.bfloat16)
    query_grad = (
        jnp.einsum("agqk,kad->qagd", score_low, key_rows, preferred_element_type=jnp.float32)
        * inv_root
    ).reshape(group_tok, local_heads, head_size)
    key_grad = (
        jnp.einsum("agqk,qagd->kad", score_low, query_block, preferred_element_type=jnp.float32)
        * inv_root
    )
    value_grad = jnp.einsum(
        "agqk,qagd->kad",
        probs_full.astype(jnp.bfloat16),
        out_block,
        preferred_element_type=jnp.float32,
    )
    query_pre_grad = (
        rotate(query_grad, cosine, -sine_table)
        .astype(jnp.bfloat16)
        .reshape(group_tok, local_heads * head_size)
    )
    keyval_pre_grad = (
        jnp.concatenate([rotate(key_grad, cosine, -sine_table), value_grad], axis=2)
        .astype(jnp.bfloat16)
        .reshape(group_tok, local_kv * 2 * head_size)
    )
    grad_query_w = outer_sum(group_one, query_pre_grad)
    grad_keyval_w = outer_sum(group_one, keyval_pre_grad)
    normed_one_grad = group_sums(
        matmul_t(query_pre_grad, full_query) + matmul_t(keyval_pre_grad, full_keyval), 3
    )
    gain_attn_grad, input_back = norm_back(inputs, scale_one, gain_attn, normed_one_grad)
    input_total = hidden_total + input_back

    sum_query, sum_keyval = scatter_sum([grad_query_w, grad_keyval_w])
    gain_sums, router_sum = finish(
        jnp.stack([gain_attn_grad, gain_ffn_grad]).reshape(-1, 128),
        router_share.reshape(-1, expert_count).astype(jnp.bfloat16),
    )
    gain_sums = gain_sums.reshape(2, model_width)
    return (
        block_out.reshape(1, rows_dev, model_width),
        input_total.reshape(1, rows_dev, model_width),
        gain_sums[0],
        sum_query,
        sum_keyval.reshape(w_keyval.shape),
        sum_out,
        gain_sums[1],
        sum_shared_in.reshape(w_shared_in.shape),
        sum_shared_out,
        router_sum.reshape(model_width, expert_count).astype(jnp.float32),
        grad_expert_in,
        grad_expert_out,
    )


def solution(mesh):
    in_specs = (
        P("col", "row", None),
        P(),
        P("col", "row"),
        P("col", "row", None),
        P("col", "row"),
        P(),
        P("col", None, "row"),
        P("col", "row"),
        P(),
        P(("row", "col"), None, None),
        P(("row", "col"), None, None),
        P("col", None),
        P("col", "row", None),
        P("col", "row", None),
    )
    out_specs = (
        P("col", "row", None),
        P("col", "row", None),
        P(),
        P("col", "row"),
        P("col", "row", None),
        P("col", "row"),
        P(),
        P("col", None, "row"),
        P("col", "row"),
        P(),
        P(("row", "col"), None, None),
        P(("row", "col"), None, None),
    )
    return jax.shard_map(
        per_device, mesh=mesh, in_specs=in_specs, out_specs=out_specs, check_vma=False
    )
```

```python
import functools

import jax
import jax.numpy as jnp
from jax import lax
from jax.experimental import pallas as pl
from jax.experimental.pallas import tpu as pltpu
from jax.sharding import PartitionSpec as P

epsilon = 1e-06
rope_base = 10000.0
masked_score = -1e30

EXPERT_ROWS = 6
PAIR_ROWS = 12
PACKED_ROWS = 16
BLOCK_PAIRS = 16
BLOCK = BLOCK_PAIRS * PACKED_ROWS
BLOCK_EXPERTS = 2 * BLOCK_PAIRS
BLOCK_SLOTS = BLOCK_PAIRS * EXPERT_ROWS
QUARTER = 512
SIDE = 128
MESH = pl.DeviceIdType.MESH


def layout(lengths, token_count):
    bounds = jnp.cumsum(lengths)
    places = jnp.arange(token_count, dtype=jnp.int32)
    segment = jnp.sum((places[:, None] >= bounds[None, :]).astype(jnp.int32), axis=1)
    starts = bounds - lengths
    owners = segment[:, None] == jnp.arange(lengths.shape[0], dtype=jnp.int32)[None, :]
    begins = jnp.sum(jnp.where(owners, starts[None, :], 0), axis=1)
    return (segment, places - begins)


def rotary(positions, head_size):
    half_size = head_size // 2
    spread = jnp.arange(half_size, dtype=jnp.float32) * (2.0 / head_size)
    frequency = rope_base ** (-spread)
    angles = positions.astype(jnp.float32)[:, None] * frequency[None, :]
    return (jnp.cos(angles), jnp.sin(angles))


def rotate(values, cosine, sine_table):
    half_size = values.shape[-1] // 2
    leading = values[..., :half_size]
    trailing = values[..., half_size:]
    cosine = cosine[:, None, :]
    sine_table = sine_table[:, None, :]
    return jnp.concatenate(
        [leading * cosine - trailing * sine_table, trailing * cosine + leading * sine_table],
        axis=-1,
    )


def normalize(values, gain):
    factor = lax.rsqrt(jnp.mean(values * values, axis=1, keepdims=True) + epsilon)
    return (factor, (values * factor * gain).astype(jnp.bfloat16))


def norm_back(values, factor, gain, incoming):
    weighted = gain * incoming
    gain_grad = jnp.sum(incoming * values * factor, axis=0)
    input_grad = factor * weighted - values * factor**3 * jnp.mean(
        weighted * values, axis=1, keepdims=True
    )
    return (gain_grad, input_grad)


def swish_parts(pre_act):
    logistic = jax.nn.sigmoid(pre_act)
    return (pre_act * logistic, logistic * (1.0 + pre_act * (1.0 - logistic)))


def matmul(matrix, partner):
    return jnp.dot(matrix, partner, preferred_element_type=jnp.float32)


def matmul_t(matrix, partner):
    return lax.dot_general(
        matrix, partner, (((1,), (1,)), ((), ())), preferred_element_type=jnp.float32
    )


def outer_sum(matrix, partner):
    return lax.dot_general(
        matrix, partner, (((0,), (0,)), ((), ())), preferred_element_type=jnp.float32
    )


def split_low(values):
    high = values.astype(jnp.bfloat16)
    return high, (values - high.astype(jnp.float32)).astype(jnp.bfloat16)


def row_places():
    row, col = lax.axis_index("row"), lax.axis_index("col")
    chip, core = row // 2, lax.rem(row, 2)
    sibling = chip * 2 + (1 - core)
    partner = (1 - chip) * 2 + core
    across = (1 - chip) * 2 + (1 - core)
    return row, col, sibling, partner, across


def row_copies(sources, targets, send_sem, recv_sem):
    row, col, sibling, partner, _ = row_places()

    def send(origin, target, peer, i):
        return pltpu.make_async_remote_copy(
            src_ref=origin,
            dst_ref=target,
            send_sem=send_sem.at[i],
            recv_sem=recv_sem.at[i],
            device_id=(peer, col),
            device_id_type=MESH,
        )

    far, near, onward = [], [], []
    for i, (source, target) in enumerate(zip(sources, targets)):
        far.append(send(source, target.at[row], partner, 3 * i))
        near.append(send(source, target.at[row], sibling, 3 * i + 1))
        onward.append(send(target.at[partner], target.at[partner], sibling, 3 * i + 2))
    return far, near, onward


def greet(peers):
    barrier = pltpu.get_barrier_semaphore()
    for peer in peers:
        pl.semaphore_signal(barrier, inc=1, device_id=peer, device_id_type=MESH)


def await_greetings(count):
    pl.semaphore_wait(pltpu.get_barrier_semaphore(), count)


def row_gather_kernel(count, *refs):
    sources, targets = refs[:count], refs[count : 2 * count]
    send_sem, recv_sem, own_sem = refs[2 * count :]
    row, col, sibling, partner, _ = row_places()
    greet([(sibling, col), (partner, col)])
    own = [
        pltpu.make_async_copy(sources[i], targets[i].at[row], own_sem.at[i]) for i in range(count)
    ]
    for copy in own:
        copy.start()
    await_greetings(2)
    far, near, onward = row_copies(sources, targets, send_sem, recv_sem)
    for copy in far + near:
        copy.start()
    for first, second in zip(far, onward):
        first.wait_recv()
        second.start()
    for copy in own:
        copy.wait()
    for copy in far:
        copy.wait_send()
    for copy in near + onward:
        copy.wait()


def group_rows(values, call):
    count = len(values)
    space = pl.BlockSpec(memory_space=pl.ANY)
    gathered = pl.pallas_call(
        functools.partial(row_gather_kernel, count),
        out_shape=[jax.ShapeDtypeStruct((4, *part.shape), part.dtype) for part in values],
        in_specs=[space] * count,
        out_specs=[space] * count,
        scratch_shapes=[
            pltpu.SemaphoreType.DMA((3 * count,)),
            pltpu.SemaphoreType.DMA((3 * count,)),
            pltpu.SemaphoreType.DMA((count,)),
        ],
        compiler_params=pltpu.CompilerParams(collective_id=1 + call, has_side_effects=True),
        cost_estimate=pl.CostEstimate(flops=0, bytes_accessed=64 << 20, transcendentals=0),
        name="group_rows",
    )(*values)
    return [part.reshape(-1, part.shape[2]) for part in gathered]


def gather_kernel(shard, normed, grads, full, group_one, group_grad, *sems):
    send_sem, recv_sem, own_sem, row_send, row_recv = sems
    row, col, sibling, partner, _ = row_places()
    along_x, along_z, along_y = col // 16, lax.rem(col // 4, 4), lax.rem(col, 4)
    other_x = 1 - along_x
    half_rows = shard.shape[0] // 2

    def place(x, z, y):
        return x * 16 + z * 4 + y

    z_near = [lax.rem(along_z + i, 4) for i in (1, 3, 2)]
    y_near = [lax.rem(along_y + i, 4) for i in (1, 3, 2)]
    z_peers = [place(along_x, z, along_y) for z in z_near]
    y_peers = [place(along_x, along_z, y) for y in y_near]
    x_peer = place(other_x, along_z, along_y)
    greet([(row, peer) for peer in z_peers + y_peers + [x_peer]])
    greet([(sibling, col), (partner, col)])
    own = [
        pltpu.make_async_copy(shard, full.at[col], own_sem.at[0]),
        pltpu.make_async_copy(normed, group_one.at[row], own_sem.at[1]),
        pltpu.make_async_copy(grads, group_grad.at[row], own_sem.at[2]),
    ]
    for copy in own:
        copy.start()
    await_greetings(9)

    def pass_on(owner, half, peers, origin=None):
        rows = pl.ds(half * half_rows, half_rows)
        target = full.at[owner, rows]
        for peer in peers:
            pltpu.make_async_remote_copy(
                src_ref=target if origin is None else origin.at[rows],
                dst_ref=target,
                send_sem=send_sem,
                recv_sem=recv_sem.at[half * 32 + owner],
                device_id=(row, peer),
                device_id_type=MESH,
            ).start()

    def await_half(owner, half):
        target = full.at[owner, pl.ds(half * half_rows, half_rows)]
        pltpu.make_async_copy(target, target, recv_sem.at[half * 32 + owner]).wait()

    pass_on(col, 0, [x_peer], shard)
    pass_on(col, 1, [x_peer], shard)
    pass_on(col, 0, z_peers, shard)
    pass_on(col, 1, y_peers, shard)
    far, near, onward = row_copies([normed, grads], [group_one, group_grad], row_send, row_recv)
    far[0].start()
    near[0].start()
    await_half(x_peer, 0)
    pass_on(x_peer, 0, z_peers)
    await_half(x_peer, 1)
    pass_on(x_peer, 1, y_peers)
    pass_on(col, 0, y_peers, shard)
    pass_on(col, 1, z_peers, shard)
    pass_on(x_peer, 0, y_peers)
    pass_on(x_peer, 1, z_peers)
    far[1].start()
    near[1].start()
    for i in range(3):
        for x in (along_x, other_x):
            owner = place(x, z_near[i], along_y)
            await_half(owner, 0)
            pass_on(owner, 0, y_peers)
            owner = place(x, along_z, y_near[i])
            await_half(owner, 1)
            pass_on(owner, 1, z_peers)
    for first, second in zip(far, onward):
        first.wait_recv()
        second.start()
    for x in (along_x, other_x):
        for i in range(4):
            for j in range(3):
                await_half(place(x, lax.rem(along_z + i, 4), y_near[j]), 0)
                await_half(place(x, z_near[j], lax.rem(along_y + i, 4)), 1)
    for copy in own:
        copy.wait()
    for copy in far:
        copy.wait_send()
    for copy in near + onward:
        copy.wait()
    sent = full.at[pl.ds(0, 31)]
    pltpu.make_async_copy(sent, sent, send_sem).wait()


def gather_start(shard, normed, grads):
    space = pl.BlockSpec(memory_space=pl.ANY)
    full, group_one, group_grad = pl.pallas_call(
        gather_kernel,
        out_shape=[
            jax.ShapeDtypeStruct((32, *shard.shape), shard.dtype),
            jax.ShapeDtypeStruct((4, *normed.shape), normed.dtype),
            jax.ShapeDtypeStruct((4, *grads.shape), grads.dtype),
        ],
        in_specs=[space] * 3,
        out_specs=[space] * 3,
        scratch_shapes=[
            pltpu.SemaphoreType.DMA,
            pltpu.SemaphoreType.DMA((64,)),
            pltpu.SemaphoreType.DMA((3,)),
            pltpu.SemaphoreType.DMA((6,)),
            pltpu.SemaphoreType.DMA((6,)),
        ],
        compiler_params=pltpu.CompilerParams(collective_id=0, has_side_effects=True),
        cost_estimate=pl.CostEstimate(flops=0, bytes_accessed=200 << 20, transcendentals=0),
        name="gather_start",
    )(shard, normed, grads)
    return [part.reshape(-1, part.shape[2]) for part in (full, group_one, group_grad)]


def row_sum_kernel(parts, total, near, far, outgoing, send_sem, recv_sem):
    row, col, sibling, partner, across = row_places()
    barrier = pltpu.get_barrier_semaphore()
    for peer in (sibling, partner):
        pl.semaphore_signal(barrier, inc=1, device_id=(peer, col), device_id_type=MESH)
    pl.semaphore_wait(barrier, 2)

    def send(origin, target, peer, i):
        return pltpu.make_async_remote_copy(
            src_ref=origin,
            dst_ref=target,
            send_sem=send_sem.at[i],
            recv_sem=recv_sem.at[i],
            device_id=(peer, col),
            device_id_type=MESH,
        )

    first = send(parts.at[across], near.at[0], sibling, 0)
    second = send(parts.at[sibling], near.at[1], sibling, 1)
    first.start()
    second.start()
    first.wait_recv()
    outgoing[...] = (
        parts[partner].astype(jnp.float32) + near[0].astype(jnp.float32)
    ).astype(jnp.bfloat16)
    third = send(outgoing, far, partner, 2)
    third.start()
    second.wait_recv()
    total[...] = parts[row].astype(jnp.float32) + near[1].astype(jnp.float32)
    third.wait_recv()
    total[...] += far[...].astype(jnp.float32)
    first.wait_send()
    second.wait_send()
    third.wait_send()


def group_sums(partial_sums, call):
    width = partial_sums.shape[1]
    parts = partial_sums.astype(jnp.bfloat16).reshape(4, -1, width)
    rows = parts.shape[1]
    space = pl.BlockSpec(memory_space=pltpu.VMEM)
    return pl.pallas_call(
        row_sum_kernel,
        out_shape=jax.ShapeDtypeStruct((rows, width), jnp.float32),
        in_specs=[space],
        out_specs=space,
        scratch_shapes=[
            pltpu.VMEM((2, rows, width), jnp.bfloat16),
            pltpu.VMEM((rows, width), jnp.bfloat16),
            pltpu.VMEM((rows, width), jnp.bfloat16),
            pltpu.SemaphoreType.DMA((3,)),
            pltpu.SemaphoreType.DMA((3,)),
        ],
        compiler_params=pltpu.CompilerParams(
            collective_id=8 + call, has_side_effects=True, vmem_limit_bytes=32 << 20
        ),
        cost_estimate=pl.CostEstimate(flops=0, bytes_accessed=64 << 20, transcendentals=0),
        name="group_sums",
    )(parts)


def finish_kernel(
    parts, grads, hidden, inputs, scale, gain, gain_ffn, result, summed, gains, *scratch
):
    near, far, outgoing, first, first_sum, second, second_sum, third = scratch[:8]
    values, buffers = scratch[8:10]
    row_send, row_recv, one_send, one_recv, two_send, two_recv = scratch[10:16]
    three_send, three_recv, gain_send, gain_recv = scratch[16:]
    row, col, sibling, partner, across = row_places()
    x, z, y = col // 16, lax.rem(col // 4, 4), lax.rem(col, 4)
    other_x = 1 - x
    half_rows = grads.shape[3] // 2
    y_peers = [(row, x * 16 + z * 4 + lax.rem(y + i, 4)) for i in (1, 2, 3)]
    z_peers = [(row, x * 16 + lax.rem(z + i, 4) * 4 + y) for i in (1, 2, 3)]
    x_peer = (row, other_x * 16 + z * 4 + y)
    row_peers = [(peer, col) for peer in (sibling, partner, across)]

    def copy(source, target, sems, at, peer):
        return pltpu.make_async_remote_copy(
            src_ref=source,
            dst_ref=target,
            send_sem=sems[0].at[at],
            recv_sem=sems[1].at[at],
            device_id=peer,
            device_id_type=MESH,
        )

    greet(row_peers + y_peers + z_peers + [x_peer])
    await_greetings(10)

    row_sems = (row_send, row_recv)
    row_copies_ = [
        copy(parts.at[across], near.at[0], row_sems, 0, row_peers[0]),
        copy(parts.at[sibling], near.at[1], row_sems, 1, row_peers[0]),
        copy(outgoing, far, row_sems, 2, row_peers[1]),
    ]
    row_copies_[0].start()
    row_copies_[1].start()
    row_copies_[0].wait_recv()
    outgoing[...] = (parts[partner].astype(jnp.float32) + near[0].astype(jnp.float32)).astype(
        jnp.bfloat16
    )
    row_copies_[2].start()

    def halves(half):
        return pl.ds(half * half_rows, half_rows)

    one, two, three = (one_send, one_recv), (two_send, two_recv), (three_send, three_recv)
    one_copies, two_copies, three_copies = {}, {}, []
    for turn, owner_x in enumerate((other_x, x)):
        for half in range(2):
            for i in range(3):
                if half == 0:
                    source = grads.at[owner_x, :, lax.rem(y + i + 1, 4), halves(0)]
                else:
                    source = grads.at[owner_x, lax.rem(z + i + 1, 4), :, halves(1)]
                at = (turn * 2 + half) * 3 + i
                peer = (y_peers, z_peers)[half][i]
                one_copies[turn, half, i] = copy(source, first.at[turn, half, i], one, at, peer)
                one_copies[turn, half, i].start()

    def add_first(turn):
        owner_x = (other_x, x)[turn]
        for half in range(2):
            for i in range(3):
                one_copies[turn, half, i].wait_recv()

            def add(k, carry, half=half):
                if half == 0:
                    total = grads[owner_x, k, y, halves(0)].astype(jnp.float32)
                else:
                    total = grads[owner_x, z, k, halves(1)].astype(jnp.float32)
                for i in range(3):
                    total = total + first[turn, half, i, k].astype(jnp.float32)
                first_sum[turn, half, k] = total.astype(jnp.bfloat16)
                return carry

            lax.fori_loop(0, 4, add, 0)
            for i in range(3):
                away = lax.rem((z, y)[half] + i + 1, 4)
                two_copies[turn, half, i] = copy(
                    first_sum.at[turn, half, away],
                    second.at[turn, half, i],
                    two,
                    (turn * 2 + half) * 3 + i,
                    (z_peers, y_peers)[half][i],
                )
                two_copies[turn, half, i].start()

    def add_second(turn, half):
        for i in range(3):
            two_copies[turn, half, i].wait_recv()
        total = first_sum[turn, half, (z, y)[half]].astype(jnp.float32)
        for i in range(3):
            total = total + second[turn, half, i].astype(jnp.float32)
        return total

    row_copies_[1].wait_recv()
    incoming = parts[row].astype(jnp.float32) + near[1].astype(jnp.float32)
    row_copies_[2].wait_recv()
    incoming = incoming + far[...].astype(jnp.float32)
    rows = inputs[...].astype(jnp.float32)
    factor = scale[...]
    weighted = gain[...] * incoming
    mean = jnp.mean(weighted * rows, axis=1, keepdims=True)
    result[...] = hidden[...] + factor * weighted - rows * (factor * factor * factor * mean)
    values[0, 0:1] = jnp.sum(incoming * rows * factor, axis=0, keepdims=True)
    values[0, 1:2] = gain_ffn[...]

    gain_sems = (gain_send, gain_recv)
    gain_copies = []
    stages = (row_peers, y_peers, z_peers, [x_peer])

    def start_gains(stage):
        at = 3 * stage
        for i, peer in enumerate(stages[stage]):
            gain_copies.append(
                copy(values.at[stage], buffers.at[at + i], gain_sems, at + i, peer)
            )
            gain_copies[-1].start()

    def add_gains(stage):
        at = 3 * stage
        total = values[stage]
        for i in range(len(stages[stage])):
            gain_copies[at + i].wait_recv()
            total = total + buffers[at + i]
        values[stage + 1] = total

    start_gains(0)
    add_first(0)
    add_gains(0)
    start_gains(1)
    add_first(1)
    add_gains(1)
    start_gains(2)
    for half in range(2):
        second_sum[half] = add_second(0, half).astype(jnp.bfloat16)
        three_copies.append(copy(second_sum.at[half], third.at[half], three, half, x_peer))
        three_copies[half].start()
    add_gains(2)
    start_gains(3)
    for half in range(2):
        total = add_second(1, half)
        three_copies[half].wait_recv()
        summed[halves(half)] = total + third[half].astype(jnp.float32)
    add_gains(3)
    gains[...] = values[4]
    for done in [*row_copies_, *one_copies.values(), *two_copies.values()]:
        done.wait_send()
    for done in [*three_copies, *gain_copies]:
        done.wait_send()


def finish(parts, grads, hidden, inputs, scale, gain, gain_ffn):
    space = pl.BlockSpec(memory_space=pltpu.VMEM)
    rows, width = hidden.shape
    half_rows, depth = grads.shape[3] // 2, grads.shape[4]
    low = jnp.bfloat16
    return pl.pallas_call(
        finish_kernel,
        out_shape=[
            jax.ShapeDtypeStruct((rows, width), jnp.float32),
            jax.ShapeDtypeStruct((2 * half_rows, depth), jnp.float32),
            jax.ShapeDtypeStruct((2, width), jnp.float32),
        ],
        in_specs=[space] * 7,
        out_specs=[space] * 3,
        scratch_shapes=[
            pltpu.VMEM((2, rows, width), low),
            pltpu.VMEM((rows, width), low),
            pltpu.VMEM((rows, width), low),
            pltpu.VMEM((2, 2, 3, 4, half_rows, depth), low),
            pltpu.VMEM((2, 2, 4, half_rows, depth), low),
            pltpu.VMEM((2, 2, 3, half_rows, depth), low),
            pltpu.VMEM((2, half_rows, depth), low),
            pltpu.VMEM((2, half_rows, depth), low),
            pltpu.VMEM((5, 2, width), jnp.float32),
            pltpu.VMEM((10, 2, width), jnp.float32),
            pltpu.SemaphoreType.DMA((3,)),
            pltpu.SemaphoreType.DMA((3,)),
            pltpu.SemaphoreType.DMA((12,)),
            pltpu.SemaphoreType.DMA((12,)),
            pltpu.SemaphoreType.DMA((12,)),
            pltpu.SemaphoreType.DMA((12,)),
            pltpu.SemaphoreType.DMA((2,)),
            pltpu.SemaphoreType.DMA((2,)),
            pltpu.SemaphoreType.DMA((10,)),
            pltpu.SemaphoreType.DMA((10,)),
        ],
        compiler_params=pltpu.CompilerParams(
            collective_id=16, has_side_effects=True, vmem_limit_bytes=56 << 20
        ),
        cost_estimate=pl.CostEstimate(flops=0, bytes_accessed=200 << 20, transcendentals=0),
        name="finish",
    )(parts, grads, hidden, inputs, scale, gain, gain_ffn)


def packed_places(shape, axis):
    index = lax.broadcasted_iota(jnp.int32, shape, axis)
    pair, place = index // PACKED_ROWS, lax.rem(index, PACKED_ROWS)
    found = []
    for part in range(-1, 3):
        if part < 0:
            valid, slot = place < PAIR_ROWS, place
        else:
            valid, slot = place >= PAIR_ROWS, 3 * (place - PAIR_ROWS) + part
        second = (slot >= EXPERT_ROWS).astype(jnp.int32)
        found.append((valid, pair, second, slot - EXPERT_ROWS * second))
    return found


def token_marks(code_block):
    marks = []
    wide = (BLOCK, BLOCK_EXPERTS)
    lanes = lax.broadcasted_iota(jnp.int32, wide, 1)
    for (valid, pair, second, _), (tall, _, _, order) in zip(
        packed_places(wide, 0), packed_places((BLOCK, SIDE), 0)
    ):
        owner = ((lanes == 2 * pair + second) & valid).astype(jnp.float32).astype(jnp.bfloat16)
        found = matmul(owner, code_block)
        hit = (found == order.astype(jnp.float32)) & tall
        marks.append((owner, hit.astype(jnp.float32)))
    return marks


def gate_weights_of(owner, hit, high, low):
    weights = hit * (matmul(owner, high) + matmul(owner, low))
    return split_low(weights)


def pack_tokens_kernel(with_gates, code, values, *refs):
    packed = refs[-1]
    marks = token_marks(code[0])
    if with_gates:
        weights = [gate_weights_of(owner, hit, refs[0][0], refs[1][0]) for owner, hit in marks]
    else:
        weights = [(hit.astype(jnp.bfloat16),) for _, hit in marks]
    copies = len(weights[0])
    last = values[:, 3 * QUARTER :]
    for part in range(3):
        columns = slice(part * QUARTER, (part + 1) * QUARTER)
        both = jnp.concatenate([*weights[0], *weights[part + 1]], axis=1)
        rows = jnp.concatenate([values[:, columns]] * copies + [last] * copies, axis=0)
        packed[:, columns] = matmul(both, rows).astype(jnp.bfloat16)


def pack_tokens(code, values, gates=()):
    blocks = code.shape[0]
    width = 3 * QUARTER
    small = pl.BlockSpec((1, BLOCK_EXPERTS, SIDE), lambda i: (i, 0, 0))
    return pl.pallas_call(
        functools.partial(pack_tokens_kernel, len(gates) > 0),
        grid=(blocks,),
        out_shape=jax.ShapeDtypeStruct((blocks * BLOCK, width), jnp.bfloat16),
        in_specs=[small, pl.BlockSpec(values.shape, lambda i: (0, 0))] + [small] * len(gates),
        out_specs=pl.BlockSpec((BLOCK, width), lambda i: (i, 0)),
        compiler_params=pltpu.CompilerParams(vmem_limit_bytes=32 << 20),
        cost_estimate=pl.CostEstimate(
            flops=blocks * BLOCK * 256 * width * 2, bytes_accessed=8 << 20, transcendentals=0
        ),
        name="pack_tokens",
    )(code, values, *gates)


def slot_marks():
    shape = (2 * BLOCK_SLOTS, BLOCK)
    rows = lax.broadcasted_iota(jnp.int32, shape, 0)
    marks = []
    for valid, pair, second, order in packed_places(shape, 1):
        hit = (rows == second * BLOCK_SLOTS + pair * EXPERT_ROWS + order) & valid
        marks.append(hit.astype(jnp.float32).astype(jnp.bfloat16))
    return marks


def unpack_slots_kernel(packed, values):
    marks = slot_marks()
    last = jnp.zeros((2 * BLOCK_SLOTS, QUARTER), jnp.float32)
    for part in range(3):
        columns = slice(part * QUARTER, (part + 1) * QUARTER)
        found = matmul(marks[0], packed[:, columns]).astype(jnp.bfloat16)
        values[0, :, columns] = found[:BLOCK_SLOTS]
        values[1, :, columns] = found[BLOCK_SLOTS:]
        last = last + matmul(marks[part + 1], packed[:, columns])
    last = last.astype(jnp.bfloat16)
    values[0, :, 3 * QUARTER :] = last[:BLOCK_SLOTS]
    values[1, :, 3 * QUARTER :] = last[BLOCK_SLOTS:]


def unpack_slots(packed):
    blocks = packed.shape[0] // BLOCK
    slots = blocks * BLOCK_SLOTS
    return pl.pallas_call(
        unpack_slots_kernel,
        grid=(blocks,),
        out_shape=jax.ShapeDtypeStruct((2, slots, 4 * QUARTER), jnp.bfloat16),
        in_specs=[pl.BlockSpec((BLOCK, 3 * QUARTER), lambda i: (i, 0))],
        out_specs=pl.BlockSpec((2, BLOCK_SLOTS, 4 * QUARTER), lambda i: (0, i, 0)),
        compiler_params=pltpu.CompilerParams(vmem_limit_bytes=32 << 20),
        cost_estimate=pl.CostEstimate(
            flops=blocks * 2 * BLOCK_SLOTS * BLOCK * 6 * QUARTER * 2,
            bytes_accessed=14 << 20,
            transcendentals=0,
        ),
        name="unpack_slots",
    )(packed)


def pack_slots_kernel(values, packed):
    marks = slot_marks()
    last = jnp.concatenate([values[0, :, 3 * QUARTER :], values[1, :, 3 * QUARTER :]], axis=0)
    for part in range(3):
        columns = slice(part * QUARTER, (part + 1) * QUARTER)
        rows = jnp.concatenate([values[0, :, columns], values[1, :, columns]], axis=0)
        found = outer_sum(marks[0], rows) + outer_sum(marks[part + 1], last)
        packed[:, columns] = found.astype(jnp.bfloat16)


def pack_slots(values):
    slots = values.shape[1]
    blocks = slots // BLOCK_SLOTS
    return pl.pallas_call(
        pack_slots_kernel,
        grid=(blocks,),
        out_shape=jax.ShapeDtypeStruct((blocks * BLOCK, 3 * QUARTER), jnp.bfloat16),
        in_specs=[pl.BlockSpec((2, BLOCK_SLOTS, 4 * QUARTER), lambda i: (0, i, 0))],
        out_specs=pl.BlockSpec((BLOCK, 3 * QUARTER), lambda i: (i, 0)),
        compiler_params=pltpu.CompilerParams(vmem_limit_bytes=32 << 20),
        cost_estimate=pl.CostEstimate(
            flops=blocks * 2 * BLOCK_SLOTS * BLOCK * 6 * QUARTER * 2,
            bytes_accessed=14 << 20,
            transcendentals=0,
        ),
        name="pack_slots",
    )(values)


def sum_tokens_kernel(code, packed, total):
    @pl.when(pl.program_id(0) == 0)
    def _():
        total[...] = jnp.zeros_like(total)

    marks = [hit.astype(jnp.bfloat16) for _, hit in token_marks(code[0])]
    last = jnp.zeros((total.shape[0], QUARTER), jnp.float32)
    for part in range(3):
        columns = slice(part * QUARTER, (part + 1) * QUARTER)
        total[:, columns] += outer_sum(marks[0], packed[:, columns])
        last = last + outer_sum(marks[part + 1], packed[:, columns])
    total[:, 3 * QUARTER :] += last


def sum_gated_kernel(code, packed, grads, high, low, total, gate_grads):
    @pl.when(pl.program_id(0) == 0)
    def _():
        total[...] = jnp.zeros_like(total)

    marks = token_marks(code[0])
    weights = [gate_weights_of(owner, hit, high[0], low[0]) for owner, hit in marks]
    last = jnp.zeros((total.shape[0], QUARTER), jnp.float32)
    whole = jnp.zeros((BLOCK, 1), jnp.float32)
    products = []
    for part in range(3):
        columns = slice(part * QUARTER, (part + 1) * QUARTER)
        rows = packed[:, columns]
        total[:, columns] += outer_sum(weights[0][0], rows) + outer_sum(weights[0][1], rows)
        last = last + outer_sum(weights[part + 1][0], rows) + outer_sum(weights[part + 1][1], rows)
        dots = jnp.sum(
            rows.astype(jnp.float32) * grads[:, columns].astype(jnp.float32),
            axis=1,
            keepdims=True,
        )
        whole = whole + dots
        products.append(dots)
    total[:, 3 * QUARTER :] += last
    found = jnp.zeros(gate_grads.shape[1:], jnp.float32)
    for (owner, hit), dots in zip(marks, [whole, *products]):
        hit = hit.astype(jnp.bfloat16)
        for spread in split_low(dots * owner.astype(jnp.float32)):
            found = found + outer_sum(hit, spread)
    gate_grads[0] = found


def sum_tokens(code, packed):
    blocks, _, tokens = code.shape
    return pl.pallas_call(
        sum_tokens_kernel,
        grid=(blocks,),
        out_shape=jax.ShapeDtypeStruct((tokens, 4 * QUARTER), jnp.float32),
        in_specs=[
            pl.BlockSpec((1, BLOCK_EXPERTS, tokens), lambda i: (i, 0, 0)),
            pl.BlockSpec((BLOCK, 3 * QUARTER), lambda i: (i, 0)),
        ],
        out_specs=pl.BlockSpec((tokens, 4 * QUARTER), lambda i: (0, 0)),
        compiler_params=pltpu.CompilerParams(vmem_limit_bytes=32 << 20),
        cost_estimate=pl.CostEstimate(
            flops=blocks * BLOCK * 128 * 6 * QUARTER * 2,
            bytes_accessed=8 << 20,
            transcendentals=0,
        ),
        name="sum_tokens",
    )(code, packed)


def sum_gated(code, packed, grads, gates):
    blocks, _, tokens = code.shape
    small = pl.BlockSpec((1, BLOCK_EXPERTS, tokens), lambda i: (i, 0, 0))
    wide = pl.BlockSpec((BLOCK, 3 * QUARTER), lambda i: (i, 0))
    return pl.pallas_call(
        sum_gated_kernel,
        grid=(blocks,),
        out_shape=[
            jax.ShapeDtypeStruct((tokens, 4 * QUARTER), jnp.float32),
            jax.ShapeDtypeStruct((blocks, tokens, BLOCK_EXPERTS), jnp.float32),
        ],
        in_specs=[small, wide, wide, small, small],
        out_specs=[
            pl.BlockSpec((tokens, 4 * QUARTER), lambda i: (0, 0)),
            pl.BlockSpec((1, tokens, BLOCK_EXPERTS), lambda i: (i, 0, 0)),
        ],
        compiler_params=pltpu.CompilerParams(vmem_limit_bytes=32 << 20),
        cost_estimate=pl.CostEstimate(
            flops=blocks * BLOCK * 128 * 12 * QUARTER * 2,
            bytes_accessed=14 << 20,
            transcendentals=0,
        ),
        name="sum_gated",
    )(code, packed, grads, *gates)


def exchange(packed):
    pairs = packed.reshape(-1, PACKED_ROWS, packed.shape[1])
    swapped = lax.all_to_all(pairs, ("row", "col"), split_axis=0, concat_axis=0, tiled=True)
    return swapped.reshape(packed.shape)


def per_device(
    block_in,
    gain_attn,
    w_query,
    w_keyval,
    w_out,
    gain_ffn,
    w_shared_in,
    w_shared_out,
    w_router,
    w_expert_in,
    w_expert_out,
    doc_lengths,
    routes,
    cotangent,
):
    row_count = lax.axis_size("row")
    rows_dev = block_in.shape[1]
    model_width = block_in.shape[2]
    group_tok = rows_dev * row_count
    head_size = w_keyval.shape[2] // 2
    local_heads = w_query.shape[1] // head_size
    local_kv = w_keyval.shape[1]
    group_size = local_heads // local_kv
    expert_count = w_router.shape[1]
    expert_ff = w_expert_out.shape[2]
    top_k = routes.shape[2]
    inv_root = head_size ** (-0.5)

    route_ids = routes.reshape(rows_dev, top_k)
    experts = jnp.arange(expert_count, dtype=jnp.int32)
    chosen = jnp.any(route_ids[:, :, None] == experts[None, None, :], axis=1)
    chosen_low = chosen.astype(jnp.bfloat16)
    tokens = jnp.arange(rows_dev, dtype=jnp.int32)
    before = (tokens[None, :] < tokens[:, None]).astype(jnp.bfloat16)
    order = matmul(before, chosen_low)
    code = jnp.where(chosen, order, -1.0).astype(jnp.bfloat16).T
    code = code.reshape(-1, BLOCK_EXPERTS, rows_dev)

    inputs = block_in.reshape(rows_dev, model_width).astype(jnp.float32)
    grad_low = cotangent.reshape(rows_dev, model_width)
    grad_rows = grad_low.astype(jnp.float32)
    scale_one, normed_one = normalize(inputs, gain_attn)
    shards = [w_query, w_keyval, w_out, w_shared_in, w_shared_out]
    shards = [part.reshape(part.shape[0], -1) for part in shards]
    full, group_one, group_grad = gather_start(
        jnp.concatenate(shards, axis=1), normed_one, grad_low
    )
    full_parts, end = [], 0
    for part in shards:
        full_parts.append(full[:, end : end + part.shape[1]])
        end += part.shape[1]
    full_query, full_keyval, full_out, full_shared_in, full_shared_out = full_parts

    segment, position = layout(doc_lengths.reshape(-1), group_tok)
    cosine, sine_table = rotary(position, head_size)
    query_pre = matmul(group_one, full_query).reshape(group_tok, local_heads, head_size)
    query_rot = rotate(query_pre, cosine, sine_table).astype(jnp.bfloat16)
    keyval_pre = matmul(group_one, full_keyval).reshape(group_tok, local_kv, 2 * head_size)
    key_rows = rotate(keyval_pre[..., :head_size], cosine, sine_table).astype(jnp.bfloat16)
    value_rows = keyval_pre[..., head_size:].astype(jnp.bfloat16)
    places = jnp.arange(group_tok, dtype=jnp.int32)
    allowed = (segment[:, None] == segment[None, :]) & (places[:, None] >= places[None, :])
    query_block = query_rot.reshape(group_tok, local_kv, group_size, head_size)

    def block_scores():
        scores = (
            jnp.einsum("qagd,kad->agqk", query_block, key_rows, preferred_element_type=jnp.float32)
            * inv_root
        )
        return jnp.where(allowed[None, None], scores, masked_score)

    scores = block_scores()
    highest = jnp.max(scores, axis=3, keepdims=True)
    weights = jnp.exp(scores - highest)
    totals = jnp.sum(weights, axis=3, keepdims=True)
    weights_low = (weights / totals).astype(jnp.bfloat16)
    attended = (
        jnp.einsum("agqk,kad->qagd", weights_low, value_rows, preferred_element_type=jnp.float32)
        .reshape(group_tok, local_heads * head_size)
        .astype(jnp.bfloat16)
    )
    log_totals = highest + jnp.log(totals)
    hidden_state = inputs + group_sums(matmul_t(attended, full_out), 0)
    scale_two, normed_two = normalize(hidden_state, gain_ffn)

    logits = matmul(normed_two, w_router)
    scores_sig = jnp.where(chosen, jax.nn.sigmoid(logits), 0.0)
    score_sum = jnp.sum(scores_sig, axis=1, keepdims=True)
    gate_weights = scores_sig / score_sum
    gates = [
        part.T.reshape(-1, BLOCK_EXPERTS, rows_dev) for part in split_low(gate_weights)
    ]
    received = exchange(pack_tokens(code, normed_two))
    send_grads, received = lax.optimization_barrier((pack_tokens(code, grad_low, gates), received))
    received_grads = exchange(send_grads)

    group_two = lax.all_gather(normed_two, "row", axis=0, tiled=True)
    shared_width = full_shared_in.shape[1] // 2
    shared_pre = matmul(group_two, full_shared_in)
    shared_gate, shared_up = shared_pre[:, :shared_width], shared_pre[:, shared_width:]
    shared_act, shared_slope = swish_parts(shared_gate)
    shared_hidden = (shared_act * shared_up).astype(jnp.bfloat16)
    shared_hidden_grad = matmul(group_grad, full_shared_out)
    grad_shared_out = outer_sum(group_grad, shared_hidden)
    shared_pre_grad = jnp.concatenate(
        [shared_hidden_grad * shared_up * shared_slope, shared_hidden_grad * shared_act], axis=1
    ).astype(jnp.bfloat16)
    grad_shared_in = outer_sum(group_two, shared_pre_grad)
    shared_sums = lax.psum_scatter(
        jnp.concatenate(
            [
                matmul_t(shared_hidden, full_shared_out).astype(jnp.bfloat16),
                matmul_t(shared_pre_grad, full_shared_in).astype(jnp.bfloat16),
            ],
            axis=1,
        ),
        "row",
        scatter_dimension=0,
        tiled=True,
    ).astype(jnp.float32)
    shared_branch, shared_input = shared_sums[:, :model_width], shared_sums[:, model_width:]

    expert_in = unpack_slots(received)
    expert_pre = jnp.einsum(
        "esd,edf->esf", expert_in, w_expert_in, preferred_element_type=jnp.float32
    )
    expert_act, expert_slope = swish_parts(expert_pre[..., :expert_ff])
    expert_hidden = (expert_act * expert_pre[..., expert_ff:]).astype(jnp.bfloat16)
    expert_out = jnp.einsum(
        "esf,edf->esd", expert_hidden, w_expert_out, preferred_element_type=jnp.float32
    ).astype(jnp.bfloat16)
    send_out, received_grads = lax.optimization_barrier((pack_slots(expert_out), received_grads))
    returned = exchange(send_out)

    out_grad = unpack_slots(received_grads)
    hidden_grad = jnp.einsum(
        "esd,edf->esf", out_grad, w_expert_out, preferred_element_type=jnp.float32
    )
    expert_pre_grad = jnp.concatenate(
        [hidden_grad * expert_pre[..., expert_ff:] * expert_slope, hidden_grad * expert_act], axis=2
    ).astype(jnp.bfloat16)
    slot_grad = jnp.einsum(
        "esf,edf->esd", expert_pre_grad, w_expert_in, preferred_element_type=jnp.float32
    ).astype(jnp.bfloat16)
    send_back, returned = lax.optimization_barrier((pack_slots(slot_grad), returned))
    returned_grad = exchange(send_back)
    grad_expert_out = jnp.einsum(
        "esd,esf->edf", out_grad, expert_hidden, preferred_element_type=jnp.float32
    )
    grad_expert_in = jnp.einsum(
        "esd,esf->edf", expert_in, expert_pre_grad, preferred_element_type=jnp.float32
    )
    routed_branch, gate_grads = sum_gated(code, returned, send_grads, gates)
    block_out = (hidden_state + shared_branch + routed_branch).astype(jnp.bfloat16)
    gate_grads = gate_grads.transpose(1, 0, 2).reshape(rows_dev, expert_count)
    logit_grad = (
        (1.0 - scores_sig)
        * (gate_grads - gate_weights * jnp.sum(gate_grads, axis=1, keepdims=True))
    ).astype(jnp.bfloat16)
    router_sum = lax.psum(outer_sum(normed_two, logit_grad), ("row", "col"))
    router_input = shared_input + matmul_t(logit_grad, w_router)
    returned_grad, router_input, block_out, grad_expert_in, grad_expert_out = (
        lax.optimization_barrier(
            (returned_grad, router_input, block_out, grad_expert_in, grad_expert_out)
        )
    )

    normed_two_grad = router_input + sum_tokens(code, returned_grad)
    gain_ffn_grad, hidden_back = norm_back(hidden_state, scale_two, gain_ffn, normed_two_grad)
    hidden_total = grad_rows + hidden_back
    (group_branch,) = group_rows([hidden_total.astype(jnp.bfloat16)], 0)
    attended_grad = matmul(group_branch, full_out).astype(jnp.bfloat16)
    grad_out_w = outer_sum(group_branch, attended)

    out_block = attended_grad.reshape(group_tok, local_kv, group_size, head_size)
    probs_full = jnp.exp(block_scores() - log_totals)
    prob_grad = jnp.einsum(
        "qagd,kad->agqk", out_block, value_rows, preferred_element_type=jnp.float32
    )
    row_delta = jnp.sum(probs_full * prob_grad, axis=3, keepdims=True)
    score_low = (probs_full * (prob_grad - row_delta)).astype(jnp.bfloat16)
    query_grad = (
        jnp.einsum("agqk,kad->qagd", score_low, key_rows, preferred_element_type=jnp.float32)
        * inv_root
    ).reshape(group_tok, local_heads, head_size)
    key_grad = (
        jnp.einsum("agqk,qagd->kad", score_low, query_block, preferred_element_type=jnp.float32)
        * inv_root
    )
    value_grad = jnp.einsum(
        "agqk,qagd->kad",
        probs_full.astype(jnp.bfloat16),
        out_block,
        preferred_element_type=jnp.float32,
    )
    query_pre_grad = (
        rotate(query_grad, cosine, -sine_table)
        .astype(jnp.bfloat16)
        .reshape(group_tok, local_heads * head_size)
    )
    keyval_pre_grad = (
        jnp.concatenate([rotate(key_grad, cosine, -sine_table), value_grad], axis=2)
        .astype(jnp.bfloat16)
        .reshape(group_tok, local_kv * 2 * head_size)
    )
    grad_query_w = outer_sum(group_one, query_pre_grad)
    grad_keyval_w = outer_sum(group_one, keyval_pre_grad)
    normed_one_parts = matmul_t(query_pre_grad, full_query) + matmul_t(
        keyval_pre_grad, full_keyval
    )
    shard_grads = [grad_query_w, grad_keyval_w, grad_out_w, grad_shared_in, grad_shared_out]
    shard_grads = jnp.concatenate([part.astype(jnp.bfloat16) for part in shard_grads], axis=1)
    input_total, shard_sums, gain_sums = finish(
        normed_one_parts.astype(jnp.bfloat16).reshape(row_count, rows_dev, model_width),
        shard_grads.reshape(2, 4, 4, -1, shard_grads.shape[1]),
        hidden_total,
        block_in.reshape(rows_dev, model_width),
        scale_one,
        gain_attn[None],
        gain_ffn_grad[None],
    )
    sums, end = [], 0
    for part, like in zip(shards, (w_query, w_keyval, w_out, w_shared_in, w_shared_out)):
        sums.append(shard_sums[:, end : end + part.shape[1]].reshape(like.shape))
        end += part.shape[1]
    return (
        block_out.reshape(1, rows_dev, model_width),
        input_total.reshape(1, rows_dev, model_width),
        gain_sums[0],
        sums[0],
        sums[1],
        sums[2],
        gain_sums[1],
        sums[3],
        sums[4],
        router_sum,
        grad_expert_in,
        grad_expert_out,
    )


def solution(mesh):
    in_specs = (
        P("col", "row", None),
        P(),
        P("col", "row"),
        P("col", "row", None),
        P("col", "row"),
        P(),
        P("col", None, "row"),
        P("col", "row"),
        P(),
        P(("row", "col"), None, None),
        P(("row", "col"), None, None),
        P("col", None),
        P("col", "row", None),
        P("col", "row", None),
    )
    out_specs = (
        P("col", "row", None),
        P("col", "row", None),
        P(),
        P("col", "row"),
        P("col", "row", None),
        P("col", "row"),
        P(),
        P("col", None, "row"),
        P("col", "row"),
        P(),
        P(("row", "col"), None, None),
        P(("row", "col"), None, None),
    )
    return jax.shard_map(
        per_device, mesh=mesh, in_specs=in_specs, out_specs=out_specs, check_vma=False
    )
```

```python
import functools

import jax
import jax.numpy as jnp
from jax import lax
from jax.experimental import pallas as pl
from jax.experimental.pallas import tpu as pltpu
from jax.sharding import PartitionSpec as P

epsilon = 1e-06
rope_base = 10000.0
masked_score = -1e30

EXPERT_ROWS = 6
PAIR_ROWS = 12
PACKED_ROWS = 16
BLOCK_PAIRS = 16
BLOCK = BLOCK_PAIRS * PACKED_ROWS
BLOCK_EXPERTS = 2 * BLOCK_PAIRS
BLOCK_SLOTS = BLOCK_PAIRS * EXPERT_ROWS
QUARTER = 512
SIDE = 128
MESH = pl.DeviceIdType.MESH


def layout(lengths, token_count):
    bounds = jnp.cumsum(lengths)
    places = jnp.arange(token_count, dtype=jnp.int32)
    segment = jnp.sum((places[:, None] >= bounds[None, :]).astype(jnp.int32), axis=1)
    starts = bounds - lengths
    owners = segment[:, None] == jnp.arange(lengths.shape[0], dtype=jnp.int32)[None, :]
    begins = jnp.sum(jnp.where(owners, starts[None, :], 0), axis=1)
    return (segment, places - begins)


def rotary(positions, head_size):
    half_size = head_size // 2
    spread = jnp.arange(half_size, dtype=jnp.float32) * (2.0 / head_size)
    frequency = rope_base ** (-spread)
    angles = positions.astype(jnp.float32)[:, None] * frequency[None, :]
    return (jnp.cos(angles), jnp.sin(angles))


def normalize(values, gain):
    factor = lax.rsqrt(jnp.mean(values * values, axis=1, keepdims=True) + epsilon)
    return (factor, (values * factor * gain).astype(jnp.bfloat16))


def norm_back(values, factor, gain, incoming):
    weighted = gain * incoming
    gain_grad = jnp.sum(incoming * values * factor, axis=0)
    input_grad = factor * weighted - values * factor**3 * jnp.mean(
        weighted * values, axis=1, keepdims=True
    )
    return (gain_grad, input_grad)


def swish_parts(pre_act):
    logistic = jax.nn.sigmoid(pre_act)
    return (pre_act * logistic, logistic * (1.0 + pre_act * (1.0 - logistic)))


def matmul(matrix, partner):
    return jnp.dot(matrix, partner, preferred_element_type=jnp.float32)


def matmul_t(matrix, partner):
    return lax.dot_general(
        matrix, partner, (((1,), (1,)), ((), ())), preferred_element_type=jnp.float32
    )


def outer_sum(matrix, partner):
    return lax.dot_general(
        matrix, partner, (((0,), (0,)), ((), ())), preferred_element_type=jnp.float32
    )


def split_low(values):
    high = values.astype(jnp.bfloat16)
    return high, (values - high.astype(jnp.float32)).astype(jnp.bfloat16)


def row_places():
    row, col = lax.axis_index("row"), lax.axis_index("col")
    chip, core = row // 2, lax.rem(row, 2)
    sibling = chip * 2 + (1 - core)
    partner = (1 - chip) * 2 + core
    across = (1 - chip) * 2 + (1 - core)
    return row, col, sibling, partner, across


def row_copies(sources, targets, send_sem, recv_sem):
    row, col, sibling, partner, _ = row_places()

    def send(origin, target, peer, i):
        return pltpu.make_async_remote_copy(
            src_ref=origin,
            dst_ref=target,
            send_sem=send_sem.at[i],
            recv_sem=recv_sem.at[i],
            device_id=(peer, col),
            device_id_type=MESH,
        )

    far, near, onward = [], [], []
    for i, (source, target) in enumerate(zip(sources, targets)):
        far.append(send(source, target.at[row], partner, 3 * i))
        near.append(send(source, target.at[row], sibling, 3 * i + 1))
        onward.append(send(target.at[partner], target.at[partner], sibling, 3 * i + 2))
    return far, near, onward


def greet(peers):
    barrier = pltpu.get_barrier_semaphore()
    for peer in peers:
        pl.semaphore_signal(barrier, inc=1, device_id=peer, device_id_type=MESH)


def await_greetings(count):
    pl.semaphore_wait(pltpu.get_barrier_semaphore(), count)


def gather_kernel(count, normed, grads, *refs):
    shards, (full, group_one, group_grad) = refs[:count], refs[count : count + 3]
    mine, send_sem, recv_sem, own_sem, row_send, row_recv = refs[count + 3 :]
    row, col, sibling, partner, _ = row_places()
    along_x, along_z, along_y = col // 16, lax.rem(col // 4, 4), lax.rem(col, 4)
    other_x = 1 - along_x
    half_rows = full.shape[1] // 2

    def place(x, z, y):
        return x * 16 + z * 4 + y

    z_near = [lax.rem(along_z + i, 4) for i in (1, 3, 2)]
    y_near = [lax.rem(along_y + i, 4) for i in (1, 3, 2)]
    z_peers = [place(along_x, z, along_y) for z in z_near]
    y_peers = [place(along_x, along_z, y) for y in y_near]
    x_peer = place(other_x, along_z, along_y)
    greet([(row, peer) for peer in z_peers + y_peers + [x_peer]])
    greet([(sibling, col), (partner, col)])
    own = [
        pltpu.make_async_copy(normed, group_one.at[row], own_sem.at[0]),
        pltpu.make_async_copy(grads, group_grad.at[row], own_sem.at[1]),
    ]
    start = 0
    for shard in shards:
        start += shard.shape[1]
        mine[:, start - shard.shape[1] : start] = shard[...]
    own.append(pltpu.make_async_copy(mine, full.at[col], own_sem.at[2]))
    for copy in own:
        copy.start()
    await_greetings(9)

    def pass_on(owner, half, peers, origin=None):
        rows = pl.ds(half * half_rows, half_rows)
        target = full.at[owner, rows]
        for peer in peers:
            pltpu.make_async_remote_copy(
                src_ref=target if origin is None else origin.at[rows],
                dst_ref=target,
                send_sem=send_sem,
                recv_sem=recv_sem.at[half * 32 + owner],
                device_id=(row, peer),
                device_id_type=MESH,
            ).start()

    def await_half(owner, half):
        target = full.at[owner, pl.ds(half * half_rows, half_rows)]
        pltpu.make_async_copy(target, target, recv_sem.at[half * 32 + owner]).wait()

    pass_on(col, 0, [x_peer], mine)
    pass_on(col, 1, [x_peer], mine)
    pass_on(col, 0, z_peers, mine)
    pass_on(col, 1, y_peers, mine)
    far, near, onward = row_copies([normed, grads], [group_one, group_grad], row_send, row_recv)
    far[0].start()
    near[0].start()
    await_half(x_peer, 0)
    pass_on(x_peer, 0, z_peers)
    await_half(x_peer, 1)
    pass_on(x_peer, 1, y_peers)
    pass_on(col, 0, y_peers, mine)
    pass_on(col, 1, z_peers, mine)
    pass_on(x_peer, 0, y_peers)
    pass_on(x_peer, 1, z_peers)
    far[1].start()
    near[1].start()
    for i in range(3):
        for x in (along_x, other_x):
            owner = place(x, z_near[i], along_y)
            await_half(owner, 0)
            pass_on(owner, 0, y_peers)
            owner = place(x, along_z, y_near[i])
            await_half(owner, 1)
            pass_on(owner, 1, z_peers)
    for first, second in zip(far, onward):
        first.wait_recv()
        second.start()
    for x in (along_x, other_x):
        for i in range(4):
            for j in range(3):
                await_half(place(x, lax.rem(along_z + i, 4), y_near[j]), 0)
                await_half(place(x, z_near[j], lax.rem(along_y + i, 4)), 1)
    for copy in own:
        copy.wait()
    for copy in far:
        copy.wait_send()
    for copy in near + onward:
        copy.wait()
    sent = full.at[pl.ds(0, 31)]
    pltpu.make_async_copy(sent, sent, send_sem).wait()


def gather_start(shards, normed, grads):
    space = pl.BlockSpec(memory_space=pl.ANY)
    count = len(shards)
    width = sum(shard.shape[1] for shard in shards)
    full, group_one, group_grad = pl.pallas_call(
        functools.partial(gather_kernel, count),
        out_shape=[
            jax.ShapeDtypeStruct((32, shards[0].shape[0], width), jnp.bfloat16),
            jax.ShapeDtypeStruct((4, *normed.shape), normed.dtype),
            jax.ShapeDtypeStruct((4, *grads.shape), grads.dtype),
        ],
        in_specs=[space] * 2 + [pl.BlockSpec(memory_space=pltpu.VMEM)] * count,
        out_specs=[space] * 3,
        scratch_shapes=[
            pltpu.VMEM((shards[0].shape[0], width), jnp.bfloat16),
            pltpu.SemaphoreType.DMA,
            pltpu.SemaphoreType.DMA((64,)),
            pltpu.SemaphoreType.DMA((3,)),
            pltpu.SemaphoreType.DMA((6,)),
            pltpu.SemaphoreType.DMA((6,)),
        ],
        compiler_params=pltpu.CompilerParams(collective_id=0, has_side_effects=True),
        cost_estimate=pl.CostEstimate(flops=0, bytes_accessed=200 << 20, transcendentals=0),
        name="gather_start",
    )(normed, grads, *shards)
    return [part.reshape(-1, part.shape[2]) for part in (full, group_one, group_grad)]


def turn(values, cosine, sine):
    return values * cosine + pltpu.roll(values, 64, 1) * sine


def score_bias(begin):
    shape = (begin.shape[0], begin.shape[0])
    keys = lax.broadcasted_iota(jnp.int32, shape, 1)
    allowed = (keys >= begin) & (keys <= lax.broadcasted_iota(jnp.int32, shape, 0))
    return jnp.where(allowed, 0.0, masked_score)


def attention_kernel(
    group_one, full, cosine, sine, begin, query, keys, values, attended, norms, parts, *scratch
):
    rows, w_pre, w_back, pre, bias, sems = scratch
    size = keys.shape[1]
    heads = query.shape[1] // size
    pre_width = w_pre.shape[1]
    loads = [
        pltpu.make_async_copy(group_one, rows, sems.at[0]),
        pltpu.make_async_copy(full.at[:, pl.ds(0, pre_width)], w_pre, sems.at[1]),
        pltpu.make_async_copy(full.at[:, pl.ds(pre_width, w_back.shape[1])], w_back, sems.at[2]),
    ]
    for load in loads:
        load.start()
    bias[...] = score_bias(begin[...])
    loads[0].wait()
    loads[1].wait()
    pre[...] = matmul(rows[...], w_pre[...])
    key_start = heads * size
    keys[...] = turn(pre[:, key_start : key_start + size], cosine[...], sine[...]).astype(
        jnp.bfloat16
    )
    values[...] = pre[:, key_start + size :].astype(jnp.bfloat16)
    lanes = lax.broadcasted_iota(jnp.int32, norms.shape, 1)
    log_totals = jnp.zeros(norms.shape, jnp.float32)
    for head in range(heads):
        columns = slice(head * size, (head + 1) * size)
        turned = turn(pre[:, columns], cosine[...], sine[...]).astype(jnp.bfloat16)
        query[:, columns] = turned
        scores = matmul_t(turned, keys[...]) * (size ** (-0.5)) + bias[...]
        highest = jnp.max(scores, axis=1, keepdims=True)
        weights = jnp.exp(scores - highest)
        total = jnp.sum(weights, axis=1, keepdims=True)
        weights = (weights * (1.0 / total)).astype(jnp.bfloat16)
        attended[:, columns] = matmul(weights, values[...]).astype(jnp.bfloat16)
        log_totals = jnp.where(lanes == head, highest + jnp.log(total), log_totals)
    norms[...] = log_totals
    loads[2].wait()
    parts[...] = matmul_t(attended[...], w_back[...]).astype(jnp.bfloat16)


def attention_forward(group_one, full, cosine, sine, begin, heads):
    tokens, width = group_one.shape
    size = cosine.shape[1]
    inner = heads * size
    pre_width = inner + 2 * size
    space = pl.BlockSpec(memory_space=pltpu.VMEM)
    away = pl.BlockSpec(memory_space=pl.ANY)
    low = jnp.bfloat16
    return pl.pallas_call(
        attention_kernel,
        out_shape=[
            jax.ShapeDtypeStruct((tokens, inner), low),
            jax.ShapeDtypeStruct((tokens, size), low),
            jax.ShapeDtypeStruct((tokens, size), low),
            jax.ShapeDtypeStruct((tokens, inner), low),
            jax.ShapeDtypeStruct((tokens, 128), jnp.float32),
            jax.ShapeDtypeStruct((tokens, width), low),
        ],
        in_specs=[away, away, space, space, space],
        out_specs=[space] * 6,
        scratch_shapes=[
            pltpu.VMEM((tokens, width), low),
            pltpu.VMEM((width, pre_width), low),
            pltpu.VMEM((width, inner), low),
            pltpu.VMEM((tokens, pre_width), jnp.float32),
            pltpu.VMEM((tokens, tokens), jnp.float32),
            pltpu.SemaphoreType.DMA((3,)),
        ],
        compiler_params=pltpu.CompilerParams(vmem_limit_bytes=56 << 20),
        cost_estimate=pl.CostEstimate(
            flops=2 * tokens * width * (pre_width + inner) + 8 * tokens * tokens * inner,
            bytes_accessed=12 << 20,
            transcendentals=heads * tokens * tokens,
        ),
        name="attention_forward",
    )(group_one, full, cosine, sine, begin)


def attention_back_kernel(
    group_branch,
    group_one_t,
    full,
    query,
    keys,
    values,
    attended,
    norms,
    cosine,
    sine,
    begin,
    begin_row,
    parts,
    grads,
    *scratch,
):
    branch, rows_t, w_pre, w_back, pre_grad, back, bias, deltas, staged, sems = scratch
    size = keys.shape[1]
    heads = query.shape[1] // size
    inner = heads * size
    pre_width = w_pre.shape[1]
    low = jnp.bfloat16
    loads = [
        pltpu.make_async_copy(group_branch, branch, sems.at[0]),
        pltpu.make_async_copy(full.at[:, pl.ds(pre_width, inner)], w_back, sems.at[1]),
        pltpu.make_async_copy(group_one_t, rows_t, sems.at[2]),
        pltpu.make_async_copy(full.at[:, pl.ds(0, pre_width)], w_pre, sems.at[3]),
    ]
    for load in loads:
        load.start()
    bias[...] = score_bias(begin[...])
    loads[0].wait()
    loads[1].wait()
    back[...] = matmul(branch[...], w_back[...]).astype(low)
    scale = size ** (-0.5)
    lanes = lax.broadcasted_iota(jnp.int32, deltas.shape, 1)
    all_deltas = jnp.zeros(deltas.shape, jnp.float32)
    for head in range(heads):
        columns = slice(head * size, (head + 1) * size)
        turned, outer = query[:, columns], back[:, columns]
        scores = matmul_t(turned, keys[...]) * scale + bias[...]
        probs = jnp.exp(scores - norms[:, head : head + 1])
        prob_grad = matmul_t(outer, values[...])
        delta = jnp.sum(probs * prob_grad, axis=1, keepdims=True)
        all_deltas = jnp.where(lanes == head, delta, all_deltas)
        score_grad = (probs * (prob_grad - delta)).astype(low)
        query_grad = matmul(score_grad, keys[...]) * scale
        pre_grad[:, columns] = turn(query_grad, cosine[...], -sine[...]).astype(low)
    deltas[...] = all_deltas
    deltas_t = jnp.transpose(deltas[...])
    norms_t = jnp.transpose(norms[...])
    shape = bias.shape
    key_places = lax.broadcasted_iota(jnp.int32, shape, 0)
    allowed = (key_places >= begin_row[...]) & (
        key_places <= lax.broadcasted_iota(jnp.int32, shape, 1)
    )
    bias[...] = jnp.where(allowed, 0.0, masked_score)
    key_grad = jnp.zeros(keys.shape, jnp.float32)
    value_grad = jnp.zeros(values.shape, jnp.float32)
    for head in range(heads):
        columns = slice(head * size, (head + 1) * size)
        turned, outer = query[:, columns], back[:, columns]
        scores = matmul_t(keys[...], turned) * scale + bias[...]
        probs = jnp.exp(scores - norms_t[head : head + 1])
        prob_grad = matmul_t(values[...], outer)
        score_grad = (probs * (prob_grad - deltas_t[head : head + 1])).astype(low)
        key_grad = key_grad + matmul(score_grad, turned)
        value_grad = value_grad + matmul(probs.astype(low), outer)
    pre_grad[:, inner : inner + size] = turn(key_grad * scale, cosine[...], -sine[...]).astype(low)
    pre_grad[:, inner + size :] = value_grad.astype(low)
    loads[2].wait()
    loads[3].wait()
    parts[...] = matmul_t(pre_grad[...], w_pre[...]).astype(low)
    blocks, depth = 4, branch.shape[1] // 4
    copies = []
    for i in range(blocks):
        block = slice(i * depth, (i + 1) * depth)
        staged[i, :, :pre_width] = matmul(rows_t[block], pre_grad[...]).astype(low)
        staged[i, :, pre_width:] = outer_sum(branch[:, block], attended[...]).astype(low)
        target = grads.at[pl.ds(i * depth, depth)]
        copies.append(pltpu.make_async_copy(staged.at[i], target, sems.at[4 + i]))
        copies[i].start()
    for copy in copies:
        copy.wait()


def attention_back(group_branch, group_one_t, full, kept, cosine, sine, begin):
    tokens, width = group_branch.shape
    size = cosine.shape[1]
    inner = kept[0].shape[1]
    pre_width = inner + 2 * size
    space = pl.BlockSpec(memory_space=pltpu.VMEM)
    away = pl.BlockSpec(memory_space=pl.ANY)
    low = jnp.bfloat16
    return pl.pallas_call(
        attention_back_kernel,
        out_shape=[
            jax.ShapeDtypeStruct((tokens, width), low),
            jax.ShapeDtypeStruct((width, pre_width + inner), low),
        ],
        in_specs=[away] * 3 + [space] * 9,
        out_specs=[space, away],
        scratch_shapes=[
            pltpu.VMEM((tokens, width), low),
            pltpu.VMEM((width, tokens), low),
            pltpu.VMEM((width, pre_width), low),
            pltpu.VMEM((width, inner), low),
            pltpu.VMEM((tokens, pre_width), low),
            pltpu.VMEM((tokens, inner), low),
            pltpu.VMEM((tokens, tokens), jnp.float32),
            pltpu.VMEM((tokens, 128), jnp.float32),
            pltpu.VMEM((4, width // 4, pre_width + inner), low),
            pltpu.SemaphoreType.DMA((8,)),
        ],
        compiler_params=pltpu.CompilerParams(vmem_limit_bytes=56 << 20),
        cost_estimate=pl.CostEstimate(
            flops=4 * tokens * width * (pre_width + inner) + 20 * tokens * tokens * inner,
            bytes_accessed=20 << 20,
            transcendentals=4 * tokens * tokens,
        ),
        name="attention_back",
    )(group_branch, group_one_t, full, *kept, cosine, sine, begin, begin.reshape(1, -1))


def remote(source, target, sems, at, peer):
    return pltpu.make_async_remote_copy(
        src_ref=source,
        dst_ref=target,
        send_sem=sems[0].at[at],
        recv_sem=sems[1].at[at],
        device_id=peer,
        device_id_type=MESH,
    )


def row_sum_copies(parts, near, far, outgoing, sems, at):
    _, col, sibling, partner, across = row_places()
    return [
        remote(parts.at[across], near.at[0], sems, at, (sibling, col)),
        remote(parts.at[sibling], near.at[1], sems, at + 1, (sibling, col)),
        remote(outgoing, far, sems, at + 2, (partner, col)),
    ]


def row_sum_forward(parts, near, outgoing, copies):
    _, _, _, partner, _ = row_places()
    copies[0].wait_recv()
    outgoing[...] = (parts[partner].astype(jnp.float32) + near[0].astype(jnp.float32)).astype(
        jnp.bfloat16
    )
    copies[2].start()


def row_sum_total(parts, near, far, copies):
    row = row_places()[0]
    copies[1].wait_recv()
    total = parts[row].astype(jnp.float32) + near[1].astype(jnp.float32)
    copies[2].wait_recv()
    return total + far[...].astype(jnp.float32)


def norm_rows_kernel(
    parts, inputs, gain, hidden, normed, scale, near, far, outgoing, send_sem, recv_sem
):
    row, col, sibling, partner, _ = row_places()
    greet([(sibling, col), (partner, col)])
    await_greetings(2)
    copies = row_sum_copies(parts, near, far, outgoing, (send_sem, recv_sem), 0)
    copies[0].start()
    copies[1].start()
    row_sum_forward(parts, near, outgoing, copies)
    total = inputs[...].astype(jnp.float32) + row_sum_total(parts, near, far, copies)
    hidden[...] = total
    factor = lax.rsqrt(jnp.mean(total * total, axis=1, keepdims=True) + epsilon)
    normed[...] = (total * factor * gain[...]).astype(jnp.bfloat16)
    scale[...] = factor
    for copy in copies:
        copy.wait_send()


def norm_rows(partial_sums, inputs, gain):
    rows, width = inputs.shape
    space = pl.BlockSpec(memory_space=pltpu.VMEM)
    return pl.pallas_call(
        norm_rows_kernel,
        out_shape=[
            jax.ShapeDtypeStruct((rows, width), jnp.float32),
            jax.ShapeDtypeStruct((rows, width), jnp.bfloat16),
            jax.ShapeDtypeStruct((rows, 1), jnp.float32),
        ],
        in_specs=[space] * 3,
        out_specs=[space] * 3,
        scratch_shapes=[
            pltpu.VMEM((2, rows, width), jnp.bfloat16),
            pltpu.VMEM((rows, width), jnp.bfloat16),
            pltpu.VMEM((rows, width), jnp.bfloat16),
            pltpu.SemaphoreType.DMA((3,)),
            pltpu.SemaphoreType.DMA((3,)),
        ],
        compiler_params=pltpu.CompilerParams(
            collective_id=8, has_side_effects=True, vmem_limit_bytes=32 << 20
        ),
        cost_estimate=pl.CostEstimate(flops=0, bytes_accessed=64 << 20, transcendentals=0),
        name="norm_rows",
    )(partial_sums.reshape(4, rows, width), inputs, gain)


class ScatterSum:
    def __init__(self, grads, scratch):
        self.grads = grads
        self.first, self.first_sum, self.second, self.second_sum, self.third = scratch[:5]
        self.one, self.two, self.three = scratch[5:7], scratch[7:9], scratch[9:11]
        row, col = lax.axis_index("row"), lax.axis_index("col")
        x, z, y = col // 16, lax.rem(col // 4, 4), lax.rem(col, 4)
        self.place = (x, z, y)
        self.half_rows = grads.shape[3] // 2
        self.y_peers = [(row, x * 16 + z * 4 + lax.rem(y + i, 4)) for i in (1, 2, 3)]
        self.z_peers = [(row, x * 16 + lax.rem(z + i, 4) * 4 + y) for i in (1, 2, 3)]
        self.x_peer = (row, (1 - x) * 16 + z * 4 + y)
        self.one_copies, self.two_copies, self.three_copies = {}, {}, []

    @staticmethod
    def scratch(grads):
        half_rows, depth = grads.shape[3] // 2, grads.shape[4]
        low = jnp.bfloat16
        return [
            pltpu.VMEM((2, 2, 3, 4, half_rows, depth), low),
            pltpu.VMEM((2, 2, 4, half_rows, depth), low),
            pltpu.VMEM((2, 2, 3, half_rows, depth), low),
            pltpu.VMEM((2, half_rows, depth), low),
            pltpu.VMEM((2, half_rows, depth), low),
        ] + [pltpu.SemaphoreType.DMA((count,)) for count in (12, 12, 12, 12, 2, 2)]

    def half(self, half):
        return pl.ds(half * self.half_rows, self.half_rows)

    def start(self):
        x, z, y = self.place
        for turn, owner_x in enumerate((1 - x, x)):
            for i in range(3):
                for half in range(2):
                    if half == 0:
                        source = self.grads.at[owner_x, :, lax.rem(y + i + 1, 4), self.half(0)]
                    else:
                        source = self.grads.at[owner_x, lax.rem(z + i + 1, 4), :, self.half(1)]
                    at = (turn * 2 + half) * 3 + i
                    peer = (self.y_peers, self.z_peers)[half][i]
                    copy = remote(source, self.first.at[turn, half, i], self.one, at, peer)
                    self.one_copies[turn, half, i] = copy
                    copy.start()

    def add_first(self, turn):
        x, z, y = self.place
        owner_x = (1 - x, x)[turn]
        for half in range(2):
            for i in range(3):
                self.one_copies[turn, half, i].wait_recv()

            def add(k, carry, half=half):
                if half == 0:
                    total = self.grads[owner_x, k, y, self.half(0)].astype(jnp.float32)
                else:
                    total = self.grads[owner_x, z, k, self.half(1)].astype(jnp.float32)
                for i in range(3):
                    total = total + self.first[turn, half, i, k].astype(jnp.float32)
                self.first_sum[turn, half, k] = total.astype(jnp.bfloat16)
                return carry

            lax.fori_loop(0, 4, add, 0)
            for i in range(3):
                away = lax.rem((z, y)[half] + i + 1, 4)
                copy = remote(
                    self.first_sum.at[turn, half, away],
                    self.second.at[turn, half, i],
                    self.two,
                    (turn * 2 + half) * 3 + i,
                    (self.z_peers, self.y_peers)[half][i],
                )
                self.two_copies[turn, half, i] = copy
                copy.start()

    def second_total(self, turn, half):
        _, z, y = self.place
        for i in range(3):
            self.two_copies[turn, half, i].wait_recv()
        total = self.first_sum[turn, half, (z, y)[half]].astype(jnp.float32)
        for i in range(3):
            total = total + self.second[turn, half, i].astype(jnp.float32)
        return total

    def add_second(self):
        for half in range(2):
            self.second_sum[half] = self.second_total(0, half).astype(jnp.bfloat16)
            copy = remote(
                self.second_sum.at[half], self.third.at[half], self.three, half, self.x_peer
            )
            self.three_copies.append(copy)
            copy.start()

    def add_third(self, pieces):
        for half in range(2):
            total = self.second_total(1, half)
            self.three_copies[half].wait_recv()
            total = total + self.third[half].astype(jnp.float32)
            start = 0
            for piece in pieces:
                piece[self.half(half)] = total[:, start : start + piece.shape[1]]
                start += piece.shape[1]

    def end(self):
        for copy in [*self.one_copies.values(), *self.two_copies.values(), *self.three_copies]:
            copy.wait_send()


def branch_rows_kernel(branch, router, grads, group, router_sum, *refs):
    pieces, scratch = refs[:2], refs[2:]
    near, far, outgoing, send, recv, own_sem, row_send, row_recv = scratch[:8]
    row, col, sibling, partner, _ = row_places()
    scatter = ScatterSum(grads, scratch[8:])
    greet([(sibling, col), (partner, col)])
    greet(scatter.y_peers + scatter.z_peers + [scatter.x_peer])
    own = pltpu.make_async_copy(branch, group.at[row], own_sem)
    own.start()
    await_greetings(9)
    far_rows, near_rows, onward = row_copies([branch], [group], send, recv)
    far_rows[0].start()
    near_rows[0].start()
    copies = row_sum_copies(router, near, far, outgoing, (row_send, row_recv), 0)
    copies[0].start()
    copies[1].start()
    scatter.start()
    row_sum_forward(router, near, outgoing, copies)
    scatter.add_first(0)
    scatter.add_first(1)
    far_rows[0].wait_recv()
    onward[0].start()
    scatter.add_second()
    router_sum[...] = row_sum_total(router, near, far, copies).astype(jnp.bfloat16)
    scatter.add_third(pieces)
    own.wait()
    far_rows[0].wait_send()
    near_rows[0].wait()
    onward[0].wait()
    for copy in copies:
        copy.wait_send()
    scatter.end()


def branch_rows(branch, router, grads, widths):
    away = pl.BlockSpec(memory_space=pl.ANY)
    space = pl.BlockSpec(memory_space=pltpu.VMEM)
    _, rows, width = router.shape
    group, router_sum, *sums = pl.pallas_call(
        branch_rows_kernel,
        out_shape=[
            jax.ShapeDtypeStruct((4, *branch.shape), branch.dtype),
            jax.ShapeDtypeStruct((rows, width), jnp.bfloat16),
        ]
        + [jax.ShapeDtypeStruct((grads.shape[3], part), jnp.float32) for part in widths],
        in_specs=[away, space, space],
        out_specs=[away, space] + [space] * len(widths),
        scratch_shapes=[
            pltpu.VMEM((2, rows, width), jnp.bfloat16),
            pltpu.VMEM((rows, width), jnp.bfloat16),
            pltpu.VMEM((rows, width), jnp.bfloat16),
            pltpu.SemaphoreType.DMA((3,)),
            pltpu.SemaphoreType.DMA((3,)),
            pltpu.SemaphoreType.DMA,
            pltpu.SemaphoreType.DMA((3,)),
            pltpu.SemaphoreType.DMA((3,)),
            *ScatterSum.scratch(grads),
        ],
        compiler_params=pltpu.CompilerParams(
            collective_id=1, has_side_effects=True, vmem_limit_bytes=32 << 20
        ),
        cost_estimate=pl.CostEstimate(flops=0, bytes_accessed=64 << 20, transcendentals=0),
        name="branch_rows",
    )(branch, router, grads)
    return group.reshape(-1, branch.shape[1]), router_sum, sums


def finish_kernel(
    parts,
    grads,
    shared_parts,
    router_part,
    stream,
    inputs,
    scale,
    gain,
    gain_ffn,
    result,
    block_out,
    router,
    gains,
    *refs,
):
    pieces, scratch = refs[:3], refs[3:]
    near, far, outgoing, values, buffers, router_in, router_own = scratch[:7]
    row_send, row_recv, gain_send, gain_recv, own_sem = scratch[7:12]
    col_send, col_recv, pass_send, pass_recv = scratch[12:16]
    scatter = ScatterSum(grads, scratch[16:])
    row, col, sibling, partner, across = row_places()
    row_peers = [(peer, col) for peer in (sibling, partner, across)]

    greet(row_peers)
    barrier = pltpu.get_barrier_semaphore()

    def greet_col(step, carry):
        peer = (row, lax.rem(col + step, 32))
        pl.semaphore_signal(barrier, inc=1, device_id=peer, device_id_type=MESH)
        return carry

    lax.fori_loop(1, 32, greet_col, 0)
    await_greetings(34)

    row_sems = (row_send, row_recv)
    attn_copies = row_sum_copies(parts, near.at[0], far.at[0], outgoing.at[0], row_sems, 0)
    shared_copies = row_sum_copies(
        shared_parts, near.at[1], far.at[1], outgoing.at[1], row_sems, 3
    )
    for copies in (attn_copies, shared_copies):
        copies[0].start()
        copies[1].start()
    row_sum_forward(parts, near.at[0], outgoing.at[0], attn_copies)

    def push(source, target, at):
        def step(i, carry):
            peer = lax.rem(col + i, 32)
            pltpu.make_async_remote_copy(
                src_ref=source(peer),
                dst_ref=target,
                send_sem=col_send.at[at],
                recv_sem=col_recv.at[at],
                device_id=(row, peer),
                device_id_type=MESH,
            ).start()
            return carry

        lax.fori_loop(1, 32, step, 0)

    def await_pushes(target, sem):
        others = target.at[pl.ds(0, 31)]
        pltpu.make_async_copy(others, others, sem).wait()

    push(lambda peer: router_part.at[peer], router_in.at[col], 0)
    router_in[col] = router_part[col]

    scatter.start()

    row_sum_forward(shared_parts, near.at[1], outgoing.at[1], shared_copies)
    incoming = row_sum_total(parts, near.at[0], far.at[0], attn_copies)
    rows = inputs[...].astype(jnp.float32)
    factor = scale[...]
    weighted = gain[...] * incoming
    mean = jnp.mean(weighted * rows, axis=1, keepdims=True)
    result[...] = factor * weighted - rows * (factor * factor * factor * mean)
    values[0, 0:1] = jnp.sum(incoming * rows * factor, axis=0, keepdims=True)
    values[0, 1:2] = gain_ffn[...]

    gain_sems = (gain_send, gain_recv)
    gain_copies = []
    stages = (row_peers, scatter.y_peers, scatter.z_peers, [scatter.x_peer])

    def start_gains(stage):
        at = 3 * stage
        for i, peer in enumerate(stages[stage]):
            gain_copies.append(
                remote(values.at[stage], buffers.at[at + i], gain_sems, at + i, peer)
            )
            gain_copies[-1].start()

    def add_gains(stage):
        at = 3 * stage
        total = values[stage]
        for i in range(len(stages[stage])):
            gain_copies[at + i].wait_recv()
            total = total + buffers[at + i]
        values[stage + 1] = total

    start_gains(0)
    await_pushes(router_in, col_recv.at[0])
    router_own[...] = jnp.sum(router_in[...].astype(jnp.float32), axis=0).astype(jnp.bfloat16)
    push(lambda peer: router_own, router.at[row, col], 1)
    own = pltpu.make_async_copy(router_own, router.at[row, col], own_sem)
    own.start()
    scatter.add_first(0)
    add_gains(0)
    start_gains(1)
    own.wait()
    await_pushes(router.at[row], col_recv.at[1])
    far_rows, near_rows, onward = row_copies([router.at[row]], [router], pass_send, pass_recv)
    far_rows[0].start()
    near_rows[0].start()
    scatter.add_first(1)
    add_gains(1)
    start_gains(2)
    shared = row_sum_total(shared_parts, near.at[1], far.at[1], shared_copies)
    block_out[...] = (stream[...] + shared).astype(jnp.bfloat16)
    far_rows[0].wait_recv()
    onward[0].start()
    scatter.add_second()
    add_gains(2)
    start_gains(3)
    scatter.add_third(pieces)
    add_gains(3)
    gains[...] = values[4]
    await_pushes(router_in, col_send.at[0])
    await_pushes(router.at[row], col_send.at[1])
    far_rows[0].wait_send()
    near_rows[0].wait()
    onward[0].wait()
    for done in [*attn_copies, *shared_copies, *gain_copies]:
        done.wait_send()
    scatter.end()


def finish(parts, grads, shared_parts, router_part, stream, inputs, scale, gain, gain_ffn, widths):
    space = pl.BlockSpec(memory_space=pltpu.VMEM)
    away = pl.BlockSpec(memory_space=pl.ANY)
    rows, width = inputs.shape
    low = jnp.bfloat16
    share = router_part.shape[1:]
    return pl.pallas_call(
        finish_kernel,
        out_shape=[
            jax.ShapeDtypeStruct((rows, width), jnp.float32),
            jax.ShapeDtypeStruct((rows, width), low),
            jax.ShapeDtypeStruct((4, 32, *share), low),
            jax.ShapeDtypeStruct((2, width), jnp.float32),
        ]
        + [jax.ShapeDtypeStruct((grads.shape[3], part), jnp.float32) for part in widths],
        in_specs=[space] * 9,
        out_specs=[space, space, away, space] + [space] * len(widths),
        scratch_shapes=[
            pltpu.VMEM((2, 2, rows, width), low),
            pltpu.VMEM((2, rows, width), low),
            pltpu.VMEM((2, rows, width), low),
            pltpu.VMEM((5, 2, width), jnp.float32),
            pltpu.VMEM((10, 2, width), jnp.float32),
            pltpu.VMEM((32, *share), low),
            pltpu.VMEM(share, low),
            pltpu.SemaphoreType.DMA((6,)),
            pltpu.SemaphoreType.DMA((6,)),
            pltpu.SemaphoreType.DMA((10,)),
            pltpu.SemaphoreType.DMA((10,)),
            pltpu.SemaphoreType.DMA,
            pltpu.SemaphoreType.DMA((2,)),
            pltpu.SemaphoreType.DMA((2,)),
            pltpu.SemaphoreType.DMA((3,)),
            pltpu.SemaphoreType.DMA((3,)),
            *ScatterSum.scratch(grads),
        ],
        compiler_params=pltpu.CompilerParams(
            collective_id=16, has_side_effects=True, vmem_limit_bytes=60 << 20
        ),
        cost_estimate=pl.CostEstimate(flops=0, bytes_accessed=200 << 20, transcendentals=0),
        name="finish",
    )(parts, grads, shared_parts, router_part, stream, inputs, scale, gain, gain_ffn)


def packed_places(shape, axis):
    index = lax.broadcasted_iota(jnp.int32, shape, axis)
    pair, place = index // PACKED_ROWS, lax.rem(index, PACKED_ROWS)
    found = []
    for part in range(-1, 3):
        if part < 0:
            valid, slot = place < PAIR_ROWS, place
        else:
            valid, slot = place >= PAIR_ROWS, 3 * (place - PAIR_ROWS) + part
        second = (slot >= EXPERT_ROWS).astype(jnp.int32)
        found.append((valid, pair, second, slot - EXPERT_ROWS * second))
    return found


def token_marks(code_block):
    marks = []
    wide = (BLOCK, BLOCK_EXPERTS)
    lanes = lax.broadcasted_iota(jnp.int32, wide, 1)
    for (valid, pair, second, _), (tall, _, _, order) in zip(
        packed_places(wide, 0), packed_places((BLOCK, SIDE), 0)
    ):
        owner = ((lanes == 2 * pair + second) & valid).astype(jnp.float32).astype(jnp.bfloat16)
        found = matmul(owner, code_block)
        hit = (found == order.astype(jnp.float32)) & tall
        marks.append((owner, hit.astype(jnp.float32)))
    return marks


def gate_weights_of(owner, hit, high, low):
    weights = hit * (matmul(owner, high) + matmul(owner, low))
    return split_low(weights)


def pack_tokens_kernel(with_gates, code, values, *refs):
    packed = refs[-1]
    marks = token_marks(code[0])
    if with_gates:
        weights = [gate_weights_of(owner, hit, refs[0][0], refs[1][0]) for owner, hit in marks]
    else:
        weights = [(hit.astype(jnp.bfloat16),) for _, hit in marks]
    copies = len(weights[0])
    last = values[:, 3 * QUARTER :]
    for part in range(3):
        columns = slice(part * QUARTER, (part + 1) * QUARTER)
        both = jnp.concatenate([*weights[0], *weights[part + 1]], axis=1)
        rows = jnp.concatenate([values[:, columns]] * copies + [last] * copies, axis=0)
        packed[:, columns] = matmul(both, rows).astype(jnp.bfloat16)


def pack_tokens(code, values, gates=()):
    blocks = code.shape[0]
    width = 3 * QUARTER
    small = pl.BlockSpec((1, BLOCK_EXPERTS, SIDE), lambda i: (i, 0, 0))
    return pl.pallas_call(
        functools.partial(pack_tokens_kernel, len(gates) > 0),
        grid=(blocks,),
        out_shape=jax.ShapeDtypeStruct((blocks * BLOCK, width), jnp.bfloat16),
        in_specs=[small, pl.BlockSpec(values.shape, lambda i: (0, 0))] + [small] * len(gates),
        out_specs=pl.BlockSpec((BLOCK, width), lambda i: (i, 0)),
        compiler_params=pltpu.CompilerParams(vmem_limit_bytes=32 << 20),
        cost_estimate=pl.CostEstimate(
            flops=blocks * BLOCK * 256 * width * 2, bytes_accessed=8 << 20, transcendentals=0
        ),
        name="pack_tokens",
    )(code, values, *gates)


def slot_marks():
    shape = (2 * BLOCK_SLOTS, BLOCK)
    rows = lax.broadcasted_iota(jnp.int32, shape, 0)
    marks = []
    for valid, pair, second, order in packed_places(shape, 1):
        hit = (rows == second * BLOCK_SLOTS + pair * EXPERT_ROWS + order) & valid
        marks.append(hit.astype(jnp.float32).astype(jnp.bfloat16))
    return marks


def unpack_slots_kernel(packed, values):
    marks = slot_marks()
    last = jnp.zeros((2 * BLOCK_SLOTS, QUARTER), jnp.float32)
    for part in range(3):
        columns = slice(part * QUARTER, (part + 1) * QUARTER)
        found = matmul(marks[0], packed[:, columns]).astype(jnp.bfloat16)
        values[0, :, columns] = found[:BLOCK_SLOTS]
        values[1, :, columns] = found[BLOCK_SLOTS:]
        last = last + matmul(marks[part + 1], packed[:, columns])
    last = last.astype(jnp.bfloat16)
    values[0, :, 3 * QUARTER :] = last[:BLOCK_SLOTS]
    values[1, :, 3 * QUARTER :] = last[BLOCK_SLOTS:]


def unpack_slots(packed):
    blocks = packed.shape[0] // BLOCK
    slots = blocks * BLOCK_SLOTS
    return pl.pallas_call(
        unpack_slots_kernel,
        grid=(blocks,),
        out_shape=jax.ShapeDtypeStruct((2, slots, 4 * QUARTER), jnp.bfloat16),
        in_specs=[pl.BlockSpec((BLOCK, 3 * QUARTER), lambda i: (i, 0))],
        out_specs=pl.BlockSpec((2, BLOCK_SLOTS, 4 * QUARTER), lambda i: (0, i, 0)),
        compiler_params=pltpu.CompilerParams(vmem_limit_bytes=32 << 20),
        cost_estimate=pl.CostEstimate(
            flops=blocks * 2 * BLOCK_SLOTS * BLOCK * 6 * QUARTER * 2,
            bytes_accessed=14 << 20,
            transcendentals=0,
        ),
        name="unpack_slots",
    )(packed)


def pack_slots_kernel(values, packed):
    marks = slot_marks()
    last = jnp.concatenate([values[0, :, 3 * QUARTER :], values[1, :, 3 * QUARTER :]], axis=0)
    for part in range(3):
        columns = slice(part * QUARTER, (part + 1) * QUARTER)
        rows = jnp.concatenate([values[0, :, columns], values[1, :, columns]], axis=0)
        found = outer_sum(marks[0], rows) + outer_sum(marks[part + 1], last)
        packed[:, columns] = found.astype(jnp.bfloat16)


def pack_slots(values):
    slots = values.shape[1]
    blocks = slots // BLOCK_SLOTS
    return pl.pallas_call(
        pack_slots_kernel,
        grid=(blocks,),
        out_shape=jax.ShapeDtypeStruct((blocks * BLOCK, 3 * QUARTER), jnp.bfloat16),
        in_specs=[pl.BlockSpec((2, BLOCK_SLOTS, 4 * QUARTER), lambda i: (0, i, 0))],
        out_specs=pl.BlockSpec((BLOCK, 3 * QUARTER), lambda i: (i, 0)),
        compiler_params=pltpu.CompilerParams(vmem_limit_bytes=32 << 20),
        cost_estimate=pl.CostEstimate(
            flops=blocks * 2 * BLOCK_SLOTS * BLOCK * 6 * QUARTER * 2,
            bytes_accessed=14 << 20,
            transcendentals=0,
        ),
        name="pack_slots",
    )(values)


def sum_tokens_kernel(code, packed, total):
    @pl.when(pl.program_id(0) == 0)
    def _():
        total[...] = jnp.zeros_like(total)

    marks = [hit.astype(jnp.bfloat16) for _, hit in token_marks(code[0])]
    last = jnp.zeros((total.shape[0], QUARTER), jnp.float32)
    for part in range(3):
        columns = slice(part * QUARTER, (part + 1) * QUARTER)
        total[:, columns] += outer_sum(marks[0], packed[:, columns])
        last = last + outer_sum(marks[part + 1], packed[:, columns])
    total[:, 3 * QUARTER :] += last


def sum_gated_kernel(code, packed, grads, high, low, total, gate_grads):
    @pl.when(pl.program_id(0) == 0)
    def _():
        total[...] = jnp.zeros_like(total)

    marks = token_marks(code[0])
    weights = [gate_weights_of(owner, hit, high[0], low[0]) for owner, hit in marks]
    last = jnp.zeros((total.shape[0], QUARTER), jnp.float32)
    whole = jnp.zeros((BLOCK, 1), jnp.float32)
    products = []
    for part in range(3):
        columns = slice(part * QUARTER, (part + 1) * QUARTER)
        rows = packed[:, columns]
        total[:, columns] += outer_sum(weights[0][0], rows) + outer_sum(weights[0][1], rows)
        last = last + outer_sum(weights[part + 1][0], rows) + outer_sum(weights[part + 1][1], rows)
        dots = jnp.sum(
            rows.astype(jnp.float32) * grads[:, columns].astype(jnp.float32),
            axis=1,
            keepdims=True,
        )
        whole = whole + dots
        products.append(dots)
    total[:, 3 * QUARTER :] += last
    found = jnp.zeros(gate_grads.shape[1:], jnp.float32)
    for (owner, hit), dots in zip(marks, [whole, *products]):
        hit = hit.astype(jnp.bfloat16)
        for spread in split_low(dots * owner.astype(jnp.float32)):
            found = found + outer_sum(hit, spread)
    gate_grads[0] = found


def sum_tokens(code, packed):
    blocks, _, tokens = code.shape
    return pl.pallas_call(
        sum_tokens_kernel,
        grid=(blocks,),
        out_shape=jax.ShapeDtypeStruct((tokens, 4 * QUARTER), jnp.float32),
        in_specs=[
            pl.BlockSpec((1, BLOCK_EXPERTS, tokens), lambda i: (i, 0, 0)),
            pl.BlockSpec((BLOCK, 3 * QUARTER), lambda i: (i, 0)),
        ],
        out_specs=pl.BlockSpec((tokens, 4 * QUARTER), lambda i: (0, 0)),
        compiler_params=pltpu.CompilerParams(vmem_limit_bytes=32 << 20),
        cost_estimate=pl.CostEstimate(
            flops=blocks * BLOCK * 128 * 6 * QUARTER * 2,
            bytes_accessed=8 << 20,
            transcendentals=0,
        ),
        name="sum_tokens",
    )(code, packed)


def sum_gated(code, packed, grads, gates):
    blocks, _, tokens = code.shape
    small = pl.BlockSpec((1, BLOCK_EXPERTS, tokens), lambda i: (i, 0, 0))
    wide = pl.BlockSpec((BLOCK, 3 * QUARTER), lambda i: (i, 0))
    return pl.pallas_call(
        sum_gated_kernel,
        grid=(blocks,),
        out_shape=[
            jax.ShapeDtypeStruct((tokens, 4 * QUARTER), jnp.float32),
            jax.ShapeDtypeStruct((blocks, tokens, BLOCK_EXPERTS), jnp.float32),
        ],
        in_specs=[small, wide, wide, small, small],
        out_specs=[
            pl.BlockSpec((tokens, 4 * QUARTER), lambda i: (0, 0)),
            pl.BlockSpec((1, tokens, BLOCK_EXPERTS), lambda i: (i, 0, 0)),
        ],
        compiler_params=pltpu.CompilerParams(vmem_limit_bytes=32 << 20),
        cost_estimate=pl.CostEstimate(
            flops=blocks * BLOCK * 128 * 12 * QUARTER * 2,
            bytes_accessed=14 << 20,
            transcendentals=0,
        ),
        name="sum_gated",
    )(code, packed, grads, *gates)


def exchange(packed):
    pairs = packed.reshape(-1, PACKED_ROWS, packed.shape[1])
    swapped = lax.all_to_all(pairs, ("row", "col"), split_axis=0, concat_axis=0, tiled=True)
    return swapped.reshape(packed.shape)


def per_device(
    block_in,
    gain_attn,
    w_query,
    w_keyval,
    w_out,
    gain_ffn,
    w_shared_in,
    w_shared_out,
    w_router,
    w_expert_in,
    w_expert_out,
    doc_lengths,
    routes,
    cotangent,
):
    row_count = lax.axis_size("row")
    rows_dev = block_in.shape[1]
    model_width = block_in.shape[2]
    group_tok = rows_dev * row_count
    head_size = w_keyval.shape[2] // 2
    local_heads = w_query.shape[1] // head_size
    local_kv = w_keyval.shape[1]
    group_size = local_heads // local_kv
    expert_count = w_router.shape[1]
    expert_ff = w_expert_out.shape[2]
    top_k = routes.shape[2]
    inv_root = head_size ** (-0.5)

    route_ids = routes.reshape(rows_dev, top_k)
    experts = jnp.arange(expert_count, dtype=jnp.int32)
    chosen = jnp.any(route_ids[:, :, None] == experts[None, None, :], axis=1)
    chosen_low = chosen.astype(jnp.bfloat16)
    tokens = jnp.arange(rows_dev, dtype=jnp.int32)
    before = (tokens[None, :] < tokens[:, None]).astype(jnp.bfloat16)
    order = matmul(before, chosen_low)
    code = jnp.where(chosen, order, -1.0).astype(jnp.bfloat16).T
    code = code.reshape(-1, BLOCK_EXPERTS, rows_dev)

    inputs = block_in.reshape(rows_dev, model_width).astype(jnp.float32)
    grad_low = cotangent.reshape(rows_dev, model_width)
    grad_rows = grad_low.astype(jnp.float32)
    scale_one, normed_one = normalize(inputs, gain_attn)
    shards = [w_query, w_keyval, w_out, w_shared_in, w_shared_out]
    shards = [part.reshape(part.shape[0], -1) for part in shards]
    full, group_one, group_grad = gather_start(shards, normed_one, grad_low)
    shared_start = w_query.shape[1] + w_keyval.shape[2] + w_out.shape[1]
    shared_width = w_shared_out.shape[1]
    full_shared_in = full[:, shared_start : shared_start + 2 * shared_width]
    full_shared_out = full[:, shared_start + 2 * shared_width :]

    segment, position = layout(doc_lengths.reshape(-1), group_tok)
    cosine, sine_table = rotary(position, head_size)
    cosine = jnp.concatenate([cosine, cosine], axis=1)
    sine_table = jnp.concatenate([-sine_table, sine_table], axis=1)
    begin = (jnp.arange(group_tok, dtype=jnp.int32) - position)[:, None]
    *kept, attended_parts = attention_forward(
        group_one, full, cosine, sine_table, begin, local_heads
    )
    hidden_state, normed_two, scale_two = norm_rows(
        attended_parts, block_in.reshape(rows_dev, model_width), gain_ffn[None]
    )

    logits = matmul(normed_two, w_router)
    scores_sig = jnp.where(chosen, jax.nn.sigmoid(logits), 0.0)
    score_sum = jnp.sum(scores_sig, axis=1, keepdims=True)
    gate_weights = scores_sig / score_sum
    gates = [
        part.T.reshape(-1, BLOCK_EXPERTS, rows_dev) for part in split_low(gate_weights)
    ]
    received = exchange(pack_tokens(code, normed_two))
    send_grads, received = lax.optimization_barrier((pack_tokens(code, grad_low, gates), received))
    received_grads = exchange(send_grads)

    group_two = lax.all_gather(normed_two, "row", axis=0, tiled=True)
    shared_pre = matmul(group_two, full_shared_in)
    shared_gate, shared_up = shared_pre[:, :shared_width], shared_pre[:, shared_width:]
    shared_act, shared_slope = swish_parts(shared_gate)
    shared_hidden = (shared_act * shared_up).astype(jnp.bfloat16)
    shared_hidden_grad = matmul(group_grad, full_shared_out)
    shared_pre_grad = jnp.concatenate(
        [shared_hidden_grad * shared_up * shared_slope, shared_hidden_grad * shared_act], axis=1
    ).astype(jnp.bfloat16)
    shared_grads = jnp.concatenate(
        [
            outer_sum(group_two, shared_pre_grad).astype(jnp.bfloat16),
            outer_sum(group_grad, shared_hidden).astype(jnp.bfloat16),
        ],
        axis=1,
    )
    shared_parts = matmul_t(shared_hidden, full_shared_out).astype(jnp.bfloat16)
    shared_input = lax.psum_scatter(
        matmul_t(shared_pre_grad, full_shared_in).astype(jnp.bfloat16),
        "row",
        scatter_dimension=0,
        tiled=True,
    ).astype(jnp.float32)

    expert_in = unpack_slots(received)
    expert_pre = jnp.einsum(
        "esd,edf->esf", expert_in, w_expert_in, preferred_element_type=jnp.float32
    )
    expert_act, expert_slope = swish_parts(expert_pre[..., :expert_ff])
    expert_hidden = (expert_act * expert_pre[..., expert_ff:]).astype(jnp.bfloat16)
    expert_out = jnp.einsum(
        "esf,edf->esd", expert_hidden, w_expert_out, preferred_element_type=jnp.float32
    ).astype(jnp.bfloat16)
    send_out, received_grads = lax.optimization_barrier((pack_slots(expert_out), received_grads))
    returned = exchange(send_out)

    out_grad = unpack_slots(received_grads)
    hidden_grad = jnp.einsum(
        "esd,edf->esf", out_grad, w_expert_out, preferred_element_type=jnp.float32
    )
    expert_pre_grad = jnp.concatenate(
        [hidden_grad * expert_pre[..., expert_ff:] * expert_slope, hidden_grad * expert_act], axis=2
    ).astype(jnp.bfloat16)
    slot_grad = jnp.einsum(
        "esf,edf->esd", expert_pre_grad, w_expert_in, preferred_element_type=jnp.float32
    ).astype(jnp.bfloat16)
    send_back, returned = lax.optimization_barrier((pack_slots(slot_grad), returned))
    returned_grad = exchange(send_back)
    grad_expert_out = jnp.einsum(
        "esd,esf->edf", out_grad, expert_hidden, preferred_element_type=jnp.float32
    )
    grad_expert_in = jnp.einsum(
        "esd,esf->edf", expert_in, expert_pre_grad, preferred_element_type=jnp.float32
    )
    routed_branch, gate_grads = sum_gated(code, returned, send_grads, gates)
    stream = hidden_state + routed_branch
    gate_grads = gate_grads.transpose(1, 0, 2).reshape(rows_dev, expert_count)
    logit_grad = (
        (1.0 - scores_sig)
        * (gate_grads - gate_weights * jnp.sum(gate_grads, axis=1, keepdims=True))
    ).astype(jnp.bfloat16)
    router_parts = outer_sum(normed_two, logit_grad).astype(jnp.bfloat16)
    router_parts = router_parts.reshape(row_count, -1, expert_count)
    router_input = shared_input + matmul_t(logit_grad, w_router)
    shadowed = (router_input, router_parts, stream, shared_grads, group_one.T)
    returned_grad, shadowed, grad_expert_in, grad_expert_out = lax.optimization_barrier(
        (returned_grad, shadowed, grad_expert_in, grad_expert_out)
    )
    router_input, router_parts, stream, shared_grads, group_one_t = shadowed

    normed_two_grad = router_input + sum_tokens(code, returned_grad)
    gain_ffn_grad, hidden_back = norm_back(hidden_state, scale_two, gain_ffn, normed_two_grad)
    hidden_total = grad_rows + hidden_back
    widths = [part.shape[1] for part in shards]
    group_branch, router_sum, shared_sums = branch_rows(
        hidden_total.astype(jnp.bfloat16),
        router_parts,
        shared_grads.reshape(2, 4, 4, -1, shared_grads.shape[1]),
        widths[3:],
    )
    normed_one_parts, shard_grads = attention_back(
        group_branch, group_one_t, full, kept, cosine, sine_table, begin
    )
    input_back, block_out, router_sum, gain_sums, *sums = finish(
        normed_one_parts.reshape(row_count, rows_dev, model_width),
        shard_grads.reshape(2, 4, 4, -1, shard_grads.shape[1]),
        shared_parts.reshape(row_count, rows_dev, model_width),
        router_sum.reshape(32, -1, expert_count),
        stream,
        block_in.reshape(rows_dev, model_width),
        scale_one,
        gain_attn[None],
        gain_ffn_grad[None],
        widths[:3],
    )
    sums = [
        part.reshape(like.shape)
        for part, like in zip(sums + shared_sums, (w_query, w_keyval, w_out, w_shared_in, w_shared_out))
    ]
    return (
        block_out.reshape(1, rows_dev, model_width),
        (hidden_total + input_back).reshape(1, rows_dev, model_width),
        gain_sums[0],
        sums[0],
        sums[1],
        sums[2],
        gain_sums[1],
        sums[3],
        sums[4],
        router_sum.reshape(model_width, expert_count).astype(jnp.float32),
        grad_expert_in,
        grad_expert_out,
    )


def solution(mesh):
    in_specs = (
        P("col", "row", None),
        P(),
        P("col", "row"),
        P("col", "row", None),
        P("col", "row"),
        P(),
        P("col", None, "row"),
        P("col", "row"),
        P(),
        P(("row", "col"), None, None),
        P(("row", "col"), None, None),
        P("col", None),
        P("col", "row", None),
        P("col", "row", None),
    )
    out_specs = (
        P("col", "row", None),
        P("col", "row", None),
        P(),
        P("col", "row"),
        P("col", "row", None),
        P("col", "row"),
        P(),
        P("col", None, "row"),
        P("col", "row"),
        P(),
        P(("row", "col"), None, None),
        P(("row", "col"), None, None),
    )
    return jax.shard_map(
        per_device, mesh=mesh, in_specs=in_specs, out_specs=out_specs, check_vma=False
    )
```

```python
import functools

import jax
import jax.numpy as jnp
import numpy as np
from jax import lax
from jax.experimental import pallas as pl
from jax.experimental.pallas import tpu as pltpu
from jax.sharding import PartitionSpec as P

epsilon = 1e-06
rope_base = 10000.0
masked_score = -1e30

EXPERT_ROWS = 6
PAIR_ROWS = 12
PACKED_ROWS = 16
BLOCK_PAIRS = 16
BLOCK = BLOCK_PAIRS * PACKED_ROWS
BLOCK_EXPERTS = 2 * BLOCK_PAIRS
BLOCK_SLOTS = BLOCK_PAIRS * EXPERT_ROWS
QUARTER = 512
SIDE = 128
MESH = pl.DeviceIdType.MESH
NDOC = 4


def swish_parts(pre_act):
    logistic = jax.nn.sigmoid(pre_act)
    return (pre_act * logistic, logistic * (1.0 + pre_act * (1.0 - logistic)))


def matmul(matrix, partner):
    return jnp.dot(matrix, partner, preferred_element_type=jnp.float32)


def matmul_t(matrix, partner):
    return lax.dot_general(
        matrix, partner, (((1,), (1,)), ((), ())), preferred_element_type=jnp.float32
    )


def outer_sum(matrix, partner):
    return lax.dot_general(
        matrix, partner, (((0,), (0,)), ((), ())), preferred_element_type=jnp.float32
    )


def split_low(values):
    high = values.astype(jnp.bfloat16)
    return high, (values - high.astype(jnp.float32)).astype(jnp.bfloat16)


def row_places():
    row, col = lax.axis_index("row"), lax.axis_index("col")
    chip, core = row // 2, lax.rem(row, 2)
    sibling = chip * 2 + (1 - core)
    partner = (1 - chip) * 2 + core
    across = (1 - chip) * 2 + (1 - core)
    return row, col, sibling, partner, across


def row_copies(sources, targets, send_sem, recv_sem):
    row, col, sibling, partner, _ = row_places()

    def send(origin, target, peer, i):
        return pltpu.make_async_remote_copy(
            src_ref=origin,
            dst_ref=target,
            send_sem=send_sem.at[i],
            recv_sem=recv_sem.at[i],
            device_id=(peer, col),
            device_id_type=MESH,
        )

    far, near, onward = [], [], []
    for i, (source, target) in enumerate(zip(sources, targets)):
        far.append(send(source, target.at[row], partner, 3 * i))
        near.append(send(source, target.at[row], sibling, 3 * i + 1))
        onward.append(send(target.at[partner], target.at[partner], sibling, 3 * i + 2))
    return far, near, onward


def greet(peers):
    barrier = pltpu.get_barrier_semaphore()
    for peer in peers:
        pl.semaphore_signal(barrier, inc=1, device_id=peer, device_id_type=MESH)


def await_greetings(count):
    pl.semaphore_wait(pltpu.get_barrier_semaphore(), count)


def turn(values, cosine, sine):
    return values * cosine + pltpu.roll(values, 64, 1) * sine


def score_bias(begin):
    shape = (begin.shape[0], begin.shape[0])
    keys = lax.broadcasted_iota(jnp.int32, shape, 1)
    allowed = (keys >= begin) & (keys <= lax.broadcasted_iota(jnp.int32, shape, 0))
    return jnp.where(allowed, 0.0, masked_score)


def attention_back_queries(query, keys, values, back, norms, cosine, sine, begin, refs):
    pre_grad, bias, deltas = refs
    size = keys.shape[1]
    bias[...] = score_bias(begin[...])
    scale = size ** (-0.5)
    lanes = lax.broadcasted_iota(jnp.int32, deltas.shape, 1)
    all_deltas = jnp.zeros(deltas.shape, jnp.float32)
    for head in range(query.shape[1] // size):
        columns = slice(head * size, (head + 1) * size)
        turned, outer = query[:, columns], back[:, columns]
        scores = matmul_t(turned, keys[...]) * scale + bias[...]
        probs = jnp.exp(scores - norms[:, head : head + 1])
        prob_grad = matmul_t(outer, values[...])
        delta = jnp.sum(probs * prob_grad, axis=1, keepdims=True)
        all_deltas = jnp.where(lanes == head, delta, all_deltas)
        score_grad = (probs * (prob_grad - delta)).astype(jnp.bfloat16)
        query_grad = matmul(score_grad, keys[...]) * scale
        pre_grad[:, columns] = turn(query_grad, cosine[...], -sine[...]).astype(jnp.bfloat16)
    deltas[...] = all_deltas


def attention_back_keys(query, keys, values, back, norms, cosine, sine, begin_row, refs):
    pre_grad, bias, deltas = refs
    low = jnp.bfloat16
    size = keys.shape[1]
    inner = query.shape[1]
    scale = size ** (-0.5)
    deltas_t = jnp.transpose(deltas[...])
    norms_t = jnp.transpose(norms[...])
    shape = bias.shape
    key_places = lax.broadcasted_iota(jnp.int32, shape, 0)
    allowed = (key_places >= begin_row[...]) & (
        key_places <= lax.broadcasted_iota(jnp.int32, shape, 1)
    )
    bias[...] = jnp.where(allowed, 0.0, masked_score)
    key_grad = jnp.zeros(keys.shape, jnp.float32)
    value_grad = jnp.zeros(values.shape, jnp.float32)
    for head in range(inner // size):
        columns = slice(head * size, (head + 1) * size)
        turned, outer = query[:, columns], back[:, columns]
        scores = matmul_t(keys[...], turned) * scale + bias[...]
        probs = jnp.exp(scores - norms_t[head : head + 1])
        prob_grad = matmul_t(values[...], outer)
        score_grad = (probs * (prob_grad - deltas_t[head : head + 1])).astype(low)
        key_grad = key_grad + matmul(score_grad, turned)
        value_grad = value_grad + matmul(probs.astype(low), outer)
    pre_grad[:, inner : inner + size] = turn(key_grad * scale, cosine[...], -sine[...]).astype(low)
    pre_grad[:, inner + size :] = value_grad.astype(low)


def remote(source, target, sems, at, peer):
    return pltpu.make_async_remote_copy(
        src_ref=source,
        dst_ref=target,
        send_sem=sems[0].at[at],
        recv_sem=sems[1].at[at],
        device_id=peer,
        device_id_type=MESH,
    )


def row_sum_copies(parts, near, far, outgoing, sems, at):
    _, col, sibling, partner, across = row_places()
    return [
        remote(parts.at[across], near.at[0], sems, at, (sibling, col)),
        remote(parts.at[sibling], near.at[1], sems, at + 1, (sibling, col)),
        remote(outgoing, far, sems, at + 2, (partner, col)),
    ]


def row_sum_forward(parts, near, outgoing, copies):
    _, _, _, partner, _ = row_places()
    copies[0].wait_recv()
    outgoing[...] = (parts[partner].astype(jnp.float32) + near[0].astype(jnp.float32)).astype(
        jnp.bfloat16
    )
    copies[2].start()


def row_sum_total(parts, near, far, copies):
    row = row_places()[0]
    copies[1].wait_recv()
    total = parts[row].astype(jnp.float32) + near[1].astype(jnp.float32)
    copies[2].wait_recv()
    return total + far[...].astype(jnp.float32)


class ScatterSum:
    def __init__(self, grads, scratch):
        self.grads = grads
        self.first, self.first_sum, self.second, self.second_sum, self.third = scratch[:5]
        self.one, self.two, self.three = scratch[5:7], scratch[7:9], scratch[9:11]
        row, col = lax.axis_index("row"), lax.axis_index("col")
        x, z, y = col // 16, lax.rem(col // 4, 4), lax.rem(col, 4)
        self.place = (x, z, y)
        self.half_rows = grads.shape[3] // 2
        self.y_peers = [(row, x * 16 + z * 4 + lax.rem(y + i, 4)) for i in (1, 2, 3)]
        self.z_peers = [(row, x * 16 + lax.rem(z + i, 4) * 4 + y) for i in (1, 2, 3)]
        self.x_peer = (row, (1 - x) * 16 + z * 4 + y)
        self.one_copies, self.two_copies, self.three_copies = {}, {}, []

    @staticmethod
    def scratch(grads):
        half_rows, depth = grads.shape[3] // 2, grads.shape[4]
        low = jnp.bfloat16
        return [
            pltpu.VMEM((2, 2, 3, 4, half_rows, depth), low),
            pltpu.VMEM((2, 2, 4, half_rows, depth), low),
            pltpu.VMEM((2, 2, 3, half_rows, depth), low),
            pltpu.VMEM((2, half_rows, depth), low),
            pltpu.VMEM((2, half_rows, depth), low),
        ] + [pltpu.SemaphoreType.DMA((count,)) for count in (12, 12, 12, 12, 2, 2)]

    def half(self, half):
        return pl.ds(half * self.half_rows, self.half_rows)

    def start(self):
        x, z, y = self.place
        for turn, owner_x in enumerate((1 - x, x)):
            for i in range(3):
                for half in range(2):
                    if half == 0:
                        source = self.grads.at[owner_x, :, lax.rem(y + i + 1, 4), self.half(0)]
                    else:
                        source = self.grads.at[owner_x, lax.rem(z + i + 1, 4), :, self.half(1)]
                    at = (turn * 2 + half) * 3 + i
                    peer = (self.y_peers, self.z_peers)[half][i]
                    copy = remote(source, self.first.at[turn, half, i], self.one, at, peer)
                    self.one_copies[turn, half, i] = copy
                    copy.start()

    def add_first(self, turn):
        x, z, y = self.place
        owner_x = (1 - x, x)[turn]
        for half in range(2):
            for i in range(3):
                self.one_copies[turn, half, i].wait_recv()

            def add(k, carry, half=half):
                if half == 0:
                    total = self.grads[owner_x, k, y, self.half(0)].astype(jnp.float32)
                else:
                    total = self.grads[owner_x, z, k, self.half(1)].astype(jnp.float32)
                for i in range(3):
                    total = total + self.first[turn, half, i, k].astype(jnp.float32)
                self.first_sum[turn, half, k] = total.astype(jnp.bfloat16)
                return carry

            lax.fori_loop(0, 4, add, 0)
            for i in range(3):
                away = lax.rem((z, y)[half] + i + 1, 4)
                copy = remote(
                    self.first_sum.at[turn, half, away],
                    self.second.at[turn, half, i],
                    self.two,
                    (turn * 2 + half) * 3 + i,
                    (self.z_peers, self.y_peers)[half][i],
                )
                self.two_copies[turn, half, i] = copy
                copy.start()

    def second_total(self, turn, half):
        _, z, y = self.place
        for i in range(3):
            self.two_copies[turn, half, i].wait_recv()
        total = self.first_sum[turn, half, (z, y)[half]].astype(jnp.float32)
        for i in range(3):
            total = total + self.second[turn, half, i].astype(jnp.float32)
        return total

    def add_second(self):
        for half in range(2):
            self.second_sum[half] = self.second_total(0, half).astype(jnp.bfloat16)
            copy = remote(
                self.second_sum.at[half], self.third.at[half], self.three, half, self.x_peer
            )
            self.three_copies.append(copy)
            copy.start()

    def add_third(self, pieces):
        for half in range(2):
            total = self.second_total(1, half)
            self.three_copies[half].wait_recv()
            total = total + self.third[half].astype(jnp.float32)
            start = 0
            for piece in pieces:
                piece[self.half(half)] = total[:, start : start + piece.shape[1]]
                start += piece.shape[1]

    def end(self):
        for copy in [*self.one_copies.values(), *self.two_copies.values(), *self.three_copies]:
            copy.wait_send()


def token_back_kernel(
    packed,
    marks,
    router_input,
    hidden,
    scale,
    gain,
    stream_grad,
    router,
    grads,
    group,
    hidden_total,
    gain_grad,
    router_sum,
    *refs,
):
    pieces, scratch = refs[:2], refs[2:]
    held, routed, branch, near, far, outgoing, load_sem, send, recv, own_sem = scratch[:10]
    row_send, row_recv = scratch[10:12]
    row, col, sibling, partner, _ = row_places()
    scatter = ScatterSum(grads, scratch[12:])
    greet([(sibling, col), (partner, col)])
    greet(scatter.y_peers + scatter.z_peers + [scatter.x_peer])
    steps = held.shape[0]
    depth = held.shape[1]
    loads = [
        pltpu.make_async_copy(packed.at[pl.ds(i * depth, depth)], held.at[i], load_sem.at[i])
        for i in range(steps)
    ]
    for load in loads:
        load.start()
    await_greetings(9)
    copies = row_sum_copies(router, near, far, outgoing, (row_send, row_recv), 0)
    copies[0].start()
    copies[1].start()
    scatter.start()
    row_sum_forward(router, near, outgoing, copies)

    for i in range(steps):
        loads[i].wait()
        rows = slice(i * depth, (i + 1) * depth)
        for part in range(4):
            columns = slice(part * QUARTER, (part + 1) * QUARTER)
            if part < 3:
                found = matmul(marks[0, :, rows], held[i, :, columns])
            else:
                found = matmul(marks[1, :, rows], held[i, :, :QUARTER])
                for j in (1, 2):
                    second = slice(j * QUARTER, (j + 1) * QUARTER)
                    found = found + matmul(marks[j + 1, :, rows], held[i, :, second])
            routed[:, columns] = found if i == 0 else routed[:, columns] + found

    incoming = router_input[...] + routed[...]
    values = hidden[...]
    factor = scale[...]
    weighted = gain[...] * incoming
    mean = jnp.mean(weighted * values, axis=1, keepdims=True)
    total = (
        stream_grad[...].astype(jnp.float32)
        + factor * weighted
        - values * (factor * factor * factor * mean)
    )
    hidden_total[...] = total
    branch[...] = total.astype(jnp.bfloat16)
    far_rows, near_rows, onward = row_copies([branch], [group], send, recv)
    far_rows[0].start()
    near_rows[0].start()
    own = pltpu.make_async_copy(branch, group.at[row], own_sem)
    own.start()
    gain_grad[...] = jnp.sum(incoming * values * factor, axis=0, keepdims=True)
    scatter.add_first(0)
    scatter.add_first(1)
    scatter.add_second()
    router_sum[...] = row_sum_total(router, near, far, copies).astype(jnp.bfloat16)
    far_rows[0].wait_recv()
    onward[0].start()
    scatter.add_third(pieces)
    own.wait()
    far_rows[0].wait_send()
    near_rows[0].wait()
    onward[0].wait()
    for copy in copies:
        copy.wait_send()
    scatter.end()


def token_back(packed, marks, router_input, hidden, scale, gain, stream_grad, router, grads, widths):
    away = pl.BlockSpec(memory_space=pl.ANY)
    space = pl.BlockSpec(memory_space=pltpu.VMEM)
    _, rows, width = router.shape
    tokens, model_width = hidden.shape
    low = jnp.bfloat16
    group, hidden_total, gain_grad, router_sum, *sums = pl.pallas_call(
        token_back_kernel,
        out_shape=[
            jax.ShapeDtypeStruct((4, tokens, model_width), low),
            jax.ShapeDtypeStruct((tokens, model_width), jnp.float32),
            jax.ShapeDtypeStruct((1, model_width), jnp.float32),
            jax.ShapeDtypeStruct((rows, width), low),
        ]
        + [jax.ShapeDtypeStruct((grads.shape[3], part), jnp.float32) for part in widths],
        in_specs=[away] + [space] * 8,
        out_specs=[away] + [space] * (3 + len(widths)),
        scratch_shapes=[
            pltpu.VMEM((4, packed.shape[0] // 4, packed.shape[1]), low),
            pltpu.VMEM((tokens, model_width), jnp.float32),
            pltpu.VMEM((tokens, model_width), low),
            pltpu.VMEM((2, rows, width), low),
            pltpu.VMEM((rows, width), low),
            pltpu.VMEM((rows, width), low),
            pltpu.SemaphoreType.DMA((4,)),
            pltpu.SemaphoreType.DMA((3,)),
            pltpu.SemaphoreType.DMA((3,)),
            pltpu.SemaphoreType.DMA,
            pltpu.SemaphoreType.DMA((3,)),
            pltpu.SemaphoreType.DMA((3,)),
            *ScatterSum.scratch(grads),
        ],
        compiler_params=pltpu.CompilerParams(
            collective_id=1, has_side_effects=True, vmem_limit_bytes=48 << 20
        ),
        cost_estimate=pl.CostEstimate(flops=0, bytes_accessed=100 << 20, transcendentals=0),
        name="token_back",
    )(packed, marks, router_input, hidden, scale, gain, stream_grad, router, grads)
    return group.reshape(-1, model_width), hidden_total, gain_grad, router_sum, sums


def finish_kernel(
    group_branch,
    group_one_t,
    full_pre,
    full_back,
    query,
    keys,
    values_in,
    attended,
    norms,
    cosine,
    sine,
    begin,
    begin_row,
    shared_parts,
    router_part,
    stream,
    inputs,
    scale,
    gain,
    gain_ffn,
    result,
    block_out,
    router,
    gains,
    *refs,
):
    pieces, scratch = refs[:3], refs[3:]
    near, far, outgoing, values, buffers, router_in, router_own = scratch[:7]
    row_send, row_recv, gain_send, gain_recv, own_sem = scratch[7:12]
    col_send, col_recv, pass_send, pass_recv = scratch[12:16]
    branch, rows_t, w_pre, w_back, pre_grad, back, bias, deltas, parts, load_sem = scratch[16:26]
    pre_grads, out_grads = scratch[26:28]
    pre_scatter = ScatterSum(pre_grads, scratch[28:39])
    out_scatter = ScatterSum(out_grads, scratch[39:])
    row, col, sibling, partner, across = row_places()
    row_peers = [(peer, col) for peer in (sibling, partner, across)]

    greet(row_peers)
    barrier = pltpu.get_barrier_semaphore()

    def greet_col(step, carry):
        peer = (row, lax.rem(col + step, 32))
        pl.semaphore_signal(barrier, inc=1, device_id=peer, device_id_type=MESH)
        return carry

    lax.fori_loop(1, 32, greet_col, 0)
    pre_width, inner = w_pre.shape[1], w_back.shape[1]
    loads = [
        pltpu.make_async_copy(group_branch, branch, load_sem.at[0]),
        pltpu.make_async_copy(full_back.at[:, pl.ds(0, inner)], w_back, load_sem.at[1]),
        pltpu.make_async_copy(group_one_t, rows_t, load_sem.at[2]),
        pltpu.make_async_copy(full_pre, w_pre, load_sem.at[3]),
    ]
    for load in loads:
        load.start()
    loads[0].wait()
    blocks, depth = 4, branch.shape[1] // 4

    def keep(target, block, rows):
        target[block // 2, 2 * (block % 2) : 2 * (block % 2) + 2] = rows.astype(
            jnp.bfloat16
        ).reshape(2, 4, 64, rows.shape[1])

    for block in range(blocks):
        columns = slice(block * depth, (block + 1) * depth)
        keep(out_grads, block, outer_sum(branch[:, columns], attended[...]))
    loads[1].wait()
    back[...] = matmul(branch[...], w_back[...]).astype(jnp.bfloat16)
    await_greetings(34)
    shared_copies = row_sum_copies(
        shared_parts, near.at[1], far.at[1], outgoing.at[1], (row_send, row_recv), 3
    )
    shared_copies[0].start()
    shared_copies[1].start()

    def push(source, target, at):
        def step(i, carry):
            peer = lax.rem(col + i, 32)
            pltpu.make_async_remote_copy(
                src_ref=source(peer),
                dst_ref=target,
                send_sem=col_send.at[at],
                recv_sem=col_recv.at[at],
                device_id=(row, peer),
                device_id_type=MESH,
            ).start()
            return carry

        lax.fori_loop(1, 32, step, 0)

    def await_pushes(target, sem):
        others = target.at[pl.ds(0, 31)]
        pltpu.make_async_copy(others, others, sem).wait()

    push(lambda peer: router_part.at[peer], router_in.at[col], 0)
    router_in[col] = router_part[col]
    out_scatter.start()
    row_sum_forward(shared_parts, near.at[1], outgoing.at[1], shared_copies)
    saved = (query, keys, values_in, back, norms, cosine, sine)
    attention_back_queries(*saved, begin, (pre_grad, bias, deltas))
    await_pushes(router_in, col_recv.at[0])
    router_own[...] = jnp.sum(router_in[...].astype(jnp.float32), axis=0).astype(jnp.bfloat16)
    push(lambda peer: router_own, router.at[row, col], 1)
    own = pltpu.make_async_copy(router_own, router.at[row, col], own_sem)
    own.start()
    out_scatter.add_first(0)
    attention_back_keys(*saved, begin_row, (pre_grad, bias, deltas))
    loads[3].wait()
    parts[...] = matmul_t(pre_grad[...], w_pre[...]).astype(jnp.bfloat16).reshape(parts.shape)
    attn_copies = row_sum_copies(
        parts, near.at[0], far.at[0], outgoing.at[0], (row_send, row_recv), 0
    )
    attn_copies[0].start()
    attn_copies[1].start()
    out_scatter.add_first(1)
    row_sum_forward(parts, near.at[0], outgoing.at[0], attn_copies)
    loads[2].wait()
    for block in range(blocks):
        rows = slice(block * depth, (block + 1) * depth)
        keep(pre_grads, block, matmul(rows_t[rows], pre_grad[...]))
    pre_scatter.start()
    own.wait()
    await_pushes(router.at[row], col_recv.at[1])
    far_rows, near_rows, onward = row_copies([router.at[row]], [router], pass_send, pass_recv)
    far_rows[0].start()
    near_rows[0].start()
    out_scatter.add_second()

    incoming = row_sum_total(parts, near.at[0], far.at[0], attn_copies)
    rows = inputs[...].astype(jnp.float32)
    factor = scale[...]
    weighted = gain[...] * incoming
    mean = jnp.mean(weighted * rows, axis=1, keepdims=True)
    result[...] = factor * weighted - rows * (factor * factor * factor * mean)
    values[0, 0:1] = jnp.sum(incoming * rows * factor, axis=0, keepdims=True)
    values[0, 1:2] = gain_ffn[...]

    gain_sems = (gain_send, gain_recv)
    gain_copies = []
    stages = (row_peers, pre_scatter.y_peers, pre_scatter.z_peers, [pre_scatter.x_peer])

    def start_gains(stage):
        at = 3 * stage
        for i, peer in enumerate(stages[stage]):
            gain_copies.append(
                remote(values.at[stage], buffers.at[at + i], gain_sems, at + i, peer)
            )
            gain_copies[-1].start()

    def add_gains(stage):
        at = 3 * stage
        total = values[stage]
        for i in range(len(stages[stage])):
            gain_copies[at + i].wait_recv()
            total = total + buffers[at + i]
        values[stage + 1] = total

    start_gains(0)
    shared = row_sum_total(shared_parts, near.at[1], far.at[1], shared_copies)
    block_out[...] = (stream[...] + shared).astype(jnp.bfloat16)
    out_scatter.add_third(pieces[2:])
    add_gains(0)
    start_gains(1)
    pre_scatter.add_first(0)
    add_gains(1)
    start_gains(2)
    pre_scatter.add_first(1)
    far_rows[0].wait_recv()
    onward[0].start()
    add_gains(2)
    start_gains(3)
    pre_scatter.add_second()
    add_gains(3)
    gains[...] = values[4]
    pre_scatter.add_third(pieces[:2])
    await_pushes(router_in, col_send.at[0])
    await_pushes(router.at[row], col_send.at[1])
    far_rows[0].wait_send()
    near_rows[0].wait()
    onward[0].wait()
    for done in [*attn_copies, *shared_copies, *gain_copies]:
        done.wait_send()
    pre_scatter.end()
    out_scatter.end()


def finish(group_branch, group_one_t, weights, kept, tables, rest, widths):
    space = pl.BlockSpec(memory_space=pltpu.VMEM)
    away = pl.BlockSpec(memory_space=pl.ANY)
    low = jnp.bfloat16
    shared_parts, router_part, stream, inputs = rest[:4]
    rows, width = inputs.shape
    tokens = 4 * rows
    share = router_part.shape[1:]
    inner = kept[0].shape[1]
    pre_width = widths[0] + widths[1]
    shard = width // 32
    pre_grads = jax.ShapeDtypeStruct((2, 4, 4, shard, pre_width), low)
    out_grads = jax.ShapeDtypeStruct((2, 4, 4, shard, inner), low)
    return pl.pallas_call(
        finish_kernel,
        out_shape=[
            jax.ShapeDtypeStruct((rows, width), jnp.float32),
            jax.ShapeDtypeStruct((rows, width), low),
            jax.ShapeDtypeStruct((4, 32, *share), low),
            jax.ShapeDtypeStruct((2, width), jnp.float32),
        ]
        + [jax.ShapeDtypeStruct((shard, part), jnp.float32) for part in widths],
        in_specs=[away] * 4 + [space] * 16,
        out_specs=[space, space, away, space] + [space] * len(widths),
        scratch_shapes=[
            pltpu.VMEM((2, 2, rows, width), low),
            pltpu.VMEM((2, rows, width), low),
            pltpu.VMEM((2, rows, width), low),
            pltpu.VMEM((5, 2, width), jnp.float32),
            pltpu.VMEM((10, 2, width), jnp.float32),
            pltpu.VMEM((32, *share), low),
            pltpu.VMEM(share, low),
            pltpu.SemaphoreType.DMA((6,)),
            pltpu.SemaphoreType.DMA((6,)),
            pltpu.SemaphoreType.DMA((10,)),
            pltpu.SemaphoreType.DMA((10,)),
            pltpu.SemaphoreType.DMA,
            pltpu.SemaphoreType.DMA((2,)),
            pltpu.SemaphoreType.DMA((2,)),
            pltpu.SemaphoreType.DMA((3,)),
            pltpu.SemaphoreType.DMA((3,)),
            pltpu.VMEM((tokens, width), low),
            pltpu.VMEM((width, tokens), low),
            pltpu.VMEM((width, pre_width), low),
            pltpu.VMEM((width, inner), low),
            pltpu.VMEM((tokens, pre_width), low),
            pltpu.VMEM((tokens, inner), low),
            pltpu.VMEM((tokens, tokens), jnp.float32),
            pltpu.VMEM((tokens, 128), jnp.float32),
            pltpu.VMEM((4, rows, width), low),
            pltpu.SemaphoreType.DMA((4,)),
            pltpu.VMEM(pre_grads.shape, low),
            pltpu.VMEM(out_grads.shape, low),
            *ScatterSum.scratch(pre_grads),
            *ScatterSum.scratch(out_grads),
        ],
        compiler_params=pltpu.CompilerParams(
            collective_id=16, has_side_effects=True, vmem_limit_bytes=60 << 20
        ),
        cost_estimate=pl.CostEstimate(flops=0, bytes_accessed=200 << 20, transcendentals=0),
        name="finish",
    )(group_branch, group_one_t, *weights, *kept, *tables, *rest)


def packed_places(shape, axis):
    index = lax.broadcasted_iota(jnp.int32, shape, axis)
    pair, place = index // PACKED_ROWS, lax.rem(index, PACKED_ROWS)
    found = []
    for part in range(-1, 3):
        if part < 0:
            valid, slot = place < PAIR_ROWS, place
        else:
            valid, slot = place >= PAIR_ROWS, 3 * (place - PAIR_ROWS) + part
        second = (slot >= EXPERT_ROWS).astype(jnp.int32)
        found.append((valid, pair, second, slot - EXPERT_ROWS * second))
    return found


def token_marks(code_block):
    marks = []
    wide = (BLOCK, BLOCK_EXPERTS)
    lanes = lax.broadcasted_iota(jnp.int32, wide, 1)
    for (valid, pair, second, _), (tall, _, _, order) in zip(
        packed_places(wide, 0), packed_places((BLOCK, SIDE), 0)
    ):
        owner = ((lanes == 2 * pair + second) & valid).astype(jnp.float32).astype(jnp.bfloat16)
        found = matmul(owner, code_block)
        hit = (found == order.astype(jnp.float32)) & tall
        marks.append((owner, hit.astype(jnp.float32)))
    return marks


def gate_weights_of(owner, hit, high, low):
    weights = hit * (matmul(owner, high) + matmul(owner, low))
    return split_low(weights)


def pack_tokens_kernel(code, values, high, low, packed):
    marks = token_marks(code[0])
    weights = [gate_weights_of(owner, hit, high[0], low[0]) for owner, hit in marks]
    last = values[:, 3 * QUARTER :]
    for part in range(3):
        columns = slice(part * QUARTER, (part + 1) * QUARTER)
        both = jnp.concatenate([*weights[0], *weights[part + 1]], axis=1)
        rows = jnp.concatenate([values[:, columns]] * 2 + [last] * 2, axis=0)
        packed[:, columns] = matmul(both, rows).astype(jnp.bfloat16)


def pack_tokens(code, values, gates):
    blocks = code.shape[0]
    width = 3 * QUARTER
    small = pl.BlockSpec((1, BLOCK_EXPERTS, SIDE), lambda i: (i, 0, 0))
    return pl.pallas_call(
        pack_tokens_kernel,
        grid=(blocks,),
        out_shape=jax.ShapeDtypeStruct((blocks * BLOCK, width), jnp.bfloat16),
        in_specs=[small, pl.BlockSpec(values.shape, lambda i: (0, 0)), small, small],
        out_specs=pl.BlockSpec((BLOCK, width), lambda i: (i, 0)),
        compiler_params=pltpu.CompilerParams(vmem_limit_bytes=32 << 20),
        cost_estimate=pl.CostEstimate(
            flops=blocks * BLOCK * 512 * width * 2, bytes_accessed=8 << 20, transcendentals=0
        ),
        name="pack_tokens",
    )(code, values, *gates)


def slot_marks():
    shape = (2 * BLOCK_SLOTS, BLOCK)
    rows = lax.broadcasted_iota(jnp.int32, shape, 0)
    marks = []
    for valid, pair, second, order in packed_places(shape, 1):
        hit = (rows == second * BLOCK_SLOTS + pair * EXPERT_ROWS + order) & valid
        marks.append(hit.astype(jnp.float32).astype(jnp.bfloat16))
    return marks


def unpack_slots_kernel(packed, values):
    marks = slot_marks()
    last = jnp.zeros((2 * BLOCK_SLOTS, QUARTER), jnp.float32)
    for part in range(3):
        columns = slice(part * QUARTER, (part + 1) * QUARTER)
        found = matmul(marks[0], packed[:, columns]).astype(jnp.bfloat16)
        values[0, :, columns] = found[:BLOCK_SLOTS]
        values[1, :, columns] = found[BLOCK_SLOTS:]
        last = last + matmul(marks[part + 1], packed[:, columns])
    last = last.astype(jnp.bfloat16)
    values[0, :, 3 * QUARTER :] = last[:BLOCK_SLOTS]
    values[1, :, 3 * QUARTER :] = last[BLOCK_SLOTS:]


def unpack_slots(packed):
    blocks = packed.shape[0] // BLOCK
    slots = blocks * BLOCK_SLOTS
    return pl.pallas_call(
        unpack_slots_kernel,
        grid=(blocks,),
        out_shape=jax.ShapeDtypeStruct((2, slots, 4 * QUARTER), jnp.bfloat16),
        in_specs=[pl.BlockSpec((BLOCK, 3 * QUARTER), lambda i: (i, 0))],
        out_specs=pl.BlockSpec((2, BLOCK_SLOTS, 4 * QUARTER), lambda i: (0, i, 0)),
        compiler_params=pltpu.CompilerParams(vmem_limit_bytes=32 << 20),
        cost_estimate=pl.CostEstimate(
            flops=blocks * 2 * BLOCK_SLOTS * BLOCK * 6 * QUARTER * 2,
            bytes_accessed=14 << 20,
            transcendentals=0,
        ),
        name="unpack_slots",
    )(packed)


def pack_slots_kernel(values, packed):
    marks = slot_marks()
    last = jnp.concatenate([values[0, :, 3 * QUARTER :], values[1, :, 3 * QUARTER :]], axis=0)
    for part in range(3):
        columns = slice(part * QUARTER, (part + 1) * QUARTER)
        rows = jnp.concatenate([values[0, :, columns], values[1, :, columns]], axis=0)
        found = outer_sum(marks[0], rows) + outer_sum(marks[part + 1], last)
        packed[:, columns] = found.astype(jnp.bfloat16)


def pack_slots(values):
    slots = values.shape[1]
    blocks = slots // BLOCK_SLOTS
    return pl.pallas_call(
        pack_slots_kernel,
        grid=(blocks,),
        out_shape=jax.ShapeDtypeStruct((blocks * BLOCK, 3 * QUARTER), jnp.bfloat16),
        in_specs=[pl.BlockSpec((2, BLOCK_SLOTS, 4 * QUARTER), lambda i: (0, i, 0))],
        out_specs=pl.BlockSpec((BLOCK, 3 * QUARTER), lambda i: (i, 0)),
        compiler_params=pltpu.CompilerParams(vmem_limit_bytes=32 << 20),
        cost_estimate=pl.CostEstimate(
            flops=blocks * 2 * BLOCK_SLOTS * BLOCK * 6 * QUARTER * 2,
            bytes_accessed=14 << 20,
            transcendentals=0,
        ),
        name="pack_slots",
    )(values)


def marks_kernel(code, marks):
    wide = (BLOCK_EXPERTS, BLOCK)
    owners = lax.broadcasted_iota(jnp.int32, wide, 0)
    for i, ((valid, pair, second, _), (tall, _, _, order)) in enumerate(
        zip(packed_places(wide, 1), packed_places((code.shape[1], BLOCK), 1))
    ):
        owner = ((owners == 2 * pair + second) & valid).astype(jnp.float32).astype(jnp.bfloat16)
        hit = (matmul(code[0], owner) == order.astype(jnp.float32)) & tall
        marks[i] = hit.astype(jnp.float32).astype(jnp.bfloat16)


def all_marks(code):
    blocks, experts, tokens = code.shape
    return pl.pallas_call(
        marks_kernel,
        grid=(blocks,),
        out_shape=jax.ShapeDtypeStruct((4, tokens, blocks * BLOCK), jnp.bfloat16),
        in_specs=[pl.BlockSpec((1, tokens, experts), lambda i: (i, 0, 0))],
        out_specs=pl.BlockSpec((4, tokens, BLOCK), lambda i: (0, 0, i)),
        cost_estimate=pl.CostEstimate(flops=1 << 26, bytes_accessed=4 << 20, transcendentals=0),
        name="all_marks",
    )(code.transpose(0, 2, 1))


def sum_gated_kernel(code, packed, grads, high, low, total, gate_grads):
    @pl.when(pl.program_id(0) == 0)
    def _():
        total[...] = jnp.zeros_like(total)

    marks = token_marks(code[0])
    weights = [gate_weights_of(owner, hit, high[0], low[0]) for owner, hit in marks]
    last = jnp.zeros((total.shape[0], QUARTER), jnp.float32)
    whole = jnp.zeros((BLOCK, 1), jnp.float32)
    products = []
    for part in range(3):
        columns = slice(part * QUARTER, (part + 1) * QUARTER)
        rows = packed[:, columns]
        total[:, columns] += outer_sum(weights[0][0], rows) + outer_sum(weights[0][1], rows)
        last = last + outer_sum(weights[part + 1][0], rows) + outer_sum(weights[part + 1][1], rows)
        dots = jnp.sum(
            rows.astype(jnp.float32) * grads[:, columns].astype(jnp.float32),
            axis=1,
            keepdims=True,
        )
        whole = whole + dots
        products.append(dots)
    total[:, 3 * QUARTER :] += last
    found = jnp.zeros(gate_grads.shape[1:], jnp.float32)
    for (owner, hit), dots in zip(marks, [whole, *products]):
        hit = hit.astype(jnp.bfloat16)
        for spread in split_low(dots * owner.astype(jnp.float32)):
            found = found + outer_sum(hit, spread)
    gate_grads[0] = found


def sum_gated(code, packed, grads, gates):
    blocks, _, tokens = code.shape
    small = pl.BlockSpec((1, BLOCK_EXPERTS, tokens), lambda i: (i, 0, 0))
    wide = pl.BlockSpec((BLOCK, 3 * QUARTER), lambda i: (i, 0))
    return pl.pallas_call(
        sum_gated_kernel,
        grid=(blocks,),
        out_shape=[
            jax.ShapeDtypeStruct((tokens, 4 * QUARTER), jnp.float32),
            jax.ShapeDtypeStruct((blocks, tokens, BLOCK_EXPERTS), jnp.float32),
        ],
        in_specs=[small, wide, wide, small, small],
        out_specs=[
            pl.BlockSpec((tokens, 4 * QUARTER), lambda i: (0, 0)),
            pl.BlockSpec((1, tokens, BLOCK_EXPERTS), lambda i: (i, 0, 0)),
        ],
        compiler_params=pltpu.CompilerParams(vmem_limit_bytes=32 << 20),
        cost_estimate=pl.CostEstimate(
            flops=blocks * BLOCK * 128 * 12 * QUARTER * 2,
            bytes_accessed=14 << 20,
            transcendentals=0,
        ),
        name="sum_gated",
    )(code, packed, grads, *gates)


class Gather:
    def __init__(self, mine, full, send_sem, recv_sem):
        self.mine, self.full = mine, full
        self.send_sem, self.recv_sem = send_sem, recv_sem
        self.row, self.col = lax.axis_index("row"), lax.axis_index("col")
        self.x, self.z, self.y = self.col // 16, lax.rem(self.col // 4, 4), lax.rem(self.col, 4)
        self.z_near = [lax.rem(self.z + i, 4) for i in (1, 3, 2)]
        self.y_near = [lax.rem(self.y + i, 4) for i in (1, 3, 2)]
        self.z_peers = [self.place(self.x, z, self.y) for z in self.z_near]
        self.y_peers = [self.place(self.x, self.z, y) for y in self.y_near]
        self.x_peer = self.place(1 - self.x, self.z, self.y)

    @staticmethod
    def place(x, z, y):
        return x * 16 + z * 4 + y

    def rows(self, half):
        half_rows = self.full.shape[1] // 2
        return pl.ds(half * half_rows, half_rows)

    def pass_on(self, owner, half, peers, own=False):
        target = self.full.at[owner, self.rows(half)]
        for peer in peers:
            pltpu.make_async_remote_copy(
                src_ref=self.mine.at[self.rows(half)] if own else target,
                dst_ref=target,
                send_sem=self.send_sem,
                recv_sem=self.recv_sem.at[half * 32 + owner],
                device_id=(self.row, peer),
                device_id_type=MESH,
            ).start()

    def await_half(self, owner, half):
        target = self.full.at[owner, self.rows(half)]
        pltpu.make_async_copy(target, target, self.recv_sem.at[half * 32 + owner]).wait()

    def start(self):
        for half in range(2):
            self.pass_on(self.col, half, [self.x_peer], own=True)
        self.pass_on(self.col, 0, self.z_peers, own=True)
        self.pass_on(self.col, 1, self.y_peers, own=True)

    def second(self):
        self.await_half(self.x_peer, 0)
        self.pass_on(self.x_peer, 0, self.z_peers)
        self.await_half(self.x_peer, 1)
        self.pass_on(self.x_peer, 1, self.y_peers)
        self.pass_on(self.col, 0, self.y_peers, own=True)
        self.pass_on(self.col, 1, self.z_peers, own=True)
        self.pass_on(self.x_peer, 0, self.y_peers)
        self.pass_on(self.x_peer, 1, self.z_peers)

    def third(self):
        for i in range(3):
            for x in (self.x, 1 - self.x):
                owner = self.place(x, self.z_near[i], self.y)
                self.await_half(owner, 0)
                self.pass_on(owner, 0, self.y_peers)
                owner = self.place(x, self.z, self.y_near[i])
                self.await_half(owner, 1)
                self.pass_on(owner, 1, self.z_peers)

    def await_all(self):
        for x in (self.x, 1 - self.x):
            for i in range(4):
                for j in range(3):
                    z, y = lax.rem(self.z + i, 4), lax.rem(self.y + i, 4)
                    self.await_half(self.place(x, z, self.y_near[j]), 0)
                    self.await_half(self.place(x, self.z_near[j], y), 1)

    def end(self):
        sent = self.full.at[pl.ds(0, 31)]
        pltpu.make_async_copy(sent, sent, self.send_sem).wait()


def head_kernel(
    inputs,
    gain_attn,
    gain_ffn,
    grads,
    lengths,
    routes,
    frequency,
    w_query,
    w_keyval,
    w_out,
    w_shared_in,
    w_shared_out,
    full_pre,
    full_back,
    group_one,
    group_grad,
    scale_one,
    cosine,
    sine,
    begin,
    begin_row,
    query,
    keys,
    values,
    attended,
    norms,
    hidden,
    normed_two,
    scale_two,
    packed,
    code,
    order,
    *scratch,
):
    mine_pre, mine_back, normed, rows, w_pre, w_back, pre, bias, parts = scratch[:9]
    near, far, outgoing, marks, staged = scratch[9:14]
    gather_send, recv_pre, recv_back, own_sem, row_send, row_recv = scratch[14:20]
    sum_send, sum_recv, load_sem, pack_sem = scratch[20:]
    low = jnp.bfloat16
    row, col, sibling, partner, _ = row_places()
    gathers = [
        Gather(mine_pre, full_pre, gather_send.at[0], recv_pre),
        Gather(mine_back, full_back, gather_send.at[1], recv_back),
    ]
    near_peers = gathers[0].z_peers + gathers[0].y_peers + [gathers[0].x_peer]
    greet([(row, peer) for peer in near_peers])
    greet([(sibling, col), (partner, col)])
    start = 0
    for mine, shards in ((mine_pre, (w_query, w_keyval)), (mine_back, (w_out, w_shared_in, w_shared_out))):
        start = 0
        for shard in shards:
            mine[:, start : start + shard.shape[1]] = shard[...]
            start += shard.shape[1]
    first = inputs[...].astype(jnp.float32)
    factor = lax.rsqrt(jnp.mean(first * first, axis=1, keepdims=True) + epsilon)
    scale_one[...] = factor
    normed[...] = (first * factor * gain_attn[...]).astype(low)
    own = [
        pltpu.make_async_copy(normed, group_one.at[row], own_sem.at[0]),
        pltpu.make_async_copy(grads, group_grad.at[row], own_sem.at[1]),
        pltpu.make_async_copy(mine_pre, full_pre.at[col], own_sem.at[2]),
        pltpu.make_async_copy(mine_back, full_back.at[col], own_sem.at[3]),
    ]
    for copy in own:
        copy.start()
    await_greetings(9)
    far_rows, near_rows, onward = row_copies(
        [normed, grads], [group_one, group_grad], row_send, row_recv
    )
    gathers[0].start()
    far_rows[0].start()
    near_rows[0].start()
    gathers[1].start()
    gathers[0].second()
    gathers[1].second()
    gathers[0].third()
    far_rows[1].start()
    near_rows[1].start()
    gathers[1].third()

    tokens = begin.shape[0]

    def document_starts(axis, shape):
        places = lax.broadcasted_iota(jnp.int32, shape, axis)
        found = jnp.zeros(shape, jnp.int32)
        bound = 0
        for i in range(NDOC - 1):
            bound = bound + lengths[0, i]
            found = jnp.where(places >= bound, bound, found)
        return places, found

    begin_row[...] = document_starts(1, begin_row.shape)[1]
    places, starts = document_starts(0, cosine.shape)
    begin[...] = starts[:, :1]
    angles = (places - starts).astype(jnp.float32) * frequency[...]
    lanes = lax.broadcasted_iota(jnp.int32, cosine.shape, 1)
    cosine[...] = jnp.cos(angles)
    sine[...] = jnp.where(lanes < cosine.shape[1] // 2, -1.0, 1.0) * jnp.sin(angles)
    bias[...] = score_bias(begin[...])

    experts = lax.broadcasted_iota(jnp.int32, order.shape, 1)
    chosen = jnp.zeros(order.shape, jnp.float32)
    for k in range(routes.shape[1]):
        chosen = jnp.where(routes[:, k : k + 1] == experts, 1.0, chosen)
    square = (order.shape[0], order.shape[0])
    before = lax.broadcasted_iota(jnp.int32, square, 1) < lax.broadcasted_iota(
        jnp.int32, square, 0
    )
    ahead = matmul(before.astype(jnp.float32).astype(low), chosen.astype(low))
    order[...] = jnp.where(chosen > 0.0, ahead, -1.0)
    code[...] = jnp.transpose(order[...]).astype(low).reshape(code.shape)

    def mark(block, carry):
        found = token_marks(code[block])
        for part in range(3):
            marks[block, part] = jnp.concatenate(
                [found[0][1].astype(low), found[part + 1][1].astype(low)], axis=1
            )
        return carry

    lax.fori_loop(0, code.shape[0], mark, 0)

    far_rows[0].wait_recv()
    onward[0].start()
    gathers[0].await_all()
    own[0].wait()
    own[2].wait()
    near_rows[0].wait_recv()
    onward[0].wait_recv()
    loads = [
        pltpu.make_async_copy(group_one, rows, load_sem.at[0]),
        pltpu.make_async_copy(full_pre, w_pre, load_sem.at[1]),
        pltpu.make_async_copy(
            full_back.at[:, :, pl.ds(0, w_back.shape[2])], w_back, load_sem.at[2]
        ),
    ]
    loads[0].start()
    loads[1].start()
    loads[0].wait()
    loads[1].wait()
    width = inputs.shape[1]
    pre[...] = matmul(
        rows[...].reshape(tokens, width), w_pre[...].reshape(width, w_pre.shape[2])
    )
    size = keys.shape[1]
    inner = query.shape[1]
    keys[...] = turn(pre[:, inner : inner + size], cosine[...], sine[...]).astype(low)
    values[...] = pre[:, inner + size :].astype(low)
    log_totals = jnp.zeros(norms.shape, jnp.float32)
    for head in range(inner // size):
        columns = slice(head * size, (head + 1) * size)
        turned = turn(pre[:, columns], cosine[...], sine[...]).astype(low)
        query[:, columns] = turned
        scores = matmul_t(turned, keys[...]) * (size ** (-0.5)) + bias[...]
        highest = jnp.max(scores, axis=1, keepdims=True)
        weights = jnp.exp(scores - highest)
        total = jnp.sum(weights, axis=1, keepdims=True)
        weights = (weights * (1.0 / total)).astype(low)
        attended[:, columns] = matmul(weights, values[...]).astype(low)
        log_totals = jnp.where(lanes == head, highest + jnp.log(total), log_totals)
    norms[...] = log_totals
    far_rows[1].wait_recv()
    onward[1].start()
    gathers[1].await_all()
    own[3].wait()
    loads[2].start()
    loads[2].wait()
    parts[...] = (
        matmul_t(attended[...], w_back[...].reshape(width, inner)).astype(low).reshape(parts.shape)
    )

    copies = row_sum_copies(parts, near, far, outgoing, (sum_send, sum_recv), 0)
    copies[0].start()
    copies[1].start()
    row_sum_forward(parts, near, outgoing, copies)
    total = inputs[...].astype(jnp.float32) + row_sum_total(parts, near, far, copies)
    hidden[...] = total
    factor = lax.rsqrt(jnp.mean(total * total, axis=1, keepdims=True) + epsilon)
    normed_two[...] = (total * factor * gain_ffn[...]).astype(low)
    scale_two[...] = factor

    def pack(block, carry):
        last = normed_two[:, 3 * QUARTER :]
        for part in range(3):
            columns = slice(part * QUARTER, (part + 1) * QUARTER)
            both = jnp.concatenate([normed_two[:, columns], last], axis=0)
            staged[block, :, columns] = matmul(marks[block, part], both).astype(low)
        target = packed.at[pl.ds(pl.multiple_of(block * BLOCK, BLOCK), BLOCK)]
        pltpu.make_async_copy(staged.at[block], target, pack_sem.at[block]).start()
        return carry

    lax.fori_loop(0, code.shape[0], pack, 0)

    own[1].wait()
    near_rows[0].wait_send()
    near_rows[1].wait()
    onward[0].wait_send()
    onward[1].wait()
    for copy in far_rows + copies:
        copy.wait_send()
    for gather in gathers:
        gather.end()
    for block in range(staged.shape[0]):
        target = packed.at[pl.ds(block * BLOCK, BLOCK)]
        pltpu.make_async_copy(staged.at[block], target, pack_sem.at[block]).wait()


def head(inputs, gain_attn, gain_ffn, grads, lengths, routes, shards, size, expert_count):
    space = pl.BlockSpec(memory_space=pltpu.VMEM)
    away = pl.BlockSpec(memory_space=pl.ANY)
    low = jnp.bfloat16
    rows, width = inputs.shape
    tokens = 4 * rows
    shard_rows = shards[0].shape[0]
    inner = shards[0].shape[1]
    pre_width = inner + shards[1].shape[1]
    back_width = sum(part.shape[1] for part in shards[2:])
    blocks = expert_count // BLOCK_EXPERTS
    spread = np.arange(size // 2, dtype=np.float32) * np.float32(2.0 / size)
    frequency = np.float32(rope_base) ** (-spread)
    frequency = jnp.asarray(np.concatenate([frequency, frequency])[None], jnp.float32)

    def full(shape, dtype):
        return jax.ShapeDtypeStruct(shape, dtype)

    return pl.pallas_call(
        head_kernel,
        out_shape=[
            full((32, shard_rows, pre_width), low),
            full((32, shard_rows, back_width), low),
            full((4, rows, width), low),
            full((4, rows, width), low),
            full((rows, 1), jnp.float32),
            full((tokens, size), jnp.float32),
            full((tokens, size), jnp.float32),
            full((tokens, 1), jnp.int32),
            full((1, tokens), jnp.int32),
            full((tokens, inner), low),
            full((tokens, size), low),
            full((tokens, size), low),
            full((tokens, inner), low),
            full((tokens, size), jnp.float32),
            full((rows, width), jnp.float32),
            full((rows, width), low),
            full((rows, 1), jnp.float32),
            full((blocks * BLOCK, 3 * QUARTER), low),
            full((blocks, BLOCK_EXPERTS, rows), low),
            full((rows, expert_count), jnp.float32),
        ],
        in_specs=[space] * 3
        + [away, pl.BlockSpec(memory_space=pltpu.SMEM)]
        + [space] * (2 + len(shards)),
        out_specs=[away] * 4 + [space] * 13 + [away] + [space] * 2,
        scratch_shapes=[
            pltpu.VMEM((shard_rows, pre_width), low),
            pltpu.VMEM((shard_rows, back_width), low),
            pltpu.VMEM((rows, width), low),
            pltpu.VMEM((4, rows, width), low),
            pltpu.VMEM((32, shard_rows, pre_width), low),
            pltpu.VMEM((32, shard_rows, inner), low),
            pltpu.VMEM((tokens, pre_width), jnp.float32),
            pltpu.VMEM((tokens, tokens), jnp.float32),
            pltpu.VMEM((4, rows, width), low),
            pltpu.VMEM((2, rows, width), low),
            pltpu.VMEM((rows, width), low),
            pltpu.VMEM((rows, width), low),
            pltpu.VMEM((blocks, 3, BLOCK, 2 * rows), low),
            pltpu.VMEM((blocks, BLOCK, 3 * QUARTER), low),
            pltpu.SemaphoreType.DMA((2,)),
            pltpu.SemaphoreType.DMA((64,)),
            pltpu.SemaphoreType.DMA((64,)),
            pltpu.SemaphoreType.DMA((4,)),
            pltpu.SemaphoreType.DMA((6,)),
            pltpu.SemaphoreType.DMA((6,)),
            pltpu.SemaphoreType.DMA((3,)),
            pltpu.SemaphoreType.DMA((3,)),
            pltpu.SemaphoreType.DMA((3,)),
            pltpu.SemaphoreType.DMA((blocks,)),
        ],
        compiler_params=pltpu.CompilerParams(
            collective_id=0, has_side_effects=True, vmem_limit_bytes=60 << 20
        ),
        cost_estimate=pl.CostEstimate(flops=0, bytes_accessed=300 << 20, transcendentals=0),
        name="head",
    )(inputs, gain_attn, gain_ffn, grads, lengths, routes, frequency, *shards)


def exchange(packed):
    pairs = packed.reshape(-1, PACKED_ROWS, packed.shape[1])
    swapped = lax.all_to_all(pairs, ("row", "col"), split_axis=0, concat_axis=0, tiled=True)
    return swapped.reshape(packed.shape)


def per_device(
    block_in,
    gain_attn,
    w_query,
    w_keyval,
    w_out,
    gain_ffn,
    w_shared_in,
    w_shared_out,
    w_router,
    w_expert_in,
    w_expert_out,
    doc_lengths,
    routes,
    cotangent,
):
    row_count = lax.axis_size("row")
    rows_dev = block_in.shape[1]
    model_width = block_in.shape[2]
    expert_count = w_router.shape[1]
    expert_ff = w_expert_out.shape[2]
    inputs = block_in.reshape(rows_dev, model_width)
    grad_low = cotangent.reshape(rows_dev, model_width)
    shards = [w_query, w_keyval, w_out, w_shared_in, w_shared_out]
    shards = [part.reshape(part.shape[0], -1) for part in shards]
    (
        full_pre,
        full_back,
        group_one,
        group_grad,
        scale_one,
        cosine,
        sine_table,
        begin,
        begin_row,
        *kept,
        hidden_state,
        normed_two,
        scale_two,
        send_rows,
        code,
        order,
    ) = head(
        inputs,
        gain_attn[None],
        gain_ffn[None],
        grad_low,
        doc_lengths,
        routes.reshape(rows_dev, -1),
        shards,
        w_keyval.shape[2] // 2,
        expert_count,
    )
    full_pre, full_back, group_one, group_grad = (
        part.reshape(-1, part.shape[2]) for part in (full_pre, full_back, group_one, group_grad)
    )
    received = exchange(send_rows)
    shared_start, shared_width = w_out.shape[1], w_shared_out.shape[1]
    full_shared_in = full_back[:, shared_start : shared_start + 2 * shared_width]
    full_shared_out = full_back[:, shared_start + 2 * shared_width :]

    logits = matmul(normed_two, w_router)
    scores_sig = jnp.where(order >= 0.0, jax.nn.sigmoid(logits), 0.0)
    score_sum = jnp.sum(scores_sig, axis=1, keepdims=True)
    gate_weights = scores_sig / score_sum
    gates = [
        part.T.reshape(-1, BLOCK_EXPERTS, rows_dev) for part in split_low(gate_weights)
    ]
    send_grads, received = lax.optimization_barrier((pack_tokens(code, grad_low, gates), received))
    received_grads = exchange(send_grads)

    group_two = lax.all_gather(normed_two, "row", axis=0, tiled=True)
    shared_pre = matmul(group_two, full_shared_in)
    shared_gate, shared_up = shared_pre[:, :shared_width], shared_pre[:, shared_width:]
    shared_act, shared_slope = swish_parts(shared_gate)
    shared_hidden = (shared_act * shared_up).astype(jnp.bfloat16)
    shared_hidden_grad = matmul(group_grad, full_shared_out)
    shared_pre_grad = jnp.concatenate(
        [shared_hidden_grad * shared_up * shared_slope, shared_hidden_grad * shared_act], axis=1
    ).astype(jnp.bfloat16)
    shared_grads = jnp.concatenate(
        [
            outer_sum(group_two, shared_pre_grad).astype(jnp.bfloat16),
            outer_sum(group_grad, shared_hidden).astype(jnp.bfloat16),
        ],
        axis=1,
    )
    shared_parts = matmul_t(shared_hidden, full_shared_out).astype(jnp.bfloat16)
    shared_input = lax.psum_scatter(
        matmul_t(shared_pre_grad, full_shared_in).astype(jnp.bfloat16),
        "row",
        scatter_dimension=0,
        tiled=True,
    ).astype(jnp.float32)

    expert_in = unpack_slots(received)
    expert_pre = jnp.einsum(
        "esd,edf->esf", expert_in, w_expert_in, preferred_element_type=jnp.float32
    )
    expert_act, expert_slope = swish_parts(expert_pre[..., :expert_ff])
    expert_hidden = (expert_act * expert_pre[..., expert_ff:]).astype(jnp.bfloat16)
    expert_out = jnp.einsum(
        "esf,edf->esd", expert_hidden, w_expert_out, preferred_element_type=jnp.float32
    ).astype(jnp.bfloat16)
    send_out, received_grads = lax.optimization_barrier((pack_slots(expert_out), received_grads))
    returned = exchange(send_out)

    out_grad = unpack_slots(received_grads)
    hidden_grad = jnp.einsum(
        "esd,edf->esf", out_grad, w_expert_out, preferred_element_type=jnp.float32
    )
    expert_pre_grad = jnp.concatenate(
        [hidden_grad * expert_pre[..., expert_ff:] * expert_slope, hidden_grad * expert_act], axis=2
    ).astype(jnp.bfloat16)
    slot_grad = jnp.einsum(
        "esf,edf->esd", expert_pre_grad, w_expert_in, preferred_element_type=jnp.float32
    ).astype(jnp.bfloat16)
    send_back, returned = lax.optimization_barrier((pack_slots(slot_grad), returned))
    returned_grad = exchange(send_back)
    grad_expert_out = jnp.einsum(
        "esd,esf->edf", out_grad, expert_hidden, preferred_element_type=jnp.float32
    )
    grad_expert_in = jnp.einsum(
        "esd,esf->edf", expert_in, expert_pre_grad, preferred_element_type=jnp.float32
    )
    routed_branch, gate_grads = sum_gated(code, returned, send_grads, gates)
    stream = hidden_state + routed_branch
    gate_grads = gate_grads.transpose(1, 0, 2).reshape(rows_dev, expert_count)
    logit_grad = (
        (1.0 - scores_sig)
        * (gate_grads - gate_weights * jnp.sum(gate_grads, axis=1, keepdims=True))
    ).astype(jnp.bfloat16)
    router_parts = outer_sum(normed_two, logit_grad).astype(jnp.bfloat16)
    router_parts = router_parts.reshape(row_count, -1, expert_count)
    router_input = shared_input + matmul_t(logit_grad, w_router)
    shadowed = (router_input, router_parts, stream, shared_grads, group_one.T, all_marks(code))
    returned_grad, shadowed, grad_expert_in, grad_expert_out = lax.optimization_barrier(
        (returned_grad, shadowed, grad_expert_in, grad_expert_out)
    )
    router_input, router_parts, stream, shared_grads, group_one_t, marks = shadowed

    widths = [part.shape[1] for part in shards]
    group_branch, hidden_total, gain_ffn_grad, router_sum, shared_sums = token_back(
        returned_grad,
        marks,
        router_input,
        hidden_state,
        scale_two,
        gain_ffn[None],
        grad_low,
        router_parts,
        shared_grads.reshape(2, 4, 4, -1, shared_grads.shape[1]),
        widths[3:],
    )
    input_back, block_out, router_sum, gain_sums, *sums = finish(
        group_branch,
        group_one_t,
        (full_pre, full_back),
        kept,
        (cosine, sine_table, begin, begin_row),
        (
            shared_parts.reshape(row_count, rows_dev, model_width),
            router_sum.reshape(32, -1, expert_count),
            stream,
            inputs,
            scale_one,
            gain_attn[None],
            gain_ffn_grad,
        ),
        widths[:3],
    )
    sums = [
        part.reshape(like.shape)
        for part, like in zip(sums + shared_sums, (w_query, w_keyval, w_out, w_shared_in, w_shared_out))
    ]
    return (
        block_out.reshape(1, rows_dev, model_width),
        (hidden_total + input_back).reshape(1, rows_dev, model_width),
        gain_sums[0],
        sums[0],
        sums[1],
        sums[2],
        gain_sums[1],
        sums[3],
        sums[4],
        router_sum.reshape(model_width, expert_count).astype(jnp.float32),
        grad_expert_in,
        grad_expert_out,
    )


def solution(mesh):
    in_specs = (
        P("col", "row", None),
        P(),
        P("col", "row"),
        P("col", "row", None),
        P("col", "row"),
        P(),
        P("col", None, "row"),
        P("col", "row"),
        P(),
        P(("row", "col"), None, None),
        P(("row", "col"), None, None),
        P("col", None),
        P("col", "row", None),
        P("col", "row", None),
    )
    out_specs = (
        P("col", "row", None),
        P("col", "row", None),
        P(),
        P("col", "row"),
        P("col", "row", None),
        P("col", "row"),
        P(),
        P("col", None, "row"),
        P("col", "row"),
        P(),
        P(("row", "col"), None, None),
        P(("row", "col"), None, None),
    )
    return jax.shard_map(
        per_device, mesh=mesh, in_specs=in_specs, out_specs=out_specs, check_vma=False
    )
```

```python
import functools

import jax
import jax.numpy as jnp
import numpy as np
from jax import lax
from jax.experimental import pallas as pl
from jax.experimental.pallas import tpu as pltpu
from jax.sharding import PartitionSpec as P

epsilon = 1e-06
rope_base = 10000.0
masked_score = -1e30

EXPERT_ROWS = 6
PAIR_ROWS = 12
PACKED_ROWS = 16
BLOCK_PAIRS = 16
BLOCK = BLOCK_PAIRS * PACKED_ROWS
BLOCK_EXPERTS = 2 * BLOCK_PAIRS
BLOCK_SLOTS = BLOCK_PAIRS * EXPERT_ROWS
QUARTER = 512
SIDE = 128
MESH = pl.DeviceIdType.MESH
NDOC = 4


def swish_parts(pre_act):
    logistic = jax.nn.sigmoid(pre_act)
    return (pre_act * logistic, logistic * (1.0 + pre_act * (1.0 - logistic)))


def matmul(matrix, partner):
    return jnp.dot(matrix, partner, preferred_element_type=jnp.float32)


def matmul_t(matrix, partner):
    return lax.dot_general(
        matrix, partner, (((1,), (1,)), ((), ())), preferred_element_type=jnp.float32
    )


def outer_sum(matrix, partner):
    return lax.dot_general(
        matrix, partner, (((0,), (0,)), ((), ())), preferred_element_type=jnp.float32
    )


def split_low(values):
    high = values.astype(jnp.bfloat16)
    return high, (values - high.astype(jnp.float32)).astype(jnp.bfloat16)


def row_places():
    row, col = lax.axis_index("row"), lax.axis_index("col")
    chip, core = row // 2, lax.rem(row, 2)
    sibling = chip * 2 + (1 - core)
    partner = (1 - chip) * 2 + core
    across = (1 - chip) * 2 + (1 - core)
    return row, col, sibling, partner, across


def row_copies(sources, targets, send_sem, recv_sem):
    row, col, sibling, partner, _ = row_places()

    def send(origin, target, peer, i):
        return pltpu.make_async_remote_copy(
            src_ref=origin,
            dst_ref=target,
            send_sem=send_sem.at[i],
            recv_sem=recv_sem.at[i],
            device_id=(peer, col),
            device_id_type=MESH,
        )

    far, near, onward = [], [], []
    for i, (source, target) in enumerate(zip(sources, targets)):
        far.append(send(source, target.at[row], partner, 3 * i))
        near.append(send(source, target.at[row], sibling, 3 * i + 1))
        onward.append(send(target.at[partner], target.at[partner], sibling, 3 * i + 2))
    return far, near, onward


def greet(peers):
    barrier = pltpu.get_barrier_semaphore()
    for peer in peers:
        pl.semaphore_signal(barrier, inc=1, device_id=peer, device_id_type=MESH)


def await_greetings(count):
    pl.semaphore_wait(pltpu.get_barrier_semaphore(), count)


def turn(values, cosine, sine):
    return values * cosine + pltpu.roll(values, 64, 1) * sine


def score_bias(begin):
    shape = (begin.shape[0], begin.shape[0])
    keys = lax.broadcasted_iota(jnp.int32, shape, 1)
    allowed = (keys >= begin) & (keys <= lax.broadcasted_iota(jnp.int32, shape, 0))
    return jnp.where(allowed, 0.0, masked_score)


def remote(source, target, sems, at, peer):
    return pltpu.make_async_remote_copy(
        src_ref=source,
        dst_ref=target,
        send_sem=sems[0].at[at],
        recv_sem=sems[1].at[at],
        device_id=peer,
        device_id_type=MESH,
    )


def row_sum_copies(parts, near, far, outgoing, sems, at):
    _, col, sibling, partner, across = row_places()
    return [
        remote(parts.at[across], near.at[0], sems, at, (sibling, col)),
        remote(parts.at[sibling], near.at[1], sems, at + 1, (sibling, col)),
        remote(outgoing, far, sems, at + 2, (partner, col)),
    ]


def row_sum_forward(parts, near, outgoing, copies):
    _, _, _, partner, _ = row_places()
    copies[0].wait_recv()
    outgoing[...] = (parts[partner].astype(jnp.float32) + near[0].astype(jnp.float32)).astype(
        jnp.bfloat16
    )
    copies[2].start()


def row_sum_total(parts, near, far, copies):
    row = row_places()[0]
    copies[1].wait_recv()
    total = parts[row].astype(jnp.float32) + near[1].astype(jnp.float32)
    copies[2].wait_recv()
    return total + far[...].astype(jnp.float32)


class ScatterSum:
    def __init__(self, grads, scratch):
        self.grads = grads
        self.first, self.first_sum, self.second, self.second_sum, self.third = scratch[:5]
        self.one, self.two, self.three = scratch[5:7], scratch[7:9], scratch[9:11]
        row, col = lax.axis_index("row"), lax.axis_index("col")
        x, z, y = col // 16, lax.rem(col // 4, 4), lax.rem(col, 4)
        self.place = (x, z, y)
        self.half_rows = grads.shape[3] // 2
        self.y_peers = [(row, x * 16 + z * 4 + lax.rem(y + i, 4)) for i in (1, 2, 3)]
        self.z_peers = [(row, x * 16 + lax.rem(z + i, 4) * 4 + y) for i in (1, 2, 3)]
        self.x_peer = (row, (1 - x) * 16 + z * 4 + y)
        self.one_copies, self.two_copies, self.three_copies = {}, {}, []

    @staticmethod
    def scratch(grads):
        half_rows, depth = grads.shape[3] // 2, grads.shape[4]
        low = jnp.bfloat16
        return [
            pltpu.VMEM((2, 3, 2, 4, half_rows, depth), low),
            pltpu.VMEM((2, 2, 4, half_rows, depth), low),
            pltpu.VMEM((2, 3, 2, half_rows, depth), low),
            pltpu.VMEM((2, half_rows, depth), low),
            pltpu.VMEM((2, half_rows, depth), low),
        ] + [pltpu.SemaphoreType.DMA((count,)) for count in (6, 6, 6, 6, 2, 2)]

    def half(self, half):
        return pl.ds(half * self.half_rows, self.half_rows)

    def start(self):
        _, z, y = self.place
        for i in range(3):
            for half in range(2):
                if half == 0:
                    source = self.grads.at[:, :, lax.rem(y + i + 1, 4), self.half(0)]
                else:
                    source = self.grads.at[:, lax.rem(z + i + 1, 4), :, self.half(1)]
                peer = (self.y_peers, self.z_peers)[half][i]
                copy = remote(source, self.first.at[half, i], self.one, half * 3 + i, peer)
                self.one_copies[half, i] = copy
                copy.start()

    def add_first(self):
        _, z, y = self.place
        for half in range(2):
            for i in range(3):
                self.one_copies[half, i].wait_recv()

            def add(k, carry, half=half):
                if half == 0:
                    total = self.grads[k // 4, lax.rem(k, 4), y, self.half(0)].astype(jnp.float32)
                else:
                    total = self.grads[k // 4, z, lax.rem(k, 4), self.half(1)].astype(jnp.float32)
                for i in range(3):
                    total = total + self.first[half, i, k // 4, lax.rem(k, 4)].astype(jnp.float32)
                self.first_sum[half, k // 4, lax.rem(k, 4)] = total.astype(jnp.bfloat16)
                return carry

            lax.fori_loop(0, 8, add, 0)
            for i in range(3):
                away = lax.rem((z, y)[half] + i + 1, 4)
                copy = remote(
                    self.first_sum.at[half, :, away],
                    self.second.at[half, i],
                    self.two,
                    half * 3 + i,
                    (self.z_peers, self.y_peers)[half][i],
                )
                self.two_copies[half, i] = copy
                copy.start()

    def second_total(self, owner_x, half):
        _, z, y = self.place
        total = self.first_sum[half, owner_x, (z, y)[half]].astype(jnp.float32)
        for i in range(3):
            total = total + self.second[half, i, owner_x].astype(jnp.float32)
        return total

    def add_second(self):
        x = self.place[0]
        for half in range(2):
            for i in range(3):
                self.two_copies[half, i].wait_recv()
            self.second_sum[half] = self.second_total(1 - x, half).astype(jnp.bfloat16)
            copy = remote(
                self.second_sum.at[half], self.third.at[half], self.three, half, self.x_peer
            )
            self.three_copies.append(copy)
            copy.start()

    def add_third(self, pieces):
        x = self.place[0]
        for half in range(2):
            total = self.second_total(x, half)
            self.three_copies[half].wait_recv()
            total = total + self.third[half].astype(jnp.float32)
            start = 0
            for piece in pieces:
                piece[self.half(half)] = total[:, start : start + piece.shape[1]]
                start += piece.shape[1]

    def end(self):
        for copy in [*self.one_copies.values(), *self.two_copies.values(), *self.three_copies]:
            copy.wait_send()


class RouterSum:
    def __init__(self, part, block, scratch):
        self.part, self.block = part, block
        self.in_y, self.sum_y, self.in_z, self.sum_z, self.in_x = scratch[:5]
        self.sems = scratch[5:]
        row, col = lax.axis_index("row"), lax.axis_index("col")
        x, z, y = col // 16, lax.rem(col // 4, 4), lax.rem(col, 4)
        self.place = (x, z, y)
        self.y_near = [lax.rem(y + i, 4) for i in (1, 2, 3)]
        self.z_near = [lax.rem(z + i, 4) for i in (1, 2, 3)]
        self.y_peers = [(row, x * 16 + z * 4 + near) for near in self.y_near]
        self.z_peers = [(row, x * 16 + near * 4 + y) for near in self.z_near]
        self.x_peer = (row, (1 - x) * 16 + z * 4 + y)
        self.copies = {}

    @staticmethod
    def scratch(share):
        low = jnp.bfloat16
        return [
            pltpu.VMEM((3, 2, 4, *share), low),
            pltpu.VMEM((2, 4, *share), low),
            pltpu.VMEM((3, 2, *share), low),
            pltpu.VMEM((2, *share), low),
            pltpu.VMEM(share, low),
            pltpu.SemaphoreType.DMA((14,)),
            pltpu.SemaphoreType.DMA((14,)),
        ]

    def send(self, stage, at, sources, targets, peers):
        copies = [
            remote(source, target, self.sems, at + i, peer)
            for i, (source, target, peer) in enumerate(zip(sources, targets, peers))
        ]
        for copy in copies:
            copy.start()
        self.copies[stage] = copies

    def wait(self, stage):
        for copy in self.copies[stage]:
            copy.wait_recv()

    def start(self):
        sources = [self.part.at[:, :, near] for near in self.y_near]
        self.send(0, 0, sources, [self.in_y.at[i] for i in range(3)], self.y_peers)

    def add_y(self):
        self.wait(0)
        total = self.part[:, :, self.place[2]].astype(jnp.float32)
        for i in range(3):
            total = total + self.in_y[i].astype(jnp.float32)
        self.sum_y[...] = total.astype(jnp.bfloat16)
        sources = [self.sum_y.at[:, near] for near in self.z_near]
        self.send(1, 3, sources, [self.in_z.at[i] for i in range(3)], self.z_peers)

    def add_z(self):
        self.wait(1)
        total = self.sum_y[:, self.place[1]].astype(jnp.float32)
        for i in range(3):
            total = total + self.in_z[i].astype(jnp.float32)
        self.sum_z[...] = total.astype(jnp.bfloat16)
        self.send(2, 6, [self.sum_z.at[1 - self.place[0]]], [self.in_x], [self.x_peer])

    def add_x(self):
        self.wait(2)
        x, z, y = self.place
        total = self.sum_z[x].astype(jnp.float32) + self.in_x[...].astype(jnp.float32)
        self.block[x, z, y] = total.astype(jnp.bfloat16)
        own = self.block.at[x, z, y]
        self.send(3, 7, [own], [own], [self.x_peer])

    def spread_z(self):
        self.wait(3)
        own = self.block.at[:, self.place[1], self.place[2]]
        self.send(4, 8, [own] * 3, [own] * 3, self.z_peers)

    def spread_y(self):
        self.wait(4)
        own = self.block.at[:, :, self.place[2]]
        self.send(5, 11, [own] * 3, [own] * 3, self.y_peers)

    def end(self):
        for copies in self.copies.values():
            for copy in copies:
                copy.wait_send()


def attention_back_rows(start, refs, sums):
    group, w_back, query, keys, values, norms, cosine, sine, begin, begin_row = refs
    back, pre_grad, bias, bias_t, deltas, key_grad, value_grad = sums
    low = jnp.bfloat16
    size = keys.shape[1]
    inner = query.shape[1]
    count = bias.shape[0]
    rows = pl.ds(pl.multiple_of(start, count), count)
    scale = size ** (-0.5)
    branch = group[pl.ds(start // 128, count // 128)].reshape(count, group.shape[2])
    back[rows] = matmul(branch, w_back[...]).astype(low)
    first = begin[rows]
    key_places = lax.broadcasted_iota(jnp.int32, bias.shape, 1)
    places = start + lax.broadcasted_iota(jnp.int32, bias.shape, 0)
    bias[...] = jnp.where((key_places >= first) & (key_places <= places), 0.0, masked_score)
    lanes = lax.broadcasted_iota(jnp.int32, deltas.shape, 1)
    all_deltas = jnp.zeros(deltas.shape, jnp.float32)
    for head in range(inner // size):
        columns = slice(head * size, (head + 1) * size)
        turned, outer = query[rows, columns], back[rows, columns]
        scores = matmul_t(turned, keys[...]) * scale + bias[...]
        probs = jnp.exp(scores - norms[rows, head : head + 1])
        prob_grad = matmul_t(outer, values[...])
        delta = jnp.sum(probs * prob_grad, axis=1, keepdims=True)
        all_deltas = jnp.where(lanes == head, delta, all_deltas)
        score_grad = (probs * (prob_grad - delta)).astype(low)
        query_grad = matmul(score_grad, keys[...]) * scale
        pre_grad[rows, columns] = turn(query_grad, cosine[rows], -sine[rows]).astype(low)
    deltas[...] = all_deltas
    deltas_t = jnp.transpose(deltas[...])
    norms_t = jnp.transpose(norms[rows])
    first = begin_row[:, rows]
    key_places = lax.broadcasted_iota(jnp.int32, bias_t.shape, 0)
    places = start + lax.broadcasted_iota(jnp.int32, bias_t.shape, 1)
    bias_t[...] = jnp.where((key_places >= first) & (key_places <= places), 0.0, masked_score)
    for head in range(inner // size):
        columns = slice(head * size, (head + 1) * size)
        turned, outer = query[rows, columns], back[rows, columns]
        scores = matmul_t(keys[...], turned) * scale + bias_t[...]
        probs = jnp.exp(scores - norms_t[head : head + 1])
        prob_grad = matmul_t(values[...], outer)
        score_grad = (probs * (prob_grad - deltas_t[head : head + 1])).astype(low)
        key_grad[...] += matmul(score_grad, turned)
        value_grad[...] += matmul(probs.astype(low), outer)


def tail_kernel(
    packed,
    marks_in,
    router_input_in,
    hidden_in,
    group_one_t,
    full_pre,
    full_back,
    shared_parts_in,
    stream_in,
    scale_two,
    gain_ffn,
    stream_grad,
    router_parts,
    shared_grads,
    query,
    keys,
    values_in,
    attended,
    norms,
    cosine,
    sine,
    begin,
    begin_row,
    inputs,
    scale_one,
    gain_attn,
    hidden_total,
    result,
    block_out,
    router,
    gain_attn_sum,
    gain_ffn_sum,
    *refs,
):
    pieces, scratch = refs[:5], refs[5:]
    held, marks, router_input, hidden, rows_t, w_pre, w_back, shared_parts, stream = scratch[:9]
    routed, group, back, pre_grad, bias, bias_t, deltas, key_grad, value_grad = scratch[9:18]
    parts, near, far, outgoing, router_near, router_far, router_outgoing = scratch[18:25]
    router_part, values, buffers, pre_grads, out_grads = scratch[25:30]
    load_sem, branch_send, branch_recv, row_send, row_recv, gain_send, gain_recv = scratch[30:37]
    pass_send, pass_recv = scratch[37:39]
    shared_scatter = ScatterSum(shared_grads, scratch[39:50])
    out_scatter = ScatterSum(out_grads, scratch[50:61])
    pre_scatter = ScatterSum(pre_grads, scratch[61:72])
    router_at = 72
    low = jnp.bfloat16
    row, col, sibling, partner, across = row_places()
    row_peers = [(peer, col) for peer in (sibling, partner, across)]
    greet(row_peers)
    greet(pre_scatter.y_peers + pre_scatter.z_peers + [pre_scatter.x_peer])
    steps, depth = held.shape[:2]
    inner = query.shape[1]
    sources = [packed.at[pl.ds(i * depth, depth)] for i in range(steps)]
    targets = [held.at[i] for i in range(steps)]
    sources[1:1] = [marks_in]
    targets[1:1] = [marks]
    sources += [router_input_in, hidden_in, full_back, shared_parts_in]
    targets += [router_input, hidden, w_back, shared_parts]
    sources += [full_pre, group_one_t, stream_in]
    targets += [w_pre, rows_t, stream]
    loads = [
        pltpu.make_async_copy(source, target, load_sem.at[i])
        for i, (source, target) in enumerate(zip(sources, targets))
    ]
    for load in loads:
        load.start()
    load_marks = loads.pop(1)
    load_input, load_hidden, load_back, load_shared, load_pre, load_rows, load_stream = loads[
        steps:
    ]
    await_greetings(10)

    row_sems = (row_send, row_recv)
    router_copies = row_sum_copies(
        router_parts, router_near, router_far, router_outgoing, row_sems, 0
    )
    router_copies[0].start()
    router_copies[1].start()
    shared_scatter.start()
    row_sum_forward(router_parts, router_near, router_outgoing, router_copies)

    load_marks.wait()
    for i in range(steps):
        loads[i].wait()
        rows = slice(i * depth, (i + 1) * depth)
        for part in range(4):
            columns = slice(part * QUARTER, (part + 1) * QUARTER)
            if part < 3:
                found = matmul(marks[0, :, rows], held[i, :, columns])
            else:
                found = matmul(marks[1, :, rows], held[i, :, :QUARTER])
                for j in (1, 2):
                    second = slice(j * QUARTER, (j + 1) * QUARTER)
                    found = found + matmul(marks[j + 1, :, rows], held[i, :, second])
            routed[:, columns] = found if i == 0 else routed[:, columns] + found
    load_input.wait()
    load_hidden.wait()
    incoming = router_input[...] + routed[...]
    state = hidden[...]
    factor = scale_two[...]
    weighted = gain_ffn[...] * incoming
    mean = jnp.mean(weighted * state, axis=1, keepdims=True)
    total = (
        stream_grad[...].astype(jnp.float32)
        + factor * weighted
        - state * (factor * factor * factor * mean)
    )
    hidden_total[...] = total
    group[row] = total.astype(low)
    far_rows, near_rows, onward = row_copies([group.at[row]], [group], branch_send, branch_recv)
    far_rows[0].start()
    near_rows[0].start()
    values[0, 1:2] = jnp.sum(incoming * state * factor, axis=0, keepdims=True)

    load_shared.wait()
    shared_copies = row_sum_copies(
        shared_parts, near.at[1], far.at[1], outgoing.at[1], row_sems, 3
    )
    shared_copies[0].start()
    shared_copies[1].start()
    router_sum = row_sum_total(router_parts, router_near, router_far, router_copies)
    router_part[...] = router_sum.astype(low).reshape(router_part.shape)
    router_scatter = RouterSum(router_part, router.at[row], scratch[router_at:])
    router_scatter.start()
    shared_scatter.add_first()
    row_sum_forward(shared_parts, near.at[1], outgoing.at[1], shared_copies)
    load_back.wait()
    near_rows[0].wait_recv()
    key_grad[...] = jnp.zeros_like(key_grad)
    value_grad[...] = jnp.zeros_like(value_grad)
    refs = (group, w_back, query, keys, values_in, norms, cosine, sine, begin, begin_row)
    sums = (back, pre_grad, bias, bias_t, deltas, key_grad, value_grad)
    chip = row // 2
    chip_rows = bias.shape[0]
    attention_back_rows(chip * chip_rows, refs, sums)
    shared_scatter.add_second()
    router_scatter.add_y()
    far_rows[0].wait_recv()
    onward[0].start()
    onward[0].wait_recv()

    def keep(target, block, rows):
        shaped = rows.astype(low).reshape(2, 4, 64, rows.shape[1])
        target[block // 2, 2 * (block % 2) : 2 * (block % 2) + 2] = shaped

    blocks, width = 4, group.shape[2] // 4
    for block in range(blocks):
        columns = slice(block * width, (block + 1) * width)
        rows = group[:, :, columns].reshape(4 * group.shape[1], width)
        keep(out_grads, block, outer_sum(rows, attended[...]))
    out_scatter.start()
    router_scatter.add_z()
    attention_back_rows((1 - chip) * chip_rows, refs, sums)
    size = keys.shape[1]
    scale = size ** (-0.5)
    pre_grad[:, inner : inner + size] = turn(key_grad[...] * scale, cosine[...], -sine[...]).astype(
        low
    )
    pre_grad[:, inner + size :] = value_grad[...].astype(low)
    load_pre.wait()
    load_rows.wait()
    block_rows = parts.shape[1]
    for block in range(4):
        rows = slice(block * block_rows, (block + 1) * block_rows)
        parts[block] = matmul_t(pre_grad[rows], w_pre[...]).astype(low)
    attn_copies = row_sum_copies(parts, near.at[0], far.at[0], outgoing.at[0], row_sems, 6)
    attn_copies[0].start()
    attn_copies[1].start()
    row_sum_forward(parts, near.at[0], outgoing.at[0], attn_copies)
    for block in range(blocks):
        rows = slice(block * width, (block + 1) * width)
        keep(pre_grads, block, matmul(rows_t[rows], pre_grad[...]))
    pre_scatter.start()
    router_scatter.add_x()
    out_scatter.add_first()
    shared_scatter.add_third(pieces[3:])
    router_scatter.spread_z()

    gain_sems = (gain_send, gain_recv)
    gain_copies = []
    stages = (row_peers, pre_scatter.y_peers, pre_scatter.z_peers, [pre_scatter.x_peer])

    def start_gains(stage):
        at = 3 * stage
        for i, peer in enumerate(stages[stage]):
            gain_copies.append(
                remote(values.at[stage], buffers.at[at + i], gain_sems, at + i, peer)
            )
            gain_copies[-1].start()

    def add_gains(stage):
        at = 3 * stage
        total = values[stage]
        for i in range(len(stages[stage])):
            gain_copies[at + i].wait_recv()
            total = total + buffers[at + i]
        values[stage + 1] = total

    incoming = row_sum_total(parts, near.at[0], far.at[0], attn_copies)
    first = inputs[...].astype(jnp.float32)
    factor = scale_one[...]
    weighted = gain_attn[...] * incoming
    mean = jnp.mean(weighted * first, axis=1, keepdims=True)
    result[...] = factor * weighted - first * (factor * factor * factor * mean)
    values[0, 0:1] = jnp.sum(incoming * first * factor, axis=0, keepdims=True)
    start_gains(0)
    router_scatter.spread_y()
    out_scatter.add_second()
    load_stream.wait()
    shared = row_sum_total(shared_parts, near.at[1], far.at[1], shared_copies)
    block_out[...] = (stream[...] + shared).astype(low)
    add_gains(0)
    start_gains(1)
    pre_scatter.add_first()
    router_scatter.wait(5)
    router_rows = row_copies([router.at[row]], [router], pass_send, pass_recv)
    router_rows[0][0].start()
    router_rows[1][0].start()
    out_scatter.add_third(pieces[2:3])
    add_gains(1)
    start_gains(2)
    pre_scatter.add_second()
    add_gains(2)
    start_gains(3)
    router_rows[0][0].wait_recv()
    router_rows[2][0].start()
    pre_scatter.add_third(pieces[:2])
    add_gains(3)
    gain_attn_sum[...] = values[4, 0:1]
    gain_ffn_sum[...] = values[4, 1:2]

    router_scatter.end()
    far_rows[0].wait_send()
    near_rows[0].wait_send()
    onward[0].wait_send()
    router_rows[0][0].wait_send()
    router_rows[1][0].wait()
    router_rows[2][0].wait()
    for done in [*router_copies, *attn_copies, *shared_copies, *gain_copies]:
        done.wait_send()
    for scatter in (shared_scatter, out_scatter, pre_scatter):
        scatter.end()


def tail(streamed, local, kept, tables, last, widths):
    space = pl.BlockSpec(memory_space=pltpu.VMEM)
    away = pl.BlockSpec(memory_space=pl.ANY)
    low = jnp.bfloat16
    packed, marks = streamed[:2]
    router_parts, shared_grads = local[3:]
    rows, width = last[0].shape
    tokens = 4 * rows
    _, router_rows, experts = router_parts.shape
    share = (router_rows // 32, experts)
    size = kept[1].shape[1]
    inner = kept[0].shape[1]
    pre_width = widths[0] + widths[1]
    shard = width // 32
    pre_grads = jax.ShapeDtypeStruct((2, 4, 4, shard, pre_width), low)
    out_grads = jax.ShapeDtypeStruct((2, 4, 4, shard, inner), low)
    dma = pltpu.SemaphoreType.DMA
    return pl.pallas_call(
        tail_kernel,
        out_shape=[
            jax.ShapeDtypeStruct((rows, width), jnp.float32),
            jax.ShapeDtypeStruct((rows, width), jnp.float32),
            jax.ShapeDtypeStruct((rows, width), low),
            jax.ShapeDtypeStruct((4, 2, 4, 4, *share), low),
            jax.ShapeDtypeStruct((1, width), jnp.float32),
            jax.ShapeDtypeStruct((1, width), jnp.float32),
        ]
        + [jax.ShapeDtypeStruct((shard, part), jnp.float32) for part in widths],
        in_specs=[away] * 9 + [space] * 17,
        out_specs=[space] * (6 + len(widths)),
        scratch_shapes=[
            pltpu.VMEM((4, packed.shape[0] // 4, packed.shape[1]), low),
            pltpu.VMEM(marks.shape, low),
            pltpu.VMEM((rows, width), jnp.float32),
            pltpu.VMEM((rows, width), jnp.float32),
            pltpu.VMEM((width, tokens), low),
            pltpu.VMEM((width, pre_width), low),
            pltpu.VMEM((width, inner), low),
            pltpu.VMEM((4, rows, width), low),
            pltpu.VMEM((rows, width), jnp.float32),
            pltpu.VMEM((rows, width), jnp.float32),
            pltpu.VMEM((4, rows, width), low),
            pltpu.VMEM((tokens, inner), low),
            pltpu.VMEM((tokens, pre_width), low),
            pltpu.VMEM((tokens // 2, tokens), jnp.float32),
            pltpu.VMEM((tokens, tokens // 2), jnp.float32),
            pltpu.VMEM((tokens // 2, 128), jnp.float32),
            pltpu.VMEM((tokens, size), jnp.float32),
            pltpu.VMEM((tokens, size), jnp.float32),
            pltpu.VMEM((4, rows, width), low),
            pltpu.VMEM((2, 2, rows, width), low),
            pltpu.VMEM((2, rows, width), low),
            pltpu.VMEM((2, rows, width), low),
            pltpu.VMEM((2, router_rows, experts), low),
            pltpu.VMEM((router_rows, experts), low),
            pltpu.VMEM((router_rows, experts), low),
            pltpu.VMEM((2, 4, 4, *share), low),
            pltpu.VMEM((5, 2, width), jnp.float32),
            pltpu.VMEM((10, 2, width), jnp.float32),
            pltpu.VMEM(pre_grads.shape, low),
            pltpu.VMEM(out_grads.shape, low),
            dma((12,)),
            dma((3,)),
            dma((3,)),
            dma((9,)),
            dma((9,)),
            dma((10,)),
            dma((10,)),
            dma((3,)),
            dma((3,)),
            *ScatterSum.scratch(shared_grads),
            *ScatterSum.scratch(out_grads),
            *ScatterSum.scratch(pre_grads),
            *RouterSum.scratch(share),
        ],
        compiler_params=pltpu.CompilerParams(
            collective_id=16, has_side_effects=True, vmem_limit_bytes=60 << 20
        ),
        cost_estimate=pl.CostEstimate(flops=0, bytes_accessed=300 << 20, transcendentals=0),
        name="tail",
    )(*streamed, *local, *kept, *tables, *last)


def packed_places(shape, axis):
    index = lax.broadcasted_iota(jnp.int32, shape, axis)
    pair, place = index // PACKED_ROWS, lax.rem(index, PACKED_ROWS)
    found = []
    for part in range(-1, 3):
        if part < 0:
            valid, slot = place < PAIR_ROWS, place
        else:
            valid, slot = place >= PAIR_ROWS, 3 * (place - PAIR_ROWS) + part
        second = (slot >= EXPERT_ROWS).astype(jnp.int32)
        found.append((valid, pair, second, slot - EXPERT_ROWS * second))
    return found


def token_marks(code_block):
    marks = []
    wide = (BLOCK, BLOCK_EXPERTS)
    lanes = lax.broadcasted_iota(jnp.int32, wide, 1)
    for (valid, pair, second, _), (tall, _, _, order) in zip(
        packed_places(wide, 0), packed_places((BLOCK, SIDE), 0)
    ):
        owner = ((lanes == 2 * pair + second) & valid).astype(jnp.float32).astype(jnp.bfloat16)
        found = matmul(owner, code_block)
        hit = (found == order.astype(jnp.float32)) & tall
        marks.append((owner, hit.astype(jnp.float32)))
    return marks


def gate_weights_of(owner, hit, high, low):
    weights = hit * (matmul(owner, high) + matmul(owner, low))
    return split_low(weights)


def pack_tokens_kernel(code, values, high, low, packed):
    marks = token_marks(code[0])
    weights = [gate_weights_of(owner, hit, high[0], low[0]) for owner, hit in marks]
    last = values[:, 3 * QUARTER :]
    for part in range(3):
        columns = slice(part * QUARTER, (part + 1) * QUARTER)
        both = jnp.concatenate([*weights[0], *weights[part + 1]], axis=1)
        rows = jnp.concatenate([values[:, columns]] * 2 + [last] * 2, axis=0)
        packed[:, columns] = matmul(both, rows).astype(jnp.bfloat16)


def pack_tokens(code, values, gates):
    blocks = code.shape[0]
    width = 3 * QUARTER
    small = pl.BlockSpec((1, BLOCK_EXPERTS, SIDE), lambda i: (i, 0, 0))
    return pl.pallas_call(
        pack_tokens_kernel,
        grid=(blocks,),
        out_shape=jax.ShapeDtypeStruct((blocks * BLOCK, width), jnp.bfloat16),
        in_specs=[small, pl.BlockSpec(values.shape, lambda i: (0, 0)), small, small],
        out_specs=pl.BlockSpec((BLOCK, width), lambda i: (i, 0)),
        compiler_params=pltpu.CompilerParams(vmem_limit_bytes=32 << 20),
        cost_estimate=pl.CostEstimate(
            flops=blocks * BLOCK * 512 * width * 2, bytes_accessed=8 << 20, transcendentals=0
        ),
        name="pack_tokens",
    )(code, values, *gates)


def slot_marks():
    shape = (2 * BLOCK_SLOTS, BLOCK)
    rows = lax.broadcasted_iota(jnp.int32, shape, 0)
    marks = []
    for valid, pair, second, order in packed_places(shape, 1):
        hit = (rows == second * BLOCK_SLOTS + pair * EXPERT_ROWS + order) & valid
        marks.append(hit.astype(jnp.float32).astype(jnp.bfloat16))
    return marks


def unpack_slots_kernel(packed, values):
    marks = slot_marks()
    last = jnp.zeros((2 * BLOCK_SLOTS, QUARTER), jnp.float32)
    for part in range(3):
        columns = slice(part * QUARTER, (part + 1) * QUARTER)
        found = matmul(marks[0], packed[:, columns]).astype(jnp.bfloat16)
        values[0, :, columns] = found[:BLOCK_SLOTS]
        values[1, :, columns] = found[BLOCK_SLOTS:]
        last = last + matmul(marks[part + 1], packed[:, columns])
    last = last.astype(jnp.bfloat16)
    values[0, :, 3 * QUARTER :] = last[:BLOCK_SLOTS]
    values[1, :, 3 * QUARTER :] = last[BLOCK_SLOTS:]


def unpack_slots(packed):
    blocks = packed.shape[0] // BLOCK
    slots = blocks * BLOCK_SLOTS
    return pl.pallas_call(
        unpack_slots_kernel,
        grid=(blocks,),
        out_shape=jax.ShapeDtypeStruct((2, slots, 4 * QUARTER), jnp.bfloat16),
        in_specs=[pl.BlockSpec((BLOCK, 3 * QUARTER), lambda i: (i, 0))],
        out_specs=pl.BlockSpec((2, BLOCK_SLOTS, 4 * QUARTER), lambda i: (0, i, 0)),
        compiler_params=pltpu.CompilerParams(vmem_limit_bytes=32 << 20),
        cost_estimate=pl.CostEstimate(
            flops=blocks * 2 * BLOCK_SLOTS * BLOCK * 6 * QUARTER * 2,
            bytes_accessed=14 << 20,
            transcendentals=0,
        ),
        name="unpack_slots",
    )(packed)


def pack_slots_kernel(values, packed):
    marks = slot_marks()
    last = jnp.concatenate([values[0, :, 3 * QUARTER :], values[1, :, 3 * QUARTER :]], axis=0)
    for part in range(3):
        columns = slice(part * QUARTER, (part + 1) * QUARTER)
        rows = jnp.concatenate([values[0, :, columns], values[1, :, columns]], axis=0)
        found = outer_sum(marks[0], rows) + outer_sum(marks[part + 1], last)
        packed[:, columns] = found.astype(jnp.bfloat16)


def pack_slots(values):
    slots = values.shape[1]
    blocks = slots // BLOCK_SLOTS
    return pl.pallas_call(
        pack_slots_kernel,
        grid=(blocks,),
        out_shape=jax.ShapeDtypeStruct((blocks * BLOCK, 3 * QUARTER), jnp.bfloat16),
        in_specs=[pl.BlockSpec((2, BLOCK_SLOTS, 4 * QUARTER), lambda i: (0, i, 0))],
        out_specs=pl.BlockSpec((BLOCK, 3 * QUARTER), lambda i: (i, 0)),
        compiler_params=pltpu.CompilerParams(vmem_limit_bytes=32 << 20),
        cost_estimate=pl.CostEstimate(
            flops=blocks * 2 * BLOCK_SLOTS * BLOCK * 6 * QUARTER * 2,
            bytes_accessed=14 << 20,
            transcendentals=0,
        ),
        name="pack_slots",
    )(values)


def marks_kernel(code, marks):
    wide = (BLOCK_EXPERTS, BLOCK)
    owners = lax.broadcasted_iota(jnp.int32, wide, 0)
    for i, ((valid, pair, second, _), (tall, _, _, order)) in enumerate(
        zip(packed_places(wide, 1), packed_places((code.shape[1], BLOCK), 1))
    ):
        owner = ((owners == 2 * pair + second) & valid).astype(jnp.float32).astype(jnp.bfloat16)
        hit = (matmul(code[0], owner) == order.astype(jnp.float32)) & tall
        marks[i] = hit.astype(jnp.float32).astype(jnp.bfloat16)


def all_marks(code):
    blocks, experts, tokens = code.shape
    return pl.pallas_call(
        marks_kernel,
        grid=(blocks,),
        out_shape=jax.ShapeDtypeStruct((4, tokens, blocks * BLOCK), jnp.bfloat16),
        in_specs=[pl.BlockSpec((1, tokens, experts), lambda i: (i, 0, 0))],
        out_specs=pl.BlockSpec((4, tokens, BLOCK), lambda i: (0, 0, i)),
        cost_estimate=pl.CostEstimate(flops=1 << 26, bytes_accessed=4 << 20, transcendentals=0),
        name="all_marks",
    )(code.transpose(0, 2, 1))


def sum_gated_kernel(code, packed, grads, high, low, total, gate_grads):
    @pl.when(pl.program_id(0) == 0)
    def _():
        total[...] = jnp.zeros_like(total)

    marks = token_marks(code[0])
    weights = [gate_weights_of(owner, hit, high[0], low[0]) for owner, hit in marks]
    last = jnp.zeros((total.shape[0], QUARTER), jnp.float32)
    whole = jnp.zeros((BLOCK, 1), jnp.float32)
    products = []
    for part in range(3):
        columns = slice(part * QUARTER, (part + 1) * QUARTER)
        rows = packed[:, columns]
        total[:, columns] += outer_sum(weights[0][0], rows) + outer_sum(weights[0][1], rows)
        last = last + outer_sum(weights[part + 1][0], rows) + outer_sum(weights[part + 1][1], rows)
        dots = jnp.sum(
            rows.astype(jnp.float32) * grads[:, columns].astype(jnp.float32),
            axis=1,
            keepdims=True,
        )
        whole = whole + dots
        products.append(dots)
    total[:, 3 * QUARTER :] += last
    found = jnp.zeros(gate_grads.shape[1:], jnp.float32)
    for (owner, hit), dots in zip(marks, [whole, *products]):
        hit = hit.astype(jnp.bfloat16)
        for spread in split_low(dots * owner.astype(jnp.float32)):
            found = found + outer_sum(hit, spread)
    gate_grads[0] = found


def sum_gated(code, packed, grads, gates):
    blocks, _, tokens = code.shape
    small = pl.BlockSpec((1, BLOCK_EXPERTS, tokens), lambda i: (i, 0, 0))
    wide = pl.BlockSpec((BLOCK, 3 * QUARTER), lambda i: (i, 0))
    return pl.pallas_call(
        sum_gated_kernel,
        grid=(blocks,),
        out_shape=[
            jax.ShapeDtypeStruct((tokens, 4 * QUARTER), jnp.float32),
            jax.ShapeDtypeStruct((blocks, tokens, BLOCK_EXPERTS), jnp.float32),
        ],
        in_specs=[small, wide, wide, small, small],
        out_specs=[
            pl.BlockSpec((tokens, 4 * QUARTER), lambda i: (0, 0)),
            pl.BlockSpec((1, tokens, BLOCK_EXPERTS), lambda i: (i, 0, 0)),
        ],
        compiler_params=pltpu.CompilerParams(vmem_limit_bytes=32 << 20),
        cost_estimate=pl.CostEstimate(
            flops=blocks * BLOCK * 128 * 12 * QUARTER * 2,
            bytes_accessed=14 << 20,
            transcendentals=0,
        ),
        name="sum_gated",
    )(code, packed, grads, *gates)


class Gather:
    def __init__(self, mine, full, send_sem, recv_sem):
        self.mine, self.full = mine, full
        self.sems = (send_sem, recv_sem)
        row, col = lax.axis_index("row"), lax.axis_index("col")
        x, z, y = col // 16, lax.rem(col // 4, 4), lax.rem(col, 4)
        self.place = (x, z, y)
        self.z_peers = [(row, x * 16 + lax.rem(z + i, 4) * 4 + y) for i in (1, 3, 2)]
        self.y_peers = [(row, x * 16 + z * 4 + lax.rem(y + i, 4)) for i in (1, 3, 2)]
        self.x_peer = (row, (1 - x) * 16 + z * 4 + y)
        self.copies = {}

    def rows(self, half):
        half_rows = self.full.shape[3] // 2
        return pl.ds(half * half_rows, half_rows)

    def send(self, key, source, target, peers):
        at = 1 + 3 * len(self.copies) - 3 if self.copies else 0
        copies = [
            remote(source, target, self.sems, at + i, peer) for i, peer in enumerate(peers)
        ]
        for copy in copies:
            copy.start()
        self.copies[key] = copies

    def wait(self, *keys):
        for key in keys:
            for copy in self.copies[key]:
                copy.wait_recv()

    def start(self):
        x, z, y = self.place
        self.send("x", self.mine, self.full.at[x, z, y], [self.x_peer])
        for half, peers in enumerate((self.z_peers, self.y_peers)):
            rows = self.rows(half)
            target = self.full.at[x, z, y, rows]
            self.send((0, half), self.mine.at[rows], target, peers)

    def second(self):
        x, z, y = self.place
        self.wait("x")
        for half, peers in enumerate((self.z_peers, self.y_peers)):
            target = self.full.at[1 - x, z, y, self.rows(half)]
            self.send((1, half), target, target, peers)

    def third(self):
        x, z, y = self.place
        for turn, owner_x in enumerate((x, 1 - x)):
            self.wait((turn, 0))
            target = self.full.at[owner_x, :, y, self.rows(0)]
            self.send((2 + turn, 0), target, target, self.y_peers)
            self.wait((turn, 1))
            target = self.full.at[owner_x, z, :, self.rows(1)]
            self.send((2 + turn, 1), target, target, self.z_peers)

    def await_all(self):
        self.wait((2, 0), (2, 1), (3, 0), (3, 1))

    def end(self):
        for copies in self.copies.values():
            for copy in copies:
                copy.wait_send()


def head_kernel(
    inputs,
    gain_attn,
    gain_ffn,
    grads,
    lengths,
    routes,
    frequency,
    w_query,
    w_keyval,
    w_out,
    w_shared_in,
    w_shared_out,
    full_pre,
    full_back,
    full_shared,
    group_one,
    group_grad,
    scale_one,
    cosine,
    sine,
    begin,
    begin_row,
    query,
    keys,
    values,
    attended,
    norms,
    hidden,
    normed_two,
    scale_two,
    packed,
    code,
    order,
    *scratch,
):
    mine_pre, mine_back, mine_shared, normed, rows, w_pre, w_back, pre, bias, parts = scratch[:10]
    near, far, outgoing, marks, staged = scratch[10:15]
    gather_send, gather_recv, own_sem, row_send, row_recv = scratch[15:20]
    sum_send, sum_recv, load_sem, pack_sem = scratch[20:]
    low = jnp.bfloat16
    row, col, sibling, partner, _ = row_places()
    gathers = [
        Gather(mine_pre, full_pre, gather_send.at[0], gather_recv.at[0]),
        Gather(mine_back, full_back, gather_send.at[1], gather_recv.at[1]),
        Gather(mine_shared, full_shared, gather_send.at[2], gather_recv.at[2]),
    ]
    place = gathers[0].place
    greet(gathers[0].z_peers + gathers[0].y_peers + [gathers[0].x_peer])
    greet([(sibling, col), (partner, col)])
    pairs = ((mine_pre, (w_query, w_keyval)), (mine_shared, (w_shared_in, w_shared_out)))
    for mine, shards in pairs:
        start = 0
        for shard in shards:
            mine[:, start : start + shard.shape[1]] = shard[...]
            start += shard.shape[1]
    mine_back[...] = w_out[...]
    first = inputs[...].astype(jnp.float32)
    factor = lax.rsqrt(jnp.mean(first * first, axis=1, keepdims=True) + epsilon)
    scale_one[...] = factor
    normed[...] = (first * factor * gain_attn[...]).astype(low)
    own = [
        pltpu.make_async_copy(normed, group_one.at[row], own_sem.at[0]),
        pltpu.make_async_copy(grads, group_grad.at[row], own_sem.at[1]),
        pltpu.make_async_copy(mine_pre, full_pre.at[place], own_sem.at[2]),
        pltpu.make_async_copy(mine_back, full_back.at[place], own_sem.at[3]),
        pltpu.make_async_copy(mine_shared, full_shared.at[place], own_sem.at[4]),
    ]
    for copy in own:
        copy.start()
    await_greetings(9)
    far_rows, near_rows, onward = row_copies(
        [normed, grads], [group_one, group_grad], row_send, row_recv
    )
    gathers[0].start()
    far_rows[0].start()
    near_rows[0].start()
    gathers[1].start()
    gathers[2].start()
    gathers[0].second()
    gathers[1].second()
    for copy in own[2:]:
        copy.wait()
    gathers[0].third()
    far_rows[1].start()
    near_rows[1].start()
    gathers[1].third()

    tokens = begin.shape[0]

    def document_starts(axis, shape):
        places = lax.broadcasted_iota(jnp.int32, shape, axis)
        found = jnp.zeros(shape, jnp.int32)
        bound = 0
        for i in range(NDOC - 1):
            bound = bound + lengths[0, i]
            found = jnp.where(places >= bound, bound, found)
        return places, found

    begin_row[...] = document_starts(1, begin_row.shape)[1]
    places, starts = document_starts(0, cosine.shape)
    begin[...] = starts[:, :1]
    angles = (places - starts).astype(jnp.float32) * frequency[...]
    lanes = lax.broadcasted_iota(jnp.int32, cosine.shape, 1)
    cosine[...] = jnp.cos(angles)
    sine[...] = jnp.where(lanes < cosine.shape[1] // 2, -1.0, 1.0) * jnp.sin(angles)
    bias[...] = score_bias(begin[...])

    experts = lax.broadcasted_iota(jnp.int32, order.shape, 1)
    chosen = jnp.zeros(order.shape, jnp.float32)
    for k in range(routes.shape[1]):
        chosen = jnp.where(routes[:, k : k + 1] == experts, 1.0, chosen)
    square = (order.shape[0], order.shape[0])
    before = lax.broadcasted_iota(jnp.int32, square, 1) < lax.broadcasted_iota(
        jnp.int32, square, 0
    )
    ahead = matmul(before.astype(jnp.float32).astype(low), chosen.astype(low))
    order[...] = jnp.where(chosen > 0.0, ahead, -1.0)
    code[...] = jnp.transpose(order[...]).astype(low).reshape(code.shape)

    def mark(block, carry):
        found = token_marks(code[block])
        for part in range(3):
            marks[block, part] = jnp.concatenate(
                [found[0][1].astype(low), found[part + 1][1].astype(low)], axis=1
            )
        return carry

    lax.fori_loop(0, code.shape[0], mark, 0)

    far_rows[0].wait_recv()
    onward[0].start()
    gathers[0].await_all()
    own[0].wait()
    near_rows[0].wait_recv()
    onward[0].wait_recv()
    loads = [
        pltpu.make_async_copy(group_one, rows, load_sem.at[0]),
        pltpu.make_async_copy(full_pre, w_pre, load_sem.at[1]),
        pltpu.make_async_copy(full_back, w_back, load_sem.at[2]),
    ]
    loads[0].start()
    loads[1].start()
    loads[0].wait()
    loads[1].wait()
    width = inputs.shape[1]
    pre[...] = matmul(
        rows[...].reshape(tokens, width), w_pre[...].reshape(width, w_pre.shape[4])
    )
    size = keys.shape[1]
    inner = query.shape[1]
    keys[...] = turn(pre[:, inner : inner + size], cosine[...], sine[...]).astype(low)
    values[...] = pre[:, inner + size :].astype(low)
    log_totals = jnp.zeros(norms.shape, jnp.float32)
    for head in range(inner // size):
        columns = slice(head * size, (head + 1) * size)
        turned = turn(pre[:, columns], cosine[...], sine[...]).astype(low)
        query[:, columns] = turned
        scores = matmul_t(turned, keys[...]) * (size ** (-0.5)) + bias[...]
        highest = jnp.max(scores, axis=1, keepdims=True)
        weights = jnp.exp(scores - highest)
        total = jnp.sum(weights, axis=1, keepdims=True)
        weights = (weights * (1.0 / total)).astype(low)
        attended[:, columns] = matmul(weights, values[...]).astype(low)
        log_totals = jnp.where(lanes == head, highest + jnp.log(total), log_totals)
    norms[...] = log_totals
    gathers[1].await_all()
    loads[2].start()
    loads[2].wait()
    parts[...] = (
        matmul_t(attended[...], w_back[...].reshape(width, inner)).astype(low).reshape(parts.shape)
    )

    copies = row_sum_copies(parts, near, far, outgoing, (sum_send, sum_recv), 0)
    copies[0].start()
    copies[1].start()
    gathers[2].second()
    row_sum_forward(parts, near, outgoing, copies)
    far_rows[1].wait_recv()
    onward[1].start()
    gathers[2].third()
    total = inputs[...].astype(jnp.float32) + row_sum_total(parts, near, far, copies)
    hidden[...] = total
    factor = lax.rsqrt(jnp.mean(total * total, axis=1, keepdims=True) + epsilon)
    normed_two[...] = (total * factor * gain_ffn[...]).astype(low)
    scale_two[...] = factor

    def pack(block, carry):
        last = normed_two[:, 3 * QUARTER :]
        for part in range(3):
            columns = slice(part * QUARTER, (part + 1) * QUARTER)
            both = jnp.concatenate([normed_two[:, columns], last], axis=0)
            staged[block, :, columns] = matmul(marks[block, part], both).astype(low)
        target = packed.at[pl.ds(pl.multiple_of(block * BLOCK, BLOCK), BLOCK)]
        pltpu.make_async_copy(staged.at[block], target, pack_sem.at[block]).start()
        return carry

    lax.fori_loop(0, code.shape[0], pack, 0)

    gathers[2].await_all()
    own[1].wait()
    near_rows[0].wait_send()
    near_rows[1].wait()
    onward[0].wait_send()
    onward[1].wait()
    for copy in far_rows + copies:
        copy.wait_send()
    for gather in gathers:
        gather.end()
    for block in range(staged.shape[0]):
        target = packed.at[pl.ds(block * BLOCK, BLOCK)]
        pltpu.make_async_copy(staged.at[block], target, pack_sem.at[block]).wait()


def head(inputs, gain_attn, gain_ffn, grads, lengths, routes, shards, size, expert_count):
    space = pl.BlockSpec(memory_space=pltpu.VMEM)
    away = pl.BlockSpec(memory_space=pl.ANY)
    low = jnp.bfloat16
    rows, width = inputs.shape
    tokens = 4 * rows
    shard_rows = shards[0].shape[0]
    inner = shards[0].shape[1]
    pre_width = inner + shards[1].shape[1]
    shared_width = shards[3].shape[1] + shards[4].shape[1]
    blocks = expert_count // BLOCK_EXPERTS
    spread = np.arange(size // 2, dtype=np.float32) * np.float32(2.0 / size)
    frequency = np.float32(rope_base) ** (-spread)
    frequency = jnp.asarray(np.concatenate([frequency, frequency])[None], jnp.float32)

    def full(shape, dtype):
        return jax.ShapeDtypeStruct(shape, dtype)

    return pl.pallas_call(
        head_kernel,
        out_shape=[
            full((2, 4, 4, shard_rows, pre_width), low),
            full((2, 4, 4, shard_rows, inner), low),
            full((2, 4, 4, shard_rows, shared_width), low),
            full((4, rows, width), low),
            full((4, rows, width), low),
            full((rows, 1), jnp.float32),
            full((tokens, size), jnp.float32),
            full((tokens, size), jnp.float32),
            full((tokens, 1), jnp.int32),
            full((1, tokens), jnp.int32),
            full((tokens, inner), low),
            full((tokens, size), low),
            full((tokens, size), low),
            full((tokens, inner), low),
            full((tokens, size), jnp.float32),
            full((rows, width), jnp.float32),
            full((rows, width), low),
            full((rows, 1), jnp.float32),
            full((blocks * BLOCK, 3 * QUARTER), low),
            full((blocks, BLOCK_EXPERTS, rows), low),
            full((rows, expert_count), jnp.float32),
        ],
        in_specs=[space] * 3
        + [away, pl.BlockSpec(memory_space=pltpu.SMEM)]
        + [space] * (2 + len(shards)),
        out_specs=[away] * 5 + [space] * 13 + [away] + [space] * 2,
        scratch_shapes=[
            pltpu.VMEM((shard_rows, pre_width), low),
            pltpu.VMEM((shard_rows, inner), low),
            pltpu.VMEM((shard_rows, shared_width), low),
            pltpu.VMEM((rows, width), low),
            pltpu.VMEM((4, rows, width), low),
            pltpu.VMEM((2, 4, 4, shard_rows, pre_width), low),
            pltpu.VMEM((2, 4, 4, shard_rows, inner), low),
            pltpu.VMEM((tokens, pre_width), jnp.float32),
            pltpu.VMEM((tokens, tokens), jnp.float32),
            pltpu.VMEM((4, rows, width), low),
            pltpu.VMEM((2, rows, width), low),
            pltpu.VMEM((rows, width), low),
            pltpu.VMEM((rows, width), low),
            pltpu.VMEM((blocks, 3, BLOCK, 2 * rows), low),
            pltpu.VMEM((blocks, BLOCK, 3 * QUARTER), low),
            pltpu.SemaphoreType.DMA((3, 25)),
            pltpu.SemaphoreType.DMA((3, 25)),
            pltpu.SemaphoreType.DMA((5,)),
            pltpu.SemaphoreType.DMA((6,)),
            pltpu.SemaphoreType.DMA((6,)),
            pltpu.SemaphoreType.DMA((3,)),
            pltpu.SemaphoreType.DMA((3,)),
            pltpu.SemaphoreType.DMA((3,)),
            pltpu.SemaphoreType.DMA((blocks,)),
        ],
        compiler_params=pltpu.CompilerParams(
            collective_id=0, has_side_effects=True, vmem_limit_bytes=60 << 20
        ),
        cost_estimate=pl.CostEstimate(flops=0, bytes_accessed=300 << 20, transcendentals=0),
        name="head",
    )(inputs, gain_attn, gain_ffn, grads, lengths, routes, frequency, *shards)


def side_by_side_kernel(first, second, both):
    both[:, : first.shape[1]] = first[...]
    both[:, first.shape[1] :] = second[...]


def side_by_side(first, second):
    shape = (first.shape[0], first.shape[1] + second.shape[1])
    return pl.pallas_call(
        side_by_side_kernel,
        out_shape=jax.ShapeDtypeStruct(shape, first.dtype),
        cost_estimate=pl.CostEstimate(flops=0, bytes_accessed=3 << 20, transcendentals=0),
        name="side_by_side",
    )(first, second)


def exchange(packed):
    pairs = packed.reshape(-1, PACKED_ROWS, packed.shape[1])
    swapped = lax.all_to_all(pairs, ("row", "col"), split_axis=0, concat_axis=0, tiled=True)
    return swapped.reshape(packed.shape)


def per_device(
    block_in,
    gain_attn,
    w_query,
    w_keyval,
    w_out,
    gain_ffn,
    w_shared_in,
    w_shared_out,
    w_router,
    w_expert_in,
    w_expert_out,
    doc_lengths,
    routes,
    cotangent,
):
    row_count = lax.axis_size("row")
    rows_dev = block_in.shape[1]
    model_width = block_in.shape[2]
    expert_count = w_router.shape[1]
    expert_ff = w_expert_out.shape[2]
    inputs = block_in.reshape(rows_dev, model_width)
    grad_low = cotangent.reshape(rows_dev, model_width)
    shards = [w_query, w_keyval, w_out, w_shared_in, w_shared_out]
    shards = [part.reshape(part.shape[0], -1) for part in shards]
    (
        full_pre,
        full_back,
        full_shared,
        group_one,
        group_grad,
        scale_one,
        cosine,
        sine_table,
        begin,
        begin_row,
        *kept,
        hidden_state,
        normed_two,
        scale_two,
        send_rows,
        code,
        order,
    ) = head(
        inputs,
        gain_attn[None],
        gain_ffn[None],
        grad_low,
        doc_lengths,
        routes.reshape(rows_dev, -1),
        shards,
        w_keyval.shape[2] // 2,
        expert_count,
    )
    full_pre, full_back, full_shared, group_one, group_grad = (
        part.reshape(-1, part.shape[-1])
        for part in (full_pre, full_back, full_shared, group_one, group_grad)
    )
    received = exchange(send_rows)
    shared_width = w_shared_out.shape[1]
    full_shared_in = full_shared[:, : 2 * shared_width]
    full_shared_out = full_shared[:, 2 * shared_width :]

    logits = matmul(normed_two, w_router)
    scores_sig = jnp.where(order >= 0.0, jax.nn.sigmoid(logits), 0.0)
    score_sum = jnp.sum(scores_sig, axis=1, keepdims=True)
    gate_weights = scores_sig / score_sum
    gates = [
        part.T.reshape(-1, BLOCK_EXPERTS, rows_dev) for part in split_low(gate_weights)
    ]
    send_grads, received = lax.optimization_barrier((pack_tokens(code, grad_low, gates), received))
    received_grads = exchange(send_grads)

    group_two = lax.all_gather(normed_two, "row", axis=0, tiled=True)
    shared_pre = matmul(group_two, full_shared_in)
    shared_gate, shared_up = shared_pre[:, :shared_width], shared_pre[:, shared_width:]
    shared_act, shared_slope = swish_parts(shared_gate)
    shared_hidden = (shared_act * shared_up).astype(jnp.bfloat16)
    shared_hidden_grad = matmul(group_grad, full_shared_out)
    shared_pre_grad = jnp.concatenate(
        [shared_hidden_grad * shared_up * shared_slope, shared_hidden_grad * shared_act], axis=1
    ).astype(jnp.bfloat16)
    shared_grads = side_by_side(
        outer_sum(group_two, shared_pre_grad).astype(jnp.bfloat16),
        outer_sum(group_grad, shared_hidden).astype(jnp.bfloat16),
    )
    shared_parts = matmul_t(shared_hidden, full_shared_out).astype(jnp.bfloat16)
    shared_input = lax.psum_scatter(
        matmul_t(shared_pre_grad, full_shared_in).astype(jnp.bfloat16),
        "row",
        scatter_dimension=0,
        tiled=True,
    ).astype(jnp.float32)

    expert_in = unpack_slots(received)
    expert_pre = jnp.einsum(
        "esd,edf->esf", expert_in, w_expert_in, preferred_element_type=jnp.float32
    )
    expert_act, expert_slope = swish_parts(expert_pre[..., :expert_ff])
    expert_hidden = (expert_act * expert_pre[..., expert_ff:]).astype(jnp.bfloat16)
    expert_out = jnp.einsum(
        "esf,edf->esd", expert_hidden, w_expert_out, preferred_element_type=jnp.float32
    ).astype(jnp.bfloat16)
    send_out, received_grads = lax.optimization_barrier((pack_slots(expert_out), received_grads))
    returned = exchange(send_out)

    out_grad = unpack_slots(received_grads)
    hidden_grad = jnp.einsum(
        "esd,edf->esf", out_grad, w_expert_out, preferred_element_type=jnp.float32
    )
    expert_pre_grad = jnp.concatenate(
        [hidden_grad * expert_pre[..., expert_ff:] * expert_slope, hidden_grad * expert_act], axis=2
    ).astype(jnp.bfloat16)
    slot_grad = jnp.einsum(
        "esf,edf->esd", expert_pre_grad, w_expert_in, preferred_element_type=jnp.float32
    ).astype(jnp.bfloat16)
    send_back, returned = lax.optimization_barrier((pack_slots(slot_grad), returned))
    returned_grad = exchange(send_back)
    grad_expert_out = jnp.einsum(
        "esd,esf->edf", out_grad, expert_hidden, preferred_element_type=jnp.float32
    )
    grad_expert_in = jnp.einsum(
        "esd,esf->edf", expert_in, expert_pre_grad, preferred_element_type=jnp.float32
    )
    routed_branch, gate_grads = sum_gated(code, returned, send_grads, gates)
    stream = hidden_state + routed_branch
    gate_grads = gate_grads.transpose(1, 0, 2).reshape(rows_dev, expert_count)
    logit_grad = (
        (1.0 - scores_sig)
        * (gate_grads - gate_weights * jnp.sum(gate_grads, axis=1, keepdims=True))
    ).astype(jnp.bfloat16)
    router_parts = outer_sum(normed_two, logit_grad).astype(jnp.bfloat16)
    router_parts = router_parts.reshape(row_count, -1, expert_count)
    router_input = shared_input + matmul_t(logit_grad, w_router)
    shadowed = (router_input, router_parts, stream, shared_grads, group_one.T, all_marks(code))
    returned_grad, shadowed, grad_expert_in, grad_expert_out = lax.optimization_barrier(
        (returned_grad, shadowed, grad_expert_in, grad_expert_out)
    )
    router_input, router_parts, stream, shared_grads, group_one_t, marks = shadowed

    widths = [part.shape[1] for part in shards]
    hidden_total, input_back, block_out, router_sum, gain_attn_sum, gain_ffn_sum, *sums = tail(
        (
            returned_grad,
            marks,
            router_input,
            hidden_state,
            group_one_t,
            full_pre,
            full_back,
            shared_parts.reshape(row_count, rows_dev, model_width),
            stream,
        ),
        (
            scale_two,
            gain_ffn[None],
            grad_low,
            router_parts,
            shared_grads.reshape(2, 4, 4, -1, shared_grads.shape[1]),
        ),
        kept,
        (cosine, sine_table, begin, begin_row),
        (inputs, scale_one, gain_attn[None]),
        widths,
    )
    sums = [
        part.reshape(like.shape)
        for part, like in zip(sums, (w_query, w_keyval, w_out, w_shared_in, w_shared_out))
    ]
    return (
        block_out.reshape(1, rows_dev, model_width),
        (hidden_total + input_back).reshape(1, rows_dev, model_width),
        gain_attn_sum[0],
        sums[0],
        sums[1],
        sums[2],
        gain_ffn_sum[0],
        sums[3],
        sums[4],
        router_sum.reshape(model_width, expert_count).astype(jnp.float32),
        grad_expert_in,
        grad_expert_out,
    )


def solution(mesh):
    in_specs = (
        P("col", "row", None),
        P(),
        P("col", "row"),
        P("col", "row", None),
        P("col", "row"),
        P(),
        P("col", None, "row"),
        P("col", "row"),
        P(),
        P(("row", "col"), None, None),
        P(("row", "col"), None, None),
        P("col", None),
        P("col", "row", None),
        P("col", "row", None),
    )
    out_specs = (
        P("col", "row", None),
        P("col", "row", None),
        P(),
        P("col", "row"),
        P("col", "row", None),
        P("col", "row"),
        P(),
        P("col", None, "row"),
        P("col", "row"),
        P(),
        P(("row", "col"), None, None),
        P(("row", "col"), None, None),
    )
    return jax.shard_map(
        per_device, mesh=mesh, in_specs=in_specs, out_specs=out_specs, check_vma=False
    )
```

```python
import functools

import jax
import jax.numpy as jnp
import numpy as np
from jax import lax
from jax.experimental import pallas as pl
from jax.experimental.pallas import tpu as pltpu
from jax.sharding import PartitionSpec as P

epsilon = 1e-06
rope_base = 10000.0
masked_score = -1e30

EXPERT_ROWS = 6
PAIR_ROWS = 12
PACKED_ROWS = 16
BLOCK_PAIRS = 16
BLOCK = BLOCK_PAIRS * PACKED_ROWS
BLOCK_EXPERTS = 2 * BLOCK_PAIRS
BLOCK_SLOTS = BLOCK_PAIRS * EXPERT_ROWS
QUARTER = 512
SIDE = 128
MESH = pl.DeviceIdType.MESH
NDOC = 4


def swish_parts(pre_act):
    logistic = jax.nn.sigmoid(pre_act)
    return (pre_act * logistic, logistic * (1.0 + pre_act * (1.0 - logistic)))


def matmul(matrix, partner):
    return jnp.dot(matrix, partner, preferred_element_type=jnp.float32)


def matmul_t(matrix, partner):
    return lax.dot_general(
        matrix, partner, (((1,), (1,)), ((), ())), preferred_element_type=jnp.float32
    )


def outer_sum(matrix, partner):
    return lax.dot_general(
        matrix, partner, (((0,), (0,)), ((), ())), preferred_element_type=jnp.float32
    )


def split_low(values):
    high = values.astype(jnp.bfloat16)
    return high, (values - high.astype(jnp.float32)).astype(jnp.bfloat16)


def row_places():
    row, col = lax.axis_index("row"), lax.axis_index("col")
    chip, core = row // 2, lax.rem(row, 2)
    sibling = chip * 2 + (1 - core)
    partner = (1 - chip) * 2 + core
    across = (1 - chip) * 2 + (1 - core)
    return row, col, sibling, partner, across


def row_copies(sources, targets, send_sem, recv_sem):
    row, col, sibling, partner, _ = row_places()

    def send(origin, target, peer, i):
        return pltpu.make_async_remote_copy(
            src_ref=origin,
            dst_ref=target,
            send_sem=send_sem.at[i],
            recv_sem=recv_sem.at[i],
            device_id=(peer, col),
            device_id_type=MESH,
        )

    far, near, onward = [], [], []
    for i, (source, target) in enumerate(zip(sources, targets)):
        far.append(send(source, target.at[row], partner, 3 * i))
        near.append(send(source, target.at[row], sibling, 3 * i + 1))
        onward.append(send(target.at[partner], target.at[partner], sibling, 3 * i + 2))
    return far, near, onward


def greet(peers):
    barrier = pltpu.get_barrier_semaphore()
    for peer in peers:
        pl.semaphore_signal(barrier, inc=1, device_id=peer, device_id_type=MESH)


def await_greetings(count):
    pl.semaphore_wait(pltpu.get_barrier_semaphore(), count)


def turn(values, cosine, sine):
    return values * cosine + pltpu.roll(values, 64, 1) * sine


def score_bias(begin):
    shape = (begin.shape[0], begin.shape[0])
    keys = lax.broadcasted_iota(jnp.int32, shape, 1)
    allowed = (keys >= begin) & (keys <= lax.broadcasted_iota(jnp.int32, shape, 0))
    return jnp.where(allowed, 0.0, masked_score)


def remote(source, target, sems, at, peer):
    return pltpu.make_async_remote_copy(
        src_ref=source,
        dst_ref=target,
        send_sem=sems[0].at[at],
        recv_sem=sems[1].at[at],
        device_id=peer,
        device_id_type=MESH,
    )


def row_sum_copies(parts, near, far, outgoing, sems, at):
    _, col, sibling, partner, across = row_places()
    return [
        remote(parts.at[across], near.at[0], sems, at, (sibling, col)),
        remote(parts.at[sibling], near.at[1], sems, at + 1, (sibling, col)),
        remote(outgoing, far, sems, at + 2, (partner, col)),
    ]


def row_sum_forward(parts, near, outgoing, copies):
    _, _, _, partner, _ = row_places()
    copies[0].wait_recv()
    outgoing[...] = (parts[partner].astype(jnp.float32) + near[0].astype(jnp.float32)).astype(
        jnp.bfloat16
    )
    copies[2].start()


def row_sum_total(parts, near, far, copies):
    row = row_places()[0]
    copies[1].wait_recv()
    total = parts[row].astype(jnp.float32) + near[1].astype(jnp.float32)
    copies[2].wait_recv()
    return total + far[...].astype(jnp.float32)


class ScatterSum:
    def __init__(self, grads, scratch):
        self.grads = grads
        self.first, self.first_sum, self.second, self.second_sum, self.third = scratch[:5]
        self.one, self.two, self.three = scratch[5:7], scratch[7:9], scratch[9:11]
        row, col = lax.axis_index("row"), lax.axis_index("col")
        x, z, y = col // 16, lax.rem(col // 4, 4), lax.rem(col, 4)
        self.place = (x, z, y)
        self.half_rows = grads.shape[3] // 2
        self.y_peers = [(row, x * 16 + z * 4 + lax.rem(y + i, 4)) for i in (1, 2, 3)]
        self.z_peers = [(row, x * 16 + lax.rem(z + i, 4) * 4 + y) for i in (1, 2, 3)]
        self.x_peer = (row, (1 - x) * 16 + z * 4 + y)
        self.one_copies, self.two_copies, self.three_copies = {}, {}, []

    @staticmethod
    def scratch(grads):
        half_rows, depth = grads.shape[3] // 2, grads.shape[4]
        low = jnp.bfloat16
        return [
            pltpu.VMEM((2, 3, 2, 4, half_rows, depth), low),
            pltpu.VMEM((2, 2, 4, half_rows, depth), low),
            pltpu.VMEM((2, 3, 2, half_rows, depth), low),
            pltpu.VMEM((2, half_rows, depth), low),
            pltpu.VMEM((2, half_rows, depth), low),
        ] + [pltpu.SemaphoreType.DMA((count,)) for count in (6, 6, 6, 6, 2, 2)]

    def half(self, half):
        return pl.ds(half * self.half_rows, self.half_rows)

    def start(self):
        _, z, y = self.place
        for i in range(3):
            for half in range(2):
                if half == 0:
                    source = self.grads.at[:, :, lax.rem(y + i + 1, 4), self.half(0)]
                else:
                    source = self.grads.at[:, lax.rem(z + i + 1, 4), :, self.half(1)]
                peer = (self.y_peers, self.z_peers)[half][i]
                copy = remote(source, self.first.at[half, i], self.one, half * 3 + i, peer)
                self.one_copies[half, i] = copy
                copy.start()

    def add_first(self):
        _, z, y = self.place
        for half in range(2):
            for i in range(3):
                self.one_copies[half, i].wait_recv()

            def add(k, carry, half=half):
                if half == 0:
                    total = self.grads[k // 4, lax.rem(k, 4), y, self.half(0)].astype(jnp.float32)
                else:
                    total = self.grads[k // 4, z, lax.rem(k, 4), self.half(1)].astype(jnp.float32)
                for i in range(3):
                    total = total + self.first[half, i, k // 4, lax.rem(k, 4)].astype(jnp.float32)
                self.first_sum[half, k // 4, lax.rem(k, 4)] = total.astype(jnp.bfloat16)
                return carry

            lax.fori_loop(0, 8, add, 0)
            for i in range(3):
                away = lax.rem((z, y)[half] + i + 1, 4)
                copy = remote(
                    self.first_sum.at[half, :, away],
                    self.second.at[half, i],
                    self.two,
                    half * 3 + i,
                    (self.z_peers, self.y_peers)[half][i],
                )
                self.two_copies[half, i] = copy
                copy.start()

    def second_total(self, owner_x, half):
        _, z, y = self.place
        total = self.first_sum[half, owner_x, (z, y)[half]].astype(jnp.float32)
        for i in range(3):
            total = total + self.second[half, i, owner_x].astype(jnp.float32)
        return total

    def add_second(self):
        x = self.place[0]
        for half in range(2):
            for i in range(3):
                self.two_copies[half, i].wait_recv()
            self.second_sum[half] = self.second_total(1 - x, half).astype(jnp.bfloat16)
            copy = remote(
                self.second_sum.at[half], self.third.at[half], self.three, half, self.x_peer
            )
            self.three_copies.append(copy)
            copy.start()

    def add_third(self, pieces):
        x = self.place[0]
        for half in range(2):
            total = self.second_total(x, half)
            self.three_copies[half].wait_recv()
            total = total + self.third[half].astype(jnp.float32)
            start = 0
            for piece in pieces:
                piece[self.half(half)] = total[:, start : start + piece.shape[1]]
                start += piece.shape[1]

    def end(self):
        for copy in [*self.one_copies.values(), *self.two_copies.values(), *self.three_copies]:
            copy.wait_send()


class RouterSum:
    def __init__(self, part, block, scratch):
        self.part, self.block = part, block
        self.in_y, self.sum_y, self.in_z, self.sum_z, self.in_x = scratch[:5]
        self.sems = scratch[5:]
        row, col = lax.axis_index("row"), lax.axis_index("col")
        x, z, y = col // 16, lax.rem(col // 4, 4), lax.rem(col, 4)
        self.place = (x, z, y)
        self.y_near = [lax.rem(y + i, 4) for i in (1, 2, 3)]
        self.z_near = [lax.rem(z + i, 4) for i in (1, 2, 3)]
        self.y_peers = [(row, x * 16 + z * 4 + near) for near in self.y_near]
        self.z_peers = [(row, x * 16 + near * 4 + y) for near in self.z_near]
        self.x_peer = (row, (1 - x) * 16 + z * 4 + y)
        self.copies = {}

    @staticmethod
    def scratch(share):
        low = jnp.bfloat16
        return [
            pltpu.VMEM((3, 2, 4, *share), low),
            pltpu.VMEM((2, 4, *share), low),
            pltpu.VMEM((3, 2, *share), low),
            pltpu.VMEM((2, *share), low),
            pltpu.VMEM(share, low),
            pltpu.SemaphoreType.DMA((14,)),
            pltpu.SemaphoreType.DMA((14,)),
        ]

    def send(self, stage, at, sources, targets, peers):
        copies = [
            remote(source, target, self.sems, at + i, peer)
            for i, (source, target, peer) in enumerate(zip(sources, targets, peers))
        ]
        for copy in copies:
            copy.start()
        self.copies[stage] = copies

    def wait(self, stage):
        for copy in self.copies[stage]:
            copy.wait_recv()

    def start(self):
        sources = [self.part.at[:, :, near] for near in self.y_near]
        self.send(0, 0, sources, [self.in_y.at[i] for i in range(3)], self.y_peers)

    def add_y(self):
        self.wait(0)
        total = self.part[:, :, self.place[2]].astype(jnp.float32)
        for i in range(3):
            total = total + self.in_y[i].astype(jnp.float32)
        self.sum_y[...] = total.astype(jnp.bfloat16)
        sources = [self.sum_y.at[:, near] for near in self.z_near]
        self.send(1, 3, sources, [self.in_z.at[i] for i in range(3)], self.z_peers)

    def add_z(self):
        self.wait(1)
        total = self.sum_y[:, self.place[1]].astype(jnp.float32)
        for i in range(3):
            total = total + self.in_z[i].astype(jnp.float32)
        self.sum_z[...] = total.astype(jnp.bfloat16)
        self.send(2, 6, [self.sum_z.at[1 - self.place[0]]], [self.in_x], [self.x_peer])

    def add_x(self):
        self.wait(2)
        x, z, y = self.place
        total = self.sum_z[x].astype(jnp.float32) + self.in_x[...].astype(jnp.float32)
        self.block[x, z, y] = total.astype(jnp.bfloat16)
        own = self.block.at[x, z, y]
        self.send(3, 7, [own], [own], [self.x_peer])

    def spread_z(self):
        self.wait(3)
        own = self.block.at[:, self.place[1], self.place[2]]
        self.send(4, 8, [own] * 3, [own] * 3, self.z_peers)

    def spread_y(self):
        self.wait(4)
        own = self.block.at[:, :, self.place[2]]
        self.send(5, 11, [own] * 3, [own] * 3, self.y_peers)

    def end(self):
        for copies in self.copies.values():
            for copy in copies:
                copy.wait_send()


def attention_back_rows(start, refs, sums):
    group, w_back, query, keys, values, norms, cosine, sine, begin, begin_row = refs
    back, pre_grad, bias, bias_t, deltas, key_grad, value_grad = sums
    low = jnp.bfloat16
    size = keys.shape[1]
    inner = query.shape[1]
    count = bias.shape[0]
    rows = pl.ds(pl.multiple_of(start, count), count)
    scale = size ** (-0.5)
    branch = group[pl.ds(start // 128, count // 128)].reshape(count, group.shape[2])
    back[rows] = matmul(branch, w_back[...]).astype(low)
    first = begin[rows]
    key_places = lax.broadcasted_iota(jnp.int32, bias.shape, 1)
    places = start + lax.broadcasted_iota(jnp.int32, bias.shape, 0)
    bias[...] = jnp.where((key_places >= first) & (key_places <= places), 0.0, masked_score)
    lanes = lax.broadcasted_iota(jnp.int32, deltas.shape, 1)
    all_deltas = jnp.zeros(deltas.shape, jnp.float32)
    for head in range(inner // size):
        columns = slice(head * size, (head + 1) * size)
        turned, outer = query[rows, columns], back[rows, columns]
        scores = matmul_t(turned, keys[...]) * scale + bias[...]
        probs = jnp.exp(scores - norms[rows, head : head + 1])
        prob_grad = matmul_t(outer, values[...])
        delta = jnp.sum(probs * prob_grad, axis=1, keepdims=True)
        all_deltas = jnp.where(lanes == head, delta, all_deltas)
        score_grad = (probs * (prob_grad - delta)).astype(low)
        query_grad = matmul(score_grad, keys[...]) * scale
        pre_grad[rows, columns] = turn(query_grad, cosine[rows], -sine[rows]).astype(low)
    deltas[...] = all_deltas
    deltas_t = jnp.transpose(deltas[...])
    norms_t = jnp.transpose(norms[rows])
    first = begin_row[:, rows]
    key_places = lax.broadcasted_iota(jnp.int32, bias_t.shape, 0)
    places = start + lax.broadcasted_iota(jnp.int32, bias_t.shape, 1)
    bias_t[...] = jnp.where((key_places >= first) & (key_places <= places), 0.0, masked_score)
    for head in range(inner // size):
        columns = slice(head * size, (head + 1) * size)
        turned, outer = query[rows, columns], back[rows, columns]
        scores = matmul_t(keys[...], turned) * scale + bias_t[...]
        probs = jnp.exp(scores - norms_t[head : head + 1])
        prob_grad = matmul_t(values[...], outer)
        score_grad = (probs * (prob_grad - deltas_t[head : head + 1])).astype(low)
        key_grad[...] += matmul(score_grad, turned)
        value_grad[...] += matmul(probs.astype(low), outer)


def tail_kernel(
    packed,
    marks_in,
    router_input_in,
    hidden_in,
    group_one_t,
    full_pre,
    full_back,
    shared_parts_in,
    stream_in,
    shared_input_in,
    scale_two,
    gain_ffn,
    stream_grad,
    router_parts,
    shared_grads,
    query,
    keys,
    values_in,
    attended,
    norms,
    cosine,
    sine,
    begin,
    begin_row,
    inputs,
    scale_one,
    gain_attn,
    hidden_total,
    result,
    block_out,
    router,
    gain_attn_sum,
    gain_ffn_sum,
    *refs,
):
    pieces, scratch = refs[:5], refs[5:]
    held, marks, router_input, hidden, rows_t, w_pre, w_back, shared_parts, stream = scratch[:9]
    routed, group, back, pre_grad, bias, bias_t, deltas, key_grad, value_grad = scratch[9:18]
    parts, near, far, outgoing, router_near, router_far, router_outgoing = scratch[18:25]
    router_part, values, buffers, pre_grads, out_grads = scratch[25:30]
    load_sem, branch_send, branch_recv, row_send, row_recv, gain_send, gain_recv = scratch[30:37]
    pass_send, pass_recv, input_parts, core_near, share_sums, share_low = scratch[37:43]
    shared_scatter = ScatterSum(shared_grads, scratch[43:54])
    out_scatter = ScatterSum(out_grads, scratch[54:65])
    pre_scatter = ScatterSum(pre_grads, scratch[65:76])
    router_at = 76
    low = jnp.bfloat16
    row, col, sibling, partner, across = row_places()
    row_peers = [(peer, col) for peer in (sibling, partner, across)]
    greet(row_peers)
    greet(pre_scatter.y_peers + pre_scatter.z_peers + [pre_scatter.x_peer])
    steps, depth = held.shape[:2]
    inner = query.shape[1]
    sources = [packed.at[pl.ds(i * depth, depth)] for i in range(steps)]
    targets = [held.at[i] for i in range(steps)]
    sources[1:1] = [marks_in]
    targets[1:1] = [marks]
    sources += [router_input_in, hidden_in, full_back, shared_parts_in]
    targets += [router_input, hidden, w_back, shared_parts]
    sources += [full_pre, group_one_t, stream_in]
    targets += [w_pre, rows_t, stream]
    loads = [
        pltpu.make_async_copy(source, target, load_sem.at[i])
        for i, (source, target) in enumerate(zip(sources, targets))
    ]
    load_parts = pltpu.make_async_copy(shared_input_in, input_parts, load_sem.at[len(loads)])
    load_parts.start()
    for load in loads:
        load.start()
    load_marks = loads.pop(1)
    load_input, load_hidden, load_back, load_shared, load_pre, load_rows, load_stream = loads[
        steps:
    ]
    await_greetings(10)

    row_sems = (row_send, row_recv)
    router_copies = row_sum_copies(
        router_parts, router_near, router_far, router_outgoing, row_sems, 0
    )
    router_copies[0].start()
    router_copies[1].start()
    core = lax.rem(row, 2)
    load_parts.wait()
    input_copy = remote(input_parts.at[1 - core], core_near.at[0], row_sems, 3, (sibling, col))
    input_copy.start()
    shared_scatter.start()
    row_sum_forward(router_parts, router_near, router_outgoing, router_copies)

    load_marks.wait()
    for i in range(steps):
        loads[i].wait()
        rows = slice(i * depth, (i + 1) * depth)
        for part in range(4):
            columns = slice(part * QUARTER, (part + 1) * QUARTER)
            if part < 3:
                found = matmul(marks[0, :, rows], held[i, :, columns])
            else:
                found = matmul(marks[1, :, rows], held[i, :, :QUARTER])
                for j in (1, 2):
                    second = slice(j * QUARTER, (j + 1) * QUARTER)
                    found = found + matmul(marks[j + 1, :, rows], held[i, :, second])
            routed[:, columns] = found if i == 0 else routed[:, columns] + found
    load_input.wait()
    load_hidden.wait()
    input_copy.wait_recv()
    shared_input = input_parts[core].astype(jnp.float32) + core_near[0].astype(jnp.float32)
    incoming = router_input[...] + routed[...] + shared_input
    state = hidden[...]
    factor = scale_two[...]
    weighted = gain_ffn[...] * incoming
    mean = jnp.mean(weighted * state, axis=1, keepdims=True)
    total = (
        stream_grad[...].astype(jnp.float32)
        + factor * weighted
        - state * (factor * factor * factor * mean)
    )
    hidden_total[...] = total
    group[row] = total.astype(low)
    far_rows, near_rows, onward = row_copies([group.at[row]], [group], branch_send, branch_recv)
    far_rows[0].start()
    near_rows[0].start()
    values[0, 1:2] = jnp.sum(incoming * state * factor, axis=0, keepdims=True)

    load_shared.wait()
    shared_copy = remote(shared_parts.at[1 - core], core_near.at[1], row_sems, 4, (sibling, col))
    shared_copy.start()
    router_sum = row_sum_total(router_parts, router_near, router_far, router_copies)
    router_part[...] = router_sum.astype(low).reshape(router_part.shape)
    router_scatter = RouterSum(router_part, router.at[row], scratch[router_at:])
    router_scatter.start()
    shared_scatter.add_first()
    load_back.wait()
    near_rows[0].wait_recv()
    key_grad[...] = jnp.zeros_like(key_grad)
    value_grad[...] = jnp.zeros_like(value_grad)
    refs = (group, w_back, query, keys, values_in, norms, cosine, sine, begin, begin_row)
    sums = (back, pre_grad, bias, bias_t, deltas, key_grad, value_grad)
    chip = row // 2
    chip_rows = bias.shape[0]
    attention_back_rows(chip * chip_rows, refs, sums)
    shared_scatter.add_second()
    router_scatter.add_y()
    far_rows[0].wait_recv()
    onward[0].start()
    onward[0].wait_recv()

    def keep(target, block, rows):
        shaped = rows.astype(low).reshape(2, 4, 64, rows.shape[1])
        target[block // 2, 2 * (block % 2) : 2 * (block % 2) + 2] = shaped

    blocks, width = 4, group.shape[2] // 4
    for block in range(blocks):
        columns = slice(block * width, (block + 1) * width)
        rows = group[:, :, columns].reshape(4 * group.shape[1], width)
        keep(out_grads, block, outer_sum(rows, attended[...]))
    out_scatter.start()
    router_scatter.add_z()
    attention_back_rows((1 - chip) * chip_rows, refs, sums)
    size = keys.shape[1]
    scale = size ** (-0.5)
    pre_grad[:, inner : inner + size] = turn(key_grad[...] * scale, cosine[...], -sine[...]).astype(
        low
    )
    pre_grad[:, inner + size :] = value_grad[...].astype(low)
    load_pre.wait()
    load_rows.wait()
    block_rows = parts.shape[1]
    for block in range(4):
        rows = slice(block * block_rows, (block + 1) * block_rows)
        parts[block] = matmul_t(pre_grad[rows], w_pre[...]).astype(low)
    attn_copies = row_sum_copies(parts, near.at[0], far.at[0], outgoing.at[0], row_sems, 6)
    attn_copies[0].start()
    attn_copies[1].start()
    row_sum_forward(parts, near.at[0], outgoing.at[0], attn_copies)
    for block in range(blocks):
        rows = slice(block * width, (block + 1) * width)
        keep(pre_grads, block, matmul(rows_t[rows], pre_grad[...]))
    pre_scatter.start()
    router_scatter.add_x()
    out_scatter.add_first()
    shared_scatter.add_third([share_sums.at[0], share_sums.at[1]])
    share_low[0] = share_sums[1].astype(low)
    share_copy = remote(share_low.at[0], share_low.at[1], row_sems, 5, (partner, col))
    share_copy.start()
    router_scatter.spread_z()

    gain_sems = (gain_send, gain_recv)
    gain_copies = []
    stages = (row_peers, pre_scatter.y_peers, pre_scatter.z_peers, [pre_scatter.x_peer])

    def start_gains(stage):
        at = 3 * stage
        for i, peer in enumerate(stages[stage]):
            gain_copies.append(
                remote(values.at[stage], buffers.at[at + i], gain_sems, at + i, peer)
            )
            gain_copies[-1].start()

    def add_gains(stage):
        at = 3 * stage
        total = values[stage]
        for i in range(len(stages[stage])):
            gain_copies[at + i].wait_recv()
            total = total + buffers[at + i]
        values[stage + 1] = total

    incoming = row_sum_total(parts, near.at[0], far.at[0], attn_copies)
    first = inputs[...].astype(jnp.float32)
    factor = scale_one[...]
    weighted = gain_attn[...] * incoming
    mean = jnp.mean(weighted * first, axis=1, keepdims=True)
    result[...] = factor * weighted - first * (factor * factor * factor * mean)
    values[0, 0:1] = jnp.sum(incoming * first * factor, axis=0, keepdims=True)
    start_gains(0)
    router_scatter.spread_y()
    out_scatter.add_second()
    load_stream.wait()
    shared_copy.wait_recv()
    shared = shared_parts[core].astype(jnp.float32) + core_near[1].astype(jnp.float32)
    block_out[...] = (stream[...] + shared).astype(low)
    add_gains(0)
    start_gains(1)
    pre_scatter.add_first()
    router_scatter.wait(5)
    router_rows = row_copies([router.at[row]], [router], pass_send, pass_recv)
    router_rows[0][0].start()
    router_rows[1][0].start()
    out_scatter.add_third(pieces[2:3])
    add_gains(1)
    start_gains(2)
    pre_scatter.add_second()
    add_gains(2)
    start_gains(3)
    router_rows[0][0].wait_recv()
    router_rows[2][0].start()
    share_copy.wait_recv()
    share = share_sums[0] + share_low[1].astype(jnp.float32)
    pieces[3][...] = share[:, : pieces[3].shape[1]]
    pieces[4][...] = share[:, pieces[3].shape[1] :]
    pre_scatter.add_third(pieces[:2])
    add_gains(3)
    gain_attn_sum[...] = values[4, 0:1]
    gain_ffn_sum[...] = values[4, 1:2]

    router_scatter.end()
    far_rows[0].wait_send()
    near_rows[0].wait_send()
    onward[0].wait_send()
    router_rows[0][0].wait_send()
    router_rows[1][0].wait()
    router_rows[2][0].wait()
    for done in [*router_copies, *attn_copies, *gain_copies, input_copy, shared_copy, share_copy]:
        done.wait_send()
    for scatter in (shared_scatter, out_scatter, pre_scatter):
        scatter.end()


def tail(streamed, local, kept, tables, last, widths):
    space = pl.BlockSpec(memory_space=pltpu.VMEM)
    away = pl.BlockSpec(memory_space=pl.ANY)
    low = jnp.bfloat16
    packed, marks = streamed[:2]
    router_parts, shared_grads = local[3:]
    rows, width = last[0].shape
    tokens = 4 * rows
    _, router_rows, experts = router_parts.shape
    share = (router_rows // 32, experts)
    size = kept[1].shape[1]
    inner = kept[0].shape[1]
    pre_width = widths[0] + widths[1]
    shard = width // 32
    pre_grads = jax.ShapeDtypeStruct((2, 4, 4, shard, pre_width), low)
    out_grads = jax.ShapeDtypeStruct((2, 4, 4, shard, inner), low)
    dma = pltpu.SemaphoreType.DMA
    return pl.pallas_call(
        tail_kernel,
        out_shape=[
            jax.ShapeDtypeStruct((rows, width), jnp.float32),
            jax.ShapeDtypeStruct((rows, width), jnp.float32),
            jax.ShapeDtypeStruct((rows, width), low),
            jax.ShapeDtypeStruct((4, 2, 4, 4, *share), low),
            jax.ShapeDtypeStruct((1, width), jnp.float32),
            jax.ShapeDtypeStruct((1, width), jnp.float32),
        ]
        + [jax.ShapeDtypeStruct((shard, part), jnp.float32) for part in widths],
        in_specs=[away] * 10 + [space] * 17,
        out_specs=[space] * (6 + len(widths)),
        scratch_shapes=[
            pltpu.VMEM((4, packed.shape[0] // 4, packed.shape[1]), low),
            pltpu.VMEM(marks.shape, low),
            pltpu.VMEM((rows, width), jnp.float32),
            pltpu.VMEM((rows, width), jnp.float32),
            pltpu.VMEM((width, tokens), low),
            pltpu.VMEM((width, pre_width), low),
            pltpu.VMEM((width, inner), low),
            pltpu.VMEM((2, rows, width), low),
            pltpu.VMEM((rows, width), jnp.float32),
            pltpu.VMEM((rows, width), jnp.float32),
            pltpu.VMEM((4, rows, width), low),
            pltpu.VMEM((tokens, inner), low),
            pltpu.VMEM((tokens, pre_width), low),
            pltpu.VMEM((tokens // 2, tokens), jnp.float32),
            pltpu.VMEM((tokens, tokens // 2), jnp.float32),
            pltpu.VMEM((tokens // 2, 128), jnp.float32),
            pltpu.VMEM((tokens, size), jnp.float32),
            pltpu.VMEM((tokens, size), jnp.float32),
            pltpu.VMEM((4, rows, width), low),
            pltpu.VMEM((1, 2, rows, width), low),
            pltpu.VMEM((1, rows, width), low),
            pltpu.VMEM((1, rows, width), low),
            pltpu.VMEM((2, router_rows, experts), low),
            pltpu.VMEM((router_rows, experts), low),
            pltpu.VMEM((router_rows, experts), low),
            pltpu.VMEM((2, 4, 4, *share), low),
            pltpu.VMEM((5, 2, width), jnp.float32),
            pltpu.VMEM((10, 2, width), jnp.float32),
            pltpu.VMEM(pre_grads.shape, low),
            pltpu.VMEM(out_grads.shape, low),
            dma((13,)),
            dma((3,)),
            dma((3,)),
            dma((9,)),
            dma((9,)),
            dma((10,)),
            dma((10,)),
            dma((3,)),
            dma((3,)),
            pltpu.VMEM((2, rows, width), low),
            pltpu.VMEM((2, rows, width), low),
            pltpu.VMEM((2, shard, widths[3] + widths[4]), jnp.float32),
            pltpu.VMEM((2, shard, widths[3] + widths[4]), low),
            *ScatterSum.scratch(shared_grads),
            *ScatterSum.scratch(out_grads),
            *ScatterSum.scratch(pre_grads),
            *RouterSum.scratch(share),
        ],
        compiler_params=pltpu.CompilerParams(
            collective_id=16, has_side_effects=True, vmem_limit_bytes=60 << 20
        ),
        cost_estimate=pl.CostEstimate(flops=0, bytes_accessed=300 << 20, transcendentals=0),
        name="tail",
    )(*streamed, *local, *kept, *tables, *last)


def packed_places(shape, axis):
    index = lax.broadcasted_iota(jnp.int32, shape, axis)
    pair, place = index // PACKED_ROWS, lax.rem(index, PACKED_ROWS)
    found = []
    for part in range(-1, 3):
        if part < 0:
            valid, slot = place < PAIR_ROWS, place
        else:
            valid, slot = place >= PAIR_ROWS, 3 * (place - PAIR_ROWS) + part
        second = (slot >= EXPERT_ROWS).astype(jnp.int32)
        found.append((valid, pair, second, slot - EXPERT_ROWS * second))
    return found


def token_marks(code_block):
    marks = []
    wide = (BLOCK, BLOCK_EXPERTS)
    lanes = lax.broadcasted_iota(jnp.int32, wide, 1)
    for (valid, pair, second, _), (tall, _, _, order) in zip(
        packed_places(wide, 0), packed_places((BLOCK, SIDE), 0)
    ):
        owner = ((lanes == 2 * pair + second) & valid).astype(jnp.float32).astype(jnp.bfloat16)
        found = matmul(owner, code_block)
        hit = (found == order.astype(jnp.float32)) & tall
        marks.append((owner, hit.astype(jnp.float32)))
    return marks


def gate_weights_of(owner, hit, high, low):
    weights = hit * (matmul(owner, high) + matmul(owner, low))
    return split_low(weights)


def pack_tokens_kernel(code, values, high, low, packed):
    marks = token_marks(code[0])
    weights = [gate_weights_of(owner, hit, high[0], low[0]) for owner, hit in marks]
    last = values[:, 3 * QUARTER :]
    for part in range(3):
        columns = slice(part * QUARTER, (part + 1) * QUARTER)
        both = jnp.concatenate([*weights[0], *weights[part + 1]], axis=1)
        rows = jnp.concatenate([values[:, columns]] * 2 + [last] * 2, axis=0)
        packed[:, columns] = matmul(both, rows).astype(jnp.bfloat16)


def pack_tokens(code, values, gates):
    blocks = code.shape[0]
    width = 3 * QUARTER
    small = pl.BlockSpec((1, BLOCK_EXPERTS, SIDE), lambda i: (i, 0, 0))
    return pl.pallas_call(
        pack_tokens_kernel,
        grid=(blocks,),
        out_shape=jax.ShapeDtypeStruct((blocks * BLOCK, width), jnp.bfloat16),
        in_specs=[small, pl.BlockSpec(values.shape, lambda i: (0, 0)), small, small],
        out_specs=pl.BlockSpec((BLOCK, width), lambda i: (i, 0)),
        compiler_params=pltpu.CompilerParams(vmem_limit_bytes=32 << 20),
        cost_estimate=pl.CostEstimate(
            flops=blocks * BLOCK * 512 * width * 2, bytes_accessed=8 << 20, transcendentals=0
        ),
        name="pack_tokens",
    )(code, values, *gates)


def slot_marks():
    shape = (2 * BLOCK_SLOTS, BLOCK)
    rows = lax.broadcasted_iota(jnp.int32, shape, 0)
    marks = []
    for valid, pair, second, order in packed_places(shape, 1):
        hit = (rows == second * BLOCK_SLOTS + pair * EXPERT_ROWS + order) & valid
        marks.append(hit.astype(jnp.float32).astype(jnp.bfloat16))
    return marks


def unpack_slots_kernel(packed, values):
    marks = slot_marks()
    last = jnp.zeros((2 * BLOCK_SLOTS, QUARTER), jnp.float32)
    for part in range(3):
        columns = slice(part * QUARTER, (part + 1) * QUARTER)
        found = matmul(marks[0], packed[:, columns]).astype(jnp.bfloat16)
        values[0, :, columns] = found[:BLOCK_SLOTS]
        values[1, :, columns] = found[BLOCK_SLOTS:]
        last = last + matmul(marks[part + 1], packed[:, columns])
    last = last.astype(jnp.bfloat16)
    values[0, :, 3 * QUARTER :] = last[:BLOCK_SLOTS]
    values[1, :, 3 * QUARTER :] = last[BLOCK_SLOTS:]


def unpack_slots(packed):
    blocks = packed.shape[0] // BLOCK
    slots = blocks * BLOCK_SLOTS
    return pl.pallas_call(
        unpack_slots_kernel,
        grid=(blocks,),
        out_shape=jax.ShapeDtypeStruct((2, slots, 4 * QUARTER), jnp.bfloat16),
        in_specs=[pl.BlockSpec((BLOCK, 3 * QUARTER), lambda i: (i, 0))],
        out_specs=pl.BlockSpec((2, BLOCK_SLOTS, 4 * QUARTER), lambda i: (0, i, 0)),
        compiler_params=pltpu.CompilerParams(vmem_limit_bytes=32 << 20),
        cost_estimate=pl.CostEstimate(
            flops=blocks * 2 * BLOCK_SLOTS * BLOCK * 6 * QUARTER * 2,
            bytes_accessed=14 << 20,
            transcendentals=0,
        ),
        name="unpack_slots",
    )(packed)


def pack_slots_kernel(values, packed):
    marks = slot_marks()
    last = jnp.concatenate([values[0, :, 3 * QUARTER :], values[1, :, 3 * QUARTER :]], axis=0)
    for part in range(3):
        columns = slice(part * QUARTER, (part + 1) * QUARTER)
        rows = jnp.concatenate([values[0, :, columns], values[1, :, columns]], axis=0)
        found = outer_sum(marks[0], rows) + outer_sum(marks[part + 1], last)
        packed[:, columns] = found.astype(jnp.bfloat16)


def pack_slots(values):
    slots = values.shape[1]
    blocks = slots // BLOCK_SLOTS
    return pl.pallas_call(
        pack_slots_kernel,
        grid=(blocks,),
        out_shape=jax.ShapeDtypeStruct((blocks * BLOCK, 3 * QUARTER), jnp.bfloat16),
        in_specs=[pl.BlockSpec((2, BLOCK_SLOTS, 4 * QUARTER), lambda i: (0, i, 0))],
        out_specs=pl.BlockSpec((BLOCK, 3 * QUARTER), lambda i: (i, 0)),
        compiler_params=pltpu.CompilerParams(vmem_limit_bytes=32 << 20),
        cost_estimate=pl.CostEstimate(
            flops=blocks * 2 * BLOCK_SLOTS * BLOCK * 6 * QUARTER * 2,
            bytes_accessed=14 << 20,
            transcendentals=0,
        ),
        name="pack_slots",
    )(values)


def marks_kernel(code, marks):
    wide = (BLOCK_EXPERTS, BLOCK)
    owners = lax.broadcasted_iota(jnp.int32, wide, 0)
    for i, ((valid, pair, second, _), (tall, _, _, order)) in enumerate(
        zip(packed_places(wide, 1), packed_places((code.shape[1], BLOCK), 1))
    ):
        owner = ((owners == 2 * pair + second) & valid).astype(jnp.float32).astype(jnp.bfloat16)
        hit = (matmul(code[0], owner) == order.astype(jnp.float32)) & tall
        marks[i] = hit.astype(jnp.float32).astype(jnp.bfloat16)


def all_marks(code):
    blocks, experts, tokens = code.shape
    return pl.pallas_call(
        marks_kernel,
        grid=(blocks,),
        out_shape=jax.ShapeDtypeStruct((4, tokens, blocks * BLOCK), jnp.bfloat16),
        in_specs=[pl.BlockSpec((1, tokens, experts), lambda i: (i, 0, 0))],
        out_specs=pl.BlockSpec((4, tokens, BLOCK), lambda i: (0, 0, i)),
        cost_estimate=pl.CostEstimate(flops=1 << 26, bytes_accessed=4 << 20, transcendentals=0),
        name="all_marks",
    )(code.transpose(0, 2, 1))


def sum_gated_kernel(code, packed, grads, high, low, total, gate_grads):
    @pl.when(pl.program_id(0) == 0)
    def _():
        total[...] = jnp.zeros_like(total)

    marks = token_marks(code[0])
    weights = [gate_weights_of(owner, hit, high[0], low[0]) for owner, hit in marks]
    last = jnp.zeros((total.shape[0], QUARTER), jnp.float32)
    whole = jnp.zeros((BLOCK, 1), jnp.float32)
    products = []
    for part in range(3):
        columns = slice(part * QUARTER, (part + 1) * QUARTER)
        rows = packed[:, columns]
        total[:, columns] += outer_sum(weights[0][0], rows) + outer_sum(weights[0][1], rows)
        last = last + outer_sum(weights[part + 1][0], rows) + outer_sum(weights[part + 1][1], rows)
        dots = jnp.sum(
            rows.astype(jnp.float32) * grads[:, columns].astype(jnp.float32),
            axis=1,
            keepdims=True,
        )
        whole = whole + dots
        products.append(dots)
    total[:, 3 * QUARTER :] += last
    found = jnp.zeros(gate_grads.shape[1:], jnp.float32)
    for (owner, hit), dots in zip(marks, [whole, *products]):
        hit = hit.astype(jnp.bfloat16)
        for spread in split_low(dots * owner.astype(jnp.float32)):
            found = found + outer_sum(hit, spread)
    gate_grads[0] = found


def sum_gated(code, packed, grads, gates):
    blocks, _, tokens = code.shape
    small = pl.BlockSpec((1, BLOCK_EXPERTS, tokens), lambda i: (i, 0, 0))
    wide = pl.BlockSpec((BLOCK, 3 * QUARTER), lambda i: (i, 0))
    return pl.pallas_call(
        sum_gated_kernel,
        grid=(blocks,),
        out_shape=[
            jax.ShapeDtypeStruct((tokens, 4 * QUARTER), jnp.float32),
            jax.ShapeDtypeStruct((blocks, tokens, BLOCK_EXPERTS), jnp.float32),
        ],
        in_specs=[small, wide, wide, small, small],
        out_specs=[
            pl.BlockSpec((tokens, 4 * QUARTER), lambda i: (0, 0)),
            pl.BlockSpec((1, tokens, BLOCK_EXPERTS), lambda i: (i, 0, 0)),
        ],
        compiler_params=pltpu.CompilerParams(vmem_limit_bytes=32 << 20),
        cost_estimate=pl.CostEstimate(
            flops=blocks * BLOCK * 128 * 12 * QUARTER * 2,
            bytes_accessed=14 << 20,
            transcendentals=0,
        ),
        name="sum_gated",
    )(code, packed, grads, *gates)


class Gather:
    def __init__(self, mine, full, send_sem, recv_sem):
        self.mine, self.full = mine, full
        self.sems = (send_sem, recv_sem)
        row, col = lax.axis_index("row"), lax.axis_index("col")
        x, z, y = col // 16, lax.rem(col // 4, 4), lax.rem(col, 4)
        self.place = (x, z, y)
        self.z_peers = [(row, x * 16 + lax.rem(z + i, 4) * 4 + y) for i in (1, 3, 2)]
        self.y_peers = [(row, x * 16 + z * 4 + lax.rem(y + i, 4)) for i in (1, 3, 2)]
        self.x_peer = (row, (1 - x) * 16 + z * 4 + y)
        self.copies = {}

    def rows(self, half):
        half_rows = self.full.shape[3] // 2
        return pl.ds(half * half_rows, half_rows)

    def send(self, key, source, target, peers):
        at = 1 + 3 * len(self.copies) - 3 if self.copies else 0
        copies = [
            remote(source, target, self.sems, at + i, peer) for i, peer in enumerate(peers)
        ]
        for copy in copies:
            copy.start()
        self.copies[key] = copies

    def wait(self, *keys):
        for key in keys:
            for copy in self.copies[key]:
                copy.wait_recv()

    def start(self):
        x, z, y = self.place
        self.send("x", self.mine, self.full.at[x, z, y], [self.x_peer])
        for half, peers in enumerate((self.z_peers, self.y_peers)):
            rows = self.rows(half)
            target = self.full.at[x, z, y, rows]
            self.send((0, half), self.mine.at[rows], target, peers)

    def second(self):
        x, z, y = self.place
        self.wait("x")
        for half, peers in enumerate((self.z_peers, self.y_peers)):
            target = self.full.at[1 - x, z, y, self.rows(half)]
            self.send((1, half), target, target, peers)

    def third(self):
        x, z, y = self.place
        for turn, owner_x in enumerate((x, 1 - x)):
            self.wait((turn, 0))
            target = self.full.at[owner_x, :, y, self.rows(0)]
            self.send((2 + turn, 0), target, target, self.y_peers)
            self.wait((turn, 1))
            target = self.full.at[owner_x, z, :, self.rows(1)]
            self.send((2 + turn, 1), target, target, self.z_peers)

    def await_all(self):
        self.wait((2, 0), (2, 1), (3, 0), (3, 1))

    def end(self):
        for copies in self.copies.values():
            for copy in copies:
                copy.wait_send()


def head_kernel(
    inputs,
    gain_attn,
    gain_ffn,
    grads,
    lengths,
    routes,
    frequency,
    w_query,
    w_keyval,
    w_out,
    w_shared_in,
    w_shared_out,
    full_pre,
    full_back,
    full_shared,
    group_one,
    chip_grad,
    chip_two,
    scale_one,
    cosine,
    sine,
    begin,
    begin_row,
    query,
    keys,
    values,
    attended,
    norms,
    hidden,
    normed_two,
    scale_two,
    packed,
    code,
    order,
    *scratch,
):
    mine_pre, mine_back, mine_shared, normed, rows, w_pre, w_back, pre, bias, parts = scratch[:10]
    near, far, outgoing, marks, staged = scratch[10:15]
    gather_send, gather_recv, own_sem, row_send, row_recv = scratch[15:20]
    sum_send, sum_recv, chip_send, chip_recv, load_sem, pack_sem = scratch[20:]
    low = jnp.bfloat16
    row, col, sibling, partner, _ = row_places()
    gathers = [
        Gather(mine_pre, full_pre, gather_send.at[0], gather_recv.at[0]),
        Gather(mine_back, full_back, gather_send.at[1], gather_recv.at[1]),
        Gather(mine_shared, full_shared, gather_send.at[2], gather_recv.at[2]),
    ]
    place = gathers[0].place
    greet(gathers[0].z_peers + gathers[0].y_peers + [gathers[0].x_peer])
    greet([(sibling, col), (partner, col)])
    pairs = ((mine_pre, (w_query, w_keyval)), (mine_shared, (w_shared_in, w_shared_out)))
    for mine, shards in pairs:
        start = 0
        for shard in shards:
            mine[:, start : start + shard.shape[1]] = shard[...]
            start += shard.shape[1]
    mine_back[...] = w_out[...]
    first = inputs[...].astype(jnp.float32)
    factor = lax.rsqrt(jnp.mean(first * first, axis=1, keepdims=True) + epsilon)
    scale_one[...] = factor
    normed[...] = (first * factor * gain_attn[...]).astype(low)
    core = lax.rem(row, 2)
    own = [
        pltpu.make_async_copy(normed, group_one.at[row], own_sem.at[0]),
        pltpu.make_async_copy(grads, chip_grad.at[core], own_sem.at[1]),
        pltpu.make_async_copy(mine_pre, full_pre.at[place], own_sem.at[2]),
        pltpu.make_async_copy(mine_back, full_back.at[place], own_sem.at[3]),
        pltpu.make_async_copy(mine_shared, full_shared.at[place], own_sem.at[4]),
        pltpu.make_async_copy(normed_two, chip_two.at[core], own_sem.at[5]),
    ]
    for copy in own[:4]:
        copy.start()
    await_greetings(9)
    far_rows, near_rows, onward = row_copies([normed], [group_one], row_send, row_recv)
    chip_sems = (chip_send, chip_recv)
    share = mine_shared.shape[1] // 2
    other_shard = remote(
        mine_shared.at[:, pl.ds(0, share)],
        mine_shared.at[:, pl.ds(share, share)],
        chip_sems,
        0,
        (partner, col),
    )
    near_grads = remote(grads, chip_grad.at[core], chip_sems, 1, (sibling, col))
    near_two = remote(normed_two, chip_two.at[core], chip_sems, 2, (sibling, col))
    other_shard.start()
    gathers[0].start()
    far_rows[0].start()
    near_rows[0].start()
    gathers[1].start()
    gathers[0].second()
    gathers[1].second()
    for copy in own[2:4]:
        copy.wait()
    gathers[0].third()
    near_grads.start()
    gathers[1].third()
    other_shard.wait_recv()
    own[4].start()
    gathers[2].start()

    tokens = begin.shape[0]

    def document_starts(axis, shape):
        places = lax.broadcasted_iota(jnp.int32, shape, axis)
        found = jnp.zeros(shape, jnp.int32)
        bound = 0
        for i in range(NDOC - 1):
            bound = bound + lengths[0, i]
            found = jnp.where(places >= bound, bound, found)
        return places, found

    begin_row[...] = document_starts(1, begin_row.shape)[1]
    places, starts = document_starts(0, cosine.shape)
    begin[...] = starts[:, :1]
    angles = (places - starts).astype(jnp.float32) * frequency[...]
    lanes = lax.broadcasted_iota(jnp.int32, cosine.shape, 1)
    cosine[...] = jnp.cos(angles)
    sine[...] = jnp.where(lanes < cosine.shape[1] // 2, -1.0, 1.0) * jnp.sin(angles)
    bias[...] = score_bias(begin[...])

    experts = lax.broadcasted_iota(jnp.int32, order.shape, 1)
    chosen = jnp.zeros(order.shape, jnp.float32)
    for k in range(routes.shape[1]):
        chosen = jnp.where(routes[:, k : k + 1] == experts, 1.0, chosen)
    square = (order.shape[0], order.shape[0])
    before = lax.broadcasted_iota(jnp.int32, square, 1) < lax.broadcasted_iota(
        jnp.int32, square, 0
    )
    ahead = matmul(before.astype(jnp.float32).astype(low), chosen.astype(low))
    order[...] = jnp.where(chosen > 0.0, ahead, -1.0)
    code[...] = jnp.transpose(order[...]).astype(low).reshape(code.shape)

    def mark(block, carry):
        found = token_marks(code[block])
        for part in range(3):
            marks[block, part] = jnp.concatenate(
                [found[0][1].astype(low), found[part + 1][1].astype(low)], axis=1
            )
        return carry

    lax.fori_loop(0, code.shape[0], mark, 0)

    far_rows[0].wait_recv()
    onward[0].start()
    gathers[0].await_all()
    own[0].wait()
    near_rows[0].wait_recv()
    onward[0].wait_recv()
    loads = [
        pltpu.make_async_copy(group_one, rows, load_sem.at[0]),
        pltpu.make_async_copy(full_pre, w_pre, load_sem.at[1]),
        pltpu.make_async_copy(full_back, w_back, load_sem.at[2]),
    ]
    loads[0].start()
    loads[1].start()
    loads[0].wait()
    loads[1].wait()
    width = inputs.shape[1]
    pre[...] = matmul(
        rows[...].reshape(tokens, width), w_pre[...].reshape(width, w_pre.shape[4])
    )
    size = keys.shape[1]
    inner = query.shape[1]
    keys[...] = turn(pre[:, inner : inner + size], cosine[...], sine[...]).astype(low)
    values[...] = pre[:, inner + size :].astype(low)
    log_totals = jnp.zeros(norms.shape, jnp.float32)
    for head in range(inner // size):
        columns = slice(head * size, (head + 1) * size)
        turned = turn(pre[:, columns], cosine[...], sine[...]).astype(low)
        query[:, columns] = turned
        scores = matmul_t(turned, keys[...]) * (size ** (-0.5)) + bias[...]
        highest = jnp.max(scores, axis=1, keepdims=True)
        weights = jnp.exp(scores - highest)
        total = jnp.sum(weights, axis=1, keepdims=True)
        weights = (weights * (1.0 / total)).astype(low)
        attended[:, columns] = matmul(weights, values[...]).astype(low)
        log_totals = jnp.where(lanes == head, highest + jnp.log(total), log_totals)
    norms[...] = log_totals
    gathers[1].await_all()
    loads[2].start()
    loads[2].wait()
    parts[...] = (
        matmul_t(attended[...], w_back[...].reshape(width, inner)).astype(low).reshape(parts.shape)
    )

    copies = row_sum_copies(parts, near, far, outgoing, (sum_send, sum_recv), 0)
    copies[0].start()
    copies[1].start()
    gathers[2].second()
    row_sum_forward(parts, near, outgoing, copies)
    own[4].wait()
    gathers[2].third()
    total = inputs[...].astype(jnp.float32) + row_sum_total(parts, near, far, copies)
    hidden[...] = total
    factor = lax.rsqrt(jnp.mean(total * total, axis=1, keepdims=True) + epsilon)
    normed_two[...] = (total * factor * gain_ffn[...]).astype(low)
    scale_two[...] = factor
    near_two.start()
    own[5].start()

    def pack(block, carry):
        last = normed_two[:, 3 * QUARTER :]
        for part in range(3):
            columns = slice(part * QUARTER, (part + 1) * QUARTER)
            both = jnp.concatenate([normed_two[:, columns], last], axis=0)
            staged[block, :, columns] = matmul(marks[block, part], both).astype(low)
        target = packed.at[pl.ds(pl.multiple_of(block * BLOCK, BLOCK), BLOCK)]
        pltpu.make_async_copy(staged.at[block], target, pack_sem.at[block]).start()
        return carry

    lax.fori_loop(0, code.shape[0], pack, 0)

    gathers[2].await_all()
    own[1].wait()
    own[5].wait()
    near_grads.wait()
    near_two.wait()
    other_shard.wait_send()
    near_rows[0].wait_send()
    onward[0].wait_send()
    for copy in far_rows + copies:
        copy.wait_send()
    for gather in gathers:
        gather.end()
    for block in range(staged.shape[0]):
        target = packed.at[pl.ds(block * BLOCK, BLOCK)]
        pltpu.make_async_copy(staged.at[block], target, pack_sem.at[block]).wait()


def head(inputs, gain_attn, gain_ffn, grads, lengths, routes, shards, size, expert_count):
    space = pl.BlockSpec(memory_space=pltpu.VMEM)
    away = pl.BlockSpec(memory_space=pl.ANY)
    low = jnp.bfloat16
    rows, width = inputs.shape
    tokens = 4 * rows
    shard_rows = shards[0].shape[0]
    inner = shards[0].shape[1]
    pre_width = inner + shards[1].shape[1]
    shared_width = shards[3].shape[1] + shards[4].shape[1]
    blocks = expert_count // BLOCK_EXPERTS
    spread = np.arange(size // 2, dtype=np.float32) * np.float32(2.0 / size)
    frequency = np.float32(rope_base) ** (-spread)
    frequency = jnp.asarray(np.concatenate([frequency, frequency])[None], jnp.float32)

    def full(shape, dtype):
        return jax.ShapeDtypeStruct(shape, dtype)

    return pl.pallas_call(
        head_kernel,
        out_shape=[
            full((2, 4, 4, shard_rows, pre_width), low),
            full((2, 4, 4, shard_rows, inner), low),
            full((2, 4, 4, shard_rows, 2 * shared_width), low),
            full((4, rows, width), low),
            full((2, rows, width), low),
            full((2, rows, width), low),
            full((rows, 1), jnp.float32),
            full((tokens, size), jnp.float32),
            full((tokens, size), jnp.float32),
            full((tokens, 1), jnp.int32),
            full((1, tokens), jnp.int32),
            full((tokens, inner), low),
            full((tokens, size), low),
            full((tokens, size), low),
            full((tokens, inner), low),
            full((tokens, size), jnp.float32),
            full((rows, width), jnp.float32),
            full((rows, width), low),
            full((rows, 1), jnp.float32),
            full((blocks * BLOCK, 3 * QUARTER), low),
            full((blocks, BLOCK_EXPERTS, rows), low),
            full((rows, expert_count), jnp.float32),
        ],
        in_specs=[space] * 3
        + [away, pl.BlockSpec(memory_space=pltpu.SMEM)]
        + [space] * (2 + len(shards)),
        out_specs=[away] * 6 + [space] * 13 + [away] + [space] * 2,
        scratch_shapes=[
            pltpu.VMEM((shard_rows, pre_width), low),
            pltpu.VMEM((shard_rows, inner), low),
            pltpu.VMEM((shard_rows, 2 * shared_width), low),
            pltpu.VMEM((rows, width), low),
            pltpu.VMEM((4, rows, width), low),
            pltpu.VMEM((2, 4, 4, shard_rows, pre_width), low),
            pltpu.VMEM((2, 4, 4, shard_rows, inner), low),
            pltpu.VMEM((tokens, pre_width), jnp.float32),
            pltpu.VMEM((tokens, tokens), jnp.float32),
            pltpu.VMEM((4, rows, width), low),
            pltpu.VMEM((2, rows, width), low),
            pltpu.VMEM((rows, width), low),
            pltpu.VMEM((rows, width), low),
            pltpu.VMEM((blocks, 3, BLOCK, 2 * rows), low),
            pltpu.VMEM((blocks, BLOCK, 3 * QUARTER), low),
            pltpu.SemaphoreType.DMA((3, 25)),
            pltpu.SemaphoreType.DMA((3, 25)),
            pltpu.SemaphoreType.DMA((6,)),
            pltpu.SemaphoreType.DMA((3,)),
            pltpu.SemaphoreType.DMA((3,)),
            pltpu.SemaphoreType.DMA((3,)),
            pltpu.SemaphoreType.DMA((3,)),
            pltpu.SemaphoreType.DMA((3,)),
            pltpu.SemaphoreType.DMA((3,)),
            pltpu.SemaphoreType.DMA((3,)),
            pltpu.SemaphoreType.DMA((blocks,)),
        ],
        compiler_params=pltpu.CompilerParams(
            collective_id=0, has_side_effects=True, vmem_limit_bytes=60 << 20
        ),
        cost_estimate=pl.CostEstimate(flops=0, bytes_accessed=300 << 20, transcendentals=0),
        name="head",
    )(inputs, gain_attn, gain_ffn, grads, lengths, routes, frequency, *shards)


def side_by_side_kernel(*refs):
    both, start = refs[-1], 0
    for part in refs[:-1]:
        both[:, start : start + part.shape[1]] = part[...]
        start += part.shape[1]


def side_by_side(*parts):
    shape = (parts[0].shape[0], sum(part.shape[1] for part in parts))
    return pl.pallas_call(
        side_by_side_kernel,
        out_shape=jax.ShapeDtypeStruct(shape, parts[0].dtype),
        cost_estimate=pl.CostEstimate(flops=0, bytes_accessed=6 << 20, transcendentals=0),
        name="side_by_side",
    )(*parts)


def exchange(packed):
    pairs = packed.reshape(-1, PACKED_ROWS, packed.shape[1])
    swapped = lax.all_to_all(pairs, ("row", "col"), split_axis=0, concat_axis=0, tiled=True)
    return swapped.reshape(packed.shape)


def per_device(
    block_in,
    gain_attn,
    w_query,
    w_keyval,
    w_out,
    gain_ffn,
    w_shared_in,
    w_shared_out,
    w_router,
    w_expert_in,
    w_expert_out,
    doc_lengths,
    routes,
    cotangent,
):
    row_count = lax.axis_size("row")
    rows_dev = block_in.shape[1]
    model_width = block_in.shape[2]
    expert_count = w_router.shape[1]
    expert_ff = w_expert_out.shape[2]
    inputs = block_in.reshape(rows_dev, model_width)
    grad_low = cotangent.reshape(rows_dev, model_width)
    shards = [w_query, w_keyval, w_out, w_shared_in, w_shared_out]
    shards = [part.reshape(part.shape[0], -1) for part in shards]
    (
        full_pre,
        full_back,
        full_shared,
        group_one,
        chip_grad,
        chip_two,
        scale_one,
        cosine,
        sine_table,
        begin,
        begin_row,
        *kept,
        hidden_state,
        normed_two,
        scale_two,
        send_rows,
        code,
        order,
    ) = head(
        inputs,
        gain_attn[None],
        gain_ffn[None],
        grad_low,
        doc_lengths,
        routes.reshape(rows_dev, -1),
        shards,
        w_keyval.shape[2] // 2,
        expert_count,
    )
    full_pre, full_back, full_shared, group_one, chip_grad, chip_two = (
        part.reshape(-1, part.shape[-1])
        for part in (full_pre, full_back, full_shared, group_one, chip_grad, chip_two)
    )
    received = exchange(send_rows)
    logits = matmul(normed_two, w_router)
    scores_sig = jnp.where(order >= 0.0, jax.nn.sigmoid(logits), 0.0)
    score_sum = jnp.sum(scores_sig, axis=1, keepdims=True)
    gate_weights = scores_sig / score_sum
    gates = [
        part.T.reshape(-1, BLOCK_EXPERTS, rows_dev) for part in split_low(gate_weights)
    ]
    send_grads, received = lax.optimization_barrier((pack_tokens(code, grad_low, gates), received))
    received_grads = exchange(send_grads)

    shared_width = w_shared_out.shape[1]
    shared_grads, shared_parts, shared_input = [], 0.0, 0.0
    for start in (0, 3 * shared_width):
        in_weights = full_shared[:, start : start + 2 * shared_width]
        out_weights = full_shared[:, start + 2 * shared_width : start + 3 * shared_width]
        shared_pre = matmul(chip_two, in_weights)
        shared_gate, shared_up = shared_pre[:, :shared_width], shared_pre[:, shared_width:]
        shared_act, shared_slope = swish_parts(shared_gate)
        shared_hidden = (shared_act * shared_up).astype(jnp.bfloat16)
        shared_hidden_grad = matmul(chip_grad, out_weights)
        shared_pre_grad = jnp.concatenate(
            [shared_hidden_grad * shared_up * shared_slope, shared_hidden_grad * shared_act],
            axis=1,
        ).astype(jnp.bfloat16)
        shared_grads.append(outer_sum(chip_two, shared_pre_grad).astype(jnp.bfloat16))
        shared_grads.append(outer_sum(chip_grad, shared_hidden).astype(jnp.bfloat16))
        shared_parts = shared_parts + matmul_t(shared_hidden, out_weights)
        shared_input = shared_input + matmul_t(shared_pre_grad, in_weights)
    shared_grads = side_by_side(*shared_grads)
    shared_parts, shared_input = (
        part.astype(jnp.bfloat16).reshape(2, rows_dev, model_width)
        for part in (shared_parts, shared_input)
    )

    expert_in = unpack_slots(received)
    expert_pre = jnp.einsum(
        "esd,edf->esf", expert_in, w_expert_in, preferred_element_type=jnp.float32
    )
    expert_act, expert_slope = swish_parts(expert_pre[..., :expert_ff])
    expert_hidden = (expert_act * expert_pre[..., expert_ff:]).astype(jnp.bfloat16)
    expert_out = jnp.einsum(
        "esf,edf->esd", expert_hidden, w_expert_out, preferred_element_type=jnp.float32
    ).astype(jnp.bfloat16)
    send_out, received_grads = lax.optimization_barrier((pack_slots(expert_out), received_grads))
    returned = exchange(send_out)

    out_grad = unpack_slots(received_grads)
    hidden_grad = jnp.einsum(
        "esd,edf->esf", out_grad, w_expert_out, preferred_element_type=jnp.float32
    )
    expert_pre_grad = jnp.concatenate(
        [hidden_grad * expert_pre[..., expert_ff:] * expert_slope, hidden_grad * expert_act], axis=2
    ).astype(jnp.bfloat16)
    slot_grad = jnp.einsum(
        "esf,edf->esd", expert_pre_grad, w_expert_in, preferred_element_type=jnp.float32
    ).astype(jnp.bfloat16)
    send_back, returned = lax.optimization_barrier((pack_slots(slot_grad), returned))
    returned_grad = exchange(send_back)
    grad_expert_out = jnp.einsum(
        "esd,esf->edf", out_grad, expert_hidden, preferred_element_type=jnp.float32
    )
    grad_expert_in = jnp.einsum(
        "esd,esf->edf", expert_in, expert_pre_grad, preferred_element_type=jnp.float32
    )
    routed_branch, gate_grads = sum_gated(code, returned, send_grads, gates)
    stream = hidden_state + routed_branch
    gate_grads = gate_grads.transpose(1, 0, 2).reshape(rows_dev, expert_count)
    logit_grad = (
        (1.0 - scores_sig)
        * (gate_grads - gate_weights * jnp.sum(gate_grads, axis=1, keepdims=True))
    ).astype(jnp.bfloat16)
    router_parts = outer_sum(normed_two, logit_grad).astype(jnp.bfloat16)
    router_parts = router_parts.reshape(row_count, -1, expert_count)
    router_input = matmul_t(logit_grad, w_router)
    shadowed = (router_input, router_parts, stream, shared_grads, group_one.T, all_marks(code))
    returned_grad, shadowed, grad_expert_in, grad_expert_out = lax.optimization_barrier(
        (returned_grad, shadowed, grad_expert_in, grad_expert_out)
    )
    router_input, router_parts, stream, shared_grads, group_one_t, marks = shadowed

    widths = [part.shape[1] for part in shards]
    hidden_total, input_back, block_out, router_sum, gain_attn_sum, gain_ffn_sum, *sums = tail(
        (
            returned_grad,
            marks,
            router_input,
            hidden_state,
            group_one_t,
            full_pre,
            full_back,
            shared_parts,
            stream,
            shared_input,
        ),
        (
            scale_two,
            gain_ffn[None],
            grad_low,
            router_parts,
            shared_grads.reshape(2, 4, 4, -1, shared_grads.shape[1]),
        ),
        kept,
        (cosine, sine_table, begin, begin_row),
        (inputs, scale_one, gain_attn[None]),
        widths,
    )
    sums = [
        part.reshape(like.shape)
        for part, like in zip(sums, (w_query, w_keyval, w_out, w_shared_in, w_shared_out))
    ]
    return (
        block_out.reshape(1, rows_dev, model_width),
        (hidden_total + input_back).reshape(1, rows_dev, model_width),
        gain_attn_sum[0],
        sums[0],
        sums[1],
        sums[2],
        gain_ffn_sum[0],
        sums[3],
        sums[4],
        router_sum.reshape(model_width, expert_count).astype(jnp.float32),
        grad_expert_in,
        grad_expert_out,
    )


def solution(mesh):
    in_specs = (
        P("col", "row", None),
        P(),
        P("col", "row"),
        P("col", "row", None),
        P("col", "row"),
        P(),
        P("col", None, "row"),
        P("col", "row"),
        P(),
        P(("row", "col"), None, None),
        P(("row", "col"), None, None),
        P("col", None),
        P("col", "row", None),
        P("col", "row", None),
    )
    out_specs = (
        P("col", "row", None),
        P("col", "row", None),
        P(),
        P("col", "row"),
        P("col", "row", None),
        P("col", "row"),
        P(),
        P("col", None, "row"),
        P("col", "row"),
        P(),
        P(("row", "col"), None, None),
        P(("row", "col"), None, None),
    )
    return jax.shard_map(
        per_device, mesh=mesh, in_specs=in_specs, out_specs=out_specs, check_vma=False
    )
```

```python
import functools

import jax
import jax.numpy as jnp
import numpy as np
from jax import lax
from jax.experimental import pallas as pl
from jax.experimental.pallas import tpu as pltpu
from jax.sharding import PartitionSpec as P

epsilon = 1e-06
rope_base = 10000.0
masked_score = -1e30

EXPERT_ROWS = 6
PAIR_ROWS = 12
PACKED_ROWS = 16
BLOCK_PAIRS = 16
BLOCK = BLOCK_PAIRS * PACKED_ROWS
BLOCK_EXPERTS = 2 * BLOCK_PAIRS
BLOCK_SLOTS = BLOCK_PAIRS * EXPERT_ROWS
QUARTER = 512
SIDE = 128
MESH = pl.DeviceIdType.MESH
NDOC = 4


def swish_parts(pre_act):
    logistic = jax.nn.sigmoid(pre_act)
    return (pre_act * logistic, logistic * (1.0 + pre_act * (1.0 - logistic)))


def matmul(matrix, partner):
    return jnp.dot(matrix, partner, preferred_element_type=jnp.float32)


def matmul_t(matrix, partner):
    return lax.dot_general(
        matrix, partner, (((1,), (1,)), ((), ())), preferred_element_type=jnp.float32
    )


def outer_sum(matrix, partner):
    return lax.dot_general(
        matrix, partner, (((0,), (0,)), ((), ())), preferred_element_type=jnp.float32
    )


def split_low(values):
    high = values.astype(jnp.bfloat16)
    return high, (values - high.astype(jnp.float32)).astype(jnp.bfloat16)


def row_places():
    row, col = lax.axis_index("row"), lax.axis_index("col")
    chip, core = row // 2, lax.rem(row, 2)
    sibling = chip * 2 + (1 - core)
    partner = (1 - chip) * 2 + core
    across = (1 - chip) * 2 + (1 - core)
    return row, col, sibling, partner, across


def row_copies(sources, targets, send_sem, recv_sem):
    row, col, sibling, partner, _ = row_places()

    def send(origin, target, peer, i):
        return pltpu.make_async_remote_copy(
            src_ref=origin,
            dst_ref=target,
            send_sem=send_sem.at[i],
            recv_sem=recv_sem.at[i],
            device_id=(peer, col),
            device_id_type=MESH,
        )

    far, near, onward = [], [], []
    for i, (source, target) in enumerate(zip(sources, targets)):
        far.append(send(source, target.at[row], partner, 3 * i))
        near.append(send(source, target.at[row], sibling, 3 * i + 1))
        onward.append(send(target.at[partner], target.at[partner], sibling, 3 * i + 2))
    return far, near, onward


def greet(peers):
    barrier = pltpu.get_barrier_semaphore()
    for peer in peers:
        pl.semaphore_signal(barrier, inc=1, device_id=peer, device_id_type=MESH)


def await_greetings(count):
    pl.semaphore_wait(pltpu.get_barrier_semaphore(), count)


def turn(values, cosine, sine):
    return values * cosine + pltpu.roll(values, 64, 1) * sine


def score_bias(begin):
    shape = (begin.shape[0], begin.shape[0])
    keys = lax.broadcasted_iota(jnp.int32, shape, 1)
    allowed = (keys >= begin) & (keys <= lax.broadcasted_iota(jnp.int32, shape, 0))
    return jnp.where(allowed, 0.0, masked_score)


def remote(source, target, sems, at, peer):
    return pltpu.make_async_remote_copy(
        src_ref=source,
        dst_ref=target,
        send_sem=sems[0].at[at],
        recv_sem=sems[1].at[at],
        device_id=peer,
        device_id_type=MESH,
    )


def row_sum_copies(parts, near, far, outgoing, sems, at):
    _, col, sibling, partner, across = row_places()
    return [
        remote(parts.at[across], near.at[0], sems, at, (sibling, col)),
        remote(parts.at[sibling], near.at[1], sems, at + 1, (sibling, col)),
        remote(outgoing, far, sems, at + 2, (partner, col)),
    ]


def row_sum_forward(parts, near, outgoing, copies):
    _, _, _, partner, _ = row_places()
    copies[0].wait_recv()
    outgoing[...] = (parts[partner].astype(jnp.float32) + near[0].astype(jnp.float32)).astype(
        jnp.bfloat16
    )
    copies[2].start()


def row_sum_total(parts, near, far, copies):
    row = row_places()[0]
    copies[1].wait_recv()
    total = parts[row].astype(jnp.float32) + near[1].astype(jnp.float32)
    copies[2].wait_recv()
    return total + far[...].astype(jnp.float32)


class ScatterSum:
    def __init__(self, grads, scratch):
        self.grads = grads
        self.first, self.first_sum, self.second, self.second_sum, self.third = scratch[:5]
        self.one, self.two, self.three = scratch[5:7], scratch[7:9], scratch[9:11]
        row, col = lax.axis_index("row"), lax.axis_index("col")
        x, z, y = col // 16, lax.rem(col // 4, 4), lax.rem(col, 4)
        self.place = (x, z, y)
        self.half_rows = grads.shape[3] // 2
        self.y_peers = [(row, x * 16 + z * 4 + lax.rem(y + i, 4)) for i in (1, 2, 3)]
        self.z_peers = [(row, x * 16 + lax.rem(z + i, 4) * 4 + y) for i in (1, 2, 3)]
        self.x_peer = (row, (1 - x) * 16 + z * 4 + y)
        self.one_copies, self.two_copies, self.three_copies = {}, {}, []

    @staticmethod
    def scratch(grads):
        half_rows, depth = grads.shape[3] // 2, grads.shape[4]
        low = jnp.bfloat16
        return [
            pltpu.VMEM((2, 3, 2, 4, half_rows, depth), low),
            pltpu.VMEM((2, 2, 4, half_rows, depth), low),
            pltpu.VMEM((2, 3, 2, half_rows, depth), low),
            pltpu.VMEM((2, half_rows, depth), low),
            pltpu.VMEM((2, half_rows, depth), low),
        ] + [pltpu.SemaphoreType.DMA((count,)) for count in (6, 6, 6, 6, 2, 2)]

    def half(self, half):
        return pl.ds(half * self.half_rows, self.half_rows)

    def start(self):
        _, z, y = self.place
        for i in range(3):
            for half in range(2):
                if half == 0:
                    source = self.grads.at[:, :, lax.rem(y + i + 1, 4), self.half(0)]
                else:
                    source = self.grads.at[:, lax.rem(z + i + 1, 4), :, self.half(1)]
                peer = (self.y_peers, self.z_peers)[half][i]
                copy = remote(source, self.first.at[half, i], self.one, half * 3 + i, peer)
                self.one_copies[half, i] = copy
                copy.start()

    def add_first(self):
        _, z, y = self.place
        for half in range(2):
            for i in range(3):
                self.one_copies[half, i].wait_recv()

            def add(k, carry, half=half):
                if half == 0:
                    total = self.grads[k // 4, lax.rem(k, 4), y, self.half(0)].astype(jnp.float32)
                else:
                    total = self.grads[k // 4, z, lax.rem(k, 4), self.half(1)].astype(jnp.float32)
                for i in range(3):
                    total = total + self.first[half, i, k // 4, lax.rem(k, 4)].astype(jnp.float32)
                self.first_sum[half, k // 4, lax.rem(k, 4)] = total.astype(jnp.bfloat16)
                return carry

            lax.fori_loop(0, 8, add, 0)
            for i in range(3):
                away = lax.rem((z, y)[half] + i + 1, 4)
                copy = remote(
                    self.first_sum.at[half, :, away],
                    self.second.at[half, i],
                    self.two,
                    half * 3 + i,
                    (self.z_peers, self.y_peers)[half][i],
                )
                self.two_copies[half, i] = copy
                copy.start()

    def second_total(self, owner_x, half):
        _, z, y = self.place
        total = self.first_sum[half, owner_x, (z, y)[half]].astype(jnp.float32)
        for i in range(3):
            total = total + self.second[half, i, owner_x].astype(jnp.float32)
        return total

    def add_second(self):
        x = self.place[0]
        for half in range(2):
            for i in range(3):
                self.two_copies[half, i].wait_recv()
            self.second_sum[half] = self.second_total(1 - x, half).astype(jnp.bfloat16)
            copy = remote(
                self.second_sum.at[half], self.third.at[half], self.three, half, self.x_peer
            )
            self.three_copies.append(copy)
            copy.start()

    def add_third(self, pieces):
        x = self.place[0]
        for half in range(2):
            total = self.second_total(x, half)
            self.three_copies[half].wait_recv()
            total = total + self.third[half].astype(jnp.float32)
            start = 0
            for piece in pieces:
                width = piece.shape[-1]
                if len(piece.shape) == 3:
                    piece[self.half(half), 0] = total[:, start : start + width]
                else:
                    piece[self.half(half)] = total[:, start : start + width]
                start += width

    def end(self):
        for copy in [*self.one_copies.values(), *self.two_copies.values(), *self.three_copies]:
            copy.wait_send()


class RouterSum:
    def __init__(self, part, block, scratch):
        self.part, self.block = part, block
        self.in_y, self.sum_y, self.in_z, self.sum_z, self.in_x = scratch[:5]
        self.sems = scratch[5:]
        row, col = lax.axis_index("row"), lax.axis_index("col")
        x, z, y = col // 16, lax.rem(col // 4, 4), lax.rem(col, 4)
        self.place = (x, z, y)
        self.y_near = [lax.rem(y + i, 4) for i in (1, 2, 3)]
        self.z_near = [lax.rem(z + i, 4) for i in (1, 2, 3)]
        self.y_peers = [(row, x * 16 + z * 4 + near) for near in self.y_near]
        self.z_peers = [(row, x * 16 + near * 4 + y) for near in self.z_near]
        self.x_peer = (row, (1 - x) * 16 + z * 4 + y)
        self.copies = {}

    @staticmethod
    def scratch(share):
        low = jnp.bfloat16
        return [
            pltpu.VMEM((3, 2, 4, *share), low),
            pltpu.VMEM((2, 4, *share), low),
            pltpu.VMEM((3, 2, *share), low),
            pltpu.VMEM((2, *share), low),
            pltpu.VMEM(share, low),
            pltpu.SemaphoreType.DMA((14,)),
            pltpu.SemaphoreType.DMA((14,)),
        ]

    def send(self, stage, at, sources, targets, peers):
        copies = [
            remote(source, target, self.sems, at + i, peer)
            for i, (source, target, peer) in enumerate(zip(sources, targets, peers))
        ]
        for copy in copies:
            copy.start()
        self.copies[stage] = copies

    def wait(self, stage):
        for copy in self.copies[stage]:
            copy.wait_recv()

    def start(self):
        sources = [self.part.at[:, :, near] for near in self.y_near]
        self.send(0, 0, sources, [self.in_y.at[i] for i in range(3)], self.y_peers)

    def add_y(self):
        self.wait(0)
        total = self.part[:, :, self.place[2]].astype(jnp.float32)
        for i in range(3):
            total = total + self.in_y[i].astype(jnp.float32)
        self.sum_y[...] = total.astype(jnp.bfloat16)
        sources = [self.sum_y.at[:, near] for near in self.z_near]
        self.send(1, 3, sources, [self.in_z.at[i] for i in range(3)], self.z_peers)

    def add_z(self):
        self.wait(1)
        total = self.sum_y[:, self.place[1]].astype(jnp.float32)
        for i in range(3):
            total = total + self.in_z[i].astype(jnp.float32)
        self.sum_z[...] = total.astype(jnp.bfloat16)
        self.send(2, 6, [self.sum_z.at[1 - self.place[0]]], [self.in_x], [self.x_peer])

    def add_x(self):
        self.wait(2)
        x, z, y = self.place
        total = self.sum_z[x].astype(jnp.float32) + self.in_x[...].astype(jnp.float32)
        self.block[x, z, y] = total.astype(jnp.bfloat16)
        own = self.block.at[x, z, y]
        self.send(3, 7, [own], [own], [self.x_peer])

    def spread_z(self):
        self.wait(3)
        own = self.block.at[:, self.place[1], self.place[2]]
        self.send(4, 8, [own] * 3, [own] * 3, self.z_peers)

    def spread_y(self):
        self.wait(4)
        own = self.block.at[:, :, self.place[2]]
        self.send(5, 11, [own] * 3, [own] * 3, self.y_peers)

    def end(self):
        for copies in self.copies.values():
            for copy in copies:
                copy.wait_send()


def attention_back_rows(start, refs, sums):
    group, w_back, query, keys, values, norms, cosine, sine, begin, begin_row = refs
    back, pre_grad, bias, bias_t, deltas, key_grad, value_grad = sums
    low = jnp.bfloat16
    size = keys.shape[1]
    inner = query.shape[1]
    count = bias.shape[0]
    rows = pl.ds(pl.multiple_of(start, count), count)
    scale = size ** (-0.5)
    branch = group[pl.ds(start // 128, count // 128)].reshape(count, group.shape[2])
    back[rows] = matmul(branch, w_back[...]).astype(low)
    first = begin[rows]
    key_places = lax.broadcasted_iota(jnp.int32, bias.shape, 1)
    places = start + lax.broadcasted_iota(jnp.int32, bias.shape, 0)
    bias[...] = jnp.where((key_places >= first) & (key_places <= places), 0.0, masked_score)
    lanes = lax.broadcasted_iota(jnp.int32, deltas.shape, 1)
    all_deltas = jnp.zeros(deltas.shape, jnp.float32)
    for head in range(inner // size):
        columns = slice(head * size, (head + 1) * size)
        turned, outer = query[rows, columns], back[rows, columns]
        scores = matmul_t(turned, keys[...]) * scale + bias[...]
        probs = jnp.exp(scores - norms[rows, head : head + 1])
        prob_grad = matmul_t(outer, values[...])
        delta = jnp.sum(probs * prob_grad, axis=1, keepdims=True)
        all_deltas = jnp.where(lanes == head, delta, all_deltas)
        score_grad = (probs * (prob_grad - delta)).astype(low)
        query_grad = matmul(score_grad, keys[...]) * scale
        pre_grad[rows, columns] = turn(query_grad, cosine[rows], -sine[rows]).astype(low)
    deltas[...] = all_deltas
    deltas_t = jnp.transpose(deltas[...])
    norms_t = jnp.transpose(norms[rows])
    first = begin_row[:, rows]
    key_places = lax.broadcasted_iota(jnp.int32, bias_t.shape, 0)
    places = start + lax.broadcasted_iota(jnp.int32, bias_t.shape, 1)
    bias_t[...] = jnp.where((key_places >= first) & (key_places <= places), 0.0, masked_score)
    for head in range(inner // size):
        columns = slice(head * size, (head + 1) * size)
        turned, outer = query[rows, columns], back[rows, columns]
        scores = matmul_t(keys[...], turned) * scale + bias_t[...]
        probs = jnp.exp(scores - norms_t[head : head + 1])
        prob_grad = matmul_t(values[...], outer)
        score_grad = (probs * (prob_grad - deltas_t[head : head + 1])).astype(low)
        key_grad[...] += matmul(score_grad, turned)
        value_grad[...] += matmul(probs.astype(low), outer)


def tail_kernel(
    packed,
    marks_in,
    router_input_in,
    hidden_in,
    group_one_t,
    full_pre,
    full_back,
    shared_parts_in,
    stream_in,
    shared_input_in,
    scale_two,
    gain_ffn,
    stream_grad,
    router_parts,
    shared_grads,
    query,
    keys,
    values_in,
    attended,
    norms,
    cosine,
    sine,
    begin,
    begin_row,
    inputs,
    scale_one,
    gain_attn,
    hidden_total,
    result,
    block_out,
    router,
    gain_attn_sum,
    gain_ffn_sum,
    *refs,
):
    pieces, scratch = refs[:5], refs[5:]
    held, marks, router_input, hidden, rows_t, w_pre, w_back, shared_parts, stream = scratch[:9]
    routed, group, back, pre_grad, bias, bias_t, deltas, key_grad, value_grad = scratch[9:18]
    parts, near, far, outgoing, router_near, router_far, router_outgoing = scratch[18:25]
    router_part, values, buffers, pre_grads, out_grads = scratch[25:30]
    load_sem, branch_send, branch_recv, row_send, row_recv, gain_send, gain_recv = scratch[30:37]
    pass_send, pass_recv, input_parts, core_near, share_sums, share_low = scratch[37:43]
    shared_scatter = ScatterSum(shared_grads, scratch[43:54])
    out_scatter = ScatterSum(out_grads, scratch[54:65])
    pre_scatter = ScatterSum(pre_grads, scratch[65:76])
    router_at = 76
    low = jnp.bfloat16
    row, col, sibling, partner, across = row_places()
    row_peers = [(peer, col) for peer in (sibling, partner, across)]
    greet(row_peers)
    greet(pre_scatter.y_peers + pre_scatter.z_peers + [pre_scatter.x_peer])
    steps, depth = 4, held.shape[1]
    inner = query.shape[1]
    sources = [packed.at[pl.ds(i * depth, depth)] for i in range(steps)]
    targets = [held.at[i % 2] for i in range(steps)]
    sources[1:1] = [marks_in]
    targets[1:1] = [marks]
    sources += [router_input_in, hidden_in, full_back, shared_parts_in]
    targets += [router_input, hidden, w_back, shared_parts]
    sources += [full_pre, group_one_t, stream_in]
    targets += [w_pre, rows_t, stream]
    loads = [
        pltpu.make_async_copy(source, target, load_sem.at[i])
        for i, (source, target) in enumerate(zip(sources, targets))
    ]
    load_parts = pltpu.make_async_copy(shared_input_in, input_parts, load_sem.at[len(loads)])
    load_parts.start()
    load_marks = loads.pop(1)
    load_marks.start()
    for load in loads[:2] + loads[steps:]:
        load.start()
    load_input, load_hidden, load_back, load_shared, load_pre, load_rows, load_stream = loads[
        steps:
    ]
    await_greetings(10)

    row_sems = (row_send, row_recv)
    router_copies = row_sum_copies(
        router_parts, router_near, router_far, router_outgoing, row_sems, 0
    )
    router_copies[0].start()
    router_copies[1].start()
    core = lax.rem(row, 2)
    load_parts.wait()
    input_copy = remote(input_parts.at[1 - core], core_near.at[0], row_sems, 3, (sibling, col))
    input_copy.start()
    shared_scatter.start()
    row_sum_forward(router_parts, router_near, router_outgoing, router_copies)

    load_marks.wait()
    for i in range(steps):
        loads[i].wait()
        rows = slice(i * depth, (i + 1) * depth)
        for part in range(4):
            columns = slice(part * QUARTER, (part + 1) * QUARTER)
            if part < 3:
                found = matmul(marks[0, :, rows], held[i % 2, :, columns])
            else:
                found = matmul(marks[1, :, rows], held[i % 2, :, :QUARTER])
                for j in (1, 2):
                    second = slice(j * QUARTER, (j + 1) * QUARTER)
                    found = found + matmul(marks[j + 1, :, rows], held[i % 2, :, second])
            routed[:, columns] = found if i == 0 else routed[:, columns] + found
        if i + 2 < steps:
            loads[i + 2].start()
    load_input.wait()
    load_hidden.wait()
    input_copy.wait_recv()
    shared_input = input_parts[core].astype(jnp.float32) + core_near[0].astype(jnp.float32)
    incoming = router_input[...] + routed[...] + shared_input
    state = hidden[...]
    factor = scale_two[...]
    weighted = gain_ffn[...] * incoming
    mean = jnp.mean(weighted * state, axis=1, keepdims=True)
    total = (
        stream_grad[...].astype(jnp.float32)
        + factor * weighted
        - state * (factor * factor * factor * mean)
    )
    hidden_total[...] = total
    group[row] = total.astype(low)
    far_rows, near_rows, onward = row_copies([group.at[row]], [group], branch_send, branch_recv)
    far_rows[0].start()
    near_rows[0].start()
    values[0, 1:2] = jnp.sum(incoming * state * factor, axis=0, keepdims=True)

    load_shared.wait()
    shared_copy = remote(shared_parts.at[1 - core], core_near.at[1], row_sems, 4, (sibling, col))
    shared_copy.start()
    router_sum = row_sum_total(router_parts, router_near, router_far, router_copies)
    router_part[...] = router_sum.astype(low).reshape(router_part.shape)
    router_scatter = RouterSum(router_part, router.at[row], scratch[router_at:])
    router_scatter.start()
    shared_scatter.add_first()
    load_back.wait()
    near_rows[0].wait_recv()
    key_grad[...] = jnp.zeros_like(key_grad)
    value_grad[...] = jnp.zeros_like(value_grad)
    refs = (group, w_back, query, keys, values_in, norms, cosine, sine, begin, begin_row)
    sums = (back, pre_grad, bias, bias_t, deltas, key_grad, value_grad)
    chip = row // 2
    chip_rows = bias.shape[0]
    attention_back_rows(chip * chip_rows, refs, sums)
    shared_scatter.add_second()
    router_scatter.add_y()
    far_rows[0].wait_recv()
    onward[0].start()
    onward[0].wait_recv()

    def keep(target, block, rows):
        shaped = rows.astype(low).reshape(2, 4, 64, rows.shape[1])
        target[block // 2, 2 * (block % 2) : 2 * (block % 2) + 2] = shaped

    blocks, width = 4, group.shape[2] // 4
    for block in range(blocks):
        columns = slice(block * width, (block + 1) * width)
        rows = group[:, :, columns].reshape(4 * group.shape[1], width)
        keep(out_grads, block, outer_sum(rows, attended[...]))
    out_scatter.start()
    router_scatter.add_z()
    attention_back_rows((1 - chip) * chip_rows, refs, sums)
    size = keys.shape[1]
    scale = size ** (-0.5)
    pre_grad[:, inner : inner + size] = turn(key_grad[...] * scale, cosine[...], -sine[...]).astype(
        low
    )
    pre_grad[:, inner + size :] = value_grad[...].astype(low)
    load_pre.wait()
    load_rows.wait()
    block_rows = parts.shape[1]
    for block in range(4):
        rows = slice(block * block_rows, (block + 1) * block_rows)
        parts[block] = matmul_t(pre_grad[rows], w_pre[...]).astype(low)
    attn_copies = row_sum_copies(parts, near.at[0], far.at[0], outgoing.at[0], row_sems, 6)
    attn_copies[0].start()
    attn_copies[1].start()
    row_sum_forward(parts, near.at[0], outgoing.at[0], attn_copies)
    for block in range(blocks):
        rows = slice(block * width, (block + 1) * width)
        keep(pre_grads, block, matmul(rows_t[rows], pre_grad[...]))
    pre_scatter.start()
    router_scatter.add_x()
    out_scatter.add_first()
    shared_scatter.add_third([share_sums.at[0], share_sums.at[1]])
    share_low[0] = share_sums[1].astype(low)
    share_copy = remote(share_low.at[0], share_low.at[1], row_sems, 5, (partner, col))
    share_copy.start()
    router_scatter.spread_z()

    gain_sems = (gain_send, gain_recv)
    gain_copies = []
    stages = (row_peers, pre_scatter.y_peers, pre_scatter.z_peers, [pre_scatter.x_peer])

    def start_gains(stage):
        at = 3 * stage
        for i, peer in enumerate(stages[stage]):
            gain_copies.append(
                remote(values.at[stage], buffers.at[at + i], gain_sems, at + i, peer)
            )
            gain_copies[-1].start()

    def add_gains(stage):
        at = 3 * stage
        total = values[stage]
        for i in range(len(stages[stage])):
            gain_copies[at + i].wait_recv()
            total = total + buffers[at + i]
        values[stage + 1] = total

    incoming = row_sum_total(parts, near.at[0], far.at[0], attn_copies)
    first = inputs[...].astype(jnp.float32)
    factor = scale_one[...]
    weighted = gain_attn[...] * incoming
    mean = jnp.mean(weighted * first, axis=1, keepdims=True)
    result[...] = factor * weighted - first * (factor * factor * factor * mean)
    values[0, 0:1] = jnp.sum(incoming * first * factor, axis=0, keepdims=True)
    start_gains(0)
    router_scatter.spread_y()
    out_scatter.add_second()
    load_stream.wait()
    shared_copy.wait_recv()
    shared = shared_parts[core].astype(jnp.float32) + core_near[1].astype(jnp.float32)
    block_out[...] = (stream[...] + shared).astype(low)
    add_gains(0)
    start_gains(1)
    pre_scatter.add_first()
    router_scatter.wait(5)
    router_rows = row_copies([router.at[row]], [router], pass_send, pass_recv)
    router_rows[0][0].start()
    router_rows[1][0].start()
    out_scatter.add_third(pieces[2:3])
    add_gains(1)
    start_gains(2)
    pre_scatter.add_second()
    add_gains(2)
    start_gains(3)
    router_rows[0][0].wait_recv()
    router_rows[2][0].start()
    share_copy.wait_recv()
    share = share_sums[0] + share_low[1].astype(jnp.float32)
    part = pieces[3].shape[2]
    for i in range(2):
        pieces[3][:, i] = share[:, i * part : (i + 1) * part]
    pieces[4][...] = share[:, 2 * part :]
    pre_scatter.add_third(pieces[:2])
    add_gains(3)
    gain_attn_sum[...] = values[4, 0:1]
    gain_ffn_sum[...] = values[4, 1:2]

    router_scatter.end()
    far_rows[0].wait_send()
    near_rows[0].wait_send()
    onward[0].wait_send()
    router_rows[0][0].wait_send()
    router_rows[1][0].wait()
    router_rows[2][0].wait()
    for done in [*router_copies, *attn_copies, *gain_copies, input_copy, shared_copy, share_copy]:
        done.wait_send()
    for scatter in (shared_scatter, out_scatter, pre_scatter):
        scatter.end()


def tail(streamed, local, kept, tables, last, widths):
    space = pl.BlockSpec(memory_space=pltpu.VMEM)
    away = pl.BlockSpec(memory_space=pl.ANY)
    low = jnp.bfloat16
    packed, marks = streamed[:2]
    router_parts, shared_grads = local[3:]
    rows, width = last[0].shape
    tokens = 4 * rows
    _, router_rows, experts = router_parts.shape
    share = (router_rows // 32, experts)
    size = kept[1].shape[1]
    inner = kept[0].shape[1]
    pre_width = widths[0] + widths[1]
    shard = width // 32
    pre_grads = jax.ShapeDtypeStruct((2, 4, 4, shard, pre_width), low)
    out_grads = jax.ShapeDtypeStruct((2, 4, 4, shard, inner), low)
    dma = pltpu.SemaphoreType.DMA
    return pl.pallas_call(
        tail_kernel,
        out_shape=[
            jax.ShapeDtypeStruct((rows, width), jnp.float32),
            jax.ShapeDtypeStruct((rows, width), jnp.float32),
            jax.ShapeDtypeStruct((rows, width), low),
            jax.ShapeDtypeStruct((4, 2, 4, 4, *share), low),
            jax.ShapeDtypeStruct((1, width), jnp.float32),
            jax.ShapeDtypeStruct((1, width), jnp.float32),
        ]
        + [
            jax.ShapeDtypeStruct(shape, jnp.float32)
            for shape in (
                (shard, widths[0]),
                (shard, 1, widths[1]),
                (shard, widths[2]),
                (shard, 2, widths[3] // 2),
                (shard, widths[4]),
            )
        ],
        in_specs=[away] * 10 + [space] * 17,
        out_specs=[space] * (6 + len(widths)),
        scratch_shapes=[
            pltpu.VMEM((2, packed.shape[0] // 4, packed.shape[1]), low),
            pltpu.VMEM(marks.shape, low),
            pltpu.VMEM((rows, width), jnp.float32),
            pltpu.VMEM((rows, width), jnp.float32),
            pltpu.VMEM((width, tokens), low),
            pltpu.VMEM((width, pre_width), low),
            pltpu.VMEM((width, inner), low),
            pltpu.VMEM((2, rows, width), low),
            pltpu.VMEM((rows, width), jnp.float32),
            pltpu.VMEM((rows, width), jnp.float32),
            pltpu.VMEM((4, rows, width), low),
            pltpu.VMEM((tokens, inner), low),
            pltpu.VMEM((tokens, pre_width), low),
            pltpu.VMEM((tokens // 2, tokens), jnp.float32),
            pltpu.VMEM((tokens, tokens // 2), jnp.float32),
            pltpu.VMEM((tokens // 2, 128), jnp.float32),
            pltpu.VMEM((tokens, size), jnp.float32),
            pltpu.VMEM((tokens, size), jnp.float32),
            pltpu.VMEM((4, rows, width), low),
            pltpu.VMEM((1, 2, rows, width), low),
            pltpu.VMEM((1, rows, width), low),
            pltpu.VMEM((1, rows, width), low),
            pltpu.VMEM((2, router_rows, experts), low),
            pltpu.VMEM((router_rows, experts), low),
            pltpu.VMEM((router_rows, experts), low),
            pltpu.VMEM((2, 4, 4, *share), low),
            pltpu.VMEM((5, 2, width), jnp.float32),
            pltpu.VMEM((10, 2, width), jnp.float32),
            pltpu.VMEM(pre_grads.shape, low),
            pltpu.VMEM(out_grads.shape, low),
            dma((13,)),
            dma((3,)),
            dma((3,)),
            dma((9,)),
            dma((9,)),
            dma((10,)),
            dma((10,)),
            dma((3,)),
            dma((3,)),
            pltpu.VMEM((2, rows, width), low),
            pltpu.VMEM((2, rows, width), low),
            pltpu.VMEM((2, shard, widths[3] + widths[4]), jnp.float32),
            pltpu.VMEM((2, shard, widths[3] + widths[4]), low),
            *ScatterSum.scratch(shared_grads),
            *ScatterSum.scratch(out_grads),
            *ScatterSum.scratch(pre_grads),
            *RouterSum.scratch(share),
        ],
        compiler_params=pltpu.CompilerParams(
            collective_id=16, has_side_effects=True, vmem_limit_bytes=60 << 20
        ),
        cost_estimate=pl.CostEstimate(flops=0, bytes_accessed=300 << 20, transcendentals=0),
        name="tail",
    )(*streamed, *local, *kept, *tables, *last)


def packed_places(shape, axis):
    index = lax.broadcasted_iota(jnp.int32, shape, axis)
    pair, place = index // PACKED_ROWS, lax.rem(index, PACKED_ROWS)
    found = []
    for part in range(-1, 3):
        if part < 0:
            valid, slot = place < PAIR_ROWS, place
        else:
            valid, slot = place >= PAIR_ROWS, 3 * (place - PAIR_ROWS) + part
        second = (slot >= EXPERT_ROWS).astype(jnp.int32)
        found.append((valid, pair, second, slot - EXPERT_ROWS * second))
    return found


def token_marks(code_block):
    marks = []
    wide = (BLOCK, BLOCK_EXPERTS)
    lanes = lax.broadcasted_iota(jnp.int32, wide, 1)
    for (valid, pair, second, _), (tall, _, _, order) in zip(
        packed_places(wide, 0), packed_places((BLOCK, SIDE), 0)
    ):
        owner = ((lanes == 2 * pair + second) & valid).astype(jnp.float32).astype(jnp.bfloat16)
        found = matmul(owner, code_block)
        hit = (found == order.astype(jnp.float32)) & tall
        marks.append((owner, hit.astype(jnp.float32)))
    return marks


def gate_weights_of(owner, hit, high, low):
    weights = hit * (matmul(owner, high) + matmul(owner, low))
    return split_low(weights)


def pack_tokens_kernel(code, values, high, low, packed):
    marks = token_marks(code[0])
    weights = [gate_weights_of(owner, hit, high[0], low[0]) for owner, hit in marks]
    last = values[:, 3 * QUARTER :]
    for part in range(3):
        columns = slice(part * QUARTER, (part + 1) * QUARTER)
        both = jnp.concatenate([*weights[0], *weights[part + 1]], axis=1)
        rows = jnp.concatenate([values[:, columns]] * 2 + [last] * 2, axis=0)
        packed[:, columns] = matmul(both, rows).astype(jnp.bfloat16)


def pack_tokens(code, values, gates):
    blocks = code.shape[0]
    width = 3 * QUARTER
    small = pl.BlockSpec((1, BLOCK_EXPERTS, SIDE), lambda i: (i, 0, 0))
    return pl.pallas_call(
        pack_tokens_kernel,
        grid=(blocks,),
        out_shape=jax.ShapeDtypeStruct((blocks * BLOCK, width), jnp.bfloat16),
        in_specs=[small, pl.BlockSpec(values.shape, lambda i: (0, 0)), small, small],
        out_specs=pl.BlockSpec((BLOCK, width), lambda i: (i, 0)),
        compiler_params=pltpu.CompilerParams(vmem_limit_bytes=32 << 20),
        cost_estimate=pl.CostEstimate(
            flops=blocks * BLOCK * 512 * width * 2, bytes_accessed=8 << 20, transcendentals=0
        ),
        name="pack_tokens",
    )(code, values, *gates)


def slot_marks():
    shape = (2 * BLOCK_SLOTS, BLOCK)
    rows = lax.broadcasted_iota(jnp.int32, shape, 0)
    marks = []
    for valid, pair, second, order in packed_places(shape, 1):
        hit = (rows == second * BLOCK_SLOTS + pair * EXPERT_ROWS + order) & valid
        marks.append(hit.astype(jnp.float32).astype(jnp.bfloat16))
    return marks


def unpack_slots_kernel(packed, values):
    marks = slot_marks()
    last = jnp.zeros((2 * BLOCK_SLOTS, QUARTER), jnp.float32)
    for part in range(3):
        columns = slice(part * QUARTER, (part + 1) * QUARTER)
        found = matmul(marks[0], packed[:, columns]).astype(jnp.bfloat16)
        values[0, :, columns] = found[:BLOCK_SLOTS]
        values[1, :, columns] = found[BLOCK_SLOTS:]
        last = last + matmul(marks[part + 1], packed[:, columns])
    last = last.astype(jnp.bfloat16)
    values[0, :, 3 * QUARTER :] = last[:BLOCK_SLOTS]
    values[1, :, 3 * QUARTER :] = last[BLOCK_SLOTS:]


def unpack_slots(packed):
    blocks = packed.shape[0] // BLOCK
    slots = blocks * BLOCK_SLOTS
    return pl.pallas_call(
        unpack_slots_kernel,
        grid=(blocks,),
        out_shape=jax.ShapeDtypeStruct((2, slots, 4 * QUARTER), jnp.bfloat16),
        in_specs=[pl.BlockSpec((BLOCK, 3 * QUARTER), lambda i: (i, 0))],
        out_specs=pl.BlockSpec((2, BLOCK_SLOTS, 4 * QUARTER), lambda i: (0, i, 0)),
        compiler_params=pltpu.CompilerParams(vmem_limit_bytes=32 << 20),
        cost_estimate=pl.CostEstimate(
            flops=blocks * 2 * BLOCK_SLOTS * BLOCK * 6 * QUARTER * 2,
            bytes_accessed=14 << 20,
            transcendentals=0,
        ),
        name="unpack_slots",
    )(packed)


def pack_slots_kernel(values, packed):
    marks = slot_marks()
    last = jnp.concatenate([values[0, :, 3 * QUARTER :], values[1, :, 3 * QUARTER :]], axis=0)
    for part in range(3):
        columns = slice(part * QUARTER, (part + 1) * QUARTER)
        rows = jnp.concatenate([values[0, :, columns], values[1, :, columns]], axis=0)
        found = outer_sum(marks[0], rows) + outer_sum(marks[part + 1], last)
        packed[:, columns] = found.astype(jnp.bfloat16)


def pack_slots(values):
    slots = values.shape[1]
    blocks = slots // BLOCK_SLOTS
    return pl.pallas_call(
        pack_slots_kernel,
        grid=(blocks,),
        out_shape=jax.ShapeDtypeStruct((blocks * BLOCK, 3 * QUARTER), jnp.bfloat16),
        in_specs=[pl.BlockSpec((2, BLOCK_SLOTS, 4 * QUARTER), lambda i: (0, i, 0))],
        out_specs=pl.BlockSpec((BLOCK, 3 * QUARTER), lambda i: (i, 0)),
        compiler_params=pltpu.CompilerParams(vmem_limit_bytes=32 << 20),
        cost_estimate=pl.CostEstimate(
            flops=blocks * 2 * BLOCK_SLOTS * BLOCK * 6 * QUARTER * 2,
            bytes_accessed=14 << 20,
            transcendentals=0,
        ),
        name="pack_slots",
    )(values)


def marks_kernel(code, marks):
    wide = (BLOCK_EXPERTS, BLOCK)
    owners = lax.broadcasted_iota(jnp.int32, wide, 0)
    for i, ((valid, pair, second, _), (tall, _, _, order)) in enumerate(
        zip(packed_places(wide, 1), packed_places((code.shape[1], BLOCK), 1))
    ):
        owner = ((owners == 2 * pair + second) & valid).astype(jnp.float32).astype(jnp.bfloat16)
        hit = (matmul(code[0], owner) == order.astype(jnp.float32)) & tall
        marks[i] = hit.astype(jnp.float32).astype(jnp.bfloat16)


def all_marks(code):
    blocks, experts, tokens = code.shape
    return pl.pallas_call(
        marks_kernel,
        grid=(blocks,),
        out_shape=jax.ShapeDtypeStruct((4, tokens, blocks * BLOCK), jnp.bfloat16),
        in_specs=[pl.BlockSpec((1, tokens, experts), lambda i: (i, 0, 0))],
        out_specs=pl.BlockSpec((4, tokens, BLOCK), lambda i: (0, 0, i)),
        cost_estimate=pl.CostEstimate(flops=1 << 26, bytes_accessed=4 << 20, transcendentals=0),
        name="all_marks",
    )(code.transpose(0, 2, 1))


def sum_gated_kernel(code, packed, grads, high, low, total, gate_grads):
    @pl.when(pl.program_id(0) == 0)
    def _():
        total[...] = jnp.zeros_like(total)

    marks = token_marks(code[0])
    weights = [gate_weights_of(owner, hit, high[0], low[0]) for owner, hit in marks]
    last = jnp.zeros((total.shape[0], QUARTER), jnp.float32)
    whole = jnp.zeros((BLOCK, 1), jnp.float32)
    products = []
    for part in range(3):
        columns = slice(part * QUARTER, (part + 1) * QUARTER)
        rows = packed[:, columns]
        total[:, columns] += outer_sum(weights[0][0], rows) + outer_sum(weights[0][1], rows)
        last = last + outer_sum(weights[part + 1][0], rows) + outer_sum(weights[part + 1][1], rows)
        dots = jnp.sum(
            rows.astype(jnp.float32) * grads[:, columns].astype(jnp.float32),
            axis=1,
            keepdims=True,
        )
        whole = whole + dots
        products.append(dots)
    total[:, 3 * QUARTER :] += last
    found = jnp.zeros(gate_grads.shape[1:], jnp.float32)
    for (owner, hit), dots in zip(marks, [whole, *products]):
        hit = hit.astype(jnp.bfloat16)
        for spread in split_low(dots * owner.astype(jnp.float32)):
            found = found + outer_sum(hit, spread)
    gate_grads[0] = found


def sum_gated(code, packed, grads, gates):
    blocks, _, tokens = code.shape
    small = pl.BlockSpec((1, BLOCK_EXPERTS, tokens), lambda i: (i, 0, 0))
    wide = pl.BlockSpec((BLOCK, 3 * QUARTER), lambda i: (i, 0))
    return pl.pallas_call(
        sum_gated_kernel,
        grid=(blocks,),
        out_shape=[
            jax.ShapeDtypeStruct((tokens, 4 * QUARTER), jnp.float32),
            jax.ShapeDtypeStruct((blocks, tokens, BLOCK_EXPERTS), jnp.float32),
        ],
        in_specs=[small, wide, wide, small, small],
        out_specs=[
            pl.BlockSpec((tokens, 4 * QUARTER), lambda i: (0, 0)),
            pl.BlockSpec((1, tokens, BLOCK_EXPERTS), lambda i: (i, 0, 0)),
        ],
        compiler_params=pltpu.CompilerParams(vmem_limit_bytes=32 << 20),
        cost_estimate=pl.CostEstimate(
            flops=blocks * BLOCK * 128 * 12 * QUARTER * 2,
            bytes_accessed=14 << 20,
            transcendentals=0,
        ),
        name="sum_gated",
    )(code, packed, grads, *gates)


class Gather:
    def __init__(self, mine, full, send_sem, recv_sem):
        self.mine, self.full = mine, full
        self.sems = (send_sem, recv_sem)
        row, col = lax.axis_index("row"), lax.axis_index("col")
        x, z, y = col // 16, lax.rem(col // 4, 4), lax.rem(col, 4)
        self.place = (x, z, y)
        self.z_peers = [(row, x * 16 + lax.rem(z + i, 4) * 4 + y) for i in (1, 3, 2)]
        self.y_peers = [(row, x * 16 + z * 4 + lax.rem(y + i, 4)) for i in (1, 3, 2)]
        self.x_peer = (row, (1 - x) * 16 + z * 4 + y)
        self.copies = {}

    def rows(self, half):
        half_rows = self.full.shape[3] // 2
        return pl.ds(half * half_rows, half_rows)

    def send(self, key, source, target, peers):
        at = 1 + 3 * len(self.copies) - 3 if self.copies else 0
        copies = [
            remote(source, target, self.sems, at + i, peer) for i, peer in enumerate(peers)
        ]
        for copy in copies:
            copy.start()
        self.copies[key] = copies

    def wait(self, *keys):
        for key in keys:
            for copy in self.copies[key]:
                copy.wait_recv()

    def start(self):
        x, z, y = self.place
        self.send("x", self.mine, self.full.at[x, z, y], [self.x_peer])
        for half, peers in enumerate((self.z_peers, self.y_peers)):
            rows = self.rows(half)
            target = self.full.at[x, z, y, rows]
            self.send((0, half), self.mine.at[rows], target, peers)

    def second(self):
        x, z, y = self.place
        self.wait("x")
        for half, peers in enumerate((self.z_peers, self.y_peers)):
            target = self.full.at[1 - x, z, y, self.rows(half)]
            self.send((1, half), target, target, peers)

    def third(self):
        x, z, y = self.place
        for turn, owner_x in enumerate((x, 1 - x)):
            self.wait((turn, 0))
            target = self.full.at[owner_x, :, y, self.rows(0)]
            self.send((2 + turn, 0), target, target, self.y_peers)
            self.wait((turn, 1))
            target = self.full.at[owner_x, z, :, self.rows(1)]
            self.send((2 + turn, 1), target, target, self.z_peers)

    def await_all(self):
        self.wait((2, 0), (2, 1), (3, 0), (3, 1))

    def end(self):
        for copies in self.copies.values():
            for copy in copies:
                copy.wait_send()


def head_kernel(
    inputs,
    gain_attn,
    gain_ffn,
    grads,
    lengths,
    routes,
    frequency,
    w_query,
    w_keyval,
    w_out,
    w_shared_in,
    w_shared_out,
    full_pre,
    full_back,
    full_shared,
    group_one,
    chip_grad,
    chip_two,
    scale_one,
    cosine,
    sine,
    begin,
    begin_row,
    query,
    keys,
    values,
    attended,
    norms,
    hidden,
    normed_two,
    scale_two,
    packed,
    code,
    order,
    *scratch,
):
    mine_pre, mine_back, mine_shared, normed, rows, w_pre, w_back, pre, bias, parts = scratch[:10]
    near, far, outgoing, marks, staged = scratch[10:15]
    gather_send, gather_recv, own_sem, row_send, row_recv = scratch[15:20]
    sum_send, sum_recv, chip_send, chip_recv, load_sem, pack_sem = scratch[20:]
    low = jnp.bfloat16
    row, col, sibling, partner, _ = row_places()
    gathers = [
        Gather(mine_pre, full_pre, gather_send.at[0], gather_recv.at[0]),
        Gather(mine_back, full_back, gather_send.at[1], gather_recv.at[1]),
        Gather(mine_shared, full_shared, gather_send.at[2], gather_recv.at[2]),
    ]
    place = gathers[0].place
    greet(gathers[0].z_peers + gathers[0].y_peers + [gathers[0].x_peer])
    greet([(sibling, col), (partner, col)])
    pre_start, shared_start = w_query.shape[1], w_shared_in.shape[2]
    mine_pre[:, :pre_start] = w_query[...]
    mine_pre[:, pre_start:] = w_keyval[:, 0]
    mine_back[...] = w_out[...]
    for i in range(2):
        mine_shared[:, i * shared_start : (i + 1) * shared_start] = w_shared_in[:, i]
    mine_shared[:, 2 * shared_start : 3 * shared_start] = w_shared_out[...]
    first = inputs[...].astype(jnp.float32)
    factor = lax.rsqrt(jnp.mean(first * first, axis=1, keepdims=True) + epsilon)
    scale_one[...] = factor
    normed[...] = (first * factor * gain_attn[...]).astype(low)
    core = lax.rem(row, 2)
    own = [
        pltpu.make_async_copy(normed, group_one.at[row], own_sem.at[0]),
        pltpu.make_async_copy(grads, chip_grad.at[core], own_sem.at[1]),
        pltpu.make_async_copy(mine_pre, full_pre.at[place], own_sem.at[2]),
        pltpu.make_async_copy(mine_back, full_back.at[place], own_sem.at[3]),
        pltpu.make_async_copy(mine_shared, full_shared.at[place], own_sem.at[4]),
        pltpu.make_async_copy(normed_two, chip_two.at[core], own_sem.at[5]),
    ]
    for copy in own[:4]:
        copy.start()
    await_greetings(9)
    far_rows, near_rows, onward = row_copies([normed], [group_one], row_send, row_recv)
    chip_sems = (chip_send, chip_recv)
    share = mine_shared.shape[1] // 2
    other_shard = remote(
        mine_shared.at[:, pl.ds(0, share)],
        mine_shared.at[:, pl.ds(share, share)],
        chip_sems,
        0,
        (partner, col),
    )
    near_grads = remote(grads, chip_grad.at[core], chip_sems, 1, (sibling, col))
    near_two = remote(normed_two, chip_two.at[core], chip_sems, 2, (sibling, col))
    other_shard.start()
    gathers[0].start()
    far_rows[0].start()
    near_rows[0].start()
    gathers[1].start()
    other_shard.wait_recv()
    own[4].start()
    gathers[2].start()
    gathers[0].second()
    gathers[1].second()
    for copy in own[2:5]:
        copy.wait()
    gathers[0].third()
    near_grads.start()
    gathers[1].third()
    gathers[2].second()

    tokens = begin.shape[0]

    def document_starts(axis, shape):
        places = lax.broadcasted_iota(jnp.int32, shape, axis)
        found = jnp.zeros(shape, jnp.int32)
        bound = 0
        for i in range(NDOC - 1):
            bound = bound + lengths[0, i]
            found = jnp.where(places >= bound, bound, found)
        return places, found

    begin_row[...] = document_starts(1, begin_row.shape)[1]
    places, starts = document_starts(0, cosine.shape)
    begin[...] = starts[:, :1]
    angles = (places - starts).astype(jnp.float32) * frequency[...]
    lanes = lax.broadcasted_iota(jnp.int32, cosine.shape, 1)
    cosine[...] = jnp.cos(angles)
    sine[...] = jnp.where(lanes < cosine.shape[1] // 2, -1.0, 1.0) * jnp.sin(angles)
    bias[...] = score_bias(begin[...])

    experts = lax.broadcasted_iota(jnp.int32, order.shape, 1)
    chosen = jnp.zeros(order.shape, jnp.float32)
    for k in range(routes.shape[1]):
        chosen = jnp.where(routes[:, k : k + 1] == experts, 1.0, chosen)
    square = (order.shape[0], order.shape[0])
    before = lax.broadcasted_iota(jnp.int32, square, 1) < lax.broadcasted_iota(
        jnp.int32, square, 0
    )
    ahead = matmul(before.astype(jnp.float32).astype(low), chosen.astype(low))
    order[...] = jnp.where(chosen > 0.0, ahead, -1.0)
    code[...] = jnp.transpose(order[...]).astype(low).reshape(code.shape)

    def mark(block, carry):
        found = token_marks(code[block])
        for part in range(3):
            marks[block, part] = jnp.concatenate(
                [found[0][1].astype(low), found[part + 1][1].astype(low)], axis=1
            )
        return carry

    lax.fori_loop(0, code.shape[0], mark, 0)

    far_rows[0].wait_recv()
    onward[0].start()
    gathers[0].await_all()
    own[0].wait()
    near_rows[0].wait_recv()
    onward[0].wait_recv()
    loads = [
        pltpu.make_async_copy(group_one, rows, load_sem.at[0]),
        pltpu.make_async_copy(full_pre, w_pre, load_sem.at[1]),
        pltpu.make_async_copy(full_back, w_back, load_sem.at[2]),
    ]
    loads[0].start()
    loads[1].start()
    loads[0].wait()
    loads[1].wait()
    width = inputs.shape[1]
    pre[...] = matmul(
        rows[...].reshape(tokens, width), w_pre[...].reshape(width, w_pre.shape[4])
    )
    size = keys.shape[1]
    inner = query.shape[1]
    keys[...] = turn(pre[:, inner : inner + size], cosine[...], sine[...]).astype(low)
    values[...] = pre[:, inner + size :].astype(low)
    log_totals = jnp.zeros(norms.shape, jnp.float32)
    for head in range(inner // size):
        columns = slice(head * size, (head + 1) * size)
        turned = turn(pre[:, columns], cosine[...], sine[...]).astype(low)
        query[:, columns] = turned
        scores = matmul_t(turned, keys[...]) * (size ** (-0.5)) + bias[...]
        highest = jnp.max(scores, axis=1, keepdims=True)
        weights = jnp.exp(scores - highest)
        total = jnp.sum(weights, axis=1, keepdims=True)
        weights = (weights * (1.0 / total)).astype(low)
        attended[:, columns] = matmul(weights, values[...]).astype(low)
        log_totals = jnp.where(lanes == head, highest + jnp.log(total), log_totals)
    norms[...] = log_totals
    gathers[2].third()
    gathers[1].await_all()
    loads[2].start()
    loads[2].wait()
    parts[...] = (
        matmul_t(attended[...], w_back[...].reshape(width, inner)).astype(low).reshape(parts.shape)
    )

    copies = row_sum_copies(parts, near, far, outgoing, (sum_send, sum_recv), 0)
    copies[0].start()
    copies[1].start()
    row_sum_forward(parts, near, outgoing, copies)
    total = inputs[...].astype(jnp.float32) + row_sum_total(parts, near, far, copies)
    hidden[...] = total
    factor = lax.rsqrt(jnp.mean(total * total, axis=1, keepdims=True) + epsilon)
    normed_two[...] = (total * factor * gain_ffn[...]).astype(low)
    scale_two[...] = factor
    near_two.start()
    own[5].start()

    def pack(block, carry):
        last = normed_two[:, 3 * QUARTER :]
        for part in range(3):
            columns = slice(part * QUARTER, (part + 1) * QUARTER)
            both = jnp.concatenate([normed_two[:, columns], last], axis=0)
            staged[block, :, columns] = matmul(marks[block, part], both).astype(low)
        target = packed.at[pl.ds(pl.multiple_of(block * BLOCK, BLOCK), BLOCK)]
        pltpu.make_async_copy(staged.at[block], target, pack_sem.at[block]).start()
        return carry

    lax.fori_loop(0, code.shape[0], pack, 0)

    gathers[2].await_all()
    own[1].wait()
    own[5].wait()
    near_grads.wait()
    near_two.wait()
    other_shard.wait_send()
    near_rows[0].wait_send()
    onward[0].wait_send()
    for copy in far_rows + copies:
        copy.wait_send()
    for gather in gathers:
        gather.end()
    for block in range(staged.shape[0]):
        target = packed.at[pl.ds(block * BLOCK, BLOCK)]
        pltpu.make_async_copy(staged.at[block], target, pack_sem.at[block]).wait()


def head(inputs, gain_attn, gain_ffn, grads, lengths, routes, shards, size, expert_count):
    space = pl.BlockSpec(memory_space=pltpu.VMEM)
    away = pl.BlockSpec(memory_space=pl.ANY)
    low = jnp.bfloat16
    rows, width = inputs.shape
    tokens = 4 * rows
    shard_rows = shards[0].shape[0]
    inner = shards[0].shape[1]
    pre_width = inner + shards[1].shape[2]
    shared_width = 2 * shards[3].shape[2] + shards[4].shape[1]
    blocks = expert_count // BLOCK_EXPERTS
    spread = np.arange(size // 2, dtype=np.float32) * np.float32(2.0 / size)
    frequency = np.float32(rope_base) ** (-spread)
    frequency = jnp.asarray(np.concatenate([frequency, frequency])[None], jnp.float32)

    def full(shape, dtype):
        return jax.ShapeDtypeStruct(shape, dtype)

    return pl.pallas_call(
        head_kernel,
        out_shape=[
            full((2, 4, 4, shard_rows, pre_width), low),
            full((2, 4, 4, shard_rows, inner), low),
            full((2, 4, 4, shard_rows, 2 * shared_width), low),
            full((4, rows, width), low),
            full((2, rows, width), low),
            full((2, rows, width), low),
            full((rows, 1), jnp.float32),
            full((tokens, size), jnp.float32),
            full((tokens, size), jnp.float32),
            full((tokens, 1), jnp.int32),
            full((1, tokens), jnp.int32),
            full((tokens, inner), low),
            full((tokens, size), low),
            full((tokens, size), low),
            full((tokens, inner), low),
            full((tokens, size), jnp.float32),
            full((rows, width), jnp.float32),
            full((rows, width), low),
            full((rows, 1), jnp.float32),
            full((blocks * BLOCK, 3 * QUARTER), low),
            full((blocks, BLOCK_EXPERTS, rows), low),
            full((rows, expert_count), jnp.float32),
        ],
        in_specs=[space] * 3
        + [away, pl.BlockSpec(memory_space=pltpu.SMEM)]
        + [space] * (2 + len(shards)),
        out_specs=[away] * 6 + [space] * 13 + [away] + [space] * 2,
        scratch_shapes=[
            pltpu.VMEM((shard_rows, pre_width), low),
            pltpu.VMEM((shard_rows, inner), low),
            pltpu.VMEM((shard_rows, 2 * shared_width), low),
            pltpu.VMEM((rows, width), low),
            pltpu.VMEM((4, rows, width), low),
            pltpu.VMEM((2, 4, 4, shard_rows, pre_width), low),
            pltpu.VMEM((2, 4, 4, shard_rows, inner), low),
            pltpu.VMEM((tokens, pre_width), jnp.float32),
            pltpu.VMEM((tokens, tokens), jnp.float32),
            pltpu.VMEM((4, rows, width), low),
            pltpu.VMEM((2, rows, width), low),
            pltpu.VMEM((rows, width), low),
            pltpu.VMEM((rows, width), low),
            pltpu.VMEM((blocks, 3, BLOCK, 2 * rows), low),
            pltpu.VMEM((blocks, BLOCK, 3 * QUARTER), low),
            pltpu.SemaphoreType.DMA((3, 25)),
            pltpu.SemaphoreType.DMA((3, 25)),
            pltpu.SemaphoreType.DMA((6,)),
            pltpu.SemaphoreType.DMA((3,)),
            pltpu.SemaphoreType.DMA((3,)),
            pltpu.SemaphoreType.DMA((3,)),
            pltpu.SemaphoreType.DMA((3,)),
            pltpu.SemaphoreType.DMA((3,)),
            pltpu.SemaphoreType.DMA((3,)),
            pltpu.SemaphoreType.DMA((3,)),
            pltpu.SemaphoreType.DMA((blocks,)),
        ],
        compiler_params=pltpu.CompilerParams(
            collective_id=0, has_side_effects=True, vmem_limit_bytes=60 << 20
        ),
        cost_estimate=pl.CostEstimate(flops=0, bytes_accessed=300 << 20, transcendentals=0),
        name="head",
    )(inputs, gain_attn, gain_ffn, grads, lengths, routes, frequency, *shards)


def side_by_side_kernel(*refs):
    both, start = refs[-1], 0
    for part in refs[:-1]:
        both[:, start : start + part.shape[1]] = part[...]
        start += part.shape[1]


def side_by_side(*parts):
    shape = (parts[0].shape[0], sum(part.shape[1] for part in parts))
    return pl.pallas_call(
        side_by_side_kernel,
        out_shape=jax.ShapeDtypeStruct(shape, parts[0].dtype),
        cost_estimate=pl.CostEstimate(flops=0, bytes_accessed=6 << 20, transcendentals=0),
        name="side_by_side",
    )(*parts)


def exchange(packed):
    pairs = packed.reshape(-1, PACKED_ROWS, packed.shape[1])
    swapped = lax.all_to_all(pairs, ("row", "col"), split_axis=0, concat_axis=0, tiled=True)
    return swapped.reshape(packed.shape)


def per_device(
    block_in,
    gain_attn,
    w_query,
    w_keyval,
    w_out,
    gain_ffn,
    w_shared_in,
    w_shared_out,
    w_router,
    w_expert_in,
    w_expert_out,
    doc_lengths,
    routes,
    cotangent,
):
    row_count = lax.axis_size("row")
    rows_dev = block_in.shape[1]
    model_width = block_in.shape[2]
    expert_count = w_router.shape[1]
    expert_ff = w_expert_out.shape[2]
    inputs = block_in.reshape(rows_dev, model_width)
    grad_low = cotangent.reshape(rows_dev, model_width)
    shards = [w_query, w_keyval, w_out, w_shared_in, w_shared_out]
    (
        full_pre,
        full_back,
        full_shared,
        group_one,
        chip_grad,
        chip_two,
        scale_one,
        cosine,
        sine_table,
        begin,
        begin_row,
        *kept,
        hidden_state,
        normed_two,
        scale_two,
        send_rows,
        code,
        order,
    ) = head(
        inputs,
        gain_attn[None],
        gain_ffn[None],
        grad_low,
        doc_lengths,
        routes.reshape(rows_dev, -1),
        shards,
        w_keyval.shape[2] // 2,
        expert_count,
    )
    full_pre, full_back, full_shared, group_one, chip_grad, chip_two = (
        part.reshape(-1, part.shape[-1])
        for part in (full_pre, full_back, full_shared, group_one, chip_grad, chip_two)
    )
    received = exchange(send_rows)
    logits = matmul(normed_two, w_router)
    scores_sig = jnp.where(order >= 0.0, jax.nn.sigmoid(logits), 0.0)
    score_sum = jnp.sum(scores_sig, axis=1, keepdims=True)
    gate_weights = scores_sig / score_sum
    gates = [
        part.T.reshape(-1, BLOCK_EXPERTS, rows_dev) for part in split_low(gate_weights)
    ]
    send_grads, received = lax.optimization_barrier((pack_tokens(code, grad_low, gates), received))
    received_grads = exchange(send_grads)

    shared_width = w_shared_out.shape[1]
    shared_grads, shared_parts, shared_input = [], 0.0, 0.0
    for start in (0, 3 * shared_width):
        in_weights = full_shared[:, start : start + 2 * shared_width]
        out_weights = full_shared[:, start + 2 * shared_width : start + 3 * shared_width]
        shared_pre = matmul(chip_two, in_weights)
        shared_gate, shared_up = shared_pre[:, :shared_width], shared_pre[:, shared_width:]
        shared_act, shared_slope = swish_parts(shared_gate)
        shared_hidden = (shared_act * shared_up).astype(jnp.bfloat16)
        shared_hidden_grad = matmul(chip_grad, out_weights)
        shared_pre_grad = jnp.concatenate(
            [shared_hidden_grad * shared_up * shared_slope, shared_hidden_grad * shared_act],
            axis=1,
        ).astype(jnp.bfloat16)
        shared_grads.append(outer_sum(chip_two, shared_pre_grad).astype(jnp.bfloat16))
        shared_grads.append(outer_sum(chip_grad, shared_hidden).astype(jnp.bfloat16))
        shared_parts = shared_parts + matmul_t(shared_hidden, out_weights)
        shared_input = shared_input + matmul_t(shared_pre_grad, in_weights)
    shared_grads = side_by_side(*shared_grads)
    shared_parts, shared_input = (
        part.astype(jnp.bfloat16).reshape(2, rows_dev, model_width)
        for part in (shared_parts, shared_input)
    )

    expert_in = unpack_slots(received)
    expert_pre = jnp.einsum(
        "esd,edf->esf", expert_in, w_expert_in, preferred_element_type=jnp.float32
    )
    expert_act, expert_slope = swish_parts(expert_pre[..., :expert_ff])
    expert_hidden = (expert_act * expert_pre[..., expert_ff:]).astype(jnp.bfloat16)
    expert_out = jnp.einsum(
        "esf,edf->esd", expert_hidden, w_expert_out, preferred_element_type=jnp.float32
    ).astype(jnp.bfloat16)
    send_out, received_grads = lax.optimization_barrier((pack_slots(expert_out), received_grads))
    returned = exchange(send_out)

    out_grad = unpack_slots(received_grads)
    hidden_grad = jnp.einsum(
        "esd,edf->esf", out_grad, w_expert_out, preferred_element_type=jnp.float32
    )
    expert_pre_grad = jnp.concatenate(
        [hidden_grad * expert_pre[..., expert_ff:] * expert_slope, hidden_grad * expert_act], axis=2
    ).astype(jnp.bfloat16)
    slot_grad = jnp.einsum(
        "esf,edf->esd", expert_pre_grad, w_expert_in, preferred_element_type=jnp.float32
    ).astype(jnp.bfloat16)
    send_back, returned = lax.optimization_barrier((pack_slots(slot_grad), returned))
    returned_grad = exchange(send_back)
    grad_expert_out = jnp.einsum(
        "esd,esf->edf", out_grad, expert_hidden, preferred_element_type=jnp.float32
    )
    grad_expert_in = jnp.einsum(
        "esd,esf->edf", expert_in, expert_pre_grad, preferred_element_type=jnp.float32
    )
    routed_branch, gate_grads = sum_gated(code, returned, send_grads, gates)
    stream = hidden_state + routed_branch
    gate_grads = gate_grads.transpose(1, 0, 2).reshape(rows_dev, expert_count)
    logit_grad = (
        (1.0 - scores_sig)
        * (gate_grads - gate_weights * jnp.sum(gate_grads, axis=1, keepdims=True))
    ).astype(jnp.bfloat16)
    router_parts = outer_sum(normed_two, logit_grad).astype(jnp.bfloat16)
    router_parts = router_parts.reshape(row_count, -1, expert_count)
    router_input = matmul_t(logit_grad, w_router)
    shadowed = (router_input, router_parts, stream, shared_grads, group_one.T, all_marks(code))
    returned_grad, shadowed, grad_expert_in, grad_expert_out = lax.optimization_barrier(
        (returned_grad, shadowed, grad_expert_in, grad_expert_out)
    )
    router_input, router_parts, stream, shared_grads, group_one_t, marks = shadowed

    widths = [part.size // part.shape[0] for part in shards]
    hidden_total, input_back, block_out, router_sum, gain_attn_sum, gain_ffn_sum, *sums = tail(
        (
            returned_grad,
            marks,
            router_input,
            hidden_state,
            group_one_t,
            full_pre,
            full_back,
            shared_parts,
            stream,
            shared_input,
        ),
        (
            scale_two,
            gain_ffn[None],
            grad_low,
            router_parts,
            shared_grads.reshape(2, 4, 4, -1, shared_grads.shape[1]),
        ),
        kept,
        (cosine, sine_table, begin, begin_row),
        (inputs, scale_one, gain_attn[None]),
        widths,
    )
    return (
        block_out.reshape(1, rows_dev, model_width),
        (hidden_total + input_back).reshape(1, rows_dev, model_width),
        gain_attn_sum[0],
        sums[0],
        sums[1],
        sums[2],
        gain_ffn_sum[0],
        sums[3],
        sums[4],
        router_sum.reshape(model_width, expert_count).astype(jnp.float32),
        grad_expert_in,
        grad_expert_out,
    )


def solution(mesh):
    in_specs = (
        P("col", "row", None),
        P(),
        P("col", "row"),
        P("col", "row", None),
        P("col", "row"),
        P(),
        P("col", None, "row"),
        P("col", "row"),
        P(),
        P(("row", "col"), None, None),
        P(("row", "col"), None, None),
        P("col", None),
        P("col", "row", None),
        P("col", "row", None),
    )
    out_specs = (
        P("col", "row", None),
        P("col", "row", None),
        P(),
        P("col", "row"),
        P("col", "row", None),
        P("col", "row"),
        P(),
        P("col", None, "row"),
        P("col", "row"),
        P(),
        P(("row", "col"), None, None),
        P(("row", "col"), None, None),
    )
    return jax.shard_map(
        per_device, mesh=mesh, in_specs=in_specs, out_specs=out_specs, check_vma=False
    )
```

```python
import functools

import jax
import jax.numpy as jnp
import numpy as np
from jax import lax
from jax.experimental import pallas as pl
from jax.experimental.pallas import tpu as pltpu
from jax.sharding import PartitionSpec as P

epsilon = 1e-06
rope_base = 10000.0
masked_score = -1e30

EXPERT_ROWS = 6
PAIR_ROWS = 12
PACKED_ROWS = 16
BLOCK_PAIRS = 16
BLOCK = BLOCK_PAIRS * PACKED_ROWS
BLOCK_EXPERTS = 2 * BLOCK_PAIRS
BLOCK_SLOTS = BLOCK_PAIRS * EXPERT_ROWS
QUARTER = 512
SIDE = 128
MESH = pl.DeviceIdType.MESH
NDOC = 4


def swish_parts(pre_act):
    logistic = jax.nn.sigmoid(pre_act)
    return (pre_act * logistic, logistic * (1.0 + pre_act * (1.0 - logistic)))


def matmul(matrix, partner):
    return jnp.dot(matrix, partner, preferred_element_type=jnp.float32)


def matmul_t(matrix, partner):
    return lax.dot_general(
        matrix, partner, (((1,), (1,)), ((), ())), preferred_element_type=jnp.float32
    )


def outer_sum(matrix, partner):
    return lax.dot_general(
        matrix, partner, (((0,), (0,)), ((), ())), preferred_element_type=jnp.float32
    )


def split_low(values):
    high = values.astype(jnp.bfloat16)
    return high, (values - high.astype(jnp.float32)).astype(jnp.bfloat16)


def row_places():
    row, col = lax.axis_index("row"), lax.axis_index("col")
    chip, core = row // 2, lax.rem(row, 2)
    sibling = chip * 2 + (1 - core)
    partner = (1 - chip) * 2 + core
    across = (1 - chip) * 2 + (1 - core)
    return row, col, sibling, partner, across


def row_copies(sources, targets, send_sem, recv_sem):
    row, col, sibling, partner, _ = row_places()

    def send(origin, target, peer, i):
        return pltpu.make_async_remote_copy(
            src_ref=origin,
            dst_ref=target,
            send_sem=send_sem.at[i],
            recv_sem=recv_sem.at[i],
            device_id=(peer, col),
            device_id_type=MESH,
        )

    far, near, onward = [], [], []
    for i, (source, target) in enumerate(zip(sources, targets)):
        far.append(send(source, target.at[row], partner, 3 * i))
        near.append(send(source, target.at[row], sibling, 3 * i + 1))
        onward.append(send(target.at[partner], target.at[partner], sibling, 3 * i + 2))
    return far, near, onward


def greet(peers):
    barrier = pltpu.get_barrier_semaphore()
    for peer in peers:
        pl.semaphore_signal(barrier, inc=1, device_id=peer, device_id_type=MESH)


def await_greetings(count):
    pl.semaphore_wait(pltpu.get_barrier_semaphore(), count)


def turn(values, cosine, sine):
    return values * cosine + pltpu.roll(values, 64, 1) * sine


def score_bias(begin):
    shape = (begin.shape[0], begin.shape[0])
    keys = lax.broadcasted_iota(jnp.int32, shape, 1)
    allowed = (keys >= begin) & (keys <= lax.broadcasted_iota(jnp.int32, shape, 0))
    return jnp.where(allowed, 0.0, masked_score)


def remote(source, target, sems, at, peer):
    return pltpu.make_async_remote_copy(
        src_ref=source,
        dst_ref=target,
        send_sem=sems[0].at[at],
        recv_sem=sems[1].at[at],
        device_id=peer,
        device_id_type=MESH,
    )


def row_sum_copies(parts, near, far, outgoing, sems, at):
    _, col, sibling, partner, across = row_places()
    return [
        remote(parts.at[across], near.at[0], sems, at, (sibling, col)),
        remote(parts.at[sibling], near.at[1], sems, at + 1, (sibling, col)),
        remote(outgoing, far, sems, at + 2, (partner, col)),
    ]


def row_sum_forward(parts, near, outgoing, copies):
    _, _, _, partner, _ = row_places()
    copies[0].wait_recv()
    outgoing[...] = (parts[partner].astype(jnp.float32) + near[0].astype(jnp.float32)).astype(
        jnp.bfloat16
    )
    copies[2].start()


def row_sum_total(parts, near, far, copies):
    row = row_places()[0]
    copies[1].wait_recv()
    total = parts[row].astype(jnp.float32) + near[1].astype(jnp.float32)
    copies[2].wait_recv()
    return total + far[...].astype(jnp.float32)


class ScatterSum:
    def __init__(self, grads, scratch):
        self.grads = grads
        self.first, self.first_sum, self.second, self.second_sum, self.third = scratch[:5]
        self.one, self.two, self.three = scratch[5:7], scratch[7:9], scratch[9:11]
        row, col = lax.axis_index("row"), lax.axis_index("col")
        x, z, y = col // 16, lax.rem(col // 4, 4), lax.rem(col, 4)
        self.place = (x, z, y)
        self.half_rows = grads.shape[3] // 2
        self.y_peers = [(row, x * 16 + z * 4 + lax.rem(y + i, 4)) for i in (1, 2, 3)]
        self.z_peers = [(row, x * 16 + lax.rem(z + i, 4) * 4 + y) for i in (1, 2, 3)]
        self.x_peer = (row, (1 - x) * 16 + z * 4 + y)
        self.one_copies, self.two_copies, self.three_copies = {}, {}, []

    @staticmethod
    def scratch(grads):
        half_rows, depth = grads.shape[3] // 2, grads.shape[4]
        low = jnp.bfloat16
        return [
            pltpu.VMEM((2, 3, 2, 4, half_rows, depth), low),
            pltpu.VMEM((2, 2, 4, half_rows, depth), low),
            pltpu.VMEM((2, 3, 2, half_rows, depth), low),
            pltpu.VMEM((2, half_rows, depth), low),
            pltpu.VMEM((2, half_rows, depth), low),
        ] + [pltpu.SemaphoreType.DMA((count,)) for count in (6, 6, 6, 6, 2, 2)]

    def half(self, half):
        return pl.ds(half * self.half_rows, self.half_rows)

    def start(self):
        _, z, y = self.place
        for i in range(3):
            for half in range(2):
                if half == 0:
                    source = self.grads.at[:, :, lax.rem(y + i + 1, 4), self.half(0)]
                else:
                    source = self.grads.at[:, lax.rem(z + i + 1, 4), :, self.half(1)]
                peer = (self.y_peers, self.z_peers)[half][i]
                copy = remote(source, self.first.at[half, i], self.one, half * 3 + i, peer)
                self.one_copies[half, i] = copy
                copy.start()

    def add_first(self):
        _, z, y = self.place
        for half in range(2):
            for i in range(3):
                self.one_copies[half, i].wait_recv()

            def add(k, carry, half=half):
                if half == 0:
                    total = self.grads[k // 4, lax.rem(k, 4), y, self.half(0)].astype(jnp.float32)
                else:
                    total = self.grads[k // 4, z, lax.rem(k, 4), self.half(1)].astype(jnp.float32)
                for i in range(3):
                    total = total + self.first[half, i, k // 4, lax.rem(k, 4)].astype(jnp.float32)
                self.first_sum[half, k // 4, lax.rem(k, 4)] = total.astype(jnp.bfloat16)
                return carry

            lax.fori_loop(0, 8, add, 0)
            for i in range(3):
                away = lax.rem((z, y)[half] + i + 1, 4)
                copy = remote(
                    self.first_sum.at[half, :, away],
                    self.second.at[half, i],
                    self.two,
                    half * 3 + i,
                    (self.z_peers, self.y_peers)[half][i],
                )
                self.two_copies[half, i] = copy
                copy.start()

    def second_total(self, owner_x, half):
        _, z, y = self.place
        total = self.first_sum[half, owner_x, (z, y)[half]].astype(jnp.float32)
        for i in range(3):
            total = total + self.second[half, i, owner_x].astype(jnp.float32)
        return total

    def add_second(self):
        x = self.place[0]
        for half in range(2):
            for i in range(3):
                self.two_copies[half, i].wait_recv()
            self.second_sum[half] = self.second_total(1 - x, half).astype(jnp.bfloat16)
            copy = remote(
                self.second_sum.at[half], self.third.at[half], self.three, half, self.x_peer
            )
            self.three_copies.append(copy)
            copy.start()

    def add_third(self, pieces):
        x = self.place[0]
        for half in range(2):
            total = self.second_total(x, half)
            self.three_copies[half].wait_recv()
            total = total + self.third[half].astype(jnp.float32)
            start = 0
            for piece in pieces:
                width = piece.shape[-1]
                if len(piece.shape) == 3:
                    piece[self.half(half), 0] = total[:, start : start + width]
                else:
                    piece[self.half(half)] = total[:, start : start + width]
                start += width

    def end(self):
        for copy in [*self.one_copies.values(), *self.two_copies.values(), *self.three_copies]:
            copy.wait_send()


class RouterSum:
    def __init__(self, part, block, scratch):
        self.part, self.block = part, block
        self.in_y, self.sum_y, self.in_z, self.sum_z, self.in_x = scratch[:5]
        self.sems = scratch[5:]
        row, col = lax.axis_index("row"), lax.axis_index("col")
        x, z, y = col // 16, lax.rem(col // 4, 4), lax.rem(col, 4)
        self.place = (x, z, y)
        self.y_near = [lax.rem(y + i, 4) for i in (1, 2, 3)]
        self.z_near = [lax.rem(z + i, 4) for i in (1, 2, 3)]
        self.y_peers = [(row, x * 16 + z * 4 + near) for near in self.y_near]
        self.z_peers = [(row, x * 16 + near * 4 + y) for near in self.z_near]
        self.x_peer = (row, (1 - x) * 16 + z * 4 + y)
        self.copies = {}

    @staticmethod
    def scratch(share):
        low = jnp.bfloat16
        return [
            pltpu.VMEM((3, 2, 4, *share), low),
            pltpu.VMEM((2, 4, *share), low),
            pltpu.VMEM((3, 2, *share), low),
            pltpu.VMEM((2, *share), low),
            pltpu.VMEM(share, low),
            pltpu.SemaphoreType.DMA((14,)),
            pltpu.SemaphoreType.DMA((14,)),
        ]

    def send(self, stage, at, sources, targets, peers):
        copies = [
            remote(source, target, self.sems, at + i, peer)
            for i, (source, target, peer) in enumerate(zip(sources, targets, peers))
        ]
        for copy in copies:
            copy.start()
        self.copies[stage] = copies

    def wait(self, stage):
        for copy in self.copies[stage]:
            copy.wait_recv()

    def start(self):
        sources = [self.part.at[:, :, near] for near in self.y_near]
        self.send(0, 0, sources, [self.in_y.at[i] for i in range(3)], self.y_peers)

    def add_y(self):
        self.wait(0)
        total = self.part[:, :, self.place[2]].astype(jnp.float32)
        for i in range(3):
            total = total + self.in_y[i].astype(jnp.float32)
        self.sum_y[...] = total.astype(jnp.bfloat16)
        sources = [self.sum_y.at[:, near] for near in self.z_near]
        self.send(1, 3, sources, [self.in_z.at[i] for i in range(3)], self.z_peers)

    def add_z(self):
        self.wait(1)
        total = self.sum_y[:, self.place[1]].astype(jnp.float32)
        for i in range(3):
            total = total + self.in_z[i].astype(jnp.float32)
        self.sum_z[...] = total.astype(jnp.bfloat16)
        self.send(2, 6, [self.sum_z.at[1 - self.place[0]]], [self.in_x], [self.x_peer])

    def add_x(self):
        self.wait(2)
        x, z, y = self.place
        total = self.sum_z[x].astype(jnp.float32) + self.in_x[...].astype(jnp.float32)
        self.block[x, z, y] = total.astype(jnp.bfloat16)
        own = self.block.at[x, z, y]
        self.send(3, 7, [own], [own], [self.x_peer])

    def spread_z(self):
        self.wait(3)
        own = self.block.at[:, self.place[1], self.place[2]]
        self.send(4, 8, [own] * 3, [own] * 3, self.z_peers)

    def spread_y(self):
        self.wait(4)
        own = self.block.at[:, :, self.place[2]]
        self.send(5, 11, [own] * 3, [own] * 3, self.y_peers)

    def end(self):
        for copies in self.copies.values():
            for copy in copies:
                copy.wait_send()


def attention_back_rows(start, refs, sums):
    group, w_back, query, keys, values, norms, cosine, sine, begin, begin_row = refs
    back, pre_grad, bias, bias_t, deltas, key_grad, value_grad = sums
    low = jnp.bfloat16
    size = keys.shape[1]
    inner = query.shape[1]
    count = bias.shape[0]
    rows = pl.ds(pl.multiple_of(start, count), count)
    scale = size ** (-0.5)
    branch = group[pl.ds(start // 128, count // 128)].reshape(count, group.shape[2])
    back[rows] = matmul(branch, w_back[...]).astype(low)
    first = begin[rows]
    key_places = lax.broadcasted_iota(jnp.int32, bias.shape, 1)
    places = start + lax.broadcasted_iota(jnp.int32, bias.shape, 0)
    bias[...] = jnp.where((key_places >= first) & (key_places <= places), 0.0, masked_score)
    lanes = lax.broadcasted_iota(jnp.int32, deltas.shape, 1)
    all_deltas = jnp.zeros(deltas.shape, jnp.float32)
    for head in range(inner // size):
        columns = slice(head * size, (head + 1) * size)
        turned, outer = query[rows, columns], back[rows, columns]
        scores = matmul_t(turned, keys[...]) * scale + bias[...]
        probs = jnp.exp(scores - norms[rows, head : head + 1])
        prob_grad = matmul_t(outer, values[...])
        delta = jnp.sum(probs * prob_grad, axis=1, keepdims=True)
        all_deltas = jnp.where(lanes == head, delta, all_deltas)
        score_grad = (probs * (prob_grad - delta)).astype(low)
        query_grad = matmul(score_grad, keys[...]) * scale
        pre_grad[rows, columns] = turn(query_grad, cosine[rows], -sine[rows]).astype(low)
    deltas[...] = all_deltas
    deltas_t = jnp.transpose(deltas[...])
    norms_t = jnp.transpose(norms[rows])
    first = begin_row[:, rows]
    key_places = lax.broadcasted_iota(jnp.int32, bias_t.shape, 0)
    places = start + lax.broadcasted_iota(jnp.int32, bias_t.shape, 1)
    bias_t[...] = jnp.where((key_places >= first) & (key_places <= places), 0.0, masked_score)
    for head in range(inner // size):
        columns = slice(head * size, (head + 1) * size)
        turned, outer = query[rows, columns], back[rows, columns]
        scores = matmul_t(keys[...], turned) * scale + bias_t[...]
        probs = jnp.exp(scores - norms_t[head : head + 1])
        prob_grad = matmul_t(values[...], outer)
        score_grad = (probs * (prob_grad - deltas_t[head : head + 1])).astype(low)
        key_grad[...] += matmul(score_grad, turned)
        value_grad[...] += matmul(probs.astype(low), outer)


def tail_kernel(
    packed,
    marks_in,
    router_input_in,
    hidden_in,
    group_one_t,
    full_pre,
    full_back,
    shared_parts_in,
    stream_in,
    shared_input_in,
    scale_two,
    gain_ffn,
    stream_grad,
    router_parts,
    shared_grads,
    query,
    keys,
    values_in,
    attended,
    norms,
    cosine,
    sine,
    begin,
    begin_row,
    inputs,
    scale_one,
    gain_attn,
    hidden_total,
    result,
    block_out,
    router,
    gain_attn_sum,
    gain_ffn_sum,
    *refs,
):
    pieces, scratch = refs[:5], refs[5:]
    held, marks, router_input, hidden, rows_t, w_pre, w_back, shared_parts, stream = scratch[:9]
    routed, group, back, pre_grad, bias, bias_t, deltas, key_grad, value_grad = scratch[9:18]
    parts, near, far, outgoing, router_near, router_far, router_outgoing = scratch[18:25]
    router_part, values, buffers, pre_grads, out_grads = scratch[25:30]
    load_sem, branch_send, branch_recv, row_send, row_recv, gain_send, gain_recv = scratch[30:37]
    pass_send, pass_recv, input_parts, core_near, share_sums, share_low = scratch[37:43]
    shared_scatter = ScatterSum(shared_grads, scratch[43:54])
    out_scatter = ScatterSum(out_grads, scratch[54:65])
    pre_scatter = ScatterSum(pre_grads, scratch[65:76])
    router_at = 76
    low = jnp.bfloat16
    row, col, sibling, partner, across = row_places()
    row_peers = [(peer, col) for peer in (sibling, partner, across)]
    greet(row_peers)
    greet(pre_scatter.y_peers + pre_scatter.z_peers + [pre_scatter.x_peer])
    steps, depth = 4, held.shape[1]
    inner = query.shape[1]
    sources = [packed.at[pl.ds(i * depth, depth)] for i in range(steps)]
    targets = [held.at[i % 2] for i in range(steps)]
    sources[1:1] = [marks_in]
    targets[1:1] = [marks]
    sources += [router_input_in, hidden_in, full_back, shared_parts_in]
    targets += [router_input, hidden, w_back, shared_parts]
    sources += [full_pre, group_one_t, stream_in]
    targets += [w_pre, rows_t, stream]
    loads = [
        pltpu.make_async_copy(source, target, load_sem.at[i])
        for i, (source, target) in enumerate(zip(sources, targets))
    ]
    load_parts = pltpu.make_async_copy(shared_input_in, input_parts, load_sem.at[len(loads)])
    load_parts.start()
    load_marks = loads.pop(1)
    load_marks.start()
    for load in loads[:2] + loads[steps:]:
        load.start()
    load_input, load_hidden, load_back, load_shared, load_pre, load_rows, load_stream = loads[
        steps:
    ]
    await_greetings(10)

    row_sems = (row_send, row_recv)
    router_copies = row_sum_copies(
        router_parts, router_near, router_far, router_outgoing, row_sems, 0
    )
    router_copies[0].start()
    router_copies[1].start()
    core = lax.rem(row, 2)
    load_parts.wait()
    input_copy = remote(input_parts.at[1 - core], core_near.at[0], row_sems, 3, (sibling, col))
    input_copy.start()
    shared_scatter.start()
    row_sum_forward(router_parts, router_near, router_outgoing, router_copies)

    load_marks.wait()
    for i in range(steps):
        loads[i].wait()
        rows = slice(i * depth, (i + 1) * depth)
        for part in range(4):
            columns = slice(part * QUARTER, (part + 1) * QUARTER)
            if part < 3:
                found = matmul(marks[0, :, rows], held[i % 2, :, columns])
            else:
                found = matmul(marks[1, :, rows], held[i % 2, :, :QUARTER])
                for j in (1, 2):
                    second = slice(j * QUARTER, (j + 1) * QUARTER)
                    found = found + matmul(marks[j + 1, :, rows], held[i % 2, :, second])
            routed[:, columns] = found if i == 0 else routed[:, columns] + found
        if i + 2 < steps:
            loads[i + 2].start()
    load_input.wait()
    load_hidden.wait()
    input_copy.wait_recv()
    shared_input = input_parts[core].astype(jnp.float32) + core_near[0].astype(jnp.float32)
    incoming = router_input[...] + routed[...] + shared_input
    state = hidden[...]
    factor = scale_two[...]
    weighted = gain_ffn[...] * incoming
    mean = jnp.mean(weighted * state, axis=1, keepdims=True)
    total = (
        stream_grad[...].astype(jnp.float32)
        + factor * weighted
        - state * (factor * factor * factor * mean)
    )
    hidden_total[...] = total
    group[row] = total.astype(low)
    far_rows, near_rows, onward = row_copies([group.at[row]], [group], branch_send, branch_recv)
    far_rows[0].start()
    near_rows[0].start()
    values[0, 1:2] = jnp.sum(incoming * state * factor, axis=0, keepdims=True)

    load_shared.wait()
    shared_copy = remote(shared_parts.at[1 - core], core_near.at[1], row_sems, 4, (sibling, col))
    shared_copy.start()
    router_sum = row_sum_total(router_parts, router_near, router_far, router_copies)
    router_part[...] = router_sum.astype(low).reshape(router_part.shape)
    router_scatter = RouterSum(router_part, router.at[row], scratch[router_at:])
    router_scatter.start()
    load_back.wait()
    near_rows[0].wait_recv()
    key_grad[...] = jnp.zeros_like(key_grad)
    value_grad[...] = jnp.zeros_like(value_grad)
    refs = (group, w_back, query, keys, values_in, norms, cosine, sine, begin, begin_row)
    sums = (back, pre_grad, bias, bias_t, deltas, key_grad, value_grad)
    chip = row // 2
    chip_rows = bias.shape[0]
    attention_back_rows(chip * chip_rows, refs, sums)
    shared_scatter.add_first()
    router_scatter.add_y()
    far_rows[0].wait_recv()
    onward[0].start()
    onward[0].wait_recv()

    def keep(target, block, rows):
        shaped = rows.astype(low).reshape(2, 4, 64, rows.shape[1])
        target[block // 2, 2 * (block % 2) : 2 * (block % 2) + 2] = shaped

    blocks, width = 4, group.shape[2] // 4
    for block in range(blocks):
        columns = slice(block * width, (block + 1) * width)
        rows = group[:, :, columns].reshape(4 * group.shape[1], width)
        keep(out_grads, block, outer_sum(rows, attended[...]))
    out_scatter.start()
    attention_back_rows((1 - chip) * chip_rows, refs, sums)
    router_scatter.add_z()
    shared_scatter.add_second()
    size = keys.shape[1]
    scale = size ** (-0.5)
    pre_grad[:, inner : inner + size] = turn(key_grad[...] * scale, cosine[...], -sine[...]).astype(
        low
    )
    pre_grad[:, inner + size :] = value_grad[...].astype(low)
    load_pre.wait()
    load_rows.wait()
    block_rows = parts.shape[1]
    for block in range(4):
        rows = slice(block * block_rows, (block + 1) * block_rows)
        parts[block] = matmul_t(pre_grad[rows], w_pre[...]).astype(low)
    attn_copies = row_sum_copies(parts, near.at[0], far.at[0], outgoing.at[0], row_sems, 6)
    attn_copies[0].start()
    attn_copies[1].start()
    row_sum_forward(parts, near.at[0], outgoing.at[0], attn_copies)
    for block in range(blocks):
        rows = slice(block * width, (block + 1) * width)
        keep(pre_grads, block, matmul(rows_t[rows], pre_grad[...]))
    pre_scatter.start()
    router_scatter.add_x()
    router_scatter.spread_z()

    gain_sems = (gain_send, gain_recv)
    gain_copies = []
    stages = (row_peers, pre_scatter.y_peers, pre_scatter.z_peers, [pre_scatter.x_peer])

    def start_gains(stage):
        at = 3 * stage
        for i, peer in enumerate(stages[stage]):
            gain_copies.append(
                remote(values.at[stage], buffers.at[at + i], gain_sems, at + i, peer)
            )
            gain_copies[-1].start()

    def add_gains(stage):
        at = 3 * stage
        total = values[stage]
        for i in range(len(stages[stage])):
            gain_copies[at + i].wait_recv()
            total = total + buffers[at + i]
        values[stage + 1] = total

    incoming = row_sum_total(parts, near.at[0], far.at[0], attn_copies)
    first = inputs[...].astype(jnp.float32)
    factor = scale_one[...]
    weighted = gain_attn[...] * incoming
    mean = jnp.mean(weighted * first, axis=1, keepdims=True)
    result[...] = factor * weighted - first * (factor * factor * factor * mean)
    values[0, 0:1] = jnp.sum(incoming * first * factor, axis=0, keepdims=True)
    start_gains(0)
    out_scatter.add_first()
    shared_scatter.add_third([share_sums.at[0], share_sums.at[1]])
    share_low[0] = share_sums[1].astype(low)
    share_copy = remote(share_low.at[0], share_low.at[1], row_sems, 5, (partner, col))
    share_copy.start()
    router_scatter.spread_y()
    out_scatter.add_second()
    load_stream.wait()
    shared_copy.wait_recv()
    shared = shared_parts[core].astype(jnp.float32) + core_near[1].astype(jnp.float32)
    block_out[...] = (stream[...] + shared).astype(low)
    add_gains(0)
    start_gains(1)
    pre_scatter.add_first()
    router_scatter.wait(5)
    router_rows = row_copies([router.at[row]], [router], pass_send, pass_recv)
    router_rows[0][0].start()
    router_rows[1][0].start()
    out_scatter.add_third(pieces[2:3])
    add_gains(1)
    start_gains(2)
    pre_scatter.add_second()
    add_gains(2)
    start_gains(3)
    router_rows[0][0].wait_recv()
    router_rows[2][0].start()
    share_copy.wait_recv()
    share = share_sums[0] + share_low[1].astype(jnp.float32)
    part = pieces[3].shape[2]
    for i in range(2):
        pieces[3][:, i] = share[:, i * part : (i + 1) * part]
    pieces[4][...] = share[:, 2 * part :]
    pre_scatter.add_third(pieces[:2])
    add_gains(3)
    gain_attn_sum[...] = values[4, 0:1]
    gain_ffn_sum[...] = values[4, 1:2]

    router_scatter.end()
    far_rows[0].wait_send()
    near_rows[0].wait_send()
    onward[0].wait_send()
    router_rows[0][0].wait_send()
    router_rows[1][0].wait()
    router_rows[2][0].wait()
    for done in [*router_copies, *attn_copies, *gain_copies, input_copy, shared_copy, share_copy]:
        done.wait_send()
    for scatter in (shared_scatter, out_scatter, pre_scatter):
        scatter.end()


def tail(streamed, local, kept, tables, last, widths):
    space = pl.BlockSpec(memory_space=pltpu.VMEM)
    away = pl.BlockSpec(memory_space=pl.ANY)
    low = jnp.bfloat16
    packed, marks = streamed[:2]
    router_parts, shared_grads = local[3:]
    rows, width = last[0].shape
    tokens = 4 * rows
    _, router_rows, experts = router_parts.shape
    share = (router_rows // 32, experts)
    size = kept[1].shape[1]
    inner = kept[0].shape[1]
    pre_width = widths[0] + widths[1]
    shard = width // 32
    pre_grads = jax.ShapeDtypeStruct((2, 4, 4, shard, pre_width), low)
    out_grads = jax.ShapeDtypeStruct((2, 4, 4, shard, inner), low)
    dma = pltpu.SemaphoreType.DMA
    return pl.pallas_call(
        tail_kernel,
        out_shape=[
            jax.ShapeDtypeStruct((rows, width), jnp.float32),
            jax.ShapeDtypeStruct((rows, width), jnp.float32),
            jax.ShapeDtypeStruct((rows, width), low),
            jax.ShapeDtypeStruct((4, 2, 4, 4, *share), low),
            jax.ShapeDtypeStruct((1, width), jnp.float32),
            jax.ShapeDtypeStruct((1, width), jnp.float32),
        ]
        + [
            jax.ShapeDtypeStruct(shape, jnp.float32)
            for shape in (
                (shard, widths[0]),
                (shard, 1, widths[1]),
                (shard, widths[2]),
                (shard, 2, widths[3] // 2),
                (shard, widths[4]),
            )
        ],
        in_specs=[away] * 10 + [space] * 17,
        out_specs=[space] * (6 + len(widths)),
        scratch_shapes=[
            pltpu.VMEM((2, packed.shape[0] // 4, packed.shape[1]), low),
            pltpu.VMEM(marks.shape, low),
            pltpu.VMEM((rows, width), jnp.float32),
            pltpu.VMEM((rows, width), jnp.float32),
            pltpu.VMEM((width, tokens), low),
            pltpu.VMEM((width, pre_width), low),
            pltpu.VMEM((width, inner), low),
            pltpu.VMEM((2, rows, width), low),
            pltpu.VMEM((rows, width), jnp.float32),
            pltpu.VMEM((rows, width), jnp.float32),
            pltpu.VMEM((4, rows, width), low),
            pltpu.VMEM((tokens, inner), low),
            pltpu.VMEM((tokens, pre_width), low),
            pltpu.VMEM((tokens // 2, tokens), jnp.float32),
            pltpu.VMEM((tokens, tokens // 2), jnp.float32),
            pltpu.VMEM((tokens // 2, 128), jnp.float32),
            pltpu.VMEM((tokens, size), jnp.float32),
            pltpu.VMEM((tokens, size), jnp.float32),
            pltpu.VMEM((4, rows, width), low),
            pltpu.VMEM((1, 2, rows, width), low),
            pltpu.VMEM((1, rows, width), low),
            pltpu.VMEM((1, rows, width), low),
            pltpu.VMEM((2, router_rows, experts), low),
            pltpu.VMEM((router_rows, experts), low),
            pltpu.VMEM((router_rows, experts), low),
            pltpu.VMEM((2, 4, 4, *share), low),
            pltpu.VMEM((5, 2, width), jnp.float32),
            pltpu.VMEM((10, 2, width), jnp.float32),
            pltpu.VMEM(pre_grads.shape, low),
            pltpu.VMEM(out_grads.shape, low),
            dma((13,)),
            dma((3,)),
            dma((3,)),
            dma((9,)),
            dma((9,)),
            dma((10,)),
            dma((10,)),
            dma((3,)),
            dma((3,)),
            pltpu.VMEM((2, rows, width), low),
            pltpu.VMEM((2, rows, width), low),
            pltpu.VMEM((2, shard, widths[3] + widths[4]), jnp.float32),
            pltpu.VMEM((2, shard, widths[3] + widths[4]), low),
            *ScatterSum.scratch(shared_grads),
            *ScatterSum.scratch(out_grads),
            *ScatterSum.scratch(pre_grads),
            *RouterSum.scratch(share),
        ],
        compiler_params=pltpu.CompilerParams(
            collective_id=16, has_side_effects=True, vmem_limit_bytes=60 << 20
        ),
        cost_estimate=pl.CostEstimate(flops=0, bytes_accessed=300 << 20, transcendentals=0),
        name="tail",
    )(*streamed, *local, *kept, *tables, *last)


def packed_places(shape, axis):
    index = lax.broadcasted_iota(jnp.int32, shape, axis)
    pair, place = index // PACKED_ROWS, lax.rem(index, PACKED_ROWS)
    found = []
    for part in range(-1, 3):
        if part < 0:
            valid, slot = place < PAIR_ROWS, place
        else:
            valid, slot = place >= PAIR_ROWS, 3 * (place - PAIR_ROWS) + part
        second = (slot >= EXPERT_ROWS).astype(jnp.int32)
        found.append((valid, pair, second, slot - EXPERT_ROWS * second))
    return found


def token_marks(code_block):
    marks = []
    wide = (BLOCK, BLOCK_EXPERTS)
    lanes = lax.broadcasted_iota(jnp.int32, wide, 1)
    for (valid, pair, second, _), (tall, _, _, order) in zip(
        packed_places(wide, 0), packed_places((BLOCK, SIDE), 0)
    ):
        owner = ((lanes == 2 * pair + second) & valid).astype(jnp.float32).astype(jnp.bfloat16)
        found = matmul(owner, code_block)
        hit = (found == order.astype(jnp.float32)) & tall
        marks.append((owner, hit.astype(jnp.float32)))
    return marks


def gate_weights_of(owner, hit, high, low):
    weights = hit * (matmul(owner, high) + matmul(owner, low))
    return split_low(weights)


def pack_tokens_kernel(code, values, high, low, packed):
    marks = token_marks(code[0])
    weights = [gate_weights_of(owner, hit, high[0], low[0]) for owner, hit in marks]
    last = values[:, 3 * QUARTER :]
    for part in range(3):
        columns = slice(part * QUARTER, (part + 1) * QUARTER)
        both = jnp.concatenate([*weights[0], *weights[part + 1]], axis=1)
        rows = jnp.concatenate([values[:, columns]] * 2 + [last] * 2, axis=0)
        packed[:, columns] = matmul(both, rows).astype(jnp.bfloat16)


def pack_tokens(code, values, gates):
    blocks = code.shape[0]
    width = 3 * QUARTER
    small = pl.BlockSpec((1, BLOCK_EXPERTS, SIDE), lambda i: (i, 0, 0))
    return pl.pallas_call(
        pack_tokens_kernel,
        grid=(blocks,),
        out_shape=jax.ShapeDtypeStruct((blocks * BLOCK, width), jnp.bfloat16),
        in_specs=[small, pl.BlockSpec(values.shape, lambda i: (0, 0)), small, small],
        out_specs=pl.BlockSpec((BLOCK, width), lambda i: (i, 0)),
        compiler_params=pltpu.CompilerParams(vmem_limit_bytes=32 << 20),
        cost_estimate=pl.CostEstimate(
            flops=blocks * BLOCK * 512 * width * 2, bytes_accessed=8 << 20, transcendentals=0
        ),
        name="pack_tokens",
    )(code, values, *gates)


def slot_marks():
    shape = (2 * BLOCK_SLOTS, BLOCK)
    rows = lax.broadcasted_iota(jnp.int32, shape, 0)
    marks = []
    for valid, pair, second, order in packed_places(shape, 1):
        hit = (rows == second * BLOCK_SLOTS + pair * EXPERT_ROWS + order) & valid
        marks.append(hit.astype(jnp.float32).astype(jnp.bfloat16))
    return marks


def unpack_slots_kernel(packed, values):
    marks = slot_marks()
    last = jnp.zeros((2 * BLOCK_SLOTS, QUARTER), jnp.float32)
    for part in range(3):
        columns = slice(part * QUARTER, (part + 1) * QUARTER)
        found = matmul(marks[0], packed[:, columns]).astype(jnp.bfloat16)
        values[0, :, columns] = found[:BLOCK_SLOTS]
        values[1, :, columns] = found[BLOCK_SLOTS:]
        last = last + matmul(marks[part + 1], packed[:, columns])
    last = last.astype(jnp.bfloat16)
    values[0, :, 3 * QUARTER :] = last[:BLOCK_SLOTS]
    values[1, :, 3 * QUARTER :] = last[BLOCK_SLOTS:]


def unpack_slots(packed):
    blocks = packed.shape[0] // BLOCK
    slots = blocks * BLOCK_SLOTS
    return pl.pallas_call(
        unpack_slots_kernel,
        grid=(blocks,),
        out_shape=jax.ShapeDtypeStruct((2, slots, 4 * QUARTER), jnp.bfloat16),
        in_specs=[pl.BlockSpec((BLOCK, 3 * QUARTER), lambda i: (i, 0))],
        out_specs=pl.BlockSpec((2, BLOCK_SLOTS, 4 * QUARTER), lambda i: (0, i, 0)),
        compiler_params=pltpu.CompilerParams(vmem_limit_bytes=32 << 20),
        cost_estimate=pl.CostEstimate(
            flops=blocks * 2 * BLOCK_SLOTS * BLOCK * 6 * QUARTER * 2,
            bytes_accessed=14 << 20,
            transcendentals=0,
        ),
        name="unpack_slots",
    )(packed)


def pack_slots_kernel(values, packed):
    marks = slot_marks()
    last = jnp.concatenate([values[0, :, 3 * QUARTER :], values[1, :, 3 * QUARTER :]], axis=0)
    for part in range(3):
        columns = slice(part * QUARTER, (part + 1) * QUARTER)
        rows = jnp.concatenate([values[0, :, columns], values[1, :, columns]], axis=0)
        found = outer_sum(marks[0], rows) + outer_sum(marks[part + 1], last)
        packed[:, columns] = found.astype(jnp.bfloat16)


def pack_slots(values):
    slots = values.shape[1]
    blocks = slots // BLOCK_SLOTS
    return pl.pallas_call(
        pack_slots_kernel,
        grid=(blocks,),
        out_shape=jax.ShapeDtypeStruct((blocks * BLOCK, 3 * QUARTER), jnp.bfloat16),
        in_specs=[pl.BlockSpec((2, BLOCK_SLOTS, 4 * QUARTER), lambda i: (0, i, 0))],
        out_specs=pl.BlockSpec((BLOCK, 3 * QUARTER), lambda i: (i, 0)),
        compiler_params=pltpu.CompilerParams(vmem_limit_bytes=32 << 20),
        cost_estimate=pl.CostEstimate(
            flops=blocks * 2 * BLOCK_SLOTS * BLOCK * 6 * QUARTER * 2,
            bytes_accessed=14 << 20,
            transcendentals=0,
        ),
        name="pack_slots",
    )(values)


def marks_kernel(code, marks):
    wide = (BLOCK_EXPERTS, BLOCK)
    owners = lax.broadcasted_iota(jnp.int32, wide, 0)
    for i, ((valid, pair, second, _), (tall, _, _, order)) in enumerate(
        zip(packed_places(wide, 1), packed_places((code.shape[1], BLOCK), 1))
    ):
        owner = ((owners == 2 * pair + second) & valid).astype(jnp.float32).astype(jnp.bfloat16)
        hit = (matmul(code[0], owner) == order.astype(jnp.float32)) & tall
        marks[i] = hit.astype(jnp.float32).astype(jnp.bfloat16)


def all_marks(code):
    blocks, experts, tokens = code.shape
    return pl.pallas_call(
        marks_kernel,
        grid=(blocks,),
        out_shape=jax.ShapeDtypeStruct((4, tokens, blocks * BLOCK), jnp.bfloat16),
        in_specs=[pl.BlockSpec((1, tokens, experts), lambda i: (i, 0, 0))],
        out_specs=pl.BlockSpec((4, tokens, BLOCK), lambda i: (0, 0, i)),
        cost_estimate=pl.CostEstimate(flops=1 << 26, bytes_accessed=4 << 20, transcendentals=0),
        name="all_marks",
    )(code.transpose(0, 2, 1))


def sum_gated_kernel(code, packed, grads, high, low, total, gate_grads):
    @pl.when(pl.program_id(0) == 0)
    def _():
        total[...] = jnp.zeros_like(total)

    marks = token_marks(code[0])
    weights = [gate_weights_of(owner, hit, high[0], low[0]) for owner, hit in marks]
    last = jnp.zeros((total.shape[0], QUARTER), jnp.float32)
    whole = jnp.zeros((BLOCK, 1), jnp.float32)
    products = []
    for part in range(3):
        columns = slice(part * QUARTER, (part + 1) * QUARTER)
        rows = packed[:, columns]
        total[:, columns] += outer_sum(weights[0][0], rows) + outer_sum(weights[0][1], rows)
        last = last + outer_sum(weights[part + 1][0], rows) + outer_sum(weights[part + 1][1], rows)
        dots = jnp.sum(
            rows.astype(jnp.float32) * grads[:, columns].astype(jnp.float32),
            axis=1,
            keepdims=True,
        )
        whole = whole + dots
        products.append(dots)
    total[:, 3 * QUARTER :] += last
    found = jnp.zeros(gate_grads.shape[1:], jnp.float32)
    for (owner, hit), dots in zip(marks, [whole, *products]):
        hit = hit.astype(jnp.bfloat16)
        for spread in split_low(dots * owner.astype(jnp.float32)):
            found = found + outer_sum(hit, spread)
    gate_grads[0] = found


def sum_gated(code, packed, grads, gates):
    blocks, _, tokens = code.shape
    small = pl.BlockSpec((1, BLOCK_EXPERTS, tokens), lambda i: (i, 0, 0))
    wide = pl.BlockSpec((BLOCK, 3 * QUARTER), lambda i: (i, 0))
    return pl.pallas_call(
        sum_gated_kernel,
        grid=(blocks,),
        out_shape=[
            jax.ShapeDtypeStruct((tokens, 4 * QUARTER), jnp.float32),
            jax.ShapeDtypeStruct((blocks, tokens, BLOCK_EXPERTS), jnp.float32),
        ],
        in_specs=[small, wide, wide, small, small],
        out_specs=[
            pl.BlockSpec((tokens, 4 * QUARTER), lambda i: (0, 0)),
            pl.BlockSpec((1, tokens, BLOCK_EXPERTS), lambda i: (i, 0, 0)),
        ],
        compiler_params=pltpu.CompilerParams(vmem_limit_bytes=32 << 20),
        cost_estimate=pl.CostEstimate(
            flops=blocks * BLOCK * 128 * 12 * QUARTER * 2,
            bytes_accessed=14 << 20,
            transcendentals=0,
        ),
        name="sum_gated",
    )(code, packed, grads, *gates)


class Gather:
    def __init__(self, mine, full, send_sem, recv_sem):
        self.mine, self.full = mine, full
        self.sems = (send_sem, recv_sem)
        row, col = lax.axis_index("row"), lax.axis_index("col")
        x, z, y = col // 16, lax.rem(col // 4, 4), lax.rem(col, 4)
        self.place = (x, z, y)
        self.z_peers = [(row, x * 16 + lax.rem(z + i, 4) * 4 + y) for i in (1, 3, 2)]
        self.y_peers = [(row, x * 16 + z * 4 + lax.rem(y + i, 4)) for i in (1, 3, 2)]
        self.x_peer = (row, (1 - x) * 16 + z * 4 + y)
        self.copies = {}

    def rows(self, half):
        half_rows = self.full.shape[3] // 2
        return pl.ds(half * half_rows, half_rows)

    def send(self, key, source, target, peers):
        at = 1 + 3 * len(self.copies) - 3 if self.copies else 0
        copies = [
            remote(source, target, self.sems, at + i, peer) for i, peer in enumerate(peers)
        ]
        for copy in copies:
            copy.start()
        self.copies[key] = copies

    def wait(self, *keys):
        for key in keys:
            for copy in self.copies[key]:
                copy.wait_recv()

    def start(self):
        x, z, y = self.place
        self.send("x", self.mine, self.full.at[x, z, y], [self.x_peer])
        for half, peers in enumerate((self.z_peers, self.y_peers)):
            rows = self.rows(half)
            target = self.full.at[x, z, y, rows]
            self.send((0, half), self.mine.at[rows], target, peers)

    def second(self):
        x, z, y = self.place
        self.wait("x")
        for half, peers in enumerate((self.z_peers, self.y_peers)):
            target = self.full.at[1 - x, z, y, self.rows(half)]
            self.send((1, half), target, target, peers)

    def third(self):
        x, z, y = self.place
        for turn, owner_x in enumerate((x, 1 - x)):
            self.wait((turn, 0))
            target = self.full.at[owner_x, :, y, self.rows(0)]
            self.send((2 + turn, 0), target, target, self.y_peers)
            self.wait((turn, 1))
            target = self.full.at[owner_x, z, :, self.rows(1)]
            self.send((2 + turn, 1), target, target, self.z_peers)

    def await_all(self):
        self.wait((2, 0), (2, 1), (3, 0), (3, 1))

    def end(self):
        for copies in self.copies.values():
            for copy in copies:
                copy.wait_send()


def head_kernel(
    inputs,
    gain_attn,
    gain_ffn,
    grads,
    lengths,
    routes,
    frequency,
    w_query,
    w_keyval,
    w_out,
    w_shared_in,
    w_shared_out,
    full_pre,
    full_back,
    full_shared,
    group_one,
    chip_grad,
    chip_two,
    scale_one,
    cosine,
    sine,
    begin,
    begin_row,
    query,
    keys,
    values,
    attended,
    norms,
    hidden,
    normed_two,
    scale_two,
    packed,
    code,
    order,
    *scratch,
):
    mine_pre, mine_back, mine_shared, normed, rows, w_pre, w_back, pre, bias, parts = scratch[:10]
    near, far, outgoing, marks, staged = scratch[10:15]
    gather_send, gather_recv, own_sem, row_send, row_recv = scratch[15:20]
    sum_send, sum_recv, chip_send, chip_recv, load_sem, pack_sem = scratch[20:]
    low = jnp.bfloat16
    row, col, sibling, partner, _ = row_places()
    gathers = [
        Gather(mine_pre, full_pre, gather_send.at[0], gather_recv.at[0]),
        Gather(mine_back, full_back, gather_send.at[1], gather_recv.at[1]),
        Gather(mine_shared, full_shared, gather_send.at[2], gather_recv.at[2]),
    ]
    place = gathers[0].place
    greet(gathers[0].z_peers + gathers[0].y_peers + [gathers[0].x_peer])
    greet([(sibling, col), (partner, col)])
    pre_start, shared_start = w_query.shape[1], w_shared_in.shape[2]
    mine_pre[:, :pre_start] = w_query[...]
    mine_pre[:, pre_start:] = w_keyval[:, 0]
    mine_back[...] = w_out[...]
    for i in range(2):
        mine_shared[:, i * shared_start : (i + 1) * shared_start] = w_shared_in[:, i]
    mine_shared[:, 2 * shared_start : 3 * shared_start] = w_shared_out[...]
    first = inputs[...].astype(jnp.float32)
    factor = lax.rsqrt(jnp.mean(first * first, axis=1, keepdims=True) + epsilon)
    scale_one[...] = factor
    normed[...] = (first * factor * gain_attn[...]).astype(low)
    core = lax.rem(row, 2)
    own = [
        pltpu.make_async_copy(normed, group_one.at[row], own_sem.at[0]),
        pltpu.make_async_copy(grads, chip_grad.at[core], own_sem.at[1]),
        pltpu.make_async_copy(mine_pre, full_pre.at[place], own_sem.at[2]),
        pltpu.make_async_copy(mine_back, full_back.at[place], own_sem.at[3]),
        pltpu.make_async_copy(mine_shared, full_shared.at[place], own_sem.at[4]),
        pltpu.make_async_copy(normed_two, chip_two.at[core], own_sem.at[5]),
    ]
    for copy in own[:4]:
        copy.start()
    await_greetings(9)
    far_rows, near_rows, onward = row_copies([normed], [group_one], row_send, row_recv)
    chip_sems = (chip_send, chip_recv)
    share = mine_shared.shape[1] // 2
    other_shard = remote(
        mine_shared.at[:, pl.ds(0, share)],
        mine_shared.at[:, pl.ds(share, share)],
        chip_sems,
        0,
        (partner, col),
    )
    near_grads = remote(grads, chip_grad.at[core], chip_sems, 1, (sibling, col))
    near_two = remote(normed_two, chip_two.at[core], chip_sems, 2, (sibling, col))
    other_shard.start()
    gathers[0].start()
    far_rows[0].start()
    near_rows[0].start()
    gathers[1].start()
    other_shard.wait_recv()
    own[4].start()
    gathers[2].start()
    gathers[0].second()
    gathers[1].second()
    for copy in own[2:5]:
        copy.wait()
    gathers[0].third()
    near_grads.start()
    gathers[1].third()
    gathers[2].second()

    tokens = begin.shape[0]

    def document_starts(axis, shape):
        places = lax.broadcasted_iota(jnp.int32, shape, axis)
        found = jnp.zeros(shape, jnp.int32)
        bound = 0
        for i in range(NDOC - 1):
            bound = bound + lengths[0, i]
            found = jnp.where(places >= bound, bound, found)
        return places, found

    begin_row[...] = document_starts(1, begin_row.shape)[1]
    places, starts = document_starts(0, cosine.shape)
    begin[...] = starts[:, :1]
    angles = (places - starts).astype(jnp.float32) * frequency[...]
    lanes = lax.broadcasted_iota(jnp.int32, cosine.shape, 1)
    cosine[...] = jnp.cos(angles)
    sine[...] = jnp.where(lanes < cosine.shape[1] // 2, -1.0, 1.0) * jnp.sin(angles)
    bias[...] = score_bias(begin[...])

    experts = lax.broadcasted_iota(jnp.int32, order.shape, 1)
    chosen = jnp.zeros(order.shape, jnp.float32)
    for k in range(routes.shape[1]):
        chosen = jnp.where(routes[:, k : k + 1] == experts, 1.0, chosen)
    square = (order.shape[0], order.shape[0])
    before = lax.broadcasted_iota(jnp.int32, square, 1) < lax.broadcasted_iota(
        jnp.int32, square, 0
    )
    ahead = matmul(before.astype(jnp.float32).astype(low), chosen.astype(low))
    order[...] = jnp.where(chosen > 0.0, ahead, -1.0)
    code[...] = jnp.transpose(order[...]).astype(low).reshape(code.shape)

    def mark(block, carry):
        found = token_marks(code[block])
        for part in range(3):
            marks[block, part] = jnp.concatenate(
                [found[0][1].astype(low), found[part + 1][1].astype(low)], axis=1
            )
        return carry

    lax.fori_loop(0, code.shape[0], mark, 0)

    far_rows[0].wait_recv()
    onward[0].start()
    gathers[0].await_all()
    own[0].wait()
    near_rows[0].wait_recv()
    onward[0].wait_recv()
    loads = [
        pltpu.make_async_copy(group_one, rows, load_sem.at[0]),
        pltpu.make_async_copy(full_pre, w_pre, load_sem.at[1]),
        pltpu.make_async_copy(full_back, w_back, load_sem.at[2]),
    ]
    loads[0].start()
    loads[1].start()
    loads[0].wait()
    loads[1].wait()
    width = inputs.shape[1]
    pre[...] = matmul(
        rows[...].reshape(tokens, width), w_pre[...].reshape(width, w_pre.shape[4])
    )
    size = keys.shape[1]
    inner = query.shape[1]
    keys[...] = turn(pre[:, inner : inner + size], cosine[...], sine[...]).astype(low)
    values[...] = pre[:, inner + size :].astype(low)
    log_totals = jnp.zeros(norms.shape, jnp.float32)
    for head in range(inner // size):
        columns = slice(head * size, (head + 1) * size)
        turned = turn(pre[:, columns], cosine[...], sine[...]).astype(low)
        query[:, columns] = turned
        scores = matmul_t(turned, keys[...]) * (size ** (-0.5)) + bias[...]
        highest = jnp.max(scores, axis=1, keepdims=True)
        weights = jnp.exp(scores - highest)
        total = jnp.sum(weights, axis=1, keepdims=True)
        weights = (weights * (1.0 / total)).astype(low)
        attended[:, columns] = matmul(weights, values[...]).astype(low)
        log_totals = jnp.where(lanes == head, highest + jnp.log(total), log_totals)
    norms[...] = log_totals
    gathers[2].third()
    gathers[1].await_all()
    loads[2].start()
    loads[2].wait()
    parts[...] = (
        matmul_t(attended[...], w_back[...].reshape(width, inner)).astype(low).reshape(parts.shape)
    )

    copies = row_sum_copies(parts, near, far, outgoing, (sum_send, sum_recv), 0)
    copies[0].start()
    copies[1].start()
    row_sum_forward(parts, near, outgoing, copies)
    total = inputs[...].astype(jnp.float32) + row_sum_total(parts, near, far, copies)
    hidden[...] = total
    factor = lax.rsqrt(jnp.mean(total * total, axis=1, keepdims=True) + epsilon)
    normed_two[...] = (total * factor * gain_ffn[...]).astype(low)
    scale_two[...] = factor
    near_two.start()
    own[5].start()

    def pack(block, carry):
        last = normed_two[:, 3 * QUARTER :]
        for part in range(3):
            columns = slice(part * QUARTER, (part + 1) * QUARTER)
            both = jnp.concatenate([normed_two[:, columns], last], axis=0)
            staged[block, :, columns] = matmul(marks[block, part], both).astype(low)
        target = packed.at[pl.ds(pl.multiple_of(block * BLOCK, BLOCK), BLOCK)]
        pltpu.make_async_copy(staged.at[block], target, pack_sem.at[block]).start()
        return carry

    lax.fori_loop(0, code.shape[0], pack, 0)

    gathers[2].await_all()
    own[1].wait()
    own[5].wait()
    near_grads.wait()
    near_two.wait()
    other_shard.wait_send()
    near_rows[0].wait_send()
    onward[0].wait_send()
    for copy in far_rows + copies:
        copy.wait_send()
    for gather in gathers:
        gather.end()
    for block in range(staged.shape[0]):
        target = packed.at[pl.ds(block * BLOCK, BLOCK)]
        pltpu.make_async_copy(staged.at[block], target, pack_sem.at[block]).wait()


def head(inputs, gain_attn, gain_ffn, grads, lengths, routes, shards, size, expert_count):
    space = pl.BlockSpec(memory_space=pltpu.VMEM)
    away = pl.BlockSpec(memory_space=pl.ANY)
    low = jnp.bfloat16
    rows, width = inputs.shape
    tokens = 4 * rows
    shard_rows = shards[0].shape[0]
    inner = shards[0].shape[1]
    pre_width = inner + shards[1].shape[2]
    shared_width = 2 * shards[3].shape[2] + shards[4].shape[1]
    blocks = expert_count // BLOCK_EXPERTS
    spread = np.arange(size // 2, dtype=np.float32) * np.float32(2.0 / size)
    frequency = np.float32(rope_base) ** (-spread)
    frequency = jnp.asarray(np.concatenate([frequency, frequency])[None], jnp.float32)

    def full(shape, dtype):
        return jax.ShapeDtypeStruct(shape, dtype)

    return pl.pallas_call(
        head_kernel,
        out_shape=[
            full((2, 4, 4, shard_rows, pre_width), low),
            full((2, 4, 4, shard_rows, inner), low),
            full((2, 4, 4, shard_rows, 2 * shared_width), low),
            full((4, rows, width), low),
            full((2, rows, width), low),
            full((2, rows, width), low),
            full((rows, 1), jnp.float32),
            full((tokens, size), jnp.float32),
            full((tokens, size), jnp.float32),
            full((tokens, 1), jnp.int32),
            full((1, tokens), jnp.int32),
            full((tokens, inner), low),
            full((tokens, size), low),
            full((tokens, size), low),
            full((tokens, inner), low),
            full((tokens, size), jnp.float32),
            full((rows, width), jnp.float32),
            full((rows, width), low),
            full((rows, 1), jnp.float32),
            full((blocks * BLOCK, 3 * QUARTER), low),
            full((blocks, BLOCK_EXPERTS, rows), low),
            full((rows, expert_count), jnp.float32),
        ],
        in_specs=[space] * 3
        + [away, pl.BlockSpec(memory_space=pltpu.SMEM)]
        + [space] * (2 + len(shards)),
        out_specs=[away] * 6 + [space] * 13 + [away] + [space] * 2,
        scratch_shapes=[
            pltpu.VMEM((shard_rows, pre_width), low),
            pltpu.VMEM((shard_rows, inner), low),
            pltpu.VMEM((shard_rows, 2 * shared_width), low),
            pltpu.VMEM((rows, width), low),
            pltpu.VMEM((4, rows, width), low),
            pltpu.VMEM((2, 4, 4, shard_rows, pre_width), low),
            pltpu.VMEM((2, 4, 4, shard_rows, inner), low),
            pltpu.VMEM((tokens, pre_width), jnp.float32),
            pltpu.VMEM((tokens, tokens), jnp.float32),
            pltpu.VMEM((4, rows, width), low),
            pltpu.VMEM((2, rows, width), low),
            pltpu.VMEM((rows, width), low),
            pltpu.VMEM((rows, width), low),
            pltpu.VMEM((blocks, 3, BLOCK, 2 * rows), low),
            pltpu.VMEM((blocks, BLOCK, 3 * QUARTER), low),
            pltpu.SemaphoreType.DMA((3, 25)),
            pltpu.SemaphoreType.DMA((3, 25)),
            pltpu.SemaphoreType.DMA((6,)),
            pltpu.SemaphoreType.DMA((3,)),
            pltpu.SemaphoreType.DMA((3,)),
            pltpu.SemaphoreType.DMA((3,)),
            pltpu.SemaphoreType.DMA((3,)),
            pltpu.SemaphoreType.DMA((3,)),
            pltpu.SemaphoreType.DMA((3,)),
            pltpu.SemaphoreType.DMA((3,)),
            pltpu.SemaphoreType.DMA((blocks,)),
        ],
        compiler_params=pltpu.CompilerParams(
            collective_id=0, has_side_effects=True, vmem_limit_bytes=60 << 20
        ),
        cost_estimate=pl.CostEstimate(flops=0, bytes_accessed=300 << 20, transcendentals=0),
        name="head",
    )(inputs, gain_attn, gain_ffn, grads, lengths, routes, frequency, *shards)


def side_by_side_kernel(*refs):
    both, start = refs[-1], 0
    for part in refs[:-1]:
        both[:, start : start + part.shape[1]] = part[...]
        start += part.shape[1]


def side_by_side(*parts):
    shape = (parts[0].shape[0], sum(part.shape[1] for part in parts))
    return pl.pallas_call(
        side_by_side_kernel,
        out_shape=jax.ShapeDtypeStruct(shape, parts[0].dtype),
        cost_estimate=pl.CostEstimate(flops=0, bytes_accessed=6 << 20, transcendentals=0),
        name="side_by_side",
    )(*parts)


def exchange(packed):
    pairs = packed.reshape(-1, PACKED_ROWS, packed.shape[1])
    swapped = lax.all_to_all(pairs, ("row", "col"), split_axis=0, concat_axis=0, tiled=True)
    return swapped.reshape(packed.shape)


def per_device(
    block_in,
    gain_attn,
    w_query,
    w_keyval,
    w_out,
    gain_ffn,
    w_shared_in,
    w_shared_out,
    w_router,
    w_expert_in,
    w_expert_out,
    doc_lengths,
    routes,
    cotangent,
):
    row_count = lax.axis_size("row")
    rows_dev = block_in.shape[1]
    model_width = block_in.shape[2]
    expert_count = w_router.shape[1]
    expert_ff = w_expert_out.shape[2]
    inputs = block_in.reshape(rows_dev, model_width)
    grad_low = cotangent.reshape(rows_dev, model_width)
    shards = [w_query, w_keyval, w_out, w_shared_in, w_shared_out]
    (
        full_pre,
        full_back,
        full_shared,
        group_one,
        chip_grad,
        chip_two,
        scale_one,
        cosine,
        sine_table,
        begin,
        begin_row,
        *kept,
        hidden_state,
        normed_two,
        scale_two,
        send_rows,
        code,
        order,
    ) = head(
        inputs,
        gain_attn[None],
        gain_ffn[None],
        grad_low,
        doc_lengths,
        routes.reshape(rows_dev, -1),
        shards,
        w_keyval.shape[2] // 2,
        expert_count,
    )
    full_pre, full_back, full_shared, group_one, chip_grad, chip_two = (
        part.reshape(-1, part.shape[-1])
        for part in (full_pre, full_back, full_shared, group_one, chip_grad, chip_two)
    )
    received = exchange(send_rows)
    logits = matmul(normed_two, w_router)
    scores_sig = jnp.where(order >= 0.0, jax.nn.sigmoid(logits), 0.0)
    score_sum = jnp.sum(scores_sig, axis=1, keepdims=True)
    gate_weights = scores_sig / score_sum
    gates = [
        part.T.reshape(-1, BLOCK_EXPERTS, rows_dev) for part in split_low(gate_weights)
    ]
    send_grads, received = lax.optimization_barrier((pack_tokens(code, grad_low, gates), received))
    received_grads = exchange(send_grads)

    shared_width = w_shared_out.shape[1]
    shared_grads, shared_parts, shared_input = [], 0.0, 0.0
    for start in (0, 3 * shared_width):
        in_weights = full_shared[:, start : start + 2 * shared_width]
        out_weights = full_shared[:, start + 2 * shared_width : start + 3 * shared_width]
        shared_pre = matmul(chip_two, in_weights)
        shared_gate, shared_up = shared_pre[:, :shared_width], shared_pre[:, shared_width:]
        shared_act, shared_slope = swish_parts(shared_gate)
        shared_hidden = (shared_act * shared_up).astype(jnp.bfloat16)
        shared_hidden_grad = matmul(chip_grad, out_weights)
        shared_pre_grad = jnp.concatenate(
            [shared_hidden_grad * shared_up * shared_slope, shared_hidden_grad * shared_act],
            axis=1,
        ).astype(jnp.bfloat16)
        shared_grads.append(outer_sum(chip_two, shared_pre_grad).astype(jnp.bfloat16))
        shared_grads.append(outer_sum(chip_grad, shared_hidden).astype(jnp.bfloat16))
        shared_parts = shared_parts + matmul_t(shared_hidden, out_weights)
        shared_input = shared_input + matmul_t(shared_pre_grad, in_weights)
    shared_grads = side_by_side(*shared_grads)
    shared_parts, shared_input = (
        part.astype(jnp.bfloat16).reshape(2, rows_dev, model_width)
        for part in (shared_parts, shared_input)
    )

    expert_in = unpack_slots(received)
    expert_pre = jnp.einsum(
        "esd,edf->esf", expert_in, w_expert_in, preferred_element_type=jnp.float32
    )
    expert_act, expert_slope = swish_parts(expert_pre[..., :expert_ff])
    expert_hidden = (expert_act * expert_pre[..., expert_ff:]).astype(jnp.bfloat16)
    expert_out = jnp.einsum(
        "esf,edf->esd", expert_hidden, w_expert_out, preferred_element_type=jnp.float32
    ).astype(jnp.bfloat16)
    send_out, received_grads = lax.optimization_barrier((pack_slots(expert_out), received_grads))
    returned = exchange(send_out)

    out_grad = unpack_slots(received_grads)
    hidden_grad = jnp.einsum(
        "esd,edf->esf", out_grad, w_expert_out, preferred_element_type=jnp.float32
    )
    expert_pre_grad = jnp.concatenate(
        [hidden_grad * expert_pre[..., expert_ff:] * expert_slope, hidden_grad * expert_act], axis=2
    ).astype(jnp.bfloat16)
    slot_grad = jnp.einsum(
        "esf,edf->esd", expert_pre_grad, w_expert_in, preferred_element_type=jnp.float32
    ).astype(jnp.bfloat16)
    send_back, returned = lax.optimization_barrier((pack_slots(slot_grad), returned))
    returned_grad = exchange(send_back)
    grad_expert_out = jnp.einsum(
        "esd,esf->edf", out_grad, expert_hidden, preferred_element_type=jnp.float32
    )
    grad_expert_in = jnp.einsum(
        "esd,esf->edf", expert_in, expert_pre_grad, preferred_element_type=jnp.float32
    )
    routed_branch, gate_grads = sum_gated(code, returned, send_grads, gates)
    stream = hidden_state + routed_branch
    gate_grads = gate_grads.transpose(1, 0, 2).reshape(rows_dev, expert_count)
    logit_grad = (
        (1.0 - scores_sig)
        * (gate_grads - gate_weights * jnp.sum(gate_grads, axis=1, keepdims=True))
    ).astype(jnp.bfloat16)
    router_parts = outer_sum(normed_two, logit_grad).astype(jnp.bfloat16)
    router_parts = router_parts.reshape(row_count, -1, expert_count)
    router_input = matmul_t(logit_grad, w_router)
    shadowed = (router_input, router_parts, stream, shared_grads, group_one.T, all_marks(code))
    returned_grad, shadowed, grad_expert_in, grad_expert_out = lax.optimization_barrier(
        (returned_grad, shadowed, grad_expert_in, grad_expert_out)
    )
    router_input, router_parts, stream, shared_grads, group_one_t, marks = shadowed

    widths = [part.size // part.shape[0] for part in shards]
    hidden_total, input_back, block_out, router_sum, gain_attn_sum, gain_ffn_sum, *sums = tail(
        (
            returned_grad,
            marks,
            router_input,
            hidden_state,
            group_one_t,
            full_pre,
            full_back,
            shared_parts,
            stream,
            shared_input,
        ),
        (
            scale_two,
            gain_ffn[None],
            grad_low,
            router_parts,
            shared_grads.reshape(2, 4, 4, -1, shared_grads.shape[1]),
        ),
        kept,
        (cosine, sine_table, begin, begin_row),
        (inputs, scale_one, gain_attn[None]),
        widths,
    )
    return (
        block_out.reshape(1, rows_dev, model_width),
        (hidden_total + input_back).reshape(1, rows_dev, model_width),
        gain_attn_sum[0],
        sums[0],
        sums[1],
        sums[2],
        gain_ffn_sum[0],
        sums[3],
        sums[4],
        router_sum.reshape(model_width, expert_count).astype(jnp.float32),
        grad_expert_in,
        grad_expert_out,
    )


def solution(mesh):
    in_specs = (
        P("col", "row", None),
        P(),
        P("col", "row"),
        P("col", "row", None),
        P("col", "row"),
        P(),
        P("col", None, "row"),
        P("col", "row"),
        P(),
        P(("row", "col"), None, None),
        P(("row", "col"), None, None),
        P("col", None),
        P("col", "row", None),
        P("col", "row", None),
    )
    out_specs = (
        P("col", "row", None),
        P("col", "row", None),
        P(),
        P("col", "row"),
        P("col", "row", None),
        P("col", "row"),
        P(),
        P("col", None, "row"),
        P("col", "row"),
        P(),
        P(("row", "col"), None, None),
        P(("row", "col"), None, None),
    )
    return jax.shard_map(
        per_device, mesh=mesh, in_specs=in_specs, out_specs=out_specs, check_vma=False
    )
```
